32 devices in a mesh: blk: 8 (over y, x, core), uly: 4 (over z).
Axes of the slice: x: 2, y: 2, z: 4, core: 2. Of those that a mesh axis runs over, the one named last changes fastest.
Arguments:
- hidden_in: bfloat16 [2048, 3072], P(('blk', 'uly')), may hold values from -6 to 6
- cached_out: bfloat16 [2048, 3072], P(('blk', 'uly')), may hold values from -6 to 6
- cache_keys: bfloat16 [2048, 3072], P(('blk', 'uly')), may hold values from -288 to 288
- cache_values: bfloat16 [2048, 3072], P(('blk', 'uly')), may hold values from -36 to 36
- refresh_idx: int32 [512], P(('blk', 'uly')), may hold values from -1 to 63, as said below
- modulation: float32 [6, 3072], replicated, may hold values from -3 to 3
- q_gain: float32 [128], replicated, may hold values from 1.5 to 4
- w_query: bfloat16 [3072, 3072], P(None, 'uly'), may hold values from -0.109375 to 0.109375
- w_out: bfloat16 [3072, 3072], P('uly'), may hold values from -0.109375 to 0.109375
- w_up: bfloat16 [3072, 12288], P(None, 'blk'), may hold values from -0.109375 to 0.109375
- w_down: bfloat16 [12288, 3072], P('blk'), may hold values from -0.0546875 to 0.0546875
Outputs:
- features: bfloat16 [2048, 3072], P(('blk', 'uly'))
The draws below stay inside these ranges and needn't reach their ends.
Inputs may be any that keep to these rules, and one draw needn't show every extreme that they name: `refresh_idx`: each device's 16 slots name distinct positions among that device's own 64 positions, live slots first and -1 in the rest. Among the devices that share a blk index, one has all 16 slots live and every other at most 8; so such a group has at most 40 live slots, and some group has exactly 40.
All inputs are finite; a program needn't handle non-finite values.
Results may differ from the reference program's by a relative error of at most 0.023.
The reference program's roundings to bfloat16 on the way count: a program that leaves them out, or rounds other values in their place, can miss the bound.
Values may be sent and summed in bfloat16 or wider, within the bound.
No kernel may reach another device: no remote copies, remote signals or barrier semaphores. Data moves between devices by JAX's collectives and lax.ppermute only.
A program may use at most 128 MiB of HBM per device.

```python
import math
import jax
import jax.numpy as jnp
from jax import lax

D = 3072
H = 24
DH = 128
FF = 12288
TOK_DEV = 64
RMAX = 16
OTHER = 8
TOKENS = 2048
N_ULY = 4
DEVICES = 32


def draw_refresh_idx(key, part):
    key = jax.random.fold_in(key, 7)
    hot_key, busy_key, count_key, order_key = jax.random.split(key, 4)
    groups = DEVICES // N_ULY
    hottest = jax.random.randint(hot_key, (groups,), 0, N_ULY)
    busiest = jax.random.randint(busy_key, (), 0, groups)
    counts = jax.random.randint(count_key, (groups, N_ULY), 0, OTHER + 1)
    counts = jnp.where(jnp.arange(groups)[:, None] == busiest, OTHER, counts)
    counts = jnp.where(jnp.arange(N_ULY)[None, :] == hottest[:, None], RMAX, counts)
    device_keys = jax.random.split(order_key, DEVICES)

    def device_order(one_key):
        return jax.random.permutation(one_key, TOK_DEV)[:RMAX]
    orders = jax.vmap(device_order)(device_keys).astype(jnp.int32)
    slot_number = jnp.arange(RMAX)[None, :]
    chosen = jnp.where(slot_number < counts.reshape(DEVICES, 1), orders, -1)
    return chosen.reshape(DEVICES * RMAX).astype(jnp.int32)


def draw_cache_keys(key, part):
    key = jax.random.fold_in(key, 13)
    base_key = jax.random.fold_in(key, 0)
    base = jnp.clip(jax.random.normal(base_key, (TOKENS, D), jnp.float32), -6.0, 6.0)
    return base.astype(jnp.bfloat16)


def level_of(rng, extent, cuts, low, high):
    factor_of, own = 1.0, jax.random.fold_in(rng, 6)
    for axis_at, shards_of in cuts:
        steps = jnp.exp(jax.random.uniform(jax.random.fold_in(own, axis_at), (shards_of,), jnp.float32, low / len(cuts), high / len(cuts)))
        factor_of = factor_of * jnp.repeat(steps, extent[axis_at] // shards_of).reshape([-1 if axis == axis_at else 1 for axis in range(len(extent))])
    return factor_of


def gaussian(rng, dims, scale, reach, cuts=(), kind=jnp.bfloat16):
    factor_of = level_of(rng, dims, cuts, -0.22, 0.18) if cuts else 1.0
    array = jax.random.normal(rng, dims, jnp.float32) * scale * factor_of
    return jnp.minimum(jnp.maximum(array, -reach), reach).astype(kind)


def setup_inputs(seed: int = 0) -> dict:
    arg_keys = jax.random.split(jax.random.key(seed), 12)
    return {
        "hidden_in": gaussian(arg_keys[0], (TOKENS, D), 1.0, 6.0, ((0, 32),)),
        "cached_out": gaussian(arg_keys[1], (TOKENS, D), 1.0, 6.0, ((0, 32),)),
        "cache_keys": draw_cache_keys(jax.random.fold_in(arg_keys[11], 71), 0),
        "cache_values": gaussian(arg_keys[3], (TOKENS, D), 6.0, 36.0, ((0, 32),)),
        "refresh_idx": draw_refresh_idx(jax.random.fold_in(arg_keys[11], 71), 0),
        "modulation": gaussian(arg_keys[5], (6, D), 0.5, 3.0, (), jnp.float32),
        "q_gain": jnp.clip(jnp.exp(jax.random.uniform(arg_keys[6], (DH,), jnp.float32, math.log(1.5), math.log(4.0))), 1.5, 4.0),
        "w_query": gaussian(arg_keys[7], (D, D), D ** -0.5, 0.109375, ((1, 4),)),
        "w_out": gaussian(arg_keys[8], (D, D), D ** -0.5, 0.109375, ((0, 4),)),
        "w_up": gaussian(arg_keys[9], (D, FF), D ** -0.5, 0.109375, ((1, 8),)),
        "w_down": gaussian(arg_keys[10], (FF, D), FF ** -0.5, 0.0546875, ((0, 8),)),
    }


def layer_norm(row_block, shift_by, scale_by):
    average = lax.optimization_barrier(jnp.mean(row_block, axis=-1, keepdims=True))
    centred = row_block - average
    spread = lax.optimization_barrier(jnp.mean(centred * centred, axis=-1, keepdims=True))
    return centred * lax.rsqrt(spread + 1e-06) * (1.0 + scale_by) + shift_by

def reference(hidden_in, cached_out, cache_keys, cache_values, refresh_idx, modulation, q_gain, w_query, w_out, w_up, w_down):
    slot_total = refresh_idx.shape[0]
    owners = jnp.arange(slot_total, dtype=jnp.int32) // RMAX
    filled = refresh_idx >= 0
    where_at = (owners * TOK_DEV + jnp.maximum(refresh_idx, 0)).astype(jnp.int32)
    picked = jnp.take(hidden_in, where_at, axis=0).astype(jnp.float32)
    rows_in = jnp.where(filled[:, None], picked, jnp.zeros((), jnp.float32))
    norm_attn = layer_norm(rows_in, modulation[0], modulation[1]).astype(jnp.bfloat16)
    projected = jnp.dot(norm_attn, w_query, preferred_element_type=jnp.float32).reshape(slot_total, H, DH)
    squares = lax.optimization_barrier(jnp.mean(projected * projected, axis=-1, keepdims=True))
    projected = projected * lax.rsqrt(squares + 1e-06) * (q_gain / math.sqrt(DH))
    queries = jnp.transpose(projected.astype(jnp.bfloat16), (1, 0, 2))
    key_heads = jnp.transpose(cache_keys.reshape(TOKENS, H, DH), (1, 0, 2))
    value_heads = jnp.transpose(cache_values.reshape(TOKENS, H, DH), (1, 0, 2))
    block_rows = math.gcd(slot_total, 512)

    def one_head(inputs):
        query_head, key_head, value_head = inputs
        key_wide = key_head.astype(jnp.float32)
        value_wide = value_head.astype(jnp.float32)

        def one_block(query_block):
            scores = jnp.dot(query_block.astype(jnp.float32), key_wide.T)
            maxima = lax.optimization_barrier(jnp.max(scores, axis=-1, keepdims=True))
            weights = jnp.exp(scores - maxima)
            denominators = lax.optimization_barrier(jnp.sum(weights, axis=-1, keepdims=True))
            rounded = lax.optimization_barrier(weights.astype(jnp.bfloat16))
            weighted = jnp.dot(rounded.astype(jnp.float32), value_wide)
            return (weighted / denominators).astype(jnp.bfloat16)
        return lax.map(one_block, query_head.reshape(-1, block_rows, DH)).reshape(-1, DH)
    attended = lax.map(one_head, (queries, key_heads, value_heads))
    attended = jnp.transpose(attended, (1, 0, 2)).reshape(slot_total, H * DH)
    branch = jnp.dot(attended, w_out, preferred_element_type=jnp.float32)
    after_attn = rows_in + modulation[2] * branch
    norm_mlp = layer_norm(after_attn, modulation[3], modulation[4]).astype(jnp.bfloat16)
    activations = jax.nn.gelu(jnp.dot(norm_mlp, w_up, preferred_element_type=jnp.float32), approximate=True).astype(jnp.bfloat16)
    mlp_out = jnp.dot(activations, w_down, preferred_element_type=jnp.float32)
    renewed = (after_attn + modulation[5] * mlp_out).astype(jnp.bfloat16)
    target = jnp.where(filled, where_at, TOKENS).astype(jnp.int32)
    return cached_out.at[target].set(renewed, mode='drop')
```

```python
import math

import jax
import jax.numpy as jnp
from jax import lax
from jax.sharding import PartitionSpec as P

DH = 128
OTHER = 8


def layer_norm(row_block, shift_by, scale_by):
    average = jnp.mean(row_block, axis=-1, keepdims=True)
    centred = row_block - average
    spread = jnp.mean(centred * centred, axis=-1, keepdims=True)
    return centred * lax.rsqrt(spread + 1e-06) * (1.0 + scale_by) + shift_by


def swap(parts, axis):
    return lax.all_to_all(parts, axis, split_axis=0, concat_axis=0, tiled=True)


def gather_permute(rows, axis):
    size = lax.axis_size(axis)
    me = lax.axis_index(axis)
    pieces = [rows]
    for step in range(1, size):
        pieces.append(lax.ppermute(rows, axis, [(i, (i + step) % size) for i in range(size)]))
    return pieces, me


def body(
    hidden_in,
    cached_out,
    cache_keys,
    cache_values,
    refresh_idx,
    modulation,
    q_gain,
    w_query,
    w_out,
    w_up,
    w_down,
):
    tokens, width = hidden_in.shape
    slots = refresh_idx.shape[0]
    uly_size = lax.axis_size("uly")
    blk_size = lax.axis_size("blk")
    local_heads = w_query.shape[1] // DH
    group = min(slots * uly_size, slots + (uly_size - 1) * OTHER)
    positions = lax.iota(jnp.int32, tokens)
    select = (positions[:, None] == refresh_idx[None, :]).astype(jnp.bfloat16)
    rows_in = jnp.einsum("ps,pd->sd", select, hidden_in, preferred_element_type=jnp.float32)
    norm_attn = layer_norm(rows_in, modulation[0], modulation[1]).astype(jnp.bfloat16)
    live_flag = jnp.broadcast_to((refresh_idx >= 0).astype(jnp.bfloat16)[:, None], (slots, DH))
    group_all = lax.all_gather(
        jnp.concatenate([norm_attn, live_flag], axis=1), "uly", axis=0, tiled=True
    )
    group_rows = group_all[:, :width]
    live = group_all[:, width].astype(jnp.float32)
    key_split = cache_keys.reshape(tokens, uly_size, local_heads, DH)
    value_split = cache_values.reshape(tokens, uly_size, local_heads, DH)
    key_rows = lax.all_to_all(key_split, "uly", split_axis=1, concat_axis=0, tiled=True)[:, 0]
    value_rows = lax.all_to_all(value_split, "uly", split_axis=1, concat_axis=0, tiled=True)[:, 0]

    everyone = slots * uly_size
    order = lax.iota(jnp.int32, everyone)
    before = (order[None, :] < order[:, None]).astype(jnp.float32)
    rank = jnp.sum(before * live[None, :], axis=1)
    compact = (
        (rank[None, :] == lax.iota(jnp.float32, group)[:, None]) & (live[None, :] > 0)
    ).astype(jnp.bfloat16)

    projected = jnp.dot(group_rows, w_query, preferred_element_type=jnp.float32).reshape(
        -1, local_heads, DH
    )
    squares = jnp.mean(projected * projected, axis=-1, keepdims=True)
    projected = projected * lax.rsqrt(squares + 1e-06) * (q_gain / math.sqrt(DH))
    projected = projected.astype(jnp.bfloat16).reshape(everyone, local_heads * DH)
    projected = jnp.dot(compact, projected, preferred_element_type=jnp.float32).astype(jnp.bfloat16)
    queries = lax.all_gather(
        projected.reshape(group, local_heads, DH), "blk", axis=0, tiled=True
    )
    scores = jnp.einsum("qhd,khd->hqk", queries, key_rows, preferred_element_type=jnp.float32)
    maxima = jnp.max(scores, axis=-1)
    weights = jnp.exp(scores - maxima[..., None])
    denominators = jnp.sum(weights, axis=-1)
    weighted = jnp.einsum(
        "hqk,khd->hqd", weights.astype(jnp.bfloat16), value_rows, preferred_element_type=jnp.float32
    )
    extra = jnp.concatenate(
        [
            jnp.broadcast_to(maxima[..., None], maxima.shape + (DH // 2,)),
            jnp.broadcast_to(denominators[..., None], maxima.shape + (DH // 2,)),
        ],
        axis=-1,
    )
    packed = jnp.concatenate([weighted, extra], axis=-1)
    packed = packed.reshape(local_heads, blk_size, group, 2 * DH).transpose(1, 0, 2, 3)
    packed = swap(packed, "blk")
    part_max = packed[..., DH]
    part_sum = packed[..., DH + DH // 2]
    top = jnp.max(part_max, axis=0)
    factor = jnp.exp(part_max - top[None])
    total = jnp.sum(part_sum * factor, axis=0)
    attended = jnp.sum(packed[..., :DH] * factor[..., None], axis=0) / total[..., None]
    attended = attended.astype(jnp.bfloat16).transpose(1, 0, 2).reshape(group, local_heads * DH)
    attended = jnp.dot(compact.T, attended, preferred_element_type=jnp.float32).astype(jnp.bfloat16)
    terms = jnp.dot(attended, w_out, preferred_element_type=jnp.float32)
    terms = swap(terms.reshape(uly_size, slots, width), "uly")
    branch = jnp.sum(terms, axis=0)
    after_attn = rows_in + modulation[2] * branch
    norm_mlp = layer_norm(after_attn, modulation[3], modulation[4]).astype(jnp.bfloat16)
    pieces, me = gather_permute(norm_mlp, "blk")
    lifted = jnp.dot(jnp.concatenate(pieces, axis=0), w_up, preferred_element_type=jnp.float32)
    activations = jax.nn.gelu(lifted, approximate=True).astype(jnp.bfloat16)
    down = jnp.dot(activations, w_down, preferred_element_type=jnp.float32).astype(jnp.bfloat16)
    down = down.reshape(blk_size, slots, width)
    total_down = down[0].astype(jnp.float32)
    for step in range(1, blk_size):
        back = lax.ppermute(
            down[step], "blk", [(i, (i - step) % blk_size) for i in range(blk_size)]
        )
        total_down = total_down + back.astype(jnp.float32)
    renewed = (after_attn + modulation[5] * total_down).astype(jnp.bfloat16)
    covered = jnp.sum(select.astype(jnp.float32), axis=1, keepdims=True)
    placed = jnp.dot(select, renewed, preferred_element_type=jnp.float32)
    blended = cached_out.astype(jnp.float32) * (1.0 - covered) + placed
    return blended.astype(jnp.bfloat16)


def solution(mesh):
    return jax.shard_map(
        body,
        mesh=mesh,
        in_specs=(
            P(("blk", "uly"), None),
            P(("blk", "uly"), None),
            P(("blk", "uly"), None),
            P(("blk", "uly"), None),
            P(("blk", "uly")),
            P(),
            P(),
            P(None, "uly"),
            P("uly", None),
            P(None, "blk"),
            P("blk", None),
        ),
        out_specs=P(("blk", "uly"), None),
        check_vma=False,
    )
```

```python
import math

import jax
import jax.numpy as jnp
from jax import lax
from jax.sharding import PartitionSpec as P

DH = 128
OTHER = 8


def layer_norm(row_block, shift_by, scale_by):
    average = jnp.mean(row_block, axis=-1, keepdims=True)
    centred = row_block - average
    spread = jnp.mean(centred * centred, axis=-1, keepdims=True)
    return centred * lax.rsqrt(spread + 1e-06) * (1.0 + scale_by) + shift_by


def trade(x, axis, flip):
    if flip == 0:
        return x
    return lax.ppermute(x, axis, [(i, i ^ flip) for i in range(lax.axis_size(axis))])


def body(
    hidden_in,
    cached_out,
    cache_keys,
    cache_values,
    refresh_idx,
    modulation,
    q_gain,
    w_query,
    w_out,
    w_up,
    w_down,
):
    f32, bf16 = jnp.float32, jnp.bfloat16
    tokens, width = hidden_in.shape
    slots = refresh_idx.shape[0]
    uly_size = lax.axis_size("uly")
    blk_size = lax.axis_size("blk")
    local_heads = w_query.shape[1] // DH
    group = min(slots * uly_size, slots + (uly_size - 1) * OTHER)
    pair = 2 if blk_size % 2 == 0 and local_heads % 2 == 0 else 1
    chips = blk_size // pair
    heads = local_heads // pair
    half = heads * DH
    me_uly = lax.axis_index("uly")
    core = lax.axis_index("blk") % pair

    positions = lax.iota(jnp.int32, tokens)
    select = (positions[:, None] == refresh_idx[None, :]).astype(bf16)
    rows_in = jnp.einsum("ps,pd->sd", select, hidden_in, preferred_element_type=f32)
    norm_attn = layer_norm(rows_in, modulation[0], modulation[1]).astype(bf16)
    live_flag = jnp.broadcast_to((refresh_idx >= 0).astype(bf16)[:, None], (slots, DH))
    to_group = jnp.concatenate([norm_attn, live_flag], axis=1)
    to_group, cache_keys, cache_values = lax.optimization_barrier(
        (to_group, cache_keys, cache_values)
    )
    group_all = lax.all_gather(to_group, "uly", axis=0, tiled=True)
    group_rows = group_all[:, :width]
    live = group_all[:, width].astype(f32)

    kv_pieces = []
    for flip_core in range(pair):
        for flip_uly in range(uly_size):
            start = ((me_uly ^ flip_uly) * pair + (core ^ flip_core)) * half
            piece = jnp.concatenate(
                [
                    lax.dynamic_slice(cache_keys, (0, start), (tokens, half)),
                    lax.dynamic_slice(cache_values, (0, start), (tokens, half)),
                ],
                axis=1,
            )
            kv_pieces.append(trade(piece, ("blk", "uly"), flip_core * uly_size + flip_uly))

    everyone = slots * uly_size
    order = lax.iota(jnp.int32, everyone)
    before = (order[None, :] < order[:, None]).astype(f32)
    rank = jnp.sum(before * live[None, :], axis=1)
    compact = ((rank[None, :] == lax.iota(f32, group)[:, None]) & (live[None, :] > 0)).astype(bf16)

    projected = jnp.dot(group_rows, w_query, preferred_element_type=f32).reshape(
        -1, local_heads, DH
    )
    squares = jnp.mean(projected * projected, axis=-1, keepdims=True)
    projected = projected * lax.rsqrt(squares + 1e-06) * (q_gain / math.sqrt(DH))
    projected = projected.astype(bf16).reshape(everyone, local_heads * DH)
    projected = jnp.dot(compact, projected, preferred_element_type=f32).astype(bf16)

    mine = lax.dynamic_slice(projected, (0, core * half), (group, half))
    queries = [mine]
    if pair == 2:
        other = lax.dynamic_slice(projected, (0, (1 - core) * half), (group, half))
        queries.append(trade(other, "blk", 1))
    queries = jnp.concatenate(queries, axis=0)
    queries = jnp.concatenate([trade(queries, "blk", j * pair) for j in range(chips)], axis=0)
    queries = queries.reshape(chips * pair * group, heads, DH)
    kv_rows = jnp.concatenate(kv_pieces, axis=0)
    key_rows = kv_rows[:, :half].reshape(-1, heads, DH)
    value_rows = kv_rows[:, half:].reshape(-1, heads, DH)

    scores = jnp.einsum("qhd,khd->hqk", queries, key_rows, preferred_element_type=f32)
    maxima = jnp.max(scores, axis=-1)
    weights = jnp.exp(scores - maxima[..., None])
    denominators = jnp.sum(weights, axis=-1)
    weighted = jnp.einsum(
        "hqk,khd->qhd", weights.astype(bf16), value_rows, preferred_element_type=f32
    )
    stats = jnp.concatenate([maxima, denominators], axis=0).T
    stats = jnp.pad(stats, ((0, 0), (0, DH - 2 * heads)))
    packed = jnp.concatenate([weighted.reshape(-1, half), stats], axis=1)
    packed = packed.reshape(chips, pair * group, half + DH)
    packed = jnp.stack([trade(packed[j], "blk", j * pair) for j in range(chips)])
    part_max = packed[..., half : half + heads]
    part_sum = packed[..., half + heads : half + 2 * heads]
    top = jnp.max(part_max, axis=0)
    factor = jnp.exp(part_max - top[None])
    total = jnp.sum(part_sum * factor, axis=0)
    parts = packed[..., :half].reshape(chips, pair * group, heads, DH)
    attended = jnp.sum(parts * factor[..., None], axis=0) / total[..., None]
    attended = attended.astype(bf16).reshape(pair, group, half)
    if pair == 2:
        theirs = trade(attended[1], "blk", 1)
        attended = jnp.where(
            core == 0,
            jnp.concatenate([attended[0], theirs], axis=1),
            jnp.concatenate([theirs, attended[0]], axis=1),
        )
    else:
        attended = attended[0]
    attended = jnp.dot(compact.T, attended, preferred_element_type=f32).astype(bf16)
    terms = jnp.dot(attended, w_out, preferred_element_type=f32)
    branch = lax.dynamic_slice(terms, (me_uly * slots, 0), (slots, width))
    terms = terms.astype(bf16)
    for flip in range(1, uly_size):
        piece = lax.dynamic_slice(terms, ((me_uly ^ flip) * slots, 0), (slots, width))
        branch = branch + trade(piece, "uly", flip).astype(f32)
    after_attn = rows_in + modulation[2] * branch
    norm_mlp = layer_norm(after_attn, modulation[3], modulation[4]).astype(bf16)

    rows = jnp.concatenate([trade(norm_mlp, "blk", j * pair) for j in range(chips)], axis=0)
    if pair == 2:
        rows = jnp.concatenate([rows, trade(rows, "blk", 1)], axis=0)
    lifted = jnp.dot(rows, w_up, preferred_element_type=f32)
    activations = jax.nn.gelu(lifted, approximate=True).astype(bf16)
    down = jnp.dot(activations, w_down, preferred_element_type=f32)
    down = down.reshape(pair, chips, slots, width)
    plane = down[0]
    if pair == 2:
        plane = plane + trade(down[1].astype(bf16), "blk", 1).astype(f32)
    total_down = plane[0]
    for j in range(1, chips):
        total_down = total_down + trade(plane[j].astype(bf16), "blk", j * pair).astype(f32)
    renewed = (after_attn + modulation[5] * total_down).astype(bf16)
    covered = jnp.sum(select.astype(f32), axis=1, keepdims=True)
    placed = jnp.dot(select, renewed, preferred_element_type=f32)
    blended = cached_out.astype(f32) * (1.0 - covered) + placed
    return blended.astype(bf16)


def solution(mesh):
    return jax.shard_map(
        body,
        mesh=mesh,
        in_specs=(
            P(("blk", "uly"), None),
            P(("blk", "uly"), None),
            P(("blk", "uly"), None),
            P(("blk", "uly"), None),
            P(("blk", "uly")),
            P(),
            P(),
            P(None, "uly"),
            P("uly", None),
            P(None, "blk"),
            P("blk", None),
        ),
        out_specs=P(("blk", "uly"), None),
        check_vma=False,
    )
```

```python
import math

import jax
import jax.numpy as jnp
from jax import lax
from jax.experimental import pallas as pl
from jax.experimental.pallas import tpu as pltpu
from jax.sharding import PartitionSpec as P

DH = 128
OTHER = 8


def layer_norm(row_block, shift_by, scale_by):
    average = jnp.mean(row_block, axis=-1, keepdims=True)
    centred = row_block - average
    spread = jnp.mean(centred * centred, axis=-1, keepdims=True)
    return centred * lax.rsqrt(spread + 1e-06) * (1.0 + scale_by) + shift_by


def trade(x, axis, flip):
    if flip == 0:
        return x
    return lax.ppermute(x, axis, [(i, i ^ flip) for i in range(lax.axis_size(axis))])


def pick_rows_kernel(idx_ref, hidden_ref, mod_ref, rows_ref, normed_ref):
    tokens, width = hidden_ref.shape
    slots = idx_ref.shape[1]
    position = lax.broadcasted_iota(jnp.int32, (tokens, slots), 0)
    select = (position == idx_ref[...]).astype(jnp.float32).astype(jnp.bfloat16)
    contract = (((0,), (0,)), ((), ()))
    rows = lax.dot_general(
        select, hidden_ref[...], contract, preferred_element_type=jnp.float32
    )
    live = lax.dot_general(
        select,
        jnp.ones((tokens, DH), jnp.bfloat16),
        contract,
        preferred_element_type=jnp.float32,
    )
    rows_ref[...] = rows
    normed = layer_norm(rows, mod_ref[0:1, :], mod_ref[1:2, :])
    normed_ref[:, :width] = normed.astype(jnp.bfloat16)
    normed_ref[:, width:] = live.astype(jnp.bfloat16)


def pick_rows(refresh_idx, hidden_in, modulation):
    slots = refresh_idx.shape[0]
    width = hidden_in.shape[1]
    return pl.pallas_call(
        pick_rows_kernel,
        out_shape=(
            jax.ShapeDtypeStruct((slots, width), jnp.float32),
            jax.ShapeDtypeStruct((slots, width + DH), jnp.bfloat16),
        ),
        name="pick_rows",
    )(refresh_idx.reshape(1, slots), hidden_in, modulation)


def stage_kv_kernel(me_ref, after_ref, key_ref, value_ref, *out_refs):
    pair, _, both = out_refs[0].shape
    half = both // 2
    for flip, out_ref in enumerate(out_refs):
        for side in range(pair):
            start = pl.multiple_of(((me_ref[0] ^ flip) * pair + side) * half, DH)
            out_ref[side, :, :half] = key_ref[:, pl.ds(start, half)]
            out_ref[side, :, half:] = value_ref[:, pl.ds(start, half)]


def stage_kv(after, cache_keys, cache_values, parts, pair):
    tokens, width = cache_keys.shape
    both = 2 * width // (parts * pair)
    whole = pl.BlockSpec(memory_space=pltpu.VMEM)
    shape = jax.ShapeDtypeStruct((pair, tokens, both), cache_keys.dtype)
    return pl.pallas_call(
        stage_kv_kernel,
        in_specs=[
            pl.BlockSpec(memory_space=pltpu.SMEM),
            pl.BlockSpec(memory_space=pl.ANY),
            whole,
            whole,
        ],
        out_shape=[shape] * parts,
        name="stage_kv",
    )(lax.axis_index("uly").astype(jnp.int32).reshape(1), after, cache_keys, cache_values)


def body(
    hidden_in,
    cached_out,
    cache_keys,
    cache_values,
    refresh_idx,
    modulation,
    q_gain,
    w_query,
    w_out,
    w_up,
    w_down,
):
    f32, bf16 = jnp.float32, jnp.bfloat16
    tokens, width = hidden_in.shape
    slots = refresh_idx.shape[0]
    uly_size = lax.axis_size("uly")
    blk_size = lax.axis_size("blk")
    local_heads = w_query.shape[1] // DH
    group = min(slots * uly_size, slots + (uly_size - 1) * OTHER)
    pair = 2 if blk_size % 2 == 0 and local_heads % 2 == 0 else 1
    chips = blk_size // pair
    heads = local_heads // pair
    half = heads * DH
    core = lax.axis_index("blk") % pair

    positions = lax.iota(jnp.int32, tokens)
    select = (positions[:, None] == refresh_idx[None, :]).astype(bf16)
    rows_in, normed = pick_rows(refresh_idx, hidden_in, modulation)
    group_all = jnp.concatenate([trade(normed, "uly", k) for k in range(uly_size)], axis=0)
    group_rows = group_all[:, :width]
    live = group_all[:, width].astype(f32)

    kv_parts = stage_kv(normed, cache_keys, cache_values, uly_size, pair)
    kv_parts = jnp.stack([trade(kv_parts[k], "uly", k) for k in range(uly_size)])
    kv_rows = [lax.dynamic_index_in_dim(kv_parts, core, 1, False).reshape(-1, 2 * half)]
    if pair == 2:
        other = lax.dynamic_index_in_dim(kv_parts, 1 - core, 1, False)
        kv_rows.append(trade(other.reshape(-1, 2 * half), "blk", 1))

    everyone = slots * uly_size
    order = lax.iota(jnp.int32, everyone)
    before = (order[None, :] < order[:, None]).astype(f32)
    rank = jnp.sum(before * live[None, :], axis=1)
    compact = ((rank[None, :] == lax.iota(f32, group)[:, None]) & (live[None, :] > 0)).astype(bf16)

    projected = jnp.dot(group_rows, w_query, preferred_element_type=f32).reshape(
        -1, local_heads, DH
    )
    squares = jnp.mean(projected * projected, axis=-1, keepdims=True)
    projected = projected * lax.rsqrt(squares + 1e-06) * (q_gain / math.sqrt(DH))
    projected = projected.astype(bf16).reshape(everyone, local_heads * DH)
    projected = jnp.dot(compact, projected, preferred_element_type=f32).astype(bf16)

    mine = lax.dynamic_slice(projected, (0, core * half), (group, half))
    queries = [mine]
    if pair == 2:
        other = lax.dynamic_slice(projected, (0, (1 - core) * half), (group, half))
        queries.append(trade(other, "blk", 1))
    queries = jnp.concatenate(queries, axis=0)
    queries = jnp.concatenate([trade(queries, "blk", j * pair) for j in range(chips)], axis=0)
    queries = queries.reshape(chips * pair * group, heads, DH)
    kv_rows = jnp.concatenate(kv_rows, axis=0)
    key_rows = kv_rows[:, :half].reshape(-1, heads, DH)
    value_rows = kv_rows[:, half:].reshape(-1, heads, DH)

    scores = jnp.einsum("qhd,khd->hqk", queries, key_rows, preferred_element_type=f32)
    maxima = jnp.max(scores, axis=-1)
    weights = jnp.exp(scores - maxima[..., None])
    denominators = jnp.sum(weights, axis=-1)
    weighted = jnp.einsum(
        "hqk,khd->qhd", weights.astype(bf16), value_rows, preferred_element_type=f32
    )
    stats = jnp.concatenate([maxima, denominators], axis=0).T
    stats = jnp.pad(stats, ((0, 0), (0, DH - 2 * heads)))
    packed = jnp.concatenate([weighted.reshape(-1, half), stats], axis=1)
    packed = packed.reshape(chips, pair * group, half + DH)
    packed = jnp.stack([trade(packed[j], "blk", j * pair) for j in range(chips)])
    part_max = packed[..., half : half + heads]
    part_sum = packed[..., half + heads : half + 2 * heads]
    top = jnp.max(part_max, axis=0)
    factor = jnp.exp(part_max - top[None])
    total = jnp.sum(part_sum * factor, axis=0)
    parts = packed[..., :half].reshape(chips, pair * group, heads, DH)
    attended = jnp.sum(parts * factor[..., None], axis=0) / total[..., None]
    attended = attended.astype(bf16).reshape(pair, group, half)
    if pair == 2:
        theirs = trade(attended[1], "blk", 1)
        attended = jnp.where(
            core == 0,
            jnp.concatenate([attended[0], theirs], axis=1),
            jnp.concatenate([theirs, attended[0]], axis=1),
        )
    else:
        attended = attended[0]
    attended = jnp.dot(compact.T, attended, preferred_element_type=f32).astype(bf16)
    terms = jnp.dot(attended, w_out, preferred_element_type=f32)
    terms = terms.reshape(uly_size, slots, width)
    branch = terms[0]
    for k in range(1, uly_size):
        branch = branch + trade(terms[k].astype(bf16), "uly", k).astype(f32)
    after_attn = rows_in + modulation[2] * branch
    norm_mlp = layer_norm(after_attn, modulation[3], modulation[4]).astype(bf16)

    rows = jnp.concatenate([trade(norm_mlp, "blk", j * pair) for j in range(chips)], axis=0)
    if pair == 2:
        rows = jnp.concatenate([rows, trade(rows, "blk", 1)], axis=0)
    lifted = jnp.dot(rows, w_up, preferred_element_type=f32)
    activations = jax.nn.gelu(lifted, approximate=True).astype(bf16)
    down = jnp.dot(activations, w_down, preferred_element_type=f32)
    down = down.reshape(pair, chips, slots, width)
    plane = down[0]
    if pair == 2:
        plane = plane + trade(down[1].astype(bf16), "blk", 1).astype(f32)
    total_down = plane[0]
    for j in range(1, chips):
        total_down = total_down + trade(plane[j].astype(bf16), "blk", j * pair).astype(f32)
    renewed = (after_attn + modulation[5] * total_down).astype(bf16)
    covered = jnp.sum(select.astype(f32), axis=1, keepdims=True)
    placed = jnp.dot(select, renewed, preferred_element_type=f32)
    blended = cached_out.astype(f32) * (1.0 - covered) + placed
    return blended.astype(bf16)


def solution(mesh):
    return jax.shard_map(
        body,
        mesh=mesh,
        in_specs=(
            P(("blk", "uly"), None),
            P(("blk", "uly"), None),
            P(("blk", "uly"), None),
            P(("blk", "uly"), None),
            P(("blk", "uly")),
            P(),
            P(),
            P(None, "uly"),
            P("uly", None),
            P(None, "blk"),
            P("blk", None),
        ),
        out_specs=P(("blk", "uly"), None),
        check_vma=False,
    )
```

```python
import functools
import math

import jax
import jax.numpy as jnp
from jax import lax
from jax.experimental import pallas as pl
from jax.experimental.pallas import tpu as pltpu
from jax.sharding import PartitionSpec as P

DH = 128
OTHER = 8
SMEM_SPEC = pl.BlockSpec(memory_space=pltpu.SMEM)
VMEM_SPEC = pl.BlockSpec(memory_space=pltpu.VMEM)
ANY_SPEC = pl.BlockSpec(memory_space=pl.ANY)


def layer_norm(row_block, shift_by, scale_by):
    average = jnp.mean(row_block, axis=-1, keepdims=True)
    centred = row_block - average
    spread = jnp.mean(centred * centred, axis=-1, keepdims=True)
    return centred * lax.rsqrt(spread + 1e-06) * (1.0 + scale_by) + shift_by


def trade(x, axis, flip):
    if flip == 0:
        return x
    return lax.ppermute(x, axis, [(i, i ^ flip) for i in range(lax.axis_size(axis))])


def pick_rows_kernel(idx_ref, hidden_ref, mod_ref, rows_ref, normed_ref):
    tokens, width = hidden_ref.shape
    slots = idx_ref.shape[1]
    position = lax.broadcasted_iota(jnp.int32, (tokens, slots), 0)
    select = (position == idx_ref[...]).astype(jnp.float32).astype(jnp.bfloat16)
    contract = (((0,), (0,)), ((), ()))
    rows = lax.dot_general(
        select, hidden_ref[...], contract, preferred_element_type=jnp.float32
    )
    live = lax.dot_general(
        select,
        jnp.ones((tokens, DH), jnp.bfloat16),
        contract,
        preferred_element_type=jnp.float32,
    )
    rows_ref[...] = rows
    normed = layer_norm(rows, mod_ref[0:1, :], mod_ref[1:2, :])
    normed_ref[:, :width] = normed.astype(jnp.bfloat16)
    normed_ref[:, width:] = live.astype(jnp.bfloat16)


def pick_rows(refresh_idx, hidden_in, modulation):
    slots = refresh_idx.shape[0]
    width = hidden_in.shape[1]
    return pl.pallas_call(
        pick_rows_kernel,
        out_shape=(
            jax.ShapeDtypeStruct((slots, width), jnp.float32),
            jax.ShapeDtypeStruct((slots, width + DH), jnp.bfloat16),
        ),
        name="pick_rows",
    )(refresh_idx.reshape(1, slots), hidden_in, modulation)


def stage_kv_kernel(me_ref, after_ref, key_ref, value_ref, *out_refs):
    parts, _, both = out_refs[0].shape
    pair = len(out_refs)
    half = both // 2
    for side, out_ref in enumerate(out_refs):
        for flip in range(parts):
            start = ((me_ref[0] ^ flip) * pair + (me_ref[1] ^ side)) * half
            start = pl.multiple_of(start, DH)
            out_ref[flip, :, :half] = key_ref[:, pl.ds(start, half)]
            out_ref[flip, :, half:] = value_ref[:, pl.ds(start, half)]


def stage_kv(me, after, cache_keys, cache_values, parts, pair):
    tokens, width = cache_keys.shape
    both = 2 * width // (parts * pair)
    shape = jax.ShapeDtypeStruct((parts, tokens, both), cache_keys.dtype)
    return pl.pallas_call(
        stage_kv_kernel,
        in_specs=[SMEM_SPEC, ANY_SPEC, VMEM_SPEC, VMEM_SPEC],
        out_shape=[shape] * pair,
        name="stage_kv",
    )(me, after, cache_keys, cache_values)


def merge_kv_kernel(sides, *refs):
    for flip, out_ref in enumerate(refs[-refs[0].shape[0] :]):
        for side in range(sides):
            out_ref[side] = refs[side][flip]


def merge_kv(sides, after):
    parts, tokens, both = sides[0].shape
    return pl.pallas_call(
        functools.partial(merge_kv_kernel, len(sides)),
        in_specs=[VMEM_SPEC] * len(sides) + [ANY_SPEC] * len(after),
        out_shape=[jax.ShapeDtypeStruct((len(sides), tokens, both), sides[0].dtype)] * parts,
        name="merge_kv",
    )(*sides, *after)


def project_kernel(pieces, me_ref, *refs):
    rows_refs, (w_ref, gain_ref) = refs[:pieces], refs[pieces : pieces + 2]
    *query_refs, spread_ref, heads_ref = refs[pieces + 2 :]
    width = w_ref.shape[0]
    group, half = query_refs[0].shape
    rows = jnp.concatenate([ref[...] for ref in rows_refs], axis=0)
    everyone = rows.shape[0]
    flags = rows[:, width:]
    shape = (everyone, everyone)
    before = lax.broadcasted_iota(jnp.int32, shape, 1) < lax.broadcasted_iota(jnp.int32, shape, 0)
    before = before.astype(jnp.float32).astype(jnp.bfloat16)
    rank = jnp.dot(before, flags, preferred_element_type=jnp.float32)
    lane = lax.broadcasted_iota(jnp.int32, rank.shape, 1).astype(jnp.float32)
    spread = jnp.where((rank == lane) & (flags.astype(jnp.float32) > 0.0), 1.0, 0.0)
    spread = spread.astype(jnp.bfloat16)
    spread_ref[...] = spread
    live_rows = lax.dot_general(
        spread[:, :group],
        rows[:, :width],
        (((0,), (0,)), ((), ())),
        preferred_element_type=jnp.float32,
    ).astype(jnp.bfloat16)
    projected = jnp.dot(live_rows, w_ref[...], preferred_element_type=jnp.float32)
    for start in range(0, projected.shape[1], DH):
        head = projected[:, start : start + DH]
        squares = jnp.mean(head * head, axis=-1, keepdims=True)
        heads_ref[:, start : start + DH] = (
            head * lax.rsqrt(squares + 1e-06) * (gain_ref[...] / math.sqrt(DH))
        )
    for side, query_ref in enumerate(query_refs):
        start = pl.multiple_of((me_ref[1] ^ side) * half, DH)
        query_ref[...] = heads_ref[:, pl.ds(start, half)].astype(jnp.bfloat16)


def project(me, rows, w_query, q_gain, group, pair):
    half = w_query.shape[1] // pair
    everyone = len(rows) * rows[0].shape[0]
    query = jax.ShapeDtypeStruct((group, half), jnp.bfloat16)
    out = pl.pallas_call(
        functools.partial(project_kernel, len(rows)),
        in_specs=[SMEM_SPEC] + [VMEM_SPEC] * (len(rows) + 2),
        out_shape=[query] * pair + [jax.ShapeDtypeStruct((everyone, DH), jnp.bfloat16)],
        scratch_shapes=[pltpu.VMEM((group, w_query.shape[1]), jnp.float32)],
        compiler_params=pltpu.CompilerParams(vmem_limit_bytes=16 << 20),
        name="project",
    )(me, *rows, w_query, q_gain.reshape(1, DH))
    return out[:-1], out[-1]


def attend_kernel(pieces, parts, *refs):
    query_refs, kv_refs, out_refs = refs[:pieces], refs[pieces:-pieces], refs[-pieces:]
    rows, half = query_refs[0].shape
    sides = kv_refs[0].shape[0]
    lane = lax.broadcasted_iota(jnp.int32, (DH, DH), 1)
    for at in range(0, pieces, 4):
        stop = min(at + 4, pieces)
        queries = jnp.concatenate([ref[...] for ref in query_refs[at:stop]], axis=0)
        stats = [jnp.zeros((DH, DH), jnp.float32) for _ in range(at, stop)]
        for head in range(half // DH):
            cols = slice(head * DH, (head + 1) * DH)
            vals = slice(half + head * DH, half + (head + 1) * DH)
            keys = [ref[side, :, cols] for ref in kv_refs for side in range(sides)]
            values = [ref[side, :, vals] for ref in kv_refs for side in range(sides)]
            scores = lax.dot_general(
                queries[:, cols],
                jnp.concatenate(keys, axis=0),
                (((1,), (1,)), ((), ())),
                preferred_element_type=jnp.float32,
            )
            maxima = jnp.max(scores, axis=-1, keepdims=True)
            weights = jnp.exp(scores - maxima)
            sums = jnp.sum(weights, axis=-1, keepdims=True)
            weighted = jnp.dot(
                weights.astype(jnp.bfloat16),
                jnp.concatenate(values, axis=0),
                preferred_element_type=jnp.float32,
            )
            for j in range(at, stop):
                mine = slice((j - at) * rows, (j - at + 1) * rows)
                out_refs[j][:rows, cols] = weighted[mine]
                pad = jnp.zeros((DH - rows, 1), jnp.float32)
                top = jnp.concatenate([maxima[mine], pad], axis=0)
                total = jnp.concatenate([sums[mine], pad], axis=0)
                stat = jnp.where(lane == 2 * head, top, stats[j - at])
                stats[j - at] = jnp.where(lane == 2 * head + 1, total, stat)
        for j in range(at, stop):
            out_refs[j][rows:, DH:] = jnp.zeros((8, half - DH), jnp.float32)
            out_refs[j][rows:, :DH] = stats[j - at].T[:8]


def attend(queries, kv_parts):
    rows, half = queries[0].shape
    return pl.pallas_call(
        functools.partial(attend_kernel, len(queries), len(kv_parts)),
        out_shape=[jax.ShapeDtypeStruct((rows + 8, half), jnp.float32)] * len(queries),
        compiler_params=pltpu.CompilerParams(vmem_limit_bytes=24 << 20),
        name="attend",
    )(*queries, *kv_parts)


def combine_kernel(pieces, *refs):
    part_refs, out_refs = refs[:pieces], refs[pieces:]
    group, half = out_refs[0].shape
    rows = group * len(out_refs)
    stats = []
    for ref in part_refs:
        packed = ref[rows:, :DH]
        packed = jnp.concatenate([packed, jnp.zeros((DH - 8, DH), jnp.float32)], axis=0)
        stats.append(packed.T[:rows])
    for head in range(half // DH):
        cols = slice(head * DH, (head + 1) * DH)
        maxima = [stat[:, 2 * head : 2 * head + 1] for stat in stats]
        top = functools.reduce(jnp.maximum, maxima)
        total = jnp.zeros_like(top)
        attended = jnp.zeros((rows, DH), jnp.float32)
        for ref, stat, maximum in zip(part_refs, stats, maxima):
            factor = jnp.exp(maximum - top)
            total = total + stat[:, 2 * head + 1 : 2 * head + 2] * factor
            attended = attended + ref[:rows, cols] * factor
        attended = attended / total
        for side, out_ref in enumerate(out_refs):
            out_ref[:, cols] = attended[side * group : (side + 1) * group].astype(jnp.bfloat16)


def combine(parts, group, pair):
    half = parts[0].shape[1]
    return pl.pallas_call(
        functools.partial(combine_kernel, len(parts)),
        out_shape=[jax.ShapeDtypeStruct((group, half), jnp.bfloat16)] * pair,
        compiler_params=pltpu.CompilerParams(vmem_limit_bytes=16 << 20),
        name="combine",
    )(*parts)


def output_kernel(sides, me_ref, spread_ref, *refs):
    side_refs, w_ref, out_refs = refs[:sides], refs[sides], refs[sides + 1 :]
    group, half = side_refs[0].shape
    slots, width = out_refs[0].shape
    spread = spread_ref[:, :group]
    attended = [
        jnp.dot(spread, ref[...], preferred_element_type=jnp.float32).astype(jnp.bfloat16)
        for ref in side_refs
    ]
    starts = [pl.multiple_of((me_ref[1] ^ side) * half, DH) for side in range(sides)]
    step = math.gcd(width, 1024)
    for col in range(0, width, step):
        terms = jnp.zeros((spread.shape[0], step), jnp.float32)
        for start, side in zip(starts, attended):
            terms = terms + jnp.dot(
                side, w_ref[pl.ds(start, half), col : col + step], preferred_element_type=jnp.float32
            )
        for k, out_ref in enumerate(out_refs):
            piece = terms[k * slots : (k + 1) * slots]
            out_ref[:, col : col + step] = piece.astype(out_ref.dtype)


def output(me, spread, sides, w_out, slots, parts):
    width = w_out.shape[1]
    return pl.pallas_call(
        functools.partial(output_kernel, len(sides)),
        in_specs=[SMEM_SPEC] + [VMEM_SPEC] * (len(sides) + 2),
        out_shape=[
            jax.ShapeDtypeStruct((slots, width), jnp.bfloat16 if k else jnp.float32)
            for k in range(parts)
        ],
        compiler_params=pltpu.CompilerParams(vmem_limit_bytes=16 << 20),
        name="output",
    )(me, spread, *sides, w_out)


def mlp_kernel(pieces, *refs):
    row_refs, (up_ref, down_hbm_ref) = refs[:pieces], refs[pieces : pieces + 2]
    *out_refs, act_ref, down_ref, sem = refs[pieces + 2 :]
    hidden, width = down_ref.shape
    copy = pltpu.make_async_copy(down_hbm_ref, down_ref, sem)
    copy.start()
    rows = jnp.concatenate([ref[...] for ref in row_refs], axis=0)
    count = out_refs[0].shape[0]
    step = math.gcd(hidden, 512)
    for col in range(0, hidden, step):
        lifted = jnp.dot(rows, up_ref[:, col : col + step], preferred_element_type=jnp.float32)
        act_ref[:, col : col + step] = jax.nn.gelu(lifted, approximate=True).astype(jnp.bfloat16)
    copy.wait()
    step = math.gcd(width, 512)
    for col in range(0, width, step):
        down = jnp.dot(
            act_ref[...], down_ref[:, col : col + step], preferred_element_type=jnp.float32
        )
        for side, out_ref in enumerate(out_refs):
            piece = down[side * count : (side + 1) * count]
            out_ref[:, col : col + step] = piece.astype(out_ref.dtype)


def mlp(rows, w_up, w_down, pair):
    count = sum(x.shape[0] for x in rows)
    hidden, width = w_down.shape
    return pl.pallas_call(
        functools.partial(mlp_kernel, len(rows)),
        in_specs=[VMEM_SPEC] * (len(rows) + 1) + [ANY_SPEC],
        out_shape=[
            jax.ShapeDtypeStruct((count // pair, width), jnp.bfloat16 if side else jnp.float32)
            for side in range(pair)
        ],
        scratch_shapes=[
            pltpu.VMEM((count, hidden), jnp.bfloat16),
            pltpu.VMEM(w_down.shape, w_down.dtype),
            pltpu.SemaphoreType.DMA,
        ],
        compiler_params=pltpu.CompilerParams(vmem_limit_bytes=32 << 20),
        name="mlp",
    )(*rows, w_up, w_down)


def body(
    hidden_in,
    cached_out,
    cache_keys,
    cache_values,
    refresh_idx,
    modulation,
    q_gain,
    w_query,
    w_out,
    w_up,
    w_down,
):
    f32, bf16 = jnp.float32, jnp.bfloat16
    tokens = hidden_in.shape[0]
    slots = refresh_idx.shape[0]
    uly_size = lax.axis_size("uly")
    blk_size = lax.axis_size("blk")
    local_heads = w_query.shape[1] // DH
    group = min(slots * uly_size, slots + (uly_size - 1) * OTHER)
    pair = 2 if blk_size % 2 == 0 and local_heads % 2 == 0 else 1
    chips = blk_size // pair
    me = jnp.stack([lax.axis_index("uly"), lax.axis_index("blk") % pair]).astype(jnp.int32)

    rows_in, normed = pick_rows(refresh_idx, hidden_in, modulation)
    group_rows = [trade(normed, "uly", k) for k in range(uly_size)]

    sides = stage_kv(me, group_rows[-1 if uly_size == 1 else 1], cache_keys, cache_values, uly_size, pair)
    sides = [trade(x, "blk", side) for side, x in enumerate(sides)]
    kv_parts = merge_kv(sides, group_rows[1:])
    kv_parts = [trade(x, "uly", k) for k, x in enumerate(kv_parts)]

    queries, spread = project(me, group_rows, w_query, q_gain, group, pair)
    queries = jnp.concatenate([trade(x, "blk", side) for side, x in enumerate(queries)], axis=0)
    queries = [trade(queries, "blk", j * pair) for j in range(chips)]
    parts = attend(queries, kv_parts)
    parts = [trade(x, "blk", j * pair) for j, x in enumerate(parts)]
    attended = combine(parts, group, pair)
    attended = [trade(x, "blk", side) for side, x in enumerate(attended)]
    terms = output(me, spread, attended, w_out, slots, uly_size)
    branch = terms[0]
    for k in range(1, uly_size):
        branch = branch + trade(terms[k], "uly", k).astype(f32)
    after_attn = rows_in + modulation[2] * branch
    norm_mlp = layer_norm(after_attn, modulation[3], modulation[4]).astype(bf16)

    rows = [trade(norm_mlp, "blk", j * pair) for j in range(chips)]
    if pair == 2:
        rows.append(trade(jnp.concatenate(rows, axis=0), "blk", 1))
    down = mlp(rows, w_up, w_down, pair)
    plane = down[0]
    if pair == 2:
        plane = plane + trade(down[1], "blk", 1).astype(f32)
    plane = plane.reshape(chips, slots, -1)
    total_down = plane[0]
    for j in range(1, chips):
        total_down = total_down + trade(plane[j].astype(bf16), "blk", j * pair).astype(f32)
    renewed = (after_attn + modulation[5] * total_down).astype(bf16)
    positions = lax.iota(jnp.int32, tokens)
    select = (positions[:, None] == refresh_idx[None, :]).astype(bf16)
    covered = jnp.sum(select.astype(f32), axis=1, keepdims=True)
    placed = jnp.dot(select, renewed, preferred_element_type=f32)
    blended = cached_out.astype(f32) * (1.0 - covered) + placed
    return blended.astype(bf16)


def solution(mesh):
    return jax.shard_map(
        body,
        mesh=mesh,
        in_specs=(
            P(("blk", "uly"), None),
            P(("blk", "uly"), None),
            P(("blk", "uly"), None),
            P(("blk", "uly"), None),
            P(("blk", "uly")),
            P(),
            P(),
            P(None, "uly"),
            P("uly", None),
            P(None, "blk"),
            P("blk", None),
        ),
        out_specs=P(("blk", "uly"), None),
        check_vma=False,
    )
```

```python
import functools
import math

import jax
import jax.numpy as jnp
from jax import lax
from jax.experimental import pallas as pl
from jax.experimental.pallas import tpu as pltpu
from jax.sharding import PartitionSpec as P

DH = 128
OTHER = 8
VMEM_SPEC = pl.BlockSpec(memory_space=pltpu.VMEM)
TOKEN = jax.ShapeDtypeStruct((8, DH), jnp.float32)
ANY_SPEC = pl.BlockSpec(memory_space=pl.ANY)


def layer_norm(row_block, shift_by, scale_by):
    average = jnp.mean(row_block, axis=-1, keepdims=True)
    centred = row_block - average
    spread = jnp.mean(centred * centred, axis=-1, keepdims=True)
    return centred * lax.rsqrt(spread + 1e-06) * (1.0 + scale_by) + shift_by


def trade(x, axis, flip):
    if flip == 0:
        return x
    return lax.ppermute(x, axis, [(i, i ^ flip) for i in range(lax.axis_size(axis))])


def in_hbm(x):
    return pltpu.with_memory_space_constraint(x, pltpu.HBM)


def hold_kernel(count, *refs):
    source_refs, sems = refs[1 : count + 1], refs[-1]
    *held_refs, token_ref = refs[count + 1 : -1]
    token_ref[...] = jnp.zeros_like(token_ref)
    copies = [
        pltpu.make_async_copy(source_ref, held_ref, sems.at[i])
        for i, (source_ref, held_ref) in enumerate(zip(source_refs, held_refs))
    ]
    for copy in copies:
        copy.start()
    for copy in copies:
        copy.wait()


def hold(after, *weights):
    count = len(weights)
    moved = sum(w.size * w.dtype.itemsize for w in weights)
    return pl.pallas_call(
        functools.partial(hold_kernel, count),
        in_specs=[VMEM_SPEC] + [ANY_SPEC] * count,
        out_specs=[VMEM_SPEC] * (count + 1),
        out_shape=[pltpu.VMEM(w.shape, w.dtype) for w in weights] + [TOKEN],
        scratch_shapes=[pltpu.SemaphoreType.DMA((count,))],
        cost_estimate=pl.CostEstimate(flops=0, bytes_accessed=moved, transcendentals=0),
        compiler_params=pltpu.CompilerParams(vmem_limit_bytes=2 << 20),
        name="hold",
    )(after, *[in_hbm(w) for w in weights])


def my_core(pair):
    return lax.rem(lax.axis_index("blk"), pair)


def enter_kernel(pair, idx_hbm, hidden_hbm, mod_hbm, key_hbm, value_hbm, *refs):
    rows_ref, normed_ref, select_ref, mod_ref, *side_refs = refs[: pair + 4]
    idx_ref, hidden_ref, sems, kv_sem = refs[pair + 4 :]
    copies = [
        pltpu.make_async_copy(source, target, sems.at[i])
        for i, (source, target) in enumerate(
            [(idx_hbm, idx_ref), (hidden_hbm, hidden_ref), (mod_hbm, mod_ref)]
        )
    ]
    for copy in copies:
        copy.start()
    parts, _, both = side_refs[0].shape
    half = both // 2
    uly, core = lax.axis_index("uly"), my_core(pair)
    kv_copies = []
    for side, side_ref in enumerate(side_refs):
        for flip in range(parts):
            start = pl.multiple_of(((uly ^ flip) * pair + (core ^ side)) * half, DH)
            for at, source in enumerate((key_hbm, value_hbm)):
                copy = pltpu.make_async_copy(
                    source.at[:, pl.ds(start, half)],
                    side_ref.at[flip, :, pl.ds(at * half, half)],
                    kv_sem.at[side, flip, at],
                )
                copy.start()
                kv_copies.append(copy)
    for copy in copies:
        copy.wait()
    tokens, width = hidden_ref.shape
    slots = idx_ref.shape[1]
    position = lax.broadcasted_iota(jnp.int32, (tokens, slots), 0)
    select = (position == idx_ref[...]).astype(jnp.float32).astype(jnp.bfloat16)
    select_ref[...] = select
    contract = (((0,), (0,)), ((), ()))
    rows = lax.dot_general(
        select, hidden_ref[...], contract, preferred_element_type=jnp.float32
    )
    live = lax.dot_general(
        select,
        jnp.ones((tokens, DH), jnp.bfloat16),
        contract,
        preferred_element_type=jnp.float32,
    )
    rows_ref[...] = rows
    normed = layer_norm(rows, mod_ref[0:1, :], mod_ref[1:2, :])
    normed_ref[:, :width] = normed.astype(jnp.bfloat16)
    normed_ref[:, width:] = live.astype(jnp.bfloat16)
    for copy in kv_copies:
        copy.wait()


def enter(refresh_idx, hidden_in, modulation, cache_keys, cache_values, parts, pair):
    slots = refresh_idx.shape[0]
    tokens, width = hidden_in.shape
    both = 2 * width // (parts * pair)
    out = pl.pallas_call(
        functools.partial(enter_kernel, pair),
        in_specs=[ANY_SPEC] * 5,
        out_specs=[VMEM_SPEC] * (pair + 4),
        out_shape=[
            pltpu.VMEM((slots, width), jnp.float32),
            pltpu.VMEM((slots, width + DH), jnp.bfloat16),
            pltpu.VMEM((tokens, slots), jnp.bfloat16),
            pltpu.VMEM(modulation.shape, modulation.dtype),
        ]
        + [pltpu.VMEM((parts, tokens, both), cache_keys.dtype)] * pair,
        scratch_shapes=[
            pltpu.VMEM((1, slots), jnp.int32),
            pltpu.VMEM(hidden_in.shape, hidden_in.dtype),
            pltpu.SemaphoreType.DMA((3,)),
            pltpu.SemaphoreType.DMA((pair, parts, 2)),
        ],
        compiler_params=pltpu.CompilerParams(vmem_limit_bytes=8 << 20),
        name="enter",
    )(
        *[
            in_hbm(x)
            for x in (refresh_idx.reshape(1, slots), hidden_in, modulation, cache_keys, cache_values)
        ]
    )
    return *out[:4], out[4:]


def merge_kv_kernel(sides, *refs):
    *refs, token_ref = refs
    token_ref[...] = jnp.zeros_like(token_ref)
    for flip, out_ref in enumerate(refs[-refs[0].shape[0] :]):
        for side in range(sides):
            out_ref[side] = refs[side][flip]


def merge_kv(sides, after):
    parts, tokens, both = sides[0].shape
    return pl.pallas_call(
        functools.partial(merge_kv_kernel, len(sides)),
        out_specs=[VMEM_SPEC] * (parts + 1),
        out_shape=[pltpu.VMEM((len(sides), tokens, both), sides[0].dtype)] * parts + [TOKEN],
        compiler_params=pltpu.CompilerParams(vmem_limit_bytes=8 << 20),
        name="merge_kv",
    )(*sides, *after)


def project_kernel(pieces, after_ref, *refs):
    rows_refs, (w_ref, gain_hbm_ref) = refs[:pieces], refs[pieces : pieces + 2]
    *query_refs, spread_ref, token_ref, heads_ref, gain_ref, sem = refs[pieces + 2 :]
    token_ref[...] = jnp.zeros_like(token_ref)
    copy = pltpu.make_async_copy(gain_hbm_ref, gain_ref, sem)
    copy.start()
    core = my_core(len(query_refs))
    width = w_ref.shape[0]
    group, half = query_refs[0].shape
    rows = jnp.concatenate([ref[...] for ref in rows_refs], axis=0)
    everyone = rows.shape[0]
    flags = rows[:, width:]
    shape = (everyone, everyone)
    before = lax.broadcasted_iota(jnp.int32, shape, 1) < lax.broadcasted_iota(jnp.int32, shape, 0)
    before = before.astype(jnp.float32).astype(jnp.bfloat16)
    rank = jnp.dot(before, flags, preferred_element_type=jnp.float32)
    lane = lax.broadcasted_iota(jnp.int32, rank.shape, 1).astype(jnp.float32)
    spread = jnp.where((rank == lane) & (flags.astype(jnp.float32) > 0.0), 1.0, 0.0)
    spread = spread.astype(jnp.bfloat16)
    spread_ref[...] = spread
    live_rows = lax.dot_general(
        spread[:, :group],
        rows[:, :width],
        (((0,), (0,)), ((), ())),
        preferred_element_type=jnp.float32,
    ).astype(jnp.bfloat16)
    projected = jnp.dot(live_rows, w_ref[...], preferred_element_type=jnp.float32)
    copy.wait()
    for start in range(0, projected.shape[1], DH):
        head = projected[:, start : start + DH]
        squares = jnp.mean(head * head, axis=-1, keepdims=True)
        heads_ref[:, start : start + DH] = (
            head * lax.rsqrt(squares + 1e-06) * (gain_ref[...] / math.sqrt(DH))
        )
    for side, query_ref in enumerate(query_refs):
        start = pl.multiple_of((core ^ side) * half, DH)
        query_ref[...] = heads_ref[:, pl.ds(start, half)].astype(jnp.bfloat16)


def project(after, rows, w_query, q_gain, group, pair):
    half = w_query.shape[1] // pair
    everyone = len(rows) * rows[0].shape[0]
    query = jax.ShapeDtypeStruct((group, half), jnp.bfloat16)
    out = pl.pallas_call(
        functools.partial(project_kernel, len(rows)),
        in_specs=[VMEM_SPEC] * (len(rows) + 2) + [ANY_SPEC],
        out_shape=[query] * pair + [jax.ShapeDtypeStruct((everyone, DH), jnp.bfloat16), TOKEN],
        scratch_shapes=[
            pltpu.VMEM((group, w_query.shape[1]), jnp.float32),
            pltpu.VMEM((1, DH), jnp.float32),
            pltpu.SemaphoreType.DMA,
        ],
        compiler_params=pltpu.CompilerParams(vmem_limit_bytes=16 << 20),
        name="project",
    )(after, *rows, w_query, in_hbm(q_gain.reshape(1, DH)))
    return out[:-2], out[-2], out[-1]


def attend_kernel(pieces, after_ref, *refs):
    query_refs, kv_refs, out_refs = refs[:pieces], refs[pieces:-pieces], refs[-pieces:]
    cores, group, half = query_refs[0].shape
    rows = cores * group
    sides = kv_refs[0].shape[0]
    lane = lax.broadcasted_iota(jnp.int32, (DH, DH), 1)
    for at in range(0, pieces, 4):
        stop = min(at + 4, pieces)
        queries = [ref[core] for ref in query_refs[at:stop] for core in range(cores)]
        queries = [x.astype(jnp.float32) for x in queries]
        queries = jnp.concatenate(queries, axis=0).astype(jnp.bfloat16)
        stats = [jnp.zeros((DH, DH), jnp.float32) for _ in range(at, stop)]
        for head in range(half // DH):
            cols = slice(head * DH, (head + 1) * DH)
            vals = slice(half + head * DH, half + (head + 1) * DH)
            keys = [ref[side, :, cols] for ref in kv_refs for side in range(sides)]
            values = [ref[side, :, vals] for ref in kv_refs for side in range(sides)]
            scores = lax.dot_general(
                queries[:, cols],
                jnp.concatenate(keys, axis=0),
                (((1,), (1,)), ((), ())),
                preferred_element_type=jnp.float32,
            )
            maxima = jnp.max(scores, axis=-1, keepdims=True)
            weights = jnp.exp(scores - maxima)
            sums = jnp.sum(weights, axis=-1, keepdims=True)
            weighted = jnp.dot(
                weights.astype(jnp.bfloat16),
                jnp.concatenate(values, axis=0),
                preferred_element_type=jnp.float32,
            )
            for j in range(at, stop):
                mine = slice((j - at) * rows, (j - at + 1) * rows)
                out_refs[j][:rows, cols] = weighted[mine]
                pad = jnp.zeros((DH - rows, 1), jnp.float32)
                top = jnp.concatenate([maxima[mine], pad], axis=0)
                total = jnp.concatenate([sums[mine], pad], axis=0)
                stat = jnp.where(lane == 2 * head, top, stats[j - at])
                stats[j - at] = jnp.where(lane == 2 * head + 1, total, stat)
        for j in range(at, stop):
            out_refs[j][rows:, DH:] = jnp.zeros((8, half - DH), jnp.float32)
            out_refs[j][rows:, :DH] = stats[j - at].T[:8]


def attend(after, queries, kv_parts):
    cores, group, half = queries[0].shape
    rows = cores * group
    return pl.pallas_call(
        functools.partial(attend_kernel, len(queries)),
        out_shape=[jax.ShapeDtypeStruct((rows + 8, half), jnp.float32)] * len(queries),
        compiler_params=pltpu.CompilerParams(vmem_limit_bytes=24 << 20),
        name="attend",
    )(after, *queries, *kv_parts)


def combine_kernel(pieces, *refs):
    part_refs, out_refs = refs[:pieces], refs[pieces:]
    group, half = out_refs[0].shape
    rows = group * len(out_refs)
    stats = []
    for ref in part_refs:
        packed = ref[rows:, :DH]
        packed = jnp.concatenate([packed, jnp.zeros((DH - 8, DH), jnp.float32)], axis=0)
        stats.append(packed.T[:rows])
    for head in range(half // DH):
        cols = slice(head * DH, (head + 1) * DH)
        maxima = [stat[:, 2 * head : 2 * head + 1] for stat in stats]
        top = functools.reduce(jnp.maximum, maxima)
        total = jnp.zeros_like(top)
        attended = jnp.zeros((rows, DH), jnp.float32)
        for ref, stat, maximum in zip(part_refs, stats, maxima):
            factor = jnp.exp(maximum - top)
            total = total + stat[:, 2 * head + 1 : 2 * head + 2] * factor
            attended = attended + ref[:rows, cols] * factor
        attended = attended / total
        for side, out_ref in enumerate(out_refs):
            out_ref[:, cols] = attended[side * group : (side + 1) * group].astype(jnp.bfloat16)


def combine(parts, group, pair):
    half = parts[0].shape[1]
    return pl.pallas_call(
        functools.partial(combine_kernel, len(parts)),
        out_shape=[jax.ShapeDtypeStruct((group, half), jnp.bfloat16)] * pair,
        compiler_params=pltpu.CompilerParams(vmem_limit_bytes=16 << 20),
        name="combine",
    )(*parts)


def output_kernel(sides, spread_ref, *refs):
    side_refs, w_ref, out_refs = refs[:sides], refs[sides], refs[sides + 1 :]
    group, half = side_refs[0].shape
    slots, width = out_refs[0].shape
    spread = spread_ref[:, :group]
    attended = [
        jnp.dot(spread, ref[...], preferred_element_type=jnp.float32).astype(jnp.bfloat16)
        for ref in side_refs
    ]
    core = my_core(sides)
    starts = [pl.multiple_of((core ^ side) * half, DH) for side in range(sides)]
    step = math.gcd(width, 1024)
    for col in range(0, width, step):
        terms = jnp.zeros((spread.shape[0], step), jnp.float32)
        for start, side in zip(starts, attended):
            terms = terms + jnp.dot(
                side, w_ref[pl.ds(start, half), col : col + step], preferred_element_type=jnp.float32
            )
        for k, out_ref in enumerate(out_refs):
            piece = terms[k * slots : (k + 1) * slots]
            out_ref[:, col : col + step] = piece.astype(out_ref.dtype)


def output(spread, sides, w_out, slots, parts):
    width = w_out.shape[1]
    return pl.pallas_call(
        functools.partial(output_kernel, len(sides)),
        out_shape=[
            jax.ShapeDtypeStruct((slots, width), jnp.bfloat16 if k else jnp.float32)
            for k in range(parts)
        ],
        compiler_params=pltpu.CompilerParams(vmem_limit_bytes=16 << 20),
        name="output",
    )(spread, *sides, w_out)


def mlp_kernel(pieces, *refs):
    row_refs, (up_ref, down_ref) = refs[:pieces], refs[pieces : pieces + 2]
    *out_refs, act_ref = refs[pieces + 2 :]
    hidden, width = down_ref.shape
    rows = [ref[j] for ref in row_refs for j in range(ref.shape[0])]
    rows = jnp.concatenate(rows, axis=0)
    count = out_refs[0].shape[0]
    step = math.gcd(hidden, 512)
    for col in range(0, hidden, step):
        lifted = jnp.dot(rows, up_ref[:, col : col + step], preferred_element_type=jnp.float32)
        act_ref[:, col : col + step] = jax.nn.gelu(lifted, approximate=True).astype(jnp.bfloat16)
    step = math.gcd(width, 512)
    for col in range(0, width, step):
        down = jnp.dot(
            act_ref[...], down_ref[:, col : col + step], preferred_element_type=jnp.float32
        )
        for side, out_ref in enumerate(out_refs):
            piece = down[side * count : (side + 1) * count]
            out_ref[:, col : col + step] = piece.astype(out_ref.dtype)


def mlp(rows, w_up, w_down, pair):
    count = sum(x.shape[0] * x.shape[1] for x in rows)
    hidden, width = w_down.shape
    return pl.pallas_call(
        functools.partial(mlp_kernel, len(rows)),
        out_shape=[
            jax.ShapeDtypeStruct((count // pair, width), jnp.bfloat16 if side else jnp.float32)
            for side in range(pair)
        ],
        scratch_shapes=[pltpu.VMEM((count, hidden), jnp.bfloat16)],
        compiler_params=pltpu.CompilerParams(vmem_limit_bytes=32 << 20),
        name="mlp",
    )(*rows, w_up, w_down)


def join_kernel(*refs):
    *part_refs, out_ref = refs
    for at, ref in enumerate(part_refs):
        out_ref[at] = ref[...]


def join(parts):
    return pl.pallas_call(
        join_kernel,
        out_shape=jax.ShapeDtypeStruct((len(parts), *parts[0].shape), parts[0].dtype),
        compiler_params=pltpu.CompilerParams(vmem_limit_bytes=8 << 20),
        name="join",
    )(*parts)


def renorm_kernel(rows_ref, mod_ref, *refs):
    *term_refs, after_ref, normed_ref = refs
    branch = term_refs[0][...]
    for ref in term_refs[1:]:
        branch = branch + ref[...].astype(jnp.float32)
    after = rows_ref[...] + mod_ref[2:3, :] * branch
    after_ref[...] = after
    normed_ref[...] = layer_norm(after, mod_ref[3:4, :], mod_ref[4:5, :]).astype(jnp.bfloat16)


def renorm(rows_in, modulation, terms):
    return pl.pallas_call(
        renorm_kernel,
        out_shape=[
            jax.ShapeDtypeStruct(rows_in.shape, jnp.float32),
            jax.ShapeDtypeStruct(rows_in.shape, jnp.bfloat16),
        ],
        compiler_params=pltpu.CompilerParams(vmem_limit_bytes=8 << 20),
        name="renorm",
    )(rows_in, modulation, *terms)


def fold_kernel(sides, *refs):
    side_refs, out_refs = refs[:sides], refs[sides:]
    slots = out_refs[0].shape[0]
    for j, out_ref in enumerate(out_refs):
        total = side_refs[0][j * slots : (j + 1) * slots]
        for ref in side_refs[1:]:
            total = total + ref[j * slots : (j + 1) * slots].astype(jnp.float32)
        out_ref[...] = total.astype(out_ref.dtype)


def fold(sides, slots):
    count, width = sides[0].shape
    return pl.pallas_call(
        functools.partial(fold_kernel, len(sides)),
        out_shape=[
            jax.ShapeDtypeStruct((slots, width), jnp.bfloat16 if j else jnp.float32)
            for j in range(count // slots)
        ],
        compiler_params=pltpu.CompilerParams(vmem_limit_bytes=8 << 20),
        name="fold",
    )(*sides)


def finish_kernel(select_ref, cached_ref, after_ref, mod_ref, *refs):
    *term_refs, out_ref = refs
    total = term_refs[0][...]
    for ref in term_refs[1:]:
        total = total + ref[...].astype(jnp.float32)
    renewed = (after_ref[...] + mod_ref[5:6, :] * total).astype(jnp.bfloat16)
    select = select_ref[...]
    placed = jnp.dot(select, renewed, preferred_element_type=jnp.float32)
    covered = jnp.sum(select.astype(jnp.float32), axis=1, keepdims=True)
    blended = cached_ref[...].astype(jnp.float32) * (1.0 - covered) + placed
    out_ref[...] = blended.astype(jnp.bfloat16)


def finish(select, cached, after_attn, modulation, terms):
    return pl.pallas_call(
        finish_kernel,
        out_shape=jax.ShapeDtypeStruct(cached.shape, jnp.bfloat16),
        compiler_params=pltpu.CompilerParams(vmem_limit_bytes=8 << 20),
        name="finish",
    )(select, cached, after_attn, modulation, *terms)


def body(
    hidden_in,
    cached_out,
    cache_keys,
    cache_values,
    refresh_idx,
    modulation,
    q_gain,
    w_query,
    w_out,
    w_up,
    w_down,
):
    slots = refresh_idx.shape[0]
    uly_size = lax.axis_size("uly")
    blk_size = lax.axis_size("blk")
    local_heads = w_query.shape[1] // DH
    group = min(slots * uly_size, slots + (uly_size - 1) * OTHER)
    pair = 2 if blk_size % 2 == 0 and local_heads % 2 == 0 else 1
    chips = blk_size // pair

    rows_in, normed, select, modulation, sides = enter(
        refresh_idx, hidden_in, modulation, cache_keys, cache_values, uly_size, pair
    )
    group_rows = [trade(normed, "uly", k) for k in range(uly_size)]
    w_query, token = hold(normed, w_query)

    sides = [trade(x, "blk", side) for side, x in enumerate(sides)]
    *kv_parts, token = merge_kv(sides, [token] + group_rows[1:])
    kv_parts = [trade(x, "uly", k) for k, x in enumerate(kv_parts)]

    queries, spread, token = project(token, group_rows, w_query, q_gain, group, pair)
    w_out, w_up, w_down, cached, token = hold(token, w_out, w_up, w_down, cached_out)
    queries = join([trade(x, "blk", side) for side, x in enumerate(queries)])
    queries = [trade(queries, "blk", j * pair) for j in range(chips)]
    parts = attend(token, queries, kv_parts)
    parts = [trade(x, "blk", j * pair) for j, x in enumerate(parts)]
    attended = combine(parts, group, pair)
    attended = [trade(x, "blk", side) for side, x in enumerate(attended)]
    terms = output(spread, attended, w_out, slots, uly_size)
    terms = [trade(x, "uly", k) for k, x in enumerate(terms)]
    after_attn, norm_mlp = renorm(rows_in, modulation, terms)

    rows = [join([trade(norm_mlp, "blk", j * pair) for j in range(chips)])]
    if pair == 2:
        rows.append(trade(rows[0], "blk", 1))
    down = mlp(rows, w_up, w_down, pair)
    down = [trade(x, "blk", side) for side, x in enumerate(down)]
    terms = [trade(x, "blk", j * pair) for j, x in enumerate(fold(down, slots))]
    return finish(select, cached, after_attn, modulation, terms)


def solution(mesh):
    return jax.shard_map(
        body,
        mesh=mesh,
        in_specs=(
            P(("blk", "uly"), None),
            P(("blk", "uly"), None),
            P(("blk", "uly"), None),
            P(("blk", "uly"), None),
            P(("blk", "uly")),
            P(),
            P(),
            P(None, "uly"),
            P("uly", None),
            P(None, "blk"),
            P("blk", None),
        ),
        out_specs=P(("blk", "uly"), None),
        check_vma=False,
    )
```

```python
import functools
import math

import jax
import jax.numpy as jnp
from jax import lax
from jax.experimental import pallas as pl
from jax.experimental.pallas import tpu as pltpu
from jax.sharding import PartitionSpec as P

DH = 128
OTHER = 8
VMEM_SPEC = pl.BlockSpec(memory_space=pltpu.VMEM)
TOKEN = jax.ShapeDtypeStruct((8, DH), jnp.float32)
ANY_SPEC = pl.BlockSpec(memory_space=pl.ANY)


def layer_norm(row_block, shift_by, scale_by):
    average = jnp.mean(row_block, axis=-1, keepdims=True)
    centred = row_block - average
    spread = jnp.mean(centred * centred, axis=-1, keepdims=True)
    return centred * lax.rsqrt(spread + 1e-06) * (1.0 + scale_by) + shift_by


def trade(x, axis, flip):
    if flip == 0:
        return x
    return lax.ppermute(x, axis, [(i, i ^ flip) for i in range(lax.axis_size(axis))])


def in_hbm(x):
    return pltpu.with_memory_space_constraint(x, pltpu.HBM)


def hold_kernel(count, *refs):
    source_refs, sems = refs[1 : count + 1], refs[-1]
    *held_refs, token_ref = refs[count + 1 : -1]
    token_ref[...] = jnp.zeros_like(token_ref)
    copies = [
        pltpu.make_async_copy(source_ref, held_ref, sems.at[i])
        for i, (source_ref, held_ref) in enumerate(zip(source_refs, held_refs))
    ]
    for copy in copies:
        copy.start()
    for copy in copies:
        copy.wait()


def hold(after, *weights):
    count = len(weights)
    moved = sum(w.size * w.dtype.itemsize for w in weights)
    return pl.pallas_call(
        functools.partial(hold_kernel, count),
        in_specs=[VMEM_SPEC] + [ANY_SPEC] * count,
        out_specs=[VMEM_SPEC] * (count + 1),
        out_shape=[pltpu.VMEM(w.shape, w.dtype) for w in weights] + [TOKEN],
        scratch_shapes=[pltpu.SemaphoreType.DMA((count,))],
        cost_estimate=pl.CostEstimate(flops=0, bytes_accessed=moved, transcendentals=0),
        compiler_params=pltpu.CompilerParams(vmem_limit_bytes=2 << 20),
        name="hold",
    )(after, *[in_hbm(w) for w in weights])


def my_core(pair):
    return lax.rem(lax.axis_index("blk"), pair)


def enter_kernel(pair, idx_hbm, hidden_hbm, mod_hbm, key_hbm, value_hbm, *refs):
    rows_ref, normed_ref, select_ref, mod_ref, *side_refs = refs[: pair + 4]
    idx_ref, hidden_ref, sems, kv_sem = refs[pair + 4 :]
    copies = [
        pltpu.make_async_copy(source, target, sems.at[i])
        for i, (source, target) in enumerate(
            [(idx_hbm, idx_ref), (hidden_hbm, hidden_ref), (mod_hbm, mod_ref)]
        )
    ]
    for copy in copies:
        copy.start()
    parts, _, both = side_refs[0].shape
    half = both // 2
    uly, core = lax.axis_index("uly"), my_core(pair)
    kv_copies = []
    for side, side_ref in enumerate(side_refs):
        for flip in range(parts):
            start = pl.multiple_of(((uly ^ flip) * pair + (core ^ side)) * half, DH)
            for at, source in enumerate((key_hbm, value_hbm)):
                copy = pltpu.make_async_copy(
                    source.at[:, pl.ds(start, half)],
                    side_ref.at[flip, :, pl.ds(at * half, half)],
                    kv_sem.at[side, flip, at],
                )
                copy.start()
                kv_copies.append(copy)
    for copy in copies:
        copy.wait()
    tokens, width = hidden_ref.shape
    slots = idx_ref.shape[1]
    position = lax.broadcasted_iota(jnp.int32, (tokens, slots), 0)
    select = (position == idx_ref[...]).astype(jnp.float32).astype(jnp.bfloat16)
    select_ref[...] = select
    contract = (((0,), (0,)), ((), ()))
    rows = lax.dot_general(
        select, hidden_ref[...], contract, preferred_element_type=jnp.float32
    )
    live = lax.dot_general(
        select,
        jnp.ones((tokens, DH), jnp.bfloat16),
        contract,
        preferred_element_type=jnp.float32,
    )
    rows_ref[...] = rows
    normed = layer_norm(rows, mod_ref[0:1, :], mod_ref[1:2, :])
    normed_ref[:, :width] = normed.astype(jnp.bfloat16)
    normed_ref[:, width:] = live.astype(jnp.bfloat16)
    for copy in kv_copies:
        copy.wait()


def enter(refresh_idx, hidden_in, modulation, cache_keys, cache_values, parts, pair):
    slots = refresh_idx.shape[0]
    tokens, width = hidden_in.shape
    both = 2 * width // (parts * pair)
    out = pl.pallas_call(
        functools.partial(enter_kernel, pair),
        in_specs=[ANY_SPEC] * 5,
        out_specs=[VMEM_SPEC] * (pair + 4),
        out_shape=[
            pltpu.VMEM((slots, width), jnp.float32),
            pltpu.VMEM((slots, width + DH), jnp.bfloat16),
            pltpu.VMEM((tokens, slots), jnp.bfloat16),
            pltpu.VMEM(modulation.shape, modulation.dtype),
        ]
        + [pltpu.VMEM((parts, tokens, both), cache_keys.dtype)] * pair,
        scratch_shapes=[
            pltpu.VMEM((1, slots), jnp.int32),
            pltpu.VMEM(hidden_in.shape, hidden_in.dtype),
            pltpu.SemaphoreType.DMA((3,)),
            pltpu.SemaphoreType.DMA((pair, parts, 2)),
        ],
        compiler_params=pltpu.CompilerParams(vmem_limit_bytes=8 << 20),
        name="enter",
    )(
        *[
            in_hbm(x)
            for x in (refresh_idx.reshape(1, slots), hidden_in, modulation, cache_keys, cache_values)
        ]
    )
    return *out[:4], out[4:]


def merge_kv_kernel(sides, flips, *refs):
    *refs, token_ref = refs
    token_ref[...] = jnp.zeros_like(token_ref)
    for flip, out_ref in zip(flips, refs[-len(flips) :]):
        for side in range(sides):
            out_ref[side] = refs[side][flip]


def merge_kv(sides, flips, after):
    _, tokens, both = sides[0].shape
    return pl.pallas_call(
        functools.partial(merge_kv_kernel, len(sides), flips),
        out_specs=[VMEM_SPEC] * (len(flips) + 1),
        out_shape=[pltpu.VMEM((len(sides), tokens, both), sides[0].dtype) for _ in flips]
        + [TOKEN],
        compiler_params=pltpu.CompilerParams(vmem_limit_bytes=8 << 20),
        name="merge_kv",
    )(*sides, *after)


def project_kernel(pieces, given, after_ref, *refs):
    rows_refs, (w_ref, gain_hbm_ref) = refs[:given], refs[given : given + 2]
    *query_refs, spread_ref, token_ref, heads_ref, gain_ref, sem = refs[given + 2 :]
    token_ref[...] = jnp.zeros_like(token_ref)
    copy = pltpu.make_async_copy(gain_hbm_ref, gain_ref, sem)
    copy.start()
    core = my_core(len(query_refs))
    width = w_ref.shape[0]
    group, half = query_refs[0].shape
    rows = [ref[...] for ref in rows_refs]
    if len(rows) > pieces:
        uly = lax.axis_index("uly")
        at_end = (uly == 0) | (uly == pieces - 1)
        rows = rows[:2] + [jnp.where(at_end, rows[i], rows[i + 1]) for i in (2, 4)]
    rows = jnp.concatenate(rows, axis=0)
    everyone = rows.shape[0]
    flags = rows[:, width:]
    shape = (everyone, everyone)
    before = lax.broadcasted_iota(jnp.int32, shape, 1) < lax.broadcasted_iota(jnp.int32, shape, 0)
    before = before.astype(jnp.float32).astype(jnp.bfloat16)
    rank = jnp.dot(before, flags, preferred_element_type=jnp.float32)
    lane = lax.broadcasted_iota(jnp.int32, rank.shape, 1).astype(jnp.float32)
    spread = jnp.where((rank == lane) & (flags.astype(jnp.float32) > 0.0), 1.0, 0.0)
    spread = spread.astype(jnp.bfloat16)
    spread_ref[...] = spread
    live_rows = lax.dot_general(
        spread[:, :group],
        rows[:, :width],
        (((0,), (0,)), ((), ())),
        preferred_element_type=jnp.float32,
    ).astype(jnp.bfloat16)
    projected = jnp.dot(live_rows, w_ref[...], preferred_element_type=jnp.float32)
    copy.wait()
    for start in range(0, projected.shape[1], DH):
        head = projected[:, start : start + DH]
        squares = jnp.mean(head * head, axis=-1, keepdims=True)
        heads_ref[:, start : start + DH] = (
            head * lax.rsqrt(squares + 1e-06) * (gain_ref[...] / math.sqrt(DH))
        )
    for side, query_ref in enumerate(query_refs):
        start = pl.multiple_of((core ^ side) * half, DH)
        query_ref[...] = heads_ref[:, pl.ds(start, half)].astype(jnp.bfloat16)


def project(after, rows, w_query, q_gain, parts, group, pair):
    half = w_query.shape[1] // pair
    everyone = parts * rows[0].shape[0]
    query = jax.ShapeDtypeStruct((group, half), jnp.bfloat16)
    out = pl.pallas_call(
        functools.partial(project_kernel, parts, len(rows)),
        in_specs=[VMEM_SPEC] * (len(rows) + 2) + [ANY_SPEC],
        out_shape=[query] * pair + [jax.ShapeDtypeStruct((everyone, DH), jnp.bfloat16), TOKEN],
        scratch_shapes=[
            pltpu.VMEM((group, w_query.shape[1]), jnp.float32),
            pltpu.VMEM((1, DH), jnp.float32),
            pltpu.SemaphoreType.DMA,
        ],
        compiler_params=pltpu.CompilerParams(vmem_limit_bytes=16 << 20),
        name="project",
    )(after, *rows, w_query, in_hbm(q_gain.reshape(1, DH)))
    return out[:-2], out[-2], out[-1]


def attend_kernel(pieces, after_ref, *refs):
    *refs, token_ref = refs
    token_ref[...] = jnp.zeros_like(token_ref)
    query_refs, kv_refs, out_refs = refs[:pieces], refs[pieces:-pieces], refs[-pieces:]
    cores, group, half = query_refs[0].shape
    rows = cores * group
    sides = kv_refs[0].shape[0]
    lane = lax.broadcasted_iota(jnp.int32, (DH, DH), 1)
    for at in range(0, pieces, 4):
        stop = min(at + 4, pieces)
        queries = [ref[core] for ref in query_refs[at:stop] for core in range(cores)]
        queries = [x.astype(jnp.float32) for x in queries]
        queries = jnp.concatenate(queries, axis=0).astype(jnp.bfloat16)
        stats = [jnp.zeros((DH, DH), jnp.float32) for _ in range(at, stop)]
        for head in range(half // DH):
            cols = slice(head * DH, (head + 1) * DH)
            vals = slice(half + head * DH, half + (head + 1) * DH)
            keys = [ref[side, :, cols] for ref in kv_refs for side in range(sides)]
            values = [ref[side, :, vals] for ref in kv_refs for side in range(sides)]
            scores = lax.dot_general(
                queries[:, cols],
                jnp.concatenate(keys, axis=0),
                (((1,), (1,)), ((), ())),
                preferred_element_type=jnp.float32,
            )
            maxima = jnp.max(scores, axis=-1, keepdims=True)
            weights = jnp.exp(scores - maxima)
            sums = jnp.sum(weights, axis=-1, keepdims=True)
            weighted = jnp.dot(
                weights.astype(jnp.bfloat16),
                jnp.concatenate(values, axis=0),
                preferred_element_type=jnp.float32,
            )
            for j in range(at, stop):
                mine = slice((j - at) * rows, (j - at + 1) * rows)
                out_refs[j][:rows, cols] = weighted[mine]
                pad = jnp.zeros((DH - rows, 1), jnp.float32)
                top = jnp.concatenate([maxima[mine], pad], axis=0)
                total = jnp.concatenate([sums[mine], pad], axis=0)
                stat = jnp.where(lane == 2 * head, top, stats[j - at])
                stats[j - at] = jnp.where(lane == 2 * head + 1, total, stat)
        for j in range(at, stop):
            out_refs[j][rows:, DH:] = jnp.zeros((8, half - DH), jnp.float32)
            out_refs[j][rows:, :DH] = stats[j - at].T[:8]


def attend(after, queries, kv_parts):
    cores, group, half = queries[0].shape
    rows = cores * group
    return pl.pallas_call(
        functools.partial(attend_kernel, len(queries)),
        out_shape=[jax.ShapeDtypeStruct((rows + 8, half), jnp.float32)] * len(queries) + [TOKEN],
        compiler_params=pltpu.CompilerParams(vmem_limit_bytes=24 << 20),
        name="attend",
    )(after, *queries, *kv_parts)


def combine_kernel(pieces, after_ref, *refs):
    part_refs, out_refs = refs[:pieces], refs[pieces:]
    group, half = out_refs[0].shape
    rows = group * len(out_refs)
    stats = []
    for ref in part_refs:
        packed = ref[rows:, :DH]
        packed = jnp.concatenate([packed, jnp.zeros((DH - 8, DH), jnp.float32)], axis=0)
        stats.append(packed.T[:rows])
    for head in range(half // DH):
        cols = slice(head * DH, (head + 1) * DH)
        maxima = [stat[:, 2 * head : 2 * head + 1] for stat in stats]
        top = functools.reduce(jnp.maximum, maxima)
        total = jnp.zeros_like(top)
        attended = jnp.zeros((rows, DH), jnp.float32)
        for ref, stat, maximum in zip(part_refs, stats, maxima):
            factor = jnp.exp(maximum - top)
            total = total + stat[:, 2 * head + 1 : 2 * head + 2] * factor
            attended = attended + ref[:rows, cols] * factor
        attended = attended / total
        for side, out_ref in enumerate(out_refs):
            out_ref[:, cols] = attended[side * group : (side + 1) * group].astype(jnp.bfloat16)


def combine(after, parts, group, pair):
    half = parts[0].shape[1]
    return pl.pallas_call(
        functools.partial(combine_kernel, len(parts)),
        out_shape=[jax.ShapeDtypeStruct((group, half), jnp.bfloat16)] * pair,
        compiler_params=pltpu.CompilerParams(vmem_limit_bytes=16 << 20),
        name="combine",
    )(after, *parts)


def output_kernel(sides, spread_ref, *refs):
    side_refs, w_ref, (*out_refs, token_ref) = refs[:sides], refs[sides], refs[sides + 1 :]
    token_ref[...] = jnp.zeros_like(token_ref)
    group, half = side_refs[0].shape
    slots, width = out_refs[0].shape
    spread = spread_ref[:, :group]
    attended = [
        jnp.dot(spread, ref[...], preferred_element_type=jnp.float32).astype(jnp.bfloat16)
        for ref in side_refs
    ]
    core = my_core(sides)
    starts = [pl.multiple_of((core ^ side) * half, DH) for side in range(sides)]
    step = math.gcd(width, 1024)
    for col in range(0, width, step):
        terms = jnp.zeros((spread.shape[0], step), jnp.float32)
        for start, side in zip(starts, attended):
            terms = terms + jnp.dot(
                side, w_ref[pl.ds(start, half), col : col + step], preferred_element_type=jnp.float32
            )
        for k, out_ref in enumerate(out_refs):
            piece = terms[k * slots : (k + 1) * slots]
            out_ref[:, col : col + step] = piece.astype(out_ref.dtype)


def output(spread, sides, w_out, slots, parts):
    width = w_out.shape[1]
    return pl.pallas_call(
        functools.partial(output_kernel, len(sides)),
        out_shape=[
            jax.ShapeDtypeStruct((slots, width), jnp.bfloat16 if k else jnp.float32)
            for k in range(parts)
        ]
        + [TOKEN],
        compiler_params=pltpu.CompilerParams(vmem_limit_bytes=16 << 20),
        name="output",
    )(spread, *sides, w_out)


def mlp_kernel(pieces, *refs):
    row_refs, (up_ref, down_ref) = refs[:pieces], refs[pieces : pieces + 2]
    *out_refs, act_ref = refs[pieces + 2 :]
    hidden, width = down_ref.shape
    rows = [ref[j] for ref in row_refs for j in range(ref.shape[0])]
    rows = jnp.concatenate(rows, axis=0)
    count = out_refs[0].shape[0]
    step = math.gcd(hidden, 512)
    for col in range(0, hidden, step):
        lifted = jnp.dot(rows, up_ref[:, col : col + step], preferred_element_type=jnp.float32)
        act_ref[:, col : col + step] = jax.nn.gelu(lifted, approximate=True).astype(jnp.bfloat16)
    step = math.gcd(width, 512)
    for col in range(0, width, step):
        down = jnp.dot(
            act_ref[...], down_ref[:, col : col + step], preferred_element_type=jnp.float32
        )
        for side, out_ref in enumerate(out_refs):
            piece = down[side * count : (side + 1) * count]
            out_ref[:, col : col + step] = piece.astype(out_ref.dtype)


def mlp(rows, w_up, w_down, pair):
    count = sum(x.shape[0] * x.shape[1] for x in rows)
    hidden, width = w_down.shape
    return pl.pallas_call(
        functools.partial(mlp_kernel, len(rows)),
        out_shape=[
            jax.ShapeDtypeStruct((count // pair, width), jnp.bfloat16 if side else jnp.float32)
            for side in range(pair)
        ],
        scratch_shapes=[pltpu.VMEM((count, hidden), jnp.bfloat16)],
        compiler_params=pltpu.CompilerParams(vmem_limit_bytes=32 << 20),
        name="mlp",
    )(*rows, w_up, w_down)


def join_kernel(*refs):
    *part_refs, out_ref = refs
    for at, ref in enumerate(part_refs):
        out_ref[at] = ref[...]


def join(parts):
    return pl.pallas_call(
        join_kernel,
        out_shape=jax.ShapeDtypeStruct((len(parts), *parts[0].shape), parts[0].dtype),
        compiler_params=pltpu.CompilerParams(vmem_limit_bytes=8 << 20),
        name="join",
    )(*parts)


def renorm_kernel(hold_ref, rows_ref, mod_ref, *refs):
    *term_refs, after_ref, normed_ref = refs
    branch = term_refs[0][...]
    for ref in term_refs[1:]:
        branch = branch + ref[...].astype(jnp.float32)
    after = rows_ref[...] + mod_ref[2:3, :] * branch
    after_ref[...] = after
    normed_ref[...] = layer_norm(after, mod_ref[3:4, :], mod_ref[4:5, :]).astype(jnp.bfloat16)


def renorm(after, rows_in, modulation, terms):
    return pl.pallas_call(
        renorm_kernel,
        out_shape=[
            jax.ShapeDtypeStruct(rows_in.shape, jnp.float32),
            jax.ShapeDtypeStruct(rows_in.shape, jnp.bfloat16),
        ],
        compiler_params=pltpu.CompilerParams(vmem_limit_bytes=8 << 20),
        name="renorm",
    )(after, rows_in, modulation, *terms)


def fold_kernel(sides, *refs):
    side_refs, out_refs = refs[:sides], refs[sides:]
    slots = out_refs[0].shape[0]
    for j, out_ref in enumerate(out_refs):
        total = side_refs[0][j * slots : (j + 1) * slots]
        for ref in side_refs[1:]:
            total = total + ref[j * slots : (j + 1) * slots].astype(jnp.float32)
        out_ref[...] = total.astype(out_ref.dtype)


def fold(sides, slots):
    count, width = sides[0].shape
    return pl.pallas_call(
        functools.partial(fold_kernel, len(sides)),
        out_shape=[
            jax.ShapeDtypeStruct((slots, width), jnp.bfloat16 if j else jnp.float32)
            for j in range(count // slots)
        ],
        compiler_params=pltpu.CompilerParams(vmem_limit_bytes=8 << 20),
        name="fold",
    )(*sides)


def finish_kernel(select_ref, cached_ref, after_ref, mod_ref, *refs):
    *term_refs, out_ref = refs
    total = term_refs[0][...]
    for ref in term_refs[1:]:
        total = total + ref[...].astype(jnp.float32)
    renewed = (after_ref[...] + mod_ref[5:6, :] * total).astype(jnp.bfloat16)
    select = select_ref[...]
    placed = jnp.dot(select, renewed, preferred_element_type=jnp.float32)
    covered = jnp.sum(select.astype(jnp.float32), axis=1, keepdims=True)
    blended = cached_ref[...].astype(jnp.float32) * (1.0 - covered) + placed
    out_ref[...] = blended.astype(jnp.bfloat16)


def finish(select, cached, after_attn, modulation, terms):
    return pl.pallas_call(
        finish_kernel,
        out_shape=jax.ShapeDtypeStruct(cached.shape, jnp.bfloat16),
        compiler_params=pltpu.CompilerParams(vmem_limit_bytes=8 << 20),
        name="finish",
    )(select, cached, after_attn, modulation, *terms)


def body(
    hidden_in,
    cached_out,
    cache_keys,
    cache_values,
    refresh_idx,
    modulation,
    q_gain,
    w_query,
    w_out,
    w_up,
    w_down,
):
    slots = refresh_idx.shape[0]
    uly_size = lax.axis_size("uly")
    blk_size = lax.axis_size("blk")
    local_heads = w_query.shape[1] // DH
    group = min(slots * uly_size, slots + (uly_size - 1) * OTHER)
    pair = 2 if blk_size % 2 == 0 and local_heads % 2 == 0 else 1
    chips = blk_size // pair

    rows_in, normed, select, modulation, sides = enter(
        refresh_idx, hidden_in, modulation, cache_keys, cache_values, uly_size, pair
    )
    sides = [trade(x, "blk", side) for side, x in enumerate(sides)]
    w_query, token = hold(normed, w_query)
    if uly_size == 4:
        inner, outward = [(1, 2), (2, 1)], [(1, 0), (2, 3)]
        near = trade(normed, "uly", 1)
        across = lax.ppermute(normed, "uly", inner)
        early = merge_kv(sides, (0, 2), [near, across])[:2]
        kv_parts = [early[0], None, trade(early[1], "uly", 2), None]
        far_across = lax.ppermute(near, "uly", inner)
        across_out = lax.ppermute(across, "uly", outward)
        far_out = lax.ppermute(far_across, "uly", outward)
        group_rows = [normed, near, across_out, far_across, far_out, across]
        later = merge_kv(sides, (1, 3), [token] + group_rows[2:5])
        kv_parts[1], kv_parts[3] = trade(later[0], "uly", 1), trade(later[1], "uly", 3)
        token = later[2]
    else:
        group_rows = [trade(normed, "uly", k) for k in range(uly_size)]
        *kv_parts, token = merge_kv(sides, range(uly_size), [token] + group_rows[1:])
        kv_parts = [trade(x, "uly", k) for k, x in enumerate(kv_parts)]

    queries, spread, token = project(token, group_rows, w_query, q_gain, uly_size, group, pair)
    w_out, token = hold(token, w_out)
    queries = join([trade(x, "blk", side) for side, x in enumerate(queries)])
    queries = [trade(queries, "blk", j * pair) for j in range(chips)]
    *parts, token = attend(token, queries, kv_parts)
    w_up, token = hold(token, w_up)
    parts = [trade(x, "blk", j * pair) for j, x in enumerate(parts)]
    attended = combine(token, parts, group, pair)
    attended = [trade(x, "blk", side) for side, x in enumerate(attended)]
    *terms, token = output(spread, attended, w_out, slots, uly_size)
    w_down, cached, token = hold(token, w_down, cached_out)
    terms = [trade(x, "uly", k) for k, x in enumerate(terms)]
    after_attn, norm_mlp = renorm(token, rows_in, modulation, terms)

    rows = [join([trade(norm_mlp, "blk", j * pair) for j in range(chips)])]
    if pair == 2:
        rows.append(trade(rows[0], "blk", 1))
    down = mlp(rows, w_up, w_down, pair)
    down = [trade(x, "blk", side) for side, x in enumerate(down)]
    terms = [trade(x, "blk", j * pair) for j, x in enumerate(fold(down, slots))]
    return finish(select, cached, after_attn, modulation, terms)


def solution(mesh):
    return jax.shard_map(
        body,
        mesh=mesh,
        in_specs=(
            P(("blk", "uly"), None),
            P(("blk", "uly"), None),
            P(("blk", "uly"), None),
            P(("blk", "uly"), None),
            P(("blk", "uly")),
            P(),
            P(),
            P(None, "uly"),
            P("uly", None),
            P(None, "blk"),
            P("blk", None),
        ),
        out_specs=P(("blk", "uly"), None),
        check_vma=False,
    )
```

```python
import functools
import math

import jax
import jax.numpy as jnp
from jax import lax
from jax.experimental import pallas as pl
from jax.experimental.pallas import tpu as pltpu
from jax.sharding import PartitionSpec as P

DH = 128
OTHER = 8
VMEM_SPEC = pl.BlockSpec(memory_space=pltpu.VMEM)
TOKEN = jax.ShapeDtypeStruct((8, DH), jnp.float32)
ANY_SPEC = pl.BlockSpec(memory_space=pl.ANY)


def layer_norm(row_block, shift_by, scale_by):
    average = jnp.mean(row_block, axis=-1, keepdims=True)
    centred = row_block - average
    spread = jnp.mean(centred * centred, axis=-1, keepdims=True)
    return centred * lax.rsqrt(spread + 1e-06) * (1.0 + scale_by) + shift_by


def trade(x, axis, flip):
    if flip == 0:
        return x
    return lax.ppermute(x, axis, [(i, i ^ flip) for i in range(lax.axis_size(axis))])


def in_hbm(x):
    return pltpu.with_memory_space_constraint(x, pltpu.HBM)


def hold_kernel(count, *refs):
    source_refs, sems = refs[1 : count + 1], refs[-1]
    *held_refs, token_ref = refs[count + 1 : -1]
    token_ref[...] = jnp.zeros_like(token_ref)
    copies = [
        pltpu.make_async_copy(source_ref, held_ref, sems.at[i])
        for i, (source_ref, held_ref) in enumerate(zip(source_refs, held_refs))
    ]
    for copy in copies:
        copy.start()
    for copy in copies:
        copy.wait()


def hold(after, *weights):
    count = len(weights)
    moved = sum(w.size * w.dtype.itemsize for w in weights)
    return pl.pallas_call(
        functools.partial(hold_kernel, count),
        in_specs=[VMEM_SPEC] + [ANY_SPEC] * count,
        out_specs=[VMEM_SPEC] * (count + 1),
        out_shape=[pltpu.VMEM(w.shape, w.dtype) for w in weights] + [TOKEN],
        scratch_shapes=[pltpu.SemaphoreType.DMA((count,))],
        cost_estimate=pl.CostEstimate(flops=0, bytes_accessed=moved, transcendentals=0),
        compiler_params=pltpu.CompilerParams(vmem_limit_bytes=2 << 20),
        name="hold",
    )(after, *[in_hbm(w) for w in weights])


def my_core(pair):
    return lax.rem(lax.axis_index("blk"), pair)


def enter_kernel(pair, idx_hbm, hidden_hbm, mod_hbm, key_hbm, value_hbm, *refs):
    rows_ref, normed_ref, select_ref, mod_ref, *side_refs = refs[: pair + 4]
    idx_ref, hidden_ref, sems, kv_sem = refs[pair + 4 :]
    copies = [
        pltpu.make_async_copy(source, target, sems.at[i])
        for i, (source, target) in enumerate(
            [(idx_hbm, idx_ref), (hidden_hbm, hidden_ref), (mod_hbm, mod_ref)]
        )
    ]
    for copy in copies:
        copy.start()
    parts, _, both = side_refs[0].shape
    half = both // 2
    uly, core = lax.axis_index("uly"), my_core(pair)
    kv_copies = []
    for side, side_ref in enumerate(side_refs):
        for flip in range(parts):
            start = pl.multiple_of(((uly ^ flip) * pair + (core ^ side)) * half, DH)
            for at, source in enumerate((key_hbm, value_hbm)):
                copy = pltpu.make_async_copy(
                    source.at[:, pl.ds(start, half)],
                    side_ref.at[flip, :, pl.ds(at * half, half)],
                    kv_sem.at[side, flip, at],
                )
                copy.start()
                kv_copies.append(copy)
    for copy in copies:
        copy.wait()
    tokens, width = hidden_ref.shape
    slots = idx_ref.shape[1]
    position = lax.broadcasted_iota(jnp.int32, (tokens, slots), 0)
    select = (position == idx_ref[...]).astype(jnp.float32).astype(jnp.bfloat16)
    select_ref[...] = select
    contract = (((0,), (0,)), ((), ()))
    rows = lax.dot_general(
        select, hidden_ref[...], contract, preferred_element_type=jnp.float32
    )
    live = lax.dot_general(
        select,
        jnp.ones((tokens, DH), jnp.bfloat16),
        contract,
        preferred_element_type=jnp.float32,
    )
    rows_ref[...] = rows
    normed = layer_norm(rows, mod_ref[0:1, :], mod_ref[1:2, :])
    normed_ref[:, :width] = normed.astype(jnp.bfloat16)
    normed_ref[:, width:] = live.astype(jnp.bfloat16)
    for copy in kv_copies:
        copy.wait()


def enter(refresh_idx, hidden_in, modulation, cache_keys, cache_values, parts, pair):
    slots = refresh_idx.shape[0]
    tokens, width = hidden_in.shape
    both = 2 * width // (parts * pair)
    out = pl.pallas_call(
        functools.partial(enter_kernel, pair),
        in_specs=[ANY_SPEC] * 5,
        out_specs=[VMEM_SPEC] * (pair + 4),
        out_shape=[
            pltpu.VMEM((slots, width), jnp.float32),
            pltpu.VMEM((slots, width + DH), jnp.bfloat16),
            pltpu.VMEM((tokens, slots), jnp.bfloat16),
            pltpu.VMEM(modulation.shape, modulation.dtype),
        ]
        + [pltpu.VMEM((parts, tokens, both), cache_keys.dtype)] * pair,
        scratch_shapes=[
            pltpu.VMEM((1, slots), jnp.int32),
            pltpu.VMEM(hidden_in.shape, hidden_in.dtype),
            pltpu.SemaphoreType.DMA((3,)),
            pltpu.SemaphoreType.DMA((pair, parts, 2)),
        ],
        compiler_params=pltpu.CompilerParams(vmem_limit_bytes=8 << 20),
        name="enter",
    )(
        *[
            in_hbm(x)
            for x in (refresh_idx.reshape(1, slots), hidden_in, modulation, cache_keys, cache_values)
        ]
    )
    return *out[:4], out[4:]


def merge_kv_kernel(sides, flips, *refs):
    *refs, token_ref = refs
    token_ref[...] = jnp.zeros_like(token_ref)
    for flip, out_ref in zip(flips, refs[-len(flips) :]):
        for side in range(sides):
            out_ref[side] = refs[side][flip]


def merge_kv(sides, flips, after):
    _, tokens, both = sides[0].shape
    return pl.pallas_call(
        functools.partial(merge_kv_kernel, len(sides), flips),
        out_specs=[VMEM_SPEC] * (len(flips) + 1),
        out_shape=[pltpu.VMEM((len(sides), tokens, both), sides[0].dtype) for _ in flips]
        + [TOKEN],
        compiler_params=pltpu.CompilerParams(vmem_limit_bytes=8 << 20),
        name="merge_kv",
    )(*sides, *after)


def project_kernel(pieces, after_ref, *refs):
    rows_refs, (w_ref, gain_hbm_ref) = refs[:pieces], refs[pieces : pieces + 2]
    *query_refs, spread_ref, token_ref, heads_ref, gain_ref, sem = refs[pieces + 2 :]
    token_ref[...] = jnp.zeros_like(token_ref)
    copy = pltpu.make_async_copy(gain_hbm_ref, gain_ref, sem)
    copy.start()
    core = my_core(len(query_refs))
    width = w_ref.shape[0]
    group, half = query_refs[0].shape
    rows = jnp.concatenate([ref[...] for ref in rows_refs], axis=0)
    everyone = rows.shape[0]
    flags = rows[:, width:]
    shape = (everyone, everyone)
    before = lax.broadcasted_iota(jnp.int32, shape, 1) < lax.broadcasted_iota(jnp.int32, shape, 0)
    before = before.astype(jnp.float32).astype(jnp.bfloat16)
    rank = jnp.dot(before, flags, preferred_element_type=jnp.float32)
    lane = lax.broadcasted_iota(jnp.int32, rank.shape, 1).astype(jnp.float32)
    spread = jnp.where((rank == lane) & (flags.astype(jnp.float32) > 0.0), 1.0, 0.0)
    spread = spread.astype(jnp.bfloat16)
    spread_ref[...] = spread
    live_rows = lax.dot_general(
        spread[:, :group],
        rows[:, :width],
        (((0,), (0,)), ((), ())),
        preferred_element_type=jnp.float32,
    ).astype(jnp.bfloat16)
    projected = jnp.dot(live_rows, w_ref[...], preferred_element_type=jnp.float32)
    copy.wait()
    for start in range(0, projected.shape[1], DH):
        head = projected[:, start : start + DH]
        squares = jnp.mean(head * head, axis=-1, keepdims=True)
        heads_ref[:, start : start + DH] = (
            head * lax.rsqrt(squares + 1e-06) * (gain_ref[...] / math.sqrt(DH))
        )
    for side, query_ref in enumerate(query_refs):
        start = pl.multiple_of((core ^ side) * half, DH)
        query_ref[...] = heads_ref[:, pl.ds(start, half)].astype(jnp.bfloat16)


def project(after, rows, w_query, q_gain, group, pair):
    half = w_query.shape[1] // pair
    everyone = len(rows) * rows[0].shape[0]
    query = jax.ShapeDtypeStruct((group, half), jnp.bfloat16)
    out = pl.pallas_call(
        functools.partial(project_kernel, len(rows)),
        in_specs=[VMEM_SPEC] * (len(rows) + 2) + [ANY_SPEC],
        out_shape=[query] * pair + [jax.ShapeDtypeStruct((everyone, DH), jnp.bfloat16), TOKEN],
        scratch_shapes=[
            pltpu.VMEM((group, w_query.shape[1]), jnp.float32),
            pltpu.VMEM((1, DH), jnp.float32),
            pltpu.SemaphoreType.DMA,
        ],
        compiler_params=pltpu.CompilerParams(vmem_limit_bytes=16 << 20),
        name="project",
    )(after, *rows, w_query, in_hbm(q_gain.reshape(1, DH)))
    return out[:-2], out[-2], out[-1]


def attend_kernel(pieces, after_ref, *refs):
    *refs, token_ref = refs
    token_ref[...] = jnp.zeros_like(token_ref)
    query_refs, kv_refs, out_refs = refs[:pieces], refs[pieces:-pieces], refs[-pieces:]
    cores, group, half = query_refs[0].shape
    rows = cores * group
    sides = kv_refs[0].shape[0]
    lane = lax.broadcasted_iota(jnp.int32, (DH, DH), 1)
    for at in range(0, pieces, 4):
        stop = min(at + 4, pieces)
        queries = [ref[core] for ref in query_refs[at:stop] for core in range(cores)]
        queries = [x.astype(jnp.float32) for x in queries]
        queries = jnp.concatenate(queries, axis=0).astype(jnp.bfloat16)
        stats = [jnp.zeros((DH, DH), jnp.float32) for _ in range(at, stop)]
        for head in range(half // DH):
            cols = slice(head * DH, (head + 1) * DH)
            vals = slice(half + head * DH, half + (head + 1) * DH)
            keys = [ref[side, :, cols] for ref in kv_refs for side in range(sides)]
            values = [ref[side, :, vals] for ref in kv_refs for side in range(sides)]
            scores = lax.dot_general(
                queries[:, cols],
                jnp.concatenate(keys, axis=0),
                (((1,), (1,)), ((), ())),
                preferred_element_type=jnp.float32,
            )
            maxima = jnp.max(scores, axis=-1, keepdims=True)
            weights = jnp.exp(scores - maxima)
            sums = jnp.sum(weights, axis=-1, keepdims=True)
            weighted = jnp.dot(
                weights.astype(jnp.bfloat16),
                jnp.concatenate(values, axis=0),
                preferred_element_type=jnp.float32,
            )
            for j in range(at, stop):
                mine = slice((j - at) * rows, (j - at + 1) * rows)
                out_refs[j][:rows, cols] = weighted[mine]
                pad = jnp.zeros((DH - rows, 1), jnp.float32)
                top = jnp.concatenate([maxima[mine], pad], axis=0)
                total = jnp.concatenate([sums[mine], pad], axis=0)
                stat = jnp.where(lane == 2 * head, top, stats[j - at])
                stats[j - at] = jnp.where(lane == 2 * head + 1, total, stat)
        for j in range(at, stop):
            out_refs[j][rows:, DH:] = jnp.zeros((8, half - DH), jnp.float32)
            out_refs[j][rows:, :DH] = stats[j - at].T[:8]


def attend(after, queries, kv_parts):
    cores, group, half = queries[0].shape
    rows = cores * group
    return pl.pallas_call(
        functools.partial(attend_kernel, len(queries)),
        out_shape=[jax.ShapeDtypeStruct((rows + 8, half), jnp.float32)] * len(queries) + [TOKEN],
        compiler_params=pltpu.CompilerParams(vmem_limit_bytes=24 << 20),
        name="attend",
    )(after, *queries, *kv_parts)


def combine_kernel(pieces, after_ref, *refs):
    part_refs, out_refs = refs[:pieces], refs[pieces:]
    group, half = out_refs[0].shape
    rows = group * len(out_refs)
    stats = []
    for ref in part_refs:
        packed = ref[rows:, :DH]
        packed = jnp.concatenate([packed, jnp.zeros((DH - 8, DH), jnp.float32)], axis=0)
        stats.append(packed.T[:rows])
    for head in range(half // DH):
        cols = slice(head * DH, (head + 1) * DH)
        maxima = [stat[:, 2 * head : 2 * head + 1] for stat in stats]
        top = functools.reduce(jnp.maximum, maxima)
        total = jnp.zeros_like(top)
        attended = jnp.zeros((rows, DH), jnp.float32)
        for ref, stat, maximum in zip(part_refs, stats, maxima):
            factor = jnp.exp(maximum - top)
            total = total + stat[:, 2 * head + 1 : 2 * head + 2] * factor
            attended = attended + ref[:rows, cols] * factor
        attended = attended / total
        for side, out_ref in enumerate(out_refs):
            out_ref[:, cols] = attended[side * group : (side + 1) * group].astype(jnp.bfloat16)


def combine(after, parts, group, pair):
    half = parts[0].shape[1]
    return pl.pallas_call(
        functools.partial(combine_kernel, len(parts)),
        out_shape=[jax.ShapeDtypeStruct((group, half), jnp.bfloat16)] * pair,
        compiler_params=pltpu.CompilerParams(vmem_limit_bytes=16 << 20),
        name="combine",
    )(after, *parts)


def output_kernel(sides, spread_ref, *refs):
    side_refs, w_ref, (*out_refs, token_ref) = refs[:sides], refs[sides], refs[sides + 1 :]
    token_ref[...] = jnp.zeros_like(token_ref)
    group, half = side_refs[0].shape
    slots, width = out_refs[0].shape
    spread = spread_ref[:, :group]
    attended = [
        jnp.dot(spread, ref[...], preferred_element_type=jnp.float32).astype(jnp.bfloat16)
        for ref in side_refs
    ]
    core = my_core(sides)
    starts = [pl.multiple_of((core ^ side) * half, DH) for side in range(sides)]
    step = math.gcd(width, 1024)
    for col in range(0, width, step):
        terms = jnp.zeros((spread.shape[0], step), jnp.float32)
        for start, side in zip(starts, attended):
            terms = terms + jnp.dot(
                side, w_ref[pl.ds(start, half), col : col + step], preferred_element_type=jnp.float32
            )
        for k, out_ref in enumerate(out_refs):
            piece = terms[k * slots : (k + 1) * slots]
            out_ref[:, col : col + step] = piece.astype(out_ref.dtype)


def output(spread, sides, w_out, slots, parts):
    width = w_out.shape[1]
    return pl.pallas_call(
        functools.partial(output_kernel, len(sides)),
        out_shape=[
            jax.ShapeDtypeStruct((slots, width), jnp.bfloat16 if k else jnp.float32)
            for k in range(parts)
        ]
        + [TOKEN],
        compiler_params=pltpu.CompilerParams(vmem_limit_bytes=16 << 20),
        name="output",
    )(spread, *sides, w_out)


def mlp_kernel(pieces, *refs):
    row_refs, (up_ref, down_ref) = refs[:pieces], refs[pieces : pieces + 2]
    *out_refs, act_ref = refs[pieces + 2 :]
    hidden, width = down_ref.shape
    rows = [ref[j] for ref in row_refs for j in range(ref.shape[0])]
    rows = jnp.concatenate(rows, axis=0)
    count = out_refs[0].shape[0]
    step = math.gcd(hidden, 512)
    for col in range(0, hidden, step):
        lifted = jnp.dot(rows, up_ref[:, col : col + step], preferred_element_type=jnp.float32)
        act_ref[:, col : col + step] = jax.nn.gelu(lifted, approximate=True).astype(jnp.bfloat16)
    step = math.gcd(width, 512)
    for col in range(0, width, step):
        down = jnp.dot(
            act_ref[...], down_ref[:, col : col + step], preferred_element_type=jnp.float32
        )
        for side, out_ref in enumerate(out_refs):
            piece = down[side * count : (side + 1) * count]
            out_ref[:, col : col + step] = piece.astype(out_ref.dtype)


def mlp(rows, w_up, w_down, pair):
    count = sum(x.shape[0] * x.shape[1] for x in rows)
    hidden, width = w_down.shape
    return pl.pallas_call(
        functools.partial(mlp_kernel, len(rows)),
        out_shape=[
            jax.ShapeDtypeStruct((count // pair, width), jnp.bfloat16 if side else jnp.float32)
            for side in range(pair)
        ],
        scratch_shapes=[pltpu.VMEM((count, hidden), jnp.bfloat16)],
        compiler_params=pltpu.CompilerParams(vmem_limit_bytes=32 << 20),
        name="mlp",
    )(*rows, w_up, w_down)


def join_kernel(count, *refs):
    part_refs, out_ref = refs[:count], refs[-1]
    for at, ref in enumerate(part_refs):
        out_ref[at] = ref[...]


def join(parts, after=()):
    return pl.pallas_call(
        functools.partial(join_kernel, len(parts)),
        out_shape=jax.ShapeDtypeStruct((len(parts), *parts[0].shape), parts[0].dtype),
        compiler_params=pltpu.CompilerParams(vmem_limit_bytes=8 << 20),
        name="join",
    )(*parts, *after)


def renorm_kernel(hold_ref, rows_ref, mod_ref, *refs):
    *term_refs, after_ref, normed_ref = refs
    branch = term_refs[0][...]
    for ref in term_refs[1:]:
        branch = branch + ref[...].astype(jnp.float32)
    after = rows_ref[...] + mod_ref[2:3, :] * branch
    after_ref[...] = after
    normed_ref[...] = layer_norm(after, mod_ref[3:4, :], mod_ref[4:5, :]).astype(jnp.bfloat16)


def renorm(after, rows_in, modulation, terms):
    return pl.pallas_call(
        renorm_kernel,
        out_shape=[
            jax.ShapeDtypeStruct(rows_in.shape, jnp.float32),
            jax.ShapeDtypeStruct(rows_in.shape, jnp.bfloat16),
        ],
        compiler_params=pltpu.CompilerParams(vmem_limit_bytes=8 << 20),
        name="renorm",
    )(after, rows_in, modulation, *terms)


def fold_kernel(sides, *refs):
    side_refs, out_refs = refs[:sides], refs[sides:]
    slots = out_refs[0].shape[0]
    for j, out_ref in enumerate(out_refs):
        total = side_refs[0][j * slots : (j + 1) * slots]
        for ref in side_refs[1:]:
            total = total + ref[j * slots : (j + 1) * slots].astype(jnp.float32)
        out_ref[...] = total.astype(out_ref.dtype)


def fold(sides, slots):
    count, width = sides[0].shape
    return pl.pallas_call(
        functools.partial(fold_kernel, len(sides)),
        out_shape=[
            jax.ShapeDtypeStruct((slots, width), jnp.bfloat16 if j else jnp.float32)
            for j in range(count // slots)
        ],
        compiler_params=pltpu.CompilerParams(vmem_limit_bytes=8 << 20),
        name="fold",
    )(*sides)


def finish_kernel(select_ref, cached_ref, after_ref, mod_ref, *refs):
    *term_refs, out_ref = refs
    total = term_refs[0][...]
    for ref in term_refs[1:]:
        total = total + ref[...].astype(jnp.float32)
    renewed = (after_ref[...] + mod_ref[5:6, :] * total).astype(jnp.bfloat16)
    select = select_ref[...]
    placed = jnp.dot(select, renewed, preferred_element_type=jnp.float32)
    covered = jnp.sum(select.astype(jnp.float32), axis=1, keepdims=True)
    blended = cached_ref[...].astype(jnp.float32) * (1.0 - covered) + placed
    out_ref[...] = blended.astype(jnp.bfloat16)


def finish(select, cached, after_attn, modulation, terms):
    return pl.pallas_call(
        finish_kernel,
        out_shape=jax.ShapeDtypeStruct(cached.shape, jnp.bfloat16),
        compiler_params=pltpu.CompilerParams(vmem_limit_bytes=8 << 20),
        name="finish",
    )(select, cached, after_attn, modulation, *terms)


def body(
    hidden_in,
    cached_out,
    cache_keys,
    cache_values,
    refresh_idx,
    modulation,
    q_gain,
    w_query,
    w_out,
    w_up,
    w_down,
):
    slots = refresh_idx.shape[0]
    uly_size = lax.axis_size("uly")
    blk_size = lax.axis_size("blk")
    local_heads = w_query.shape[1] // DH
    group = min(slots * uly_size, slots + (uly_size - 1) * OTHER)
    pair = 2 if blk_size % 2 == 0 and local_heads % 2 == 0 else 1
    chips = blk_size // pair

    rows_in, normed, select, modulation, sides = enter(
        refresh_idx, hidden_in, modulation, cache_keys, cache_values, uly_size, pair
    )
    sides = [trade(x, "blk", side) for side, x in enumerate(sides)]
    w_query, token = hold(normed, w_query)
    group_rows = [trade(normed, "uly", k) for k in range(uly_size)]
    early = tuple(range(min(2, uly_size)))
    late = tuple(range(len(early), uly_size))
    *kv_parts, _ = merge_kv(sides, early, [normed])
    kv_parts = [trade(x, "uly", k) for k, x in zip(early, kv_parts)]
    *later, token = merge_kv(sides, late, [token] + group_rows[1:])
    kv_parts += [trade(x, "uly", k) for k, x in zip(late, later)]

    queries, spread, token = project(token, group_rows, w_query, q_gain, group, pair)
    w_out, token = hold(token, w_out)
    queries = [trade(x, "blk", side) for side, x in enumerate(queries)]
    queries = join(queries, kv_parts[1 : len(early)])
    queries = [trade(queries, "blk", j * pair) for j in range(chips)]
    *parts, token = attend(token, queries, kv_parts)
    w_up, token = hold(token, w_up)
    parts = [trade(x, "blk", j * pair) for j, x in enumerate(parts)]
    attended = combine(token, parts, group, pair)
    attended = [trade(x, "blk", side) for side, x in enumerate(attended)]
    *terms, token = output(spread, attended, w_out, slots, uly_size)
    w_down, cached, token = hold(token, w_down, cached_out)
    terms = [trade(x, "uly", k) for k, x in enumerate(terms)]
    after_attn, norm_mlp = renorm(token, rows_in, modulation, terms)

    rows = [join([trade(norm_mlp, "blk", j * pair) for j in range(chips)])]
    if pair == 2:
        rows.append(trade(rows[0], "blk", 1))
    down = mlp(rows, w_up, w_down, pair)
    down = [trade(x, "blk", side) for side, x in enumerate(down)]
    terms = [trade(x, "blk", j * pair) for j, x in enumerate(fold(down, slots))]
    return finish(select, cached, after_attn, modulation, terms)


def solution(mesh):
    return jax.shard_map(
        body,
        mesh=mesh,
        in_specs=(
            P(("blk", "uly"), None),
            P(("blk", "uly"), None),
            P(("blk", "uly"), None),
            P(("blk", "uly"), None),
            P(("blk", "uly")),
            P(),
            P(),
            P(None, "uly"),
            P("uly", None),
            P(None, "blk"),
            P("blk", None),
        ),
        out_specs=P(("blk", "uly"), None),
        check_vma=False,
    )
```

```python
import functools
import math

import jax
import jax.numpy as jnp
from jax import lax
from jax.experimental import pallas as pl
from jax.experimental.pallas import tpu as pltpu
from jax.sharding import PartitionSpec as P

DH = 128
OTHER = 8
VMEM_SPEC = pl.BlockSpec(memory_space=pltpu.VMEM)
TOKEN = jax.ShapeDtypeStruct((8, DH), jnp.float32)
ANY_SPEC = pl.BlockSpec(memory_space=pl.ANY)


def layer_norm(row_block, shift_by, scale_by):
    average = jnp.mean(row_block, axis=-1, keepdims=True)
    centred = row_block - average
    spread = jnp.mean(centred * centred, axis=-1, keepdims=True)
    return centred * lax.rsqrt(spread + 1e-06) * (1.0 + scale_by) + shift_by


def trade(x, axis, flip):
    if flip == 0:
        return x
    return lax.ppermute(x, axis, [(i, i ^ flip) for i in range(lax.axis_size(axis))])


def in_hbm(x):
    return pltpu.with_memory_space_constraint(x, pltpu.HBM)


def hold_kernel(count, *refs):
    source_refs, sems = refs[1 : count + 1], refs[-1]
    *held_refs, token_ref = refs[count + 1 : -1]
    token_ref[...] = jnp.zeros_like(token_ref)
    copies = [
        pltpu.make_async_copy(source_ref, held_ref, sems.at[i])
        for i, (source_ref, held_ref) in enumerate(zip(source_refs, held_refs))
    ]
    for copy in copies:
        copy.start()
    for copy in copies:
        copy.wait()


def hold(after, *weights):
    count = len(weights)
    moved = sum(w.size * w.dtype.itemsize for w in weights)
    return pl.pallas_call(
        functools.partial(hold_kernel, count),
        in_specs=[VMEM_SPEC] + [ANY_SPEC] * count,
        out_specs=[VMEM_SPEC] * (count + 1),
        out_shape=[pltpu.VMEM(w.shape, w.dtype) for w in weights] + [TOKEN],
        scratch_shapes=[pltpu.SemaphoreType.DMA((count,))],
        cost_estimate=pl.CostEstimate(flops=0, bytes_accessed=moved, transcendentals=0),
        compiler_params=pltpu.CompilerParams(vmem_limit_bytes=2 << 20),
        name="hold",
    )(after, *[in_hbm(w) for w in weights])


def my_core(pair):
    return lax.rem(lax.axis_index("blk"), pair)


def enter_kernel(pair, idx_hbm, hidden_hbm, mod_hbm, key_hbm, value_hbm, *refs):
    rows_ref, normed_ref, select_ref, mod_ref, *side_refs = refs[: pair + 4]
    idx_ref, hidden_ref, sems, kv_sem = refs[pair + 4 :]
    copies = [
        pltpu.make_async_copy(source, target, sems.at[i])
        for i, (source, target) in enumerate(
            [(idx_hbm, idx_ref), (hidden_hbm, hidden_ref), (mod_hbm, mod_ref)]
        )
    ]
    for copy in copies:
        copy.start()
    parts, _, both = side_refs[0].shape
    half = both // 2
    uly, core = lax.axis_index("uly"), my_core(pair)
    kv_copies = []
    for side, side_ref in enumerate(side_refs):
        for flip in range(parts):
            start = pl.multiple_of(((uly ^ flip) * pair + (core ^ side)) * half, DH)
            for at, source in enumerate((key_hbm, value_hbm)):
                copy = pltpu.make_async_copy(
                    source.at[:, pl.ds(start, half)],
                    side_ref.at[flip, :, pl.ds(at * half, half)],
                    kv_sem.at[side, flip, at],
                )
                copy.start()
                kv_copies.append(copy)
    for copy in copies:
        copy.wait()
    tokens, width = hidden_ref.shape
    slots = idx_ref.shape[1]
    position = lax.broadcasted_iota(jnp.int32, (tokens, slots), 0)
    select = (position == idx_ref[...]).astype(jnp.float32).astype(jnp.bfloat16)
    select_ref[...] = select
    contract = (((0,), (0,)), ((), ()))
    rows = lax.dot_general(
        select, hidden_ref[...], contract, preferred_element_type=jnp.float32
    )
    live = lax.dot_general(
        select,
        jnp.ones((tokens, DH), jnp.bfloat16),
        contract,
        preferred_element_type=jnp.float32,
    )
    rows_ref[...] = rows
    normed = layer_norm(rows, mod_ref[0:1, :], mod_ref[1:2, :])
    normed_ref[:, :width] = normed.astype(jnp.bfloat16)
    normed_ref[:, width:] = live.astype(jnp.bfloat16)
    for copy in kv_copies:
        copy.wait()


def enter(refresh_idx, hidden_in, modulation, cache_keys, cache_values, parts, pair):
    slots = refresh_idx.shape[0]
    tokens, width = hidden_in.shape
    both = 2 * width // (parts * pair)
    out = pl.pallas_call(
        functools.partial(enter_kernel, pair),
        in_specs=[ANY_SPEC] * 5,
        out_specs=[VMEM_SPEC] * (pair + 4),
        out_shape=[
            pltpu.VMEM((slots, width), jnp.float32),
            pltpu.VMEM((slots, width + DH), jnp.bfloat16),
            pltpu.VMEM((tokens, slots), jnp.bfloat16),
            pltpu.VMEM(modulation.shape, modulation.dtype),
        ]
        + [pltpu.VMEM((parts, tokens, both), cache_keys.dtype)] * pair,
        scratch_shapes=[
            pltpu.VMEM((1, slots), jnp.int32),
            pltpu.VMEM(hidden_in.shape, hidden_in.dtype),
            pltpu.SemaphoreType.DMA((3,)),
            pltpu.SemaphoreType.DMA((pair, parts, 2)),
        ],
        compiler_params=pltpu.CompilerParams(vmem_limit_bytes=8 << 20),
        name="enter",
    )(
        *[
            in_hbm(x)
            for x in (refresh_idx.reshape(1, slots), hidden_in, modulation, cache_keys, cache_values)
        ]
    )
    return *out[:4], out[4:]


def merge_kv_kernel(sides, flips, *refs):
    *refs, token_ref = refs
    token_ref[...] = jnp.zeros_like(token_ref)
    for flip, out_ref in zip(flips, refs[-len(flips) :]):
        for side in range(sides):
            out_ref[side] = refs[side][flip]


def merge_kv(sides, flips, after):
    _, tokens, both = sides[0].shape
    return pl.pallas_call(
        functools.partial(merge_kv_kernel, len(sides), flips),
        out_specs=[VMEM_SPEC] * (len(flips) + 1),
        out_shape=[pltpu.VMEM((len(sides), tokens, both), sides[0].dtype) for _ in flips]
        + [TOKEN],
        compiler_params=pltpu.CompilerParams(vmem_limit_bytes=8 << 20),
        name="merge_kv",
    )(*sides, *after)


def project_kernel(pieces, after_ref, *refs):
    rows_refs, (w_ref, gain_hbm_ref) = refs[:pieces], refs[pieces : pieces + 2]
    *query_refs, spread_ref, token_ref, heads_ref, gain_ref, sem = refs[pieces + 2 :]
    token_ref[...] = jnp.zeros_like(token_ref)
    copy = pltpu.make_async_copy(gain_hbm_ref, gain_ref, sem)
    copy.start()
    core = my_core(len(query_refs))
    width = w_ref.shape[0]
    group, half = query_refs[0].shape
    rows = jnp.concatenate([ref[...] for ref in rows_refs], axis=0)
    everyone = rows.shape[0]
    flags = rows[:, width:]
    shape = (everyone, everyone)
    before = lax.broadcasted_iota(jnp.int32, shape, 1) < lax.broadcasted_iota(jnp.int32, shape, 0)
    before = before.astype(jnp.float32).astype(jnp.bfloat16)
    rank = jnp.dot(before, flags, preferred_element_type=jnp.float32)
    lane = lax.broadcasted_iota(jnp.int32, rank.shape, 1).astype(jnp.float32)
    spread = jnp.where((rank == lane) & (flags.astype(jnp.float32) > 0.0), 1.0, 0.0)
    spread = spread.astype(jnp.bfloat16)
    spread_ref[...] = spread
    live_rows = lax.dot_general(
        spread[:, :group],
        rows[:, :width],
        (((0,), (0,)), ((), ())),
        preferred_element_type=jnp.float32,
    ).astype(jnp.bfloat16)
    projected = jnp.dot(live_rows, w_ref[...], preferred_element_type=jnp.float32)
    copy.wait()
    for start in range(0, projected.shape[1], DH):
        head = projected[:, start : start + DH]
        squares = jnp.mean(head * head, axis=-1, keepdims=True)
        heads_ref[:, start : start + DH] = (
            head * lax.rsqrt(squares + 1e-06) * (gain_ref[...] / math.sqrt(DH))
        )
    for side, query_ref in enumerate(query_refs):
        start = pl.multiple_of((core ^ side) * half, DH)
        query_ref[...] = heads_ref[:, pl.ds(start, half)].astype(jnp.bfloat16)


def project(after, rows, w_query, q_gain, group, pair):
    half = w_query.shape[1] // pair
    everyone = len(rows) * rows[0].shape[0]
    query = jax.ShapeDtypeStruct((group, half), jnp.bfloat16)
    out = pl.pallas_call(
        functools.partial(project_kernel, len(rows)),
        in_specs=[VMEM_SPEC] * (len(rows) + 2) + [ANY_SPEC],
        out_shape=[query] * pair + [jax.ShapeDtypeStruct((everyone, DH), jnp.bfloat16), TOKEN],
        scratch_shapes=[
            pltpu.VMEM((group, w_query.shape[1]), jnp.float32),
            pltpu.VMEM((1, DH), jnp.float32),
            pltpu.SemaphoreType.DMA,
        ],
        compiler_params=pltpu.CompilerParams(vmem_limit_bytes=16 << 20),
        name="project",
    )(after, *rows, w_query, in_hbm(q_gain.reshape(1, DH)))
    return out[:-2], out[-2], out[-1]


def attend_kernel(pieces, after_ref, *refs):
    *refs, token_ref = refs
    token_ref[...] = jnp.zeros_like(token_ref)
    query_refs, kv_refs, out_refs = refs[:pieces], refs[pieces:-pieces], refs[-pieces:]
    cores, group, half = query_refs[0].shape
    rows = cores * group
    sides = kv_refs[0].shape[0]
    lane = lax.broadcasted_iota(jnp.int32, (DH, DH), 1)
    for at in range(0, pieces, 4):
        stop = min(at + 4, pieces)
        queries = [ref[core] for ref in query_refs[at:stop] for core in range(cores)]
        queries = [x.astype(jnp.float32) for x in queries]
        queries = jnp.concatenate(queries, axis=0).astype(jnp.bfloat16)
        stats = [jnp.zeros((DH, DH), jnp.float32) for _ in range(at, stop)]
        for head in range(half // DH):
            cols = slice(head * DH, (head + 1) * DH)
            vals = slice(half + head * DH, half + (head + 1) * DH)
            keys = [ref[side, :, cols] for ref in kv_refs for side in range(sides)]
            values = [ref[side, :, vals] for ref in kv_refs for side in range(sides)]
            scores = lax.dot_general(
                queries[:, cols],
                jnp.concatenate(keys, axis=0),
                (((1,), (1,)), ((), ())),
                preferred_element_type=jnp.float32,
            )
            maxima = jnp.max(scores, axis=-1, keepdims=True)
            weights = jnp.exp(scores - maxima)
            sums = jnp.sum(weights, axis=-1, keepdims=True)
            weighted = jnp.dot(
                weights.astype(jnp.bfloat16),
                jnp.concatenate(values, axis=0),
                preferred_element_type=jnp.float32,
            )
            for j in range(at, stop):
                mine = slice((j - at) * rows, (j - at + 1) * rows)
                out_refs[j][:rows, cols] = weighted[mine]
                pad = jnp.zeros((DH - rows, 1), jnp.float32)
                top = jnp.concatenate([maxima[mine], pad], axis=0)
                total = jnp.concatenate([sums[mine], pad], axis=0)
                stat = jnp.where(lane == 2 * head, top, stats[j - at])
                stats[j - at] = jnp.where(lane == 2 * head + 1, total, stat)
        for j in range(at, stop):
            out_refs[j][rows:, DH:] = jnp.zeros((8, half - DH), jnp.float32)
            out_refs[j][rows:, :DH] = stats[j - at].T[:8]


def attend(after, queries, kv_parts):
    cores, group, half = queries[0].shape
    rows = cores * group
    return pl.pallas_call(
        functools.partial(attend_kernel, len(queries)),
        out_shape=[jax.ShapeDtypeStruct((rows + 8, half), jnp.float32)] * len(queries) + [TOKEN],
        compiler_params=pltpu.CompilerParams(vmem_limit_bytes=24 << 20),
        name="attend",
    )(after, *queries, *kv_parts)


def combine_kernel(pieces, after_ref, *refs):
    part_refs, out_refs = refs[:pieces], refs[pieces:]
    group, half = out_refs[0].shape
    rows = group * len(out_refs)
    stats = []
    for ref in part_refs:
        packed = ref[rows:, :DH]
        packed = jnp.concatenate([packed, jnp.zeros((DH - 8, DH), jnp.float32)], axis=0)
        stats.append(packed.T[:rows])
    for head in range(half // DH):
        cols = slice(head * DH, (head + 1) * DH)
        maxima = [stat[:, 2 * head : 2 * head + 1] for stat in stats]
        top = functools.reduce(jnp.maximum, maxima)
        total = jnp.zeros_like(top)
        attended = jnp.zeros((rows, DH), jnp.float32)
        for ref, stat, maximum in zip(part_refs, stats, maxima):
            factor = jnp.exp(maximum - top)
            total = total + stat[:, 2 * head + 1 : 2 * head + 2] * factor
            attended = attended + ref[:rows, cols] * factor
        attended = attended / total
        for side, out_ref in enumerate(out_refs):
            out_ref[:, cols] = attended[side * group : (side + 1) * group].astype(jnp.bfloat16)


def combine(after, parts, group, pair):
    half = parts[0].shape[1]
    return pl.pallas_call(
        functools.partial(combine_kernel, len(parts)),
        out_shape=[jax.ShapeDtypeStruct((group, half), jnp.bfloat16)] * pair,
        compiler_params=pltpu.CompilerParams(vmem_limit_bytes=16 << 20),
        name="combine",
    )(after, *parts)


def output_kernel(sides, spread_ref, *refs):
    side_refs, w_ref, (*out_refs, token_ref) = refs[:sides], refs[sides], refs[sides + 1 :]
    token_ref[...] = jnp.zeros_like(token_ref)
    group, half = side_refs[0].shape
    slots, width = out_refs[0].shape
    spread = spread_ref[:, :group]
    attended = [
        jnp.dot(spread, ref[...], preferred_element_type=jnp.float32).astype(jnp.bfloat16)
        for ref in side_refs
    ]
    core = my_core(sides)
    starts = [pl.multiple_of((core ^ side) * half, DH) for side in range(sides)]
    step = math.gcd(width, 1024)
    for col in range(0, width, step):
        terms = jnp.zeros((spread.shape[0], step), jnp.float32)
        for start, side in zip(starts, attended):
            terms = terms + jnp.dot(
                side, w_ref[pl.ds(start, half), col : col + step], preferred_element_type=jnp.float32
            )
        for k, out_ref in enumerate(out_refs):
            piece = terms[k * slots : (k + 1) * slots]
            out_ref[:, col : col + step] = piece.astype(out_ref.dtype)


def output(spread, sides, w_out, slots, parts):
    width = w_out.shape[1]
    return pl.pallas_call(
        functools.partial(output_kernel, len(sides)),
        out_shape=[
            jax.ShapeDtypeStruct((slots, width), jnp.bfloat16 if k else jnp.float32)
            for k in range(parts)
        ]
        + [TOKEN],
        compiler_params=pltpu.CompilerParams(vmem_limit_bytes=16 << 20),
        name="output",
    )(spread, *sides, w_out)


def mlp_kernel(pieces, *refs):
    row_refs, (up_ref, down_ref) = refs[:pieces], refs[pieces : pieces + 2]
    *out_refs, act_ref = refs[pieces + 2 :]
    hidden, width = down_ref.shape
    rows = [ref[j] for ref in row_refs for j in range(ref.shape[0])]
    rows = jnp.concatenate(rows, axis=0)
    count = out_refs[0].shape[0]
    step = math.gcd(hidden, 512)
    for col in range(0, hidden, step):
        lifted = jnp.dot(rows, up_ref[:, col : col + step], preferred_element_type=jnp.float32)
        act_ref[:, col : col + step] = jax.nn.gelu(lifted, approximate=True).astype(jnp.bfloat16)
    step = math.gcd(width, 512)
    for col in range(0, width, step):
        down = jnp.dot(
            act_ref[...], down_ref[:, col : col + step], preferred_element_type=jnp.float32
        )
        for side, out_ref in enumerate(out_refs):
            piece = down[side * count : (side + 1) * count]
            out_ref[:, col : col + step] = piece.astype(out_ref.dtype)


def mlp(rows, w_up, w_down, pair):
    count = sum(x.shape[0] * x.shape[1] for x in rows)
    hidden, width = w_down.shape
    return pl.pallas_call(
        functools.partial(mlp_kernel, len(rows)),
        out_shape=[
            jax.ShapeDtypeStruct((count // pair, width), jnp.bfloat16 if side else jnp.float32)
            for side in range(pair)
        ],
        scratch_shapes=[pltpu.VMEM((count, hidden), jnp.bfloat16)],
        compiler_params=pltpu.CompilerParams(vmem_limit_bytes=32 << 20),
        name="mlp",
    )(*rows, w_up, w_down)


def join_kernel(count, *refs):
    part_refs, out_ref = refs[:count], refs[-1]
    for at, ref in enumerate(part_refs):
        out_ref[at] = ref[...]


def join(parts, after=()):
    return pl.pallas_call(
        functools.partial(join_kernel, len(parts)),
        out_shape=jax.ShapeDtypeStruct((len(parts), *parts[0].shape), parts[0].dtype),
        compiler_params=pltpu.CompilerParams(vmem_limit_bytes=8 << 20),
        name="join",
    )(*parts, *after)


def renorm_kernel(hold_ref, rows_ref, mod_ref, *refs):
    *term_refs, after_ref, normed_ref = refs
    branch = term_refs[0][...]
    for ref in term_refs[1:]:
        branch = branch + ref[...].astype(jnp.float32)
    after = rows_ref[...] + mod_ref[2:3, :] * branch
    after_ref[...] = after
    normed_ref[...] = layer_norm(after, mod_ref[3:4, :], mod_ref[4:5, :]).astype(jnp.bfloat16)


def renorm(after, rows_in, modulation, terms):
    return pl.pallas_call(
        renorm_kernel,
        out_shape=[
            jax.ShapeDtypeStruct(rows_in.shape, jnp.float32),
            jax.ShapeDtypeStruct(rows_in.shape, jnp.bfloat16),
        ],
        compiler_params=pltpu.CompilerParams(vmem_limit_bytes=8 << 20),
        name="renorm",
    )(after, rows_in, modulation, *terms)


def fold_kernel(sides, *refs):
    side_refs, out_refs = refs[:sides], refs[sides:]
    slots = out_refs[0].shape[0]
    for j, out_ref in enumerate(out_refs):
        total = side_refs[0][j * slots : (j + 1) * slots]
        for ref in side_refs[1:]:
            total = total + ref[j * slots : (j + 1) * slots].astype(jnp.float32)
        out_ref[...] = total.astype(out_ref.dtype)


def fold(sides, slots):
    count, width = sides[0].shape
    return pl.pallas_call(
        functools.partial(fold_kernel, len(sides)),
        out_shape=[
            jax.ShapeDtypeStruct((slots, width), jnp.bfloat16 if j else jnp.float32)
            for j in range(count // slots)
        ],
        compiler_params=pltpu.CompilerParams(vmem_limit_bytes=8 << 20),
        name="fold",
    )(*sides)


def finish_kernel(select_ref, cached_ref, after_ref, mod_ref, *refs):
    *term_refs, out_ref = refs
    total = term_refs[0][...]
    for ref in term_refs[1:]:
        total = total + ref[...].astype(jnp.float32)
    renewed = (after_ref[...] + mod_ref[5:6, :] * total).astype(jnp.bfloat16)
    select = select_ref[...]
    placed = jnp.dot(select, renewed, preferred_element_type=jnp.float32)
    covered = jnp.sum(select.astype(jnp.float32), axis=1, keepdims=True)
    blended = cached_ref[...].astype(jnp.float32) * (1.0 - covered) + placed
    out_ref[...] = blended.astype(jnp.bfloat16)


def finish(select, cached, after_attn, modulation, terms):
    return pl.pallas_call(
        finish_kernel,
        out_shape=jax.ShapeDtypeStruct(cached.shape, jnp.bfloat16),
        compiler_params=pltpu.CompilerParams(vmem_limit_bytes=8 << 20),
        name="finish",
    )(select, cached, after_attn, modulation, *terms)


def body(
    hidden_in,
    cached_out,
    cache_keys,
    cache_values,
    refresh_idx,
    modulation,
    q_gain,
    w_query,
    w_out,
    w_up,
    w_down,
):
    slots = refresh_idx.shape[0]
    uly_size = lax.axis_size("uly")
    blk_size = lax.axis_size("blk")
    local_heads = w_query.shape[1] // DH
    group = min(slots * uly_size, slots + (uly_size - 1) * OTHER)
    pair = 2 if blk_size % 2 == 0 and local_heads % 2 == 0 else 1
    chips = blk_size // pair

    rows_in, normed, select, modulation, sides = enter(
        refresh_idx, hidden_in, modulation, cache_keys, cache_values, uly_size, pair
    )
    sides = [trade(x, "blk", side) for side, x in enumerate(sides)]
    have = {0: normed}
    for k in sorted(range(1, uly_size), key=lambda k: (bin(k).count("1"), -k)):
        low = k & -k
        have[k] = trade(have[k ^ low], "uly", low)
    group_rows = [have[k] for k in range(uly_size)]
    early = tuple(range(uly_size))[uly_size // 2 : uly_size // 2 + 1]
    late = tuple(k for k in reversed(range(uly_size)) if k not in early)
    *first, token = merge_kv(sides, early, [group_rows[early[0]]])
    w_query, token = hold(token, w_query)
    first = [trade(x, "uly", k) for k, x in zip(early, first)]
    *later, token = merge_kv(sides, late, [token] + group_rows[1:])
    kv_parts = first + [trade(x, "uly", k) for k, x in zip(late, later)]

    queries, spread, token = project(token, group_rows, w_query, q_gain, group, pair)
    w_out, token = hold(token, w_out)
    queries = [trade(x, "blk", side) for side, x in enumerate(queries)]
    queries = join(queries)
    queries = [trade(queries, "blk", j * pair) for j in range(chips)]
    *parts, token = attend(token, queries, kv_parts)
    w_up, token = hold(token, w_up)
    parts = [trade(x, "blk", j * pair) for j, x in enumerate(parts)]
    attended = combine(token, parts, group, pair)
    attended = [trade(x, "blk", side) for side, x in enumerate(attended)]
    *terms, token = output(spread, attended, w_out, slots, uly_size)
    w_down, cached, token = hold(token, w_down, cached_out)
    terms = [trade(x, "uly", k) for k, x in enumerate(terms)]
    after_attn, norm_mlp = renorm(token, rows_in, modulation, terms)

    rows = [join([trade(norm_mlp, "blk", j * pair) for j in range(chips)])]
    if pair == 2:
        rows.append(trade(rows[0], "blk", 1))
    down = mlp(rows, w_up, w_down, pair)
    down = [trade(x, "blk", side) for side, x in enumerate(down)]
    terms = [trade(x, "blk", j * pair) for j, x in enumerate(fold(down, slots))]
    return finish(select, cached, after_attn, modulation, terms)


def solution(mesh):
    return jax.shard_map(
        body,
        mesh=mesh,
        in_specs=(
            P(("blk", "uly"), None),
            P(("blk", "uly"), None),
            P(("blk", "uly"), None),
            P(("blk", "uly"), None),
            P(("blk", "uly")),
            P(),
            P(),
            P(None, "uly"),
            P("uly", None),
            P(None, "blk"),
            P("blk", None),
        ),
        out_specs=P(("blk", "uly"), None),
        check_vma=False,
    )
```

```python
import functools
import math

import jax
import jax.numpy as jnp
from jax import lax
from jax.experimental import pallas as pl
from jax.experimental.pallas import tpu as pltpu
from jax.sharding import PartitionSpec as P

DH = 128
OTHER = 8
VMEM_SPEC = pl.BlockSpec(memory_space=pltpu.VMEM)
TOKEN = jax.ShapeDtypeStruct((8, DH), jnp.float32)
ANY_SPEC = pl.BlockSpec(memory_space=pl.ANY)


def double(x, axis, scale, count, on_arrival=()):
    have = {0: x}
    for k in sorted(range(1, count), key=lambda k: (bin(k).count("1"), -k)):
        low = k & -k
        have[k] = trade(have[k ^ low], axis, low * scale)
        if k in on_arrival:
            have[k] = on_arrival[k](have[k])
    return [have[k] for k in range(count)]


def layer_norm(row_block, shift_by, scale_by):
    average = jnp.mean(row_block, axis=-1, keepdims=True)
    centred = row_block - average
    spread = jnp.mean(centred * centred, axis=-1, keepdims=True)
    return centred * lax.rsqrt(spread + 1e-06) * (1.0 + scale_by) + shift_by


def trade(x, axis, flip):
    if flip == 0:
        return x
    return lax.ppermute(x, axis, [(i, i ^ flip) for i in range(lax.axis_size(axis))])


def in_hbm(x):
    return pltpu.with_memory_space_constraint(x, pltpu.HBM)


def hold_kernel(count, *refs):
    source_refs, sems = refs[1 : count + 1], refs[-1]
    *held_refs, token_ref = refs[count + 1 : -1]
    token_ref[...] = jnp.zeros_like(token_ref)
    copies = [
        pltpu.make_async_copy(source_ref, held_ref, sems.at[i])
        for i, (source_ref, held_ref) in enumerate(zip(source_refs, held_refs))
    ]
    for copy in copies:
        copy.start()
    for copy in copies:
        copy.wait()


def hold(after, *weights):
    count = len(weights)
    moved = sum(w.size * w.dtype.itemsize for w in weights)
    return pl.pallas_call(
        functools.partial(hold_kernel, count),
        in_specs=[VMEM_SPEC] + [ANY_SPEC] * count,
        out_specs=[VMEM_SPEC] * (count + 1),
        out_shape=[pltpu.VMEM(w.shape, w.dtype) for w in weights] + [TOKEN],
        scratch_shapes=[pltpu.SemaphoreType.DMA((count,))],
        cost_estimate=pl.CostEstimate(flops=0, bytes_accessed=moved, transcendentals=0),
        compiler_params=pltpu.CompilerParams(vmem_limit_bytes=2 << 20),
        name="hold",
    )(after, *[in_hbm(w) for w in weights])


def my_core(pair):
    return lax.rem(lax.axis_index("blk"), pair)


def enter_kernel(pair, idx_hbm, hidden_hbm, mod_hbm, key_hbm, value_hbm, *refs):
    rows_ref, normed_ref, select_ref, mod_ref, *side_refs = refs[: pair + 4]
    idx_ref, hidden_ref, sems, kv_sem = refs[pair + 4 :]
    copies = [
        pltpu.make_async_copy(source, target, sems.at[i])
        for i, (source, target) in enumerate(
            [(idx_hbm, idx_ref), (hidden_hbm, hidden_ref), (mod_hbm, mod_ref)]
        )
    ]
    for copy in copies:
        copy.start()
    parts, _, both = side_refs[0].shape
    half = both // 2
    uly, core = lax.axis_index("uly"), my_core(pair)
    kv_copies = []
    for side, side_ref in enumerate(side_refs):
        for flip in range(parts):
            start = pl.multiple_of(((uly ^ flip) * pair + (core ^ side)) * half, DH)
            for at, source in enumerate((key_hbm, value_hbm)):
                copy = pltpu.make_async_copy(
                    source.at[:, pl.ds(start, half)],
                    side_ref.at[flip, :, pl.ds(at * half, half)],
                    kv_sem.at[side, flip, at],
                )
                copy.start()
                kv_copies.append(copy)
    for copy in copies:
        copy.wait()
    tokens, width = hidden_ref.shape
    slots = idx_ref.shape[1]
    position = lax.broadcasted_iota(jnp.int32, (tokens, slots), 0)
    select = (position == idx_ref[...]).astype(jnp.float32).astype(jnp.bfloat16)
    select_ref[...] = select
    contract = (((0,), (0,)), ((), ()))
    rows = lax.dot_general(
        select, hidden_ref[...], contract, preferred_element_type=jnp.float32
    )
    live = lax.dot_general(
        select,
        jnp.ones((tokens, DH), jnp.bfloat16),
        contract,
        preferred_element_type=jnp.float32,
    )
    rows_ref[...] = rows
    normed = layer_norm(rows, mod_ref[0:1, :], mod_ref[1:2, :])
    normed_ref[:, :width] = normed.astype(jnp.bfloat16)
    normed_ref[:, width:] = live.astype(jnp.bfloat16)
    for copy in kv_copies:
        copy.wait()


def enter(refresh_idx, hidden_in, modulation, cache_keys, cache_values, parts, pair):
    slots = refresh_idx.shape[0]
    tokens, width = hidden_in.shape
    both = 2 * width // (parts * pair)
    out = pl.pallas_call(
        functools.partial(enter_kernel, pair),
        in_specs=[ANY_SPEC] * 5,
        out_specs=[VMEM_SPEC] * (pair + 4),
        out_shape=[
            pltpu.VMEM((slots, width), jnp.float32),
            pltpu.VMEM((slots, width + DH), jnp.bfloat16),
            pltpu.VMEM((tokens, slots), jnp.bfloat16),
            pltpu.VMEM(modulation.shape, modulation.dtype),
        ]
        + [pltpu.VMEM((parts, tokens, both), cache_keys.dtype)] * pair,
        scratch_shapes=[
            pltpu.VMEM((1, slots), jnp.int32),
            pltpu.VMEM(hidden_in.shape, hidden_in.dtype),
            pltpu.SemaphoreType.DMA((3,)),
            pltpu.SemaphoreType.DMA((pair, parts, 2)),
        ],
        compiler_params=pltpu.CompilerParams(vmem_limit_bytes=8 << 20),
        name="enter",
    )(
        *[
            in_hbm(x)
            for x in (refresh_idx.reshape(1, slots), hidden_in, modulation, cache_keys, cache_values)
        ]
    )
    return *out[:4], out[4:]


def merge_kv_kernel(sides, flips, *refs):
    *refs, token_ref = refs
    token_ref[...] = jnp.zeros_like(token_ref)
    for flip, out_ref in zip(flips, refs[-len(flips) :]):
        for side in range(sides):
            out_ref[side] = refs[side][flip]


def merge_kv(sides, flips, after):
    _, tokens, both = sides[0].shape
    *merged, token = pl.pallas_call(
        functools.partial(merge_kv_kernel, len(sides), flips),
        out_specs=[VMEM_SPEC] * (len(flips) + 1),
        out_shape=[pltpu.VMEM((len(sides), tokens, both), sides[0].dtype) for _ in flips]
        + [TOKEN],
        compiler_params=pltpu.CompilerParams(vmem_limit_bytes=8 << 20),
        name="merge_kv",
    )(*sides, *after)
    return merged, token


def relay_kernel(x_ref, after_ref, out_ref):
    out_ref[...] = x_ref[...]


def relay(x, after):
    return pl.pallas_call(
        relay_kernel,
        out_specs=VMEM_SPEC,
        out_shape=pltpu.VMEM(x.shape, x.dtype),
        compiler_params=pltpu.CompilerParams(vmem_limit_bytes=2 << 20),
        name="relay",
    )(x, after)


def project_kernel(pieces, after_ref, *refs):
    rows_refs, (w_ref, gain_hbm_ref) = refs[:pieces], refs[pieces : pieces + 2]
    *query_refs, spread_ref, token_ref, heads_ref, gain_ref, sem = refs[pieces + 2 :]
    token_ref[...] = jnp.zeros_like(token_ref)
    copy = pltpu.make_async_copy(gain_hbm_ref, gain_ref, sem)
    copy.start()
    core = my_core(len(query_refs))
    width = w_ref.shape[0]
    group, half = query_refs[0].shape
    rows = jnp.concatenate([ref[...] for ref in rows_refs], axis=0)
    everyone = rows.shape[0]
    flags = rows[:, width:]
    shape = (everyone, everyone)
    before = lax.broadcasted_iota(jnp.int32, shape, 1) < lax.broadcasted_iota(jnp.int32, shape, 0)
    before = before.astype(jnp.float32).astype(jnp.bfloat16)
    rank = jnp.dot(before, flags, preferred_element_type=jnp.float32)
    lane = lax.broadcasted_iota(jnp.int32, rank.shape, 1).astype(jnp.float32)
    spread = jnp.where((rank == lane) & (flags.astype(jnp.float32) > 0.0), 1.0, 0.0)
    spread = spread.astype(jnp.bfloat16)
    spread_ref[...] = spread
    live_rows = lax.dot_general(
        spread[:, :group],
        rows[:, :width],
        (((0,), (0,)), ((), ())),
        preferred_element_type=jnp.float32,
    ).astype(jnp.bfloat16)
    projected = jnp.dot(live_rows, w_ref[...], preferred_element_type=jnp.float32)
    copy.wait()
    for start in range(0, projected.shape[1], DH):
        head = projected[:, start : start + DH]
        squares = jnp.mean(head * head, axis=-1, keepdims=True)
        heads_ref[:, start : start + DH] = (
            head * lax.rsqrt(squares + 1e-06) * (gain_ref[...] / math.sqrt(DH))
        )
    for side, query_ref in enumerate(query_refs):
        start = pl.multiple_of((core ^ side) * half, DH)
        query_ref[...] = heads_ref[:, pl.ds(start, half)].astype(jnp.bfloat16)


def project(after, rows, w_query, q_gain, group, pair):
    half = w_query.shape[1] // pair
    everyone = len(rows) * rows[0].shape[0]
    query = jax.ShapeDtypeStruct((group, half), jnp.bfloat16)
    out = pl.pallas_call(
        functools.partial(project_kernel, len(rows)),
        in_specs=[VMEM_SPEC] * (len(rows) + 2) + [ANY_SPEC],
        out_shape=[query] * pair + [jax.ShapeDtypeStruct((everyone, DH), jnp.bfloat16), TOKEN],
        scratch_shapes=[
            pltpu.VMEM((group, w_query.shape[1]), jnp.float32),
            pltpu.VMEM((1, DH), jnp.float32),
            pltpu.SemaphoreType.DMA,
        ],
        compiler_params=pltpu.CompilerParams(vmem_limit_bytes=16 << 20),
        name="project",
    )(after, *rows, w_query, in_hbm(q_gain.reshape(1, DH)))
    return out[:-2], out[-2], out[-1]


def attend_kernel(pieces, after_ref, *refs):
    *refs, token_ref = refs
    token_ref[...] = jnp.zeros_like(token_ref)
    query_refs, kv_refs, out_refs = refs[:pieces], refs[pieces:-pieces], refs[-pieces:]
    cores, group, half = query_refs[0].shape
    rows = cores * group
    sides = kv_refs[0].shape[0]
    lane = lax.broadcasted_iota(jnp.int32, (DH, DH), 1)
    for at in range(0, pieces, 4):
        stop = min(at + 4, pieces)
        queries = [ref[core] for ref in query_refs[at:stop] for core in range(cores)]
        queries = [x.astype(jnp.float32) for x in queries]
        queries = jnp.concatenate(queries, axis=0).astype(jnp.bfloat16)
        stats = [jnp.zeros((DH, DH), jnp.float32) for _ in range(at, stop)]
        for head in range(half // DH):
            cols = slice(head * DH, (head + 1) * DH)
            vals = slice(half + head * DH, half + (head + 1) * DH)
            keys = [ref[side, :, cols] for ref in kv_refs for side in range(sides)]
            values = [ref[side, :, vals] for ref in kv_refs for side in range(sides)]
            scores = lax.dot_general(
                queries[:, cols],
                jnp.concatenate(keys, axis=0),
                (((1,), (1,)), ((), ())),
                preferred_element_type=jnp.float32,
            )
            maxima = jnp.max(scores, axis=-1, keepdims=True)
            weights = jnp.exp(scores - maxima)
            sums = jnp.sum(weights, axis=-1, keepdims=True)
            weighted = jnp.dot(
                weights.astype(jnp.bfloat16),
                jnp.concatenate(values, axis=0),
                preferred_element_type=jnp.float32,
            )
            for j in range(at, stop):
                mine = slice((j - at) * rows, (j - at + 1) * rows)
                out_refs[j][:rows, cols] = weighted[mine]
                pad = jnp.zeros((DH - rows, 1), jnp.float32)
                top = jnp.concatenate([maxima[mine], pad], axis=0)
                total = jnp.concatenate([sums[mine], pad], axis=0)
                stat = jnp.where(lane == 2 * head, top, stats[j - at])
                stats[j - at] = jnp.where(lane == 2 * head + 1, total, stat)
        for j in range(at, stop):
            out_refs[j][rows:, DH:] = jnp.zeros((8, half - DH), jnp.float32)
            out_refs[j][rows:, :DH] = stats[j - at].T[:8]


def attend(after, queries, kv_parts):
    cores, group, half = queries[0].shape
    rows = cores * group
    return pl.pallas_call(
        functools.partial(attend_kernel, len(queries)),
        out_shape=[jax.ShapeDtypeStruct((rows + 8, half), jnp.float32)] * len(queries) + [TOKEN],
        compiler_params=pltpu.CompilerParams(vmem_limit_bytes=24 << 20),
        name="attend",
    )(after, *queries, *kv_parts)


def combine_kernel(pieces, after_ref, *refs):
    part_refs, out_refs = refs[:pieces], refs[pieces:]
    group, half = out_refs[0].shape
    rows = group * len(out_refs)
    stats = []
    for ref in part_refs:
        packed = ref[rows:, :DH]
        packed = jnp.concatenate([packed, jnp.zeros((DH - 8, DH), jnp.float32)], axis=0)
        stats.append(packed.T[:rows])
    for head in range(half // DH):
        cols = slice(head * DH, (head + 1) * DH)
        maxima = [stat[:, 2 * head : 2 * head + 1] for stat in stats]
        top = functools.reduce(jnp.maximum, maxima)
        total = jnp.zeros_like(top)
        attended = jnp.zeros((rows, DH), jnp.float32)
        for ref, stat, maximum in zip(part_refs, stats, maxima):
            factor = jnp.exp(maximum - top)
            total = total + stat[:, 2 * head + 1 : 2 * head + 2] * factor
            attended = attended + ref[:rows, cols] * factor
        attended = attended / total
        for side, out_ref in enumerate(out_refs):
            out_ref[:, cols] = attended[side * group : (side + 1) * group].astype(jnp.bfloat16)


def combine(after, parts, group, pair):
    half = parts[0].shape[1]
    return pl.pallas_call(
        functools.partial(combine_kernel, len(parts)),
        out_shape=[jax.ShapeDtypeStruct((group, half), jnp.bfloat16)] * pair,
        compiler_params=pltpu.CompilerParams(vmem_limit_bytes=16 << 20),
        name="combine",
    )(after, *parts)


def output_kernel(sides, spread_ref, *refs):
    side_refs, w_ref, (*out_refs, token_ref) = refs[:sides], refs[sides], refs[sides + 1 :]
    token_ref[...] = jnp.zeros_like(token_ref)
    group, half = side_refs[0].shape
    slots, width = out_refs[0].shape
    spread = spread_ref[:, :group]
    attended = [
        jnp.dot(spread, ref[...], preferred_element_type=jnp.float32).astype(jnp.bfloat16)
        for ref in side_refs
    ]
    core = my_core(sides)
    starts = [pl.multiple_of((core ^ side) * half, DH) for side in range(sides)]
    step = math.gcd(width, 1024)
    for col in range(0, width, step):
        terms = jnp.zeros((spread.shape[0], step), jnp.float32)
        for start, side in zip(starts, attended):
            terms = terms + jnp.dot(
                side, w_ref[pl.ds(start, half), col : col + step], preferred_element_type=jnp.float32
            )
        for k, out_ref in enumerate(out_refs):
            piece = terms[k * slots : (k + 1) * slots]
            out_ref[:, col : col + step] = piece.astype(out_ref.dtype)


def output(spread, sides, w_out, slots, parts):
    width = w_out.shape[1]
    return pl.pallas_call(
        functools.partial(output_kernel, len(sides)),
        out_shape=[
            jax.ShapeDtypeStruct((slots, width), jnp.bfloat16 if k else jnp.float32)
            for k in range(parts)
        ]
        + [TOKEN],
        compiler_params=pltpu.CompilerParams(vmem_limit_bytes=16 << 20),
        name="output",
    )(spread, *sides, w_out)


def mlp_kernel(pieces, *refs):
    row_refs, (up_ref, down_ref) = refs[:pieces], refs[pieces : pieces + 2]
    *out_refs, act_ref = refs[pieces + 2 :]
    hidden, width = down_ref.shape
    rows = [ref[j] for ref in row_refs for j in range(ref.shape[0])]
    rows = jnp.concatenate(rows, axis=0)
    count = out_refs[0].shape[0]
    step = math.gcd(hidden, 512)
    for col in range(0, hidden, step):
        lifted = jnp.dot(rows, up_ref[:, col : col + step], preferred_element_type=jnp.float32)
        act_ref[:, col : col + step] = jax.nn.gelu(lifted, approximate=True).astype(jnp.bfloat16)
    step = math.gcd(width, 512)
    for col in range(0, width, step):
        down = jnp.dot(
            act_ref[...], down_ref[:, col : col + step], preferred_element_type=jnp.float32
        )
        for side, out_ref in enumerate(out_refs):
            piece = down[side * count : (side + 1) * count]
            out_ref[:, col : col + step] = piece.astype(out_ref.dtype)


def mlp(rows, w_up, w_down, pair):
    count = sum(x.shape[0] * x.shape[1] for x in rows)
    hidden, width = w_down.shape
    return pl.pallas_call(
        functools.partial(mlp_kernel, len(rows)),
        out_shape=[
            jax.ShapeDtypeStruct((count // pair, width), jnp.bfloat16 if side else jnp.float32)
            for side in range(pair)
        ],
        scratch_shapes=[pltpu.VMEM((count, hidden), jnp.bfloat16)],
        compiler_params=pltpu.CompilerParams(vmem_limit_bytes=32 << 20),
        name="mlp",
    )(*rows, w_up, w_down)


def join_kernel(count, *refs):
    part_refs, out_ref = refs[:count], refs[-1]
    for at, ref in enumerate(part_refs):
        out_ref[at] = ref[...]


def join(parts, after=()):
    return pl.pallas_call(
        functools.partial(join_kernel, len(parts)),
        out_shape=jax.ShapeDtypeStruct((len(parts), *parts[0].shape), parts[0].dtype),
        compiler_params=pltpu.CompilerParams(vmem_limit_bytes=8 << 20),
        name="join",
    )(*parts, *after)


def renorm_kernel(hold_ref, rows_ref, mod_ref, *refs):
    *term_refs, after_ref, normed_ref = refs
    branch = term_refs[0][...]
    for ref in term_refs[1:]:
        branch = branch + ref[...].astype(jnp.float32)
    after = rows_ref[...] + mod_ref[2:3, :] * branch
    after_ref[...] = after
    normed_ref[...] = layer_norm(after, mod_ref[3:4, :], mod_ref[4:5, :]).astype(jnp.bfloat16)


def renorm(after, rows_in, modulation, terms):
    return pl.pallas_call(
        renorm_kernel,
        out_shape=[
            jax.ShapeDtypeStruct(rows_in.shape, jnp.float32),
            jax.ShapeDtypeStruct(rows_in.shape, jnp.bfloat16),
        ],
        compiler_params=pltpu.CompilerParams(vmem_limit_bytes=8 << 20),
        name="renorm",
    )(after, rows_in, modulation, *terms)


def fold_kernel(sides, *refs):
    side_refs, out_refs = refs[:sides], refs[sides:]
    slots = out_refs[0].shape[0]
    for j, out_ref in enumerate(out_refs):
        total = side_refs[0][j * slots : (j + 1) * slots]
        for ref in side_refs[1:]:
            total = total + ref[j * slots : (j + 1) * slots].astype(jnp.float32)
        out_ref[...] = total.astype(out_ref.dtype)


def fold(sides, slots):
    count, width = sides[0].shape
    return pl.pallas_call(
        functools.partial(fold_kernel, len(sides)),
        out_shape=[
            jax.ShapeDtypeStruct((slots, width), jnp.bfloat16 if j else jnp.float32)
            for j in range(count // slots)
        ],
        compiler_params=pltpu.CompilerParams(vmem_limit_bytes=8 << 20),
        name="fold",
    )(*sides)


def finish_kernel(select_ref, cached_ref, after_ref, mod_ref, *refs):
    *term_refs, out_ref = refs
    total = term_refs[0][...]
    for ref in term_refs[1:]:
        total = total + ref[...].astype(jnp.float32)
    renewed = (after_ref[...] + mod_ref[5:6, :] * total).astype(jnp.bfloat16)
    select = select_ref[...]
    placed = jnp.dot(select, renewed, preferred_element_type=jnp.float32)
    covered = jnp.sum(select.astype(jnp.float32), axis=1, keepdims=True)
    blended = cached_ref[...].astype(jnp.float32) * (1.0 - covered) + placed
    out_ref[...] = blended.astype(jnp.bfloat16)


def finish(select, cached, after_attn, modulation, terms):
    return pl.pallas_call(
        finish_kernel,
        out_shape=jax.ShapeDtypeStruct(cached.shape, jnp.bfloat16),
        compiler_params=pltpu.CompilerParams(vmem_limit_bytes=8 << 20),
        name="finish",
    )(select, cached, after_attn, modulation, *terms)


def body(
    hidden_in,
    cached_out,
    cache_keys,
    cache_values,
    refresh_idx,
    modulation,
    q_gain,
    w_query,
    w_out,
    w_up,
    w_down,
):
    slots = refresh_idx.shape[0]
    uly_size = lax.axis_size("uly")
    blk_size = lax.axis_size("blk")
    local_heads = w_query.shape[1] // DH
    group = min(slots * uly_size, slots + (uly_size - 1) * OTHER)
    pair = 2 if blk_size % 2 == 0 and local_heads % 2 == 0 else 1
    chips = blk_size // pair

    rows_in, normed, select, modulation, sides = enter(
        refresh_idx, hidden_in, modulation, cache_keys, cache_values, uly_size, pair
    )
    sides = [trade(x, "blk", side) for side, x in enumerate(sides)]
    w_query, token = hold(normed, w_query)
    half_way = uly_size // 2
    group_rows = double(normed, "uly", 1, uly_size, {half_way: lambda x: relay(x, token)})
    cuts = [[half_way], [k for k in reversed(range(uly_size)) if k not in (1, half_way)]]
    first, token = merge_kv(sides, cuts[0], [group_rows[half_way]])
    second, token = merge_kv(sides, cuts[1], [token] + group_rows[1:])
    kv_parts = [trade(x, "uly", k) for k, x in zip(cuts[0] + cuts[1], first + second)]

    queries, spread, token = project(token, group_rows, w_query, q_gain, group, pair)
    last, _ = merge_kv(sides, [1], [token])
    kv_parts.append(trade(last[0], "uly", 1))
    w_out, token = hold(token, w_out)
    queries = join([trade(x, "blk", side) for side, x in enumerate(queries)])
    queries = double(queries, "blk", pair, chips)
    *parts, token = attend(token, queries, kv_parts)
    w_up, token = hold(token, w_up)
    parts = [trade(x, "blk", j * pair) for j, x in enumerate(parts)]
    attended = combine(token, parts, group, pair)
    attended = [trade(x, "blk", side) for side, x in enumerate(attended)]
    *terms, token = output(spread, attended, w_out, slots, uly_size)
    w_down, cached, token = hold(token, w_down, cached_out)
    terms = [trade(x, "uly", k) for k, x in enumerate(terms)]
    after_attn, norm_mlp = renorm(token, rows_in, modulation, terms)

    rows = [join([trade(norm_mlp, "blk", j * pair) for j in range(chips)])]
    if pair == 2:
        rows.append(trade(rows[0], "blk", 1))
    down = mlp(rows, w_up, w_down, pair)
    down = [trade(x, "blk", side) for side, x in enumerate(down)]
    terms = [trade(x, "blk", j * pair) for j, x in enumerate(fold(down, slots))]
    return finish(select, cached, after_attn, modulation, terms)


def solution(mesh):
    return jax.shard_map(
        body,
        mesh=mesh,
        in_specs=(
            P(("blk", "uly"), None),
            P(("blk", "uly"), None),
            P(("blk", "uly"), None),
            P(("blk", "uly"), None),
            P(("blk", "uly")),
            P(),
            P(),
            P(None, "uly"),
            P("uly", None),
            P(None, "blk"),
            P("blk", None),
        ),
        out_specs=P(("blk", "uly"), None),
        check_vma=False,
    )
```

```python
import functools
import math

import jax
import jax.numpy as jnp
from jax import lax
from jax.experimental import pallas as pl
from jax.experimental.pallas import tpu as pltpu
from jax.sharding import PartitionSpec as P

DH = 128
OTHER = 8
VMEM_SPEC = pl.BlockSpec(memory_space=pltpu.VMEM)
TOKEN = jax.ShapeDtypeStruct((8, DH), jnp.float32)
ANY_SPEC = pl.BlockSpec(memory_space=pl.ANY)


def swap_chips(parts, pair):
    size = lax.axis_size("blk")
    groups = [[i for i in range(size) if i % pair == core] for core in range(pair)]
    return lax.all_to_all(
        parts, "blk", split_axis=0, concat_axis=0, tiled=True, axis_index_groups=groups
    )


def my_chip(pair):
    return lax.axis_index("blk") // pair


def double(x, axis, scale, count, on_arrival=()):
    have = {0: x}
    for k in sorted(range(1, count), key=lambda k: (bin(k).count("1"), -k)):
        low = k & -k
        have[k] = trade(have[k ^ low], axis, low * scale)
        if k in on_arrival:
            have[k] = on_arrival[k](have[k])
    return [have[k] for k in range(count)]


def layer_norm(row_block, shift_by, scale_by):
    average = jnp.mean(row_block, axis=-1, keepdims=True)
    centred = row_block - average
    spread = jnp.mean(centred * centred, axis=-1, keepdims=True)
    return centred * lax.rsqrt(spread + 1e-06) * (1.0 + scale_by) + shift_by


def trade(x, axis, flip):
    if flip == 0:
        return x
    return lax.ppermute(x, axis, [(i, i ^ flip) for i in range(lax.axis_size(axis))])


def in_hbm(x):
    return pltpu.with_memory_space_constraint(x, pltpu.HBM)


def hold_kernel(count, *refs):
    source_refs, sems = refs[1 : count + 1], refs[-1]
    *held_refs, token_ref = refs[count + 1 : -1]
    token_ref[...] = jnp.zeros_like(token_ref)
    copies = [
        pltpu.make_async_copy(source_ref, held_ref, sems.at[i])
        for i, (source_ref, held_ref) in enumerate(zip(source_refs, held_refs))
    ]
    for copy in copies:
        copy.start()
    for copy in copies:
        copy.wait()


def hold(after, *weights):
    count = len(weights)
    moved = sum(w.size * w.dtype.itemsize for w in weights)
    return pl.pallas_call(
        functools.partial(hold_kernel, count),
        in_specs=[VMEM_SPEC] + [ANY_SPEC] * count,
        out_specs=[VMEM_SPEC] * (count + 1),
        out_shape=[pltpu.VMEM(w.shape, w.dtype) for w in weights] + [TOKEN],
        scratch_shapes=[pltpu.SemaphoreType.DMA((count,))],
        cost_estimate=pl.CostEstimate(flops=0, bytes_accessed=moved, transcendentals=0),
        compiler_params=pltpu.CompilerParams(vmem_limit_bytes=2 << 20),
        name="hold",
    )(after, *[in_hbm(w) for w in weights])


def my_core(pair):
    return lax.rem(lax.axis_index("blk"), pair)


def enter_kernel(pair, idx_hbm, hidden_hbm, mod_hbm, key_hbm, value_hbm, *refs):
    rows_ref, normed_ref, select_ref, mod_ref, *side_refs = refs[: pair + 4]
    idx_ref, hidden_ref, sems, kv_sem = refs[pair + 4 :]
    copies = [
        pltpu.make_async_copy(source, target, sems.at[i])
        for i, (source, target) in enumerate(
            [(idx_hbm, idx_ref), (hidden_hbm, hidden_ref), (mod_hbm, mod_ref)]
        )
    ]
    for copy in copies:
        copy.start()
    parts, _, both = side_refs[0].shape
    half = both // 2
    uly, core = lax.axis_index("uly"), my_core(pair)
    kv_copies = []
    for side, side_ref in enumerate(side_refs):
        for flip in range(parts):
            start = pl.multiple_of(((uly ^ flip) * pair + (core ^ side)) * half, DH)
            for at, source in enumerate((key_hbm, value_hbm)):
                copy = pltpu.make_async_copy(
                    source.at[:, pl.ds(start, half)],
                    side_ref.at[flip, :, pl.ds(at * half, half)],
                    kv_sem.at[side, flip, at],
                )
                copy.start()
                kv_copies.append(copy)
    for copy in copies:
        copy.wait()
    tokens, width = hidden_ref.shape
    slots = idx_ref.shape[1]
    position = lax.broadcasted_iota(jnp.int32, (tokens, slots), 0)
    select = (position == idx_ref[...]).astype(jnp.float32).astype(jnp.bfloat16)
    select_ref[...] = select
    contract = (((0,), (0,)), ((), ()))
    rows = lax.dot_general(
        select, hidden_ref[...], contract, preferred_element_type=jnp.float32
    )
    live = lax.dot_general(
        select,
        jnp.ones((tokens, DH), jnp.bfloat16),
        contract,
        preferred_element_type=jnp.float32,
    )
    rows_ref[...] = rows
    normed = layer_norm(rows, mod_ref[0:1, :], mod_ref[1:2, :])
    normed_ref[:, :width] = normed.astype(jnp.bfloat16)
    normed_ref[:, width:] = live.astype(jnp.bfloat16)
    for copy in kv_copies:
        copy.wait()


def enter(refresh_idx, hidden_in, modulation, cache_keys, cache_values, parts, pair):
    slots = refresh_idx.shape[0]
    tokens, width = hidden_in.shape
    both = 2 * width // (parts * pair)
    out = pl.pallas_call(
        functools.partial(enter_kernel, pair),
        in_specs=[ANY_SPEC] * 5,
        out_specs=[VMEM_SPEC] * (pair + 4),
        out_shape=[
            pltpu.VMEM((slots, width), jnp.float32),
            pltpu.VMEM((slots, width + DH), jnp.bfloat16),
            pltpu.VMEM((tokens, slots), jnp.bfloat16),
            pltpu.VMEM(modulation.shape, modulation.dtype),
        ]
        + [pltpu.VMEM((parts, tokens, both), cache_keys.dtype)] * pair,
        scratch_shapes=[
            pltpu.VMEM((1, slots), jnp.int32),
            pltpu.VMEM(hidden_in.shape, hidden_in.dtype),
            pltpu.SemaphoreType.DMA((3,)),
            pltpu.SemaphoreType.DMA((pair, parts, 2)),
        ],
        compiler_params=pltpu.CompilerParams(vmem_limit_bytes=8 << 20),
        name="enter",
    )(
        *[
            in_hbm(x)
            for x in (refresh_idx.reshape(1, slots), hidden_in, modulation, cache_keys, cache_values)
        ]
    )
    return *out[:4], out[4:]


def merge_kv_kernel(sides, flips, *refs):
    *refs, token_ref = refs
    token_ref[...] = jnp.zeros_like(token_ref)
    for flip, out_ref in zip(flips, refs[-len(flips) :]):
        for side in range(sides):
            out_ref[side] = refs[side][flip]


def merge_kv(sides, flips, after):
    _, tokens, both = sides[0].shape
    *merged, token = pl.pallas_call(
        functools.partial(merge_kv_kernel, len(sides), flips),
        out_specs=[VMEM_SPEC] * (len(flips) + 1),
        out_shape=[pltpu.VMEM((len(sides), tokens, both), sides[0].dtype) for _ in flips]
        + [TOKEN],
        compiler_params=pltpu.CompilerParams(vmem_limit_bytes=8 << 20),
        name="merge_kv",
    )(*sides, *after)
    return merged, token


def relay_kernel(x_ref, after_ref, out_ref):
    out_ref[...] = x_ref[...]


def relay(x, after):
    return pl.pallas_call(
        relay_kernel,
        out_specs=VMEM_SPEC,
        out_shape=pltpu.VMEM(x.shape, x.dtype),
        compiler_params=pltpu.CompilerParams(vmem_limit_bytes=2 << 20),
        name="relay",
    )(x, after)


def project_kernel(pieces, after_ref, *refs):
    rows_refs, (w_ref, gain_hbm_ref) = refs[:pieces], refs[pieces : pieces + 2]
    *query_refs, spread_ref, token_ref, heads_ref, gain_ref, sem = refs[pieces + 2 :]
    token_ref[...] = jnp.zeros_like(token_ref)
    copy = pltpu.make_async_copy(gain_hbm_ref, gain_ref, sem)
    copy.start()
    core = my_core(len(query_refs))
    width = w_ref.shape[0]
    group, half = query_refs[0].shape
    rows = jnp.concatenate([ref[...] for ref in rows_refs], axis=0)
    everyone = rows.shape[0]
    flags = rows[:, width:]
    shape = (everyone, everyone)
    before = lax.broadcasted_iota(jnp.int32, shape, 1) < lax.broadcasted_iota(jnp.int32, shape, 0)
    before = before.astype(jnp.float32).astype(jnp.bfloat16)
    rank = jnp.dot(before, flags, preferred_element_type=jnp.float32)
    lane = lax.broadcasted_iota(jnp.int32, rank.shape, 1).astype(jnp.float32)
    spread = jnp.where((rank == lane) & (flags.astype(jnp.float32) > 0.0), 1.0, 0.0)
    spread = spread.astype(jnp.bfloat16)
    spread_ref[...] = spread
    live_rows = lax.dot_general(
        spread[:, :group],
        rows[:, :width],
        (((0,), (0,)), ((), ())),
        preferred_element_type=jnp.float32,
    ).astype(jnp.bfloat16)
    projected = jnp.dot(live_rows, w_ref[...], preferred_element_type=jnp.float32)
    copy.wait()
    for start in range(0, projected.shape[1], DH):
        head = projected[:, start : start + DH]
        squares = jnp.mean(head * head, axis=-1, keepdims=True)
        heads_ref[:, start : start + DH] = (
            head * lax.rsqrt(squares + 1e-06) * (gain_ref[...] / math.sqrt(DH))
        )
    for side, query_ref in enumerate(query_refs):
        start = pl.multiple_of((core ^ side) * half, DH)
        query_ref[...] = heads_ref[:, pl.ds(start, half)].astype(jnp.bfloat16)


def project(after, rows, w_query, q_gain, group, pair):
    half = w_query.shape[1] // pair
    everyone = len(rows) * rows[0].shape[0]
    query = jax.ShapeDtypeStruct((group, half), jnp.bfloat16)
    out = pl.pallas_call(
        functools.partial(project_kernel, len(rows)),
        in_specs=[VMEM_SPEC] * (len(rows) + 2) + [ANY_SPEC],
        out_shape=[query] * pair + [jax.ShapeDtypeStruct((everyone, DH), jnp.bfloat16), TOKEN],
        scratch_shapes=[
            pltpu.VMEM((group, w_query.shape[1]), jnp.float32),
            pltpu.VMEM((1, DH), jnp.float32),
            pltpu.SemaphoreType.DMA,
        ],
        compiler_params=pltpu.CompilerParams(vmem_limit_bytes=16 << 20),
        name="project",
    )(after, *rows, w_query, in_hbm(q_gain.reshape(1, DH)))
    return out[:-2], out[-2], out[-1]


def attend_kernel(pieces, after_ref, *refs):
    *refs, out_ref, token_ref = refs
    token_ref[...] = jnp.zeros_like(token_ref)
    query_refs, kv_refs = refs[:pieces], refs[pieces:]
    chip = my_chip(query_refs[0].shape[0])
    cores, group, half = query_refs[0].shape
    rows = cores * group
    sides = kv_refs[0].shape[0]
    lane = lax.broadcasted_iota(jnp.int32, (DH, DH), 1)
    for at in range(0, pieces, 4):
        stop = min(at + 4, pieces)
        queries = [ref[core] for ref in query_refs[at:stop] for core in range(cores)]
        queries = [x.astype(jnp.float32) for x in queries]
        queries = jnp.concatenate(queries, axis=0).astype(jnp.bfloat16)
        stats = [jnp.zeros((DH, DH), jnp.float32) for _ in range(at, stop)]
        for head in range(half // DH):
            cols = slice(head * DH, (head + 1) * DH)
            vals = slice(half + head * DH, half + (head + 1) * DH)
            keys = [ref[side, :, cols] for ref in kv_refs for side in range(sides)]
            values = [ref[side, :, vals] for ref in kv_refs for side in range(sides)]
            scores = lax.dot_general(
                queries[:, cols],
                jnp.concatenate(keys, axis=0),
                (((1,), (1,)), ((), ())),
                preferred_element_type=jnp.float32,
            )
            maxima = jnp.max(scores, axis=-1, keepdims=True)
            weights = jnp.exp(scores - maxima)
            sums = jnp.sum(weights, axis=-1, keepdims=True)
            weighted = jnp.dot(
                weights.astype(jnp.bfloat16),
                jnp.concatenate(values, axis=0),
                preferred_element_type=jnp.float32,
            )
            for j in range(at, stop):
                mine = slice((j - at) * rows, (j - at + 1) * rows)
                out_ref[chip ^ j, :rows, cols] = weighted[mine]
                pad = jnp.zeros((DH - rows, 1), jnp.float32)
                top = jnp.concatenate([maxima[mine], pad], axis=0)
                total = jnp.concatenate([sums[mine], pad], axis=0)
                stat = jnp.where(lane == 2 * head, top, stats[j - at])
                stats[j - at] = jnp.where(lane == 2 * head + 1, total, stat)
        for j in range(at, stop):
            out_ref[chip ^ j, rows:, DH:] = jnp.zeros((8, half - DH), jnp.float32)
            out_ref[chip ^ j, rows:, :DH] = stats[j - at].T[:8]


def attend(after, queries, kv_parts):
    cores, group, half = queries[0].shape
    rows = cores * group
    return pl.pallas_call(
        functools.partial(attend_kernel, len(queries)),
        out_shape=[
            jax.ShapeDtypeStruct((len(queries), rows + 8, half), jnp.float32),
            TOKEN,
        ],
        compiler_params=pltpu.CompilerParams(vmem_limit_bytes=24 << 20),
        name="attend",
    )(after, *queries, *kv_parts)


def combine_kernel(after_ref, packed_ref, *out_refs):
    part_refs = [packed_ref.at[j] for j in range(packed_ref.shape[0])]
    group, half = out_refs[0].shape
    rows = group * len(out_refs)
    stats = []
    for ref in part_refs:
        packed = ref[rows:, :DH]
        packed = jnp.concatenate([packed, jnp.zeros((DH - 8, DH), jnp.float32)], axis=0)
        stats.append(packed.T[:rows])
    for head in range(half // DH):
        cols = slice(head * DH, (head + 1) * DH)
        maxima = [stat[:, 2 * head : 2 * head + 1] for stat in stats]
        top = functools.reduce(jnp.maximum, maxima)
        total = jnp.zeros_like(top)
        attended = jnp.zeros((rows, DH), jnp.float32)
        for ref, stat, maximum in zip(part_refs, stats, maxima):
            factor = jnp.exp(maximum - top)
            total = total + stat[:, 2 * head + 1 : 2 * head + 2] * factor
            attended = attended + ref[:rows, cols] * factor
        attended = attended / total
        for side, out_ref in enumerate(out_refs):
            out_ref[:, cols] = attended[side * group : (side + 1) * group].astype(jnp.bfloat16)


def combine(after, parts, group, pair):
    half = parts.shape[2]
    return pl.pallas_call(
        combine_kernel,
        out_shape=[jax.ShapeDtypeStruct((group, half), jnp.bfloat16)] * pair,
        compiler_params=pltpu.CompilerParams(vmem_limit_bytes=16 << 20),
        name="combine",
    )(after, parts)


def output_kernel(sides, spread_ref, *refs):
    side_refs, w_ref, (own_ref, out_ref, token_ref) = refs[:sides], refs[sides], refs[sides + 1 :]
    uly = lax.axis_index("uly")
    token_ref[...] = jnp.zeros_like(token_ref)
    group, half = side_refs[0].shape
    slots, width = own_ref.shape
    spread = spread_ref[:, :group]
    attended = [
        jnp.dot(spread, ref[...], preferred_element_type=jnp.float32).astype(jnp.bfloat16)
        for ref in side_refs
    ]
    core = my_core(sides)
    starts = [pl.multiple_of((core ^ side) * half, DH) for side in range(sides)]
    step = math.gcd(width, 1024)
    for col in range(0, width, step):
        terms = jnp.zeros((spread.shape[0], step), jnp.float32)
        for start, side in zip(starts, attended):
            terms = terms + jnp.dot(
                side, w_ref[pl.ds(start, half), col : col + step], preferred_element_type=jnp.float32
            )
        own_ref[:, col : col + step] = terms[:slots]
        for k in range(out_ref.shape[0]):
            piece = terms[k * slots : (k + 1) * slots]
            out_ref[uly ^ k, :, col : col + step] = piece.astype(out_ref.dtype)


def output(spread, sides, w_out, slots, parts):
    width = w_out.shape[1]
    return pl.pallas_call(
        functools.partial(output_kernel, len(sides)),
        out_shape=[
            jax.ShapeDtypeStruct((slots, width), jnp.float32),
            jax.ShapeDtypeStruct((parts, slots, width), jnp.bfloat16),
            TOKEN,
        ],
        compiler_params=pltpu.CompilerParams(vmem_limit_bytes=16 << 20),
        name="output",
    )(spread, *sides, w_out)


def mlp_kernel(pieces, *refs):
    row_refs, (up_ref, down_ref) = refs[:pieces], refs[pieces : pieces + 2]
    *out_refs, act_ref = refs[pieces + 2 :]
    hidden, width = down_ref.shape
    rows = [ref[j] for ref in row_refs for j in range(ref.shape[0])]
    rows = jnp.concatenate(rows, axis=0)
    count = out_refs[0].shape[0]
    step = math.gcd(hidden, 512)
    for col in range(0, hidden, step):
        lifted = jnp.dot(rows, up_ref[:, col : col + step], preferred_element_type=jnp.float32)
        act_ref[:, col : col + step] = jax.nn.gelu(lifted, approximate=True).astype(jnp.bfloat16)
    step = math.gcd(width, 512)
    for col in range(0, width, step):
        down = jnp.dot(
            act_ref[...], down_ref[:, col : col + step], preferred_element_type=jnp.float32
        )
        for side, out_ref in enumerate(out_refs):
            piece = down[side * count : (side + 1) * count]
            out_ref[:, col : col + step] = piece.astype(out_ref.dtype)


def mlp(rows, w_up, w_down, pair):
    count = sum(x.shape[0] * x.shape[1] for x in rows)
    hidden, width = w_down.shape
    return pl.pallas_call(
        functools.partial(mlp_kernel, len(rows)),
        out_shape=[
            jax.ShapeDtypeStruct((count // pair, width), jnp.bfloat16 if side else jnp.float32)
            for side in range(pair)
        ],
        scratch_shapes=[pltpu.VMEM((count, hidden), jnp.bfloat16)],
        compiler_params=pltpu.CompilerParams(vmem_limit_bytes=32 << 20),
        name="mlp",
    )(*rows, w_up, w_down)


def join_kernel(count, *refs):
    part_refs, out_ref = refs[:count], refs[-1]
    for at, ref in enumerate(part_refs):
        out_ref[at] = ref[...]


def join(parts, after=()):
    return pl.pallas_call(
        functools.partial(join_kernel, len(parts)),
        out_shape=jax.ShapeDtypeStruct((len(parts), *parts[0].shape), parts[0].dtype),
        compiler_params=pltpu.CompilerParams(vmem_limit_bytes=8 << 20),
        name="join",
    )(*parts, *after)


def renorm_kernel(hold_ref, rows_ref, mod_ref, own_ref, terms_ref, after_ref, normed_ref):
    branch = own_ref[...]
    uly = lax.axis_index("uly")
    for k in range(1, terms_ref.shape[0]):
        branch = branch + terms_ref[uly ^ k].astype(jnp.float32)
    after = rows_ref[...] + mod_ref[2:3, :] * branch
    after_ref[...] = after
    normed_ref[...] = layer_norm(after, mod_ref[3:4, :], mod_ref[4:5, :]).astype(jnp.bfloat16)


def renorm(after, rows_in, modulation, terms):
    return pl.pallas_call(
        renorm_kernel,
        out_shape=[
            jax.ShapeDtypeStruct(rows_in.shape, jnp.float32),
            jax.ShapeDtypeStruct(rows_in.shape, jnp.bfloat16),
        ],
        compiler_params=pltpu.CompilerParams(vmem_limit_bytes=8 << 20),
        name="renorm",
    )(after, rows_in, modulation, *terms)


def fold_kernel(sides, *refs):
    side_refs, own_ref, out_ref = refs[:sides], refs[sides], refs[sides + 1]
    chips, slots, _ = out_ref.shape
    chip = my_chip(sides)
    for j in range(chips):
        total = side_refs[0][j * slots : (j + 1) * slots]
        for ref in side_refs[1:]:
            total = total + ref[j * slots : (j + 1) * slots].astype(jnp.float32)
        if j == 0:
            own_ref[...] = total
        out_ref[chip ^ j] = total.astype(out_ref.dtype)


def fold(sides, slots):
    count, width = sides[0].shape
    return pl.pallas_call(
        functools.partial(fold_kernel, len(sides)),
        out_shape=[
            jax.ShapeDtypeStruct((slots, width), jnp.float32),
            jax.ShapeDtypeStruct((count // slots, slots, width), jnp.bfloat16),
        ],
        compiler_params=pltpu.CompilerParams(vmem_limit_bytes=8 << 20),
        name="fold",
    )(*sides)


def finish_kernel(
    pair, select_ref, cached_ref, after_ref, mod_ref, own_ref, terms_ref, out_ref
):
    total = own_ref[...]
    chip = my_chip(pair)
    for j in range(1, terms_ref.shape[0]):
        total = total + terms_ref[chip ^ j].astype(jnp.float32)
    renewed = (after_ref[...] + mod_ref[5:6, :] * total).astype(jnp.bfloat16)
    select = select_ref[...]
    placed = jnp.dot(select, renewed, preferred_element_type=jnp.float32)
    covered = jnp.sum(select.astype(jnp.float32), axis=1, keepdims=True)
    blended = cached_ref[...].astype(jnp.float32) * (1.0 - covered) + placed
    out_ref[...] = blended.astype(jnp.bfloat16)


def finish(select, cached, after_attn, modulation, terms, pair):
    return pl.pallas_call(
        functools.partial(finish_kernel, pair),
        out_shape=jax.ShapeDtypeStruct(cached.shape, jnp.bfloat16),
        compiler_params=pltpu.CompilerParams(vmem_limit_bytes=8 << 20),
        name="finish",
    )(select, cached, after_attn, modulation, *terms)


def body(
    hidden_in,
    cached_out,
    cache_keys,
    cache_values,
    refresh_idx,
    modulation,
    q_gain,
    w_query,
    w_out,
    w_up,
    w_down,
):
    slots = refresh_idx.shape[0]
    uly_size = lax.axis_size("uly")
    blk_size = lax.axis_size("blk")
    local_heads = w_query.shape[1] // DH
    group = min(slots * uly_size, slots + (uly_size - 1) * OTHER)
    pair = 2 if blk_size % 2 == 0 and local_heads % 2 == 0 else 1
    chips = blk_size // pair

    rows_in, normed, select, modulation, sides = enter(
        refresh_idx, hidden_in, modulation, cache_keys, cache_values, uly_size, pair
    )
    sides = [trade(x, "blk", side) for side, x in enumerate(sides)]
    w_query, token = hold(normed, w_query)
    half_way = uly_size // 2
    group_rows = double(normed, "uly", 1, uly_size, {half_way: lambda x: relay(x, token)})
    cuts = [[half_way], [k for k in reversed(range(uly_size)) if k not in (1, half_way)]]
    first, token = merge_kv(sides, cuts[0], [group_rows[half_way]])
    second, token = merge_kv(sides, cuts[1], [token] + group_rows[1:])
    kv_parts = [trade(x, "uly", k) for k, x in zip(cuts[0] + cuts[1], first + second)]

    queries, spread, token = project(token, group_rows, w_query, q_gain, group, pair)
    last, _ = merge_kv(sides, [1], [token])
    kv_parts.append(trade(last[0], "uly", 1))
    w_out, token = hold(token, w_out)
    queries = join([trade(x, "blk", side) for side, x in enumerate(queries)])
    queries = double(queries, "blk", pair, chips)
    parts, token = attend(token, queries, kv_parts)
    w_up, token = hold(token, w_up)
    parts = swap_chips(parts, pair)
    attended = combine(token, parts, group, pair)
    attended = [trade(x, "blk", side) for side, x in enumerate(attended)]
    own, terms, token = output(spread, attended, w_out, slots, uly_size)
    w_down, cached, token = hold(token, w_down, cached_out)
    terms = [own, lax.all_to_all(terms, "uly", split_axis=0, concat_axis=0, tiled=True)]
    after_attn, norm_mlp = renorm(token, rows_in, modulation, terms)

    rows = [join([trade(norm_mlp, "blk", j * pair) for j in range(chips)])]
    if pair == 2:
        rows.append(trade(rows[0], "blk", 1))
    down = mlp(rows, w_up, w_down, pair)
    down = [trade(x, "blk", side) for side, x in enumerate(down)]
    own, terms = fold(down, slots)
    terms = [own, swap_chips(terms, pair)]
    return finish(select, cached, after_attn, modulation, terms, pair)


def solution(mesh):
    return jax.shard_map(
        body,
        mesh=mesh,
        in_specs=(
            P(("blk", "uly"), None),
            P(("blk", "uly"), None),
            P(("blk", "uly"), None),
            P(("blk", "uly"), None),
            P(("blk", "uly")),
            P(),
            P(),
            P(None, "uly"),
            P("uly", None),
            P(None, "blk"),
            P("blk", None),
        ),
        out_specs=P(("blk", "uly"), None),
        check_vma=False,
    )
```

```python
import functools
import math

import jax
import jax.numpy as jnp
from jax import lax
from jax.experimental import pallas as pl
from jax.experimental.pallas import tpu as pltpu
from jax.sharding import PartitionSpec as P

DH = 128
OTHER = 8
VMEM_SPEC = pl.BlockSpec(memory_space=pltpu.VMEM)
TOKEN = jax.ShapeDtypeStruct((8, DH), jnp.float32)
ANY_SPEC = pl.BlockSpec(memory_space=pl.ANY)


def double(x, axis, scale, count, on_arrival=()):
    have = {0: x}
    for k in sorted(range(1, count), key=lambda k: (bin(k).count("1"), -k)):
        low = k & -k
        have[k] = trade(have[k ^ low], axis, low * scale)
        if k in on_arrival:
            have[k] = on_arrival[k](have[k])
    return [have[k] for k in range(count)]


def pack_shared(shared, share):
    step = shared.shape[1] // 8
    per = 8 // share
    row = lax.broadcasted_iota(jnp.int32, (8, step), 0)
    blocks = []
    for first in range(0, 8, per):
        block = shared[:, first * step : (first + 1) * step]
        for i in range(1, per):
            piece = shared[:, (first + i) * step : (first + i + 1) * step]
            block = jnp.where(row >= i * share, pltpu.roll(piece, i * share, axis=0), block)
        blocks.append(block)
    return jnp.concatenate(blocks, axis=0)


def pack(main, shared, share):
    step = main.shape[1] // 8
    blocks = [main[:, c * step : (c + 1) * step] for c in range(8)]
    return jnp.concatenate(blocks + [pack_shared(shared, share)], axis=0)


def unpack(packed, share):
    per = 8 // share
    main, shared = [], []
    for c in range(8):
        main.append(packed[8 * c : 8 * c + 8])
        block = packed[64 + 8 * (c // per) : 72 + 8 * (c // per)]
        shift = (8 - share * (c % per)) % 8
        shared.append(pltpu.roll(block, shift, axis=0) if shift else block)
    return jnp.concatenate(main, axis=1), jnp.concatenate(shared, axis=1)


def layer_norm(row_block, shift_by, scale_by):
    average = jnp.mean(row_block, axis=-1, keepdims=True)
    centred = row_block - average
    spread = jnp.mean(centred * centred, axis=-1, keepdims=True)
    return centred * lax.rsqrt(spread + 1e-06) * (1.0 + scale_by) + shift_by


def trade(x, axis, flip):
    if flip == 0:
        return x
    return lax.ppermute(x, axis, [(i, i ^ flip) for i in range(lax.axis_size(axis))])


def in_hbm(x):
    return pltpu.with_memory_space_constraint(x, pltpu.HBM)


def hold_kernel(count, *refs):
    source_refs, sems = refs[1 : count + 1], refs[-1]
    *held_refs, token_ref = refs[count + 1 : -1]
    token_ref[...] = jnp.zeros_like(token_ref)
    copies = [
        pltpu.make_async_copy(source_ref, held_ref, sems.at[i])
        for i, (source_ref, held_ref) in enumerate(zip(source_refs, held_refs))
    ]
    for copy in copies:
        copy.start()
    for copy in copies:
        copy.wait()


def hold(after, *weights):
    count = len(weights)
    moved = sum(w.size * w.dtype.itemsize for w in weights)
    return pl.pallas_call(
        functools.partial(hold_kernel, count),
        in_specs=[VMEM_SPEC] + [ANY_SPEC] * count,
        out_specs=[VMEM_SPEC] * (count + 1),
        out_shape=[pltpu.VMEM(w.shape, w.dtype) for w in weights] + [TOKEN],
        scratch_shapes=[pltpu.SemaphoreType.DMA((count,))],
        cost_estimate=pl.CostEstimate(flops=0, bytes_accessed=moved, transcendentals=0),
        compiler_params=pltpu.CompilerParams(vmem_limit_bytes=2 << 20),
        name="hold",
    )(after, *[in_hbm(w) for w in weights])


def my_core(pair):
    return lax.rem(lax.axis_index("blk"), pair)


def enter_kernel(pair, idx_hbm, hidden_hbm, mod_hbm, key_hbm, value_hbm, *refs):
    rows_ref, normed_ref, select_ref, mod_ref, *side_refs = refs[: pair + 4]
    idx_ref, hidden_ref, sems, kv_sem = refs[pair + 4 :]
    copies = [
        pltpu.make_async_copy(source, target, sems.at[i])
        for i, (source, target) in enumerate(
            [(idx_hbm, idx_ref), (hidden_hbm, hidden_ref), (mod_hbm, mod_ref)]
        )
    ]
    for copy in copies:
        copy.start()
    parts, _, both = side_refs[0].shape
    half = both // 2
    uly, core = lax.axis_index("uly"), my_core(pair)
    kv_copies = []
    for side, side_ref in enumerate(side_refs):
        for flip in range(parts):
            start = pl.multiple_of(((uly ^ flip) * pair + (core ^ side)) * half, DH)
            for at, source in enumerate((key_hbm, value_hbm)):
                copy = pltpu.make_async_copy(
                    source.at[:, pl.ds(start, half)],
                    side_ref.at[flip, :, pl.ds(at * half, half)],
                    kv_sem.at[side, flip, at],
                )
                copy.start()
                kv_copies.append(copy)
    for copy in copies:
        copy.wait()
    tokens, width = hidden_ref.shape
    slots = idx_ref.shape[1]
    position = lax.broadcasted_iota(jnp.int32, (tokens, slots), 0)
    select = (position == idx_ref[...]).astype(jnp.float32).astype(jnp.bfloat16)
    select_ref[...] = select
    contract = (((0,), (0,)), ((), ()))
    rows = lax.dot_general(
        select, hidden_ref[...], contract, preferred_element_type=jnp.float32
    )
    live = lax.dot_general(
        select,
        jnp.ones((tokens, DH), jnp.bfloat16),
        contract,
        preferred_element_type=jnp.float32,
    )
    rows_ref[...] = rows
    normed = layer_norm(rows, mod_ref[0:1, :], mod_ref[1:2, :])
    normed_ref[:, :width] = normed.astype(jnp.bfloat16)
    normed_ref[:, width:] = live.astype(jnp.bfloat16)
    for copy in kv_copies:
        copy.wait()


def enter(refresh_idx, hidden_in, modulation, cache_keys, cache_values, parts, pair):
    slots = refresh_idx.shape[0]
    tokens, width = hidden_in.shape
    both = 2 * width // (parts * pair)
    out = pl.pallas_call(
        functools.partial(enter_kernel, pair),
        in_specs=[ANY_SPEC] * 5,
        out_specs=[VMEM_SPEC] * (pair + 4),
        out_shape=[
            pltpu.VMEM((slots, width), jnp.float32),
            pltpu.VMEM((slots, width + DH), jnp.bfloat16),
            pltpu.VMEM((tokens, slots), jnp.bfloat16),
            pltpu.VMEM(modulation.shape, modulation.dtype),
        ]
        + [pltpu.VMEM((parts, tokens, both), cache_keys.dtype)] * pair,
        scratch_shapes=[
            pltpu.VMEM((1, slots), jnp.int32),
            pltpu.VMEM(hidden_in.shape, hidden_in.dtype),
            pltpu.SemaphoreType.DMA((3,)),
            pltpu.SemaphoreType.DMA((pair, parts, 2)),
        ],
        compiler_params=pltpu.CompilerParams(vmem_limit_bytes=8 << 20),
        name="enter",
    )(
        *[
            in_hbm(x)
            for x in (refresh_idx.reshape(1, slots), hidden_in, modulation, cache_keys, cache_values)
        ]
    )
    return *out[:4], out[4:]


def merge_kv_kernel(sides, flips, *refs):
    *refs, token_ref = refs
    token_ref[...] = jnp.zeros_like(token_ref)
    for flip, out_ref in zip(flips, refs[-len(flips) :]):
        for side in range(sides):
            out_ref[side] = refs[side][flip]


def merge_kv(sides, flips, after):
    _, tokens, both = sides[0].shape
    *merged, token = pl.pallas_call(
        functools.partial(merge_kv_kernel, len(sides), flips),
        out_specs=[VMEM_SPEC] * (len(flips) + 1),
        out_shape=[pltpu.VMEM((len(sides), tokens, both), sides[0].dtype) for _ in flips]
        + [TOKEN],
        compiler_params=pltpu.CompilerParams(vmem_limit_bytes=8 << 20),
        name="merge_kv",
    )(*sides, *after)
    return merged, token


def relay_kernel(x_ref, after_ref, out_ref):
    out_ref[...] = x_ref[...]


def relay(x, after):
    return pl.pallas_call(
        relay_kernel,
        out_specs=VMEM_SPEC,
        out_shape=pltpu.VMEM(x.shape, x.dtype),
        compiler_params=pltpu.CompilerParams(vmem_limit_bytes=2 << 20),
        name="relay",
    )(x, after)


def project_kernel(pieces, after_ref, *refs):
    rows_refs, (w_ref, gain_hbm_ref) = refs[:pieces], refs[pieces : pieces + 2]
    *query_refs, spread_ref, token_ref, heads_ref, gain_ref, sem = refs[pieces + 2 :]
    token_ref[...] = jnp.zeros_like(token_ref)
    copy = pltpu.make_async_copy(gain_hbm_ref, gain_ref, sem)
    copy.start()
    core = my_core(len(query_refs))
    width = w_ref.shape[0]
    group, half = query_refs[0].shape
    rows = jnp.concatenate([ref[...] for ref in rows_refs], axis=0)
    everyone = rows.shape[0]
    flags = rows[:, width:]
    shape = (everyone, everyone)
    before = lax.broadcasted_iota(jnp.int32, shape, 1) < lax.broadcasted_iota(jnp.int32, shape, 0)
    before = before.astype(jnp.float32).astype(jnp.bfloat16)
    rank = jnp.dot(before, flags, preferred_element_type=jnp.float32)
    lane = lax.broadcasted_iota(jnp.int32, rank.shape, 1).astype(jnp.float32)
    spread = jnp.where((rank == lane) & (flags.astype(jnp.float32) > 0.0), 1.0, 0.0)
    spread = spread.astype(jnp.bfloat16)
    spread_ref[...] = spread
    live_rows = lax.dot_general(
        spread[:, :group],
        rows[:, :width],
        (((0,), (0,)), ((), ())),
        preferred_element_type=jnp.float32,
    ).astype(jnp.bfloat16)
    projected = jnp.dot(live_rows, w_ref[...], preferred_element_type=jnp.float32)
    copy.wait()
    for start in range(0, projected.shape[1], DH):
        head = projected[:, start : start + DH]
        squares = jnp.mean(head * head, axis=-1, keepdims=True)
        heads_ref[:, start : start + DH] = (
            head * lax.rsqrt(squares + 1e-06) * (gain_ref[...] / math.sqrt(DH))
        )
    for side, query_ref in enumerate(query_refs):
        start = pl.multiple_of((core ^ side) * half, DH)
        query_ref[...] = heads_ref[:, pl.ds(start, half)].astype(jnp.bfloat16)


def project(after, rows, w_query, q_gain, group, pair):
    half = w_query.shape[1] // pair
    everyone = len(rows) * rows[0].shape[0]
    query = jax.ShapeDtypeStruct((group, half), jnp.bfloat16)
    out = pl.pallas_call(
        functools.partial(project_kernel, len(rows)),
        in_specs=[VMEM_SPEC] * (len(rows) + 2) + [ANY_SPEC],
        out_shape=[query] * pair + [jax.ShapeDtypeStruct((everyone, DH), jnp.bfloat16), TOKEN],
        scratch_shapes=[
            pltpu.VMEM((group, w_query.shape[1]), jnp.float32),
            pltpu.VMEM((1, DH), jnp.float32),
            pltpu.SemaphoreType.DMA,
        ],
        compiler_params=pltpu.CompilerParams(vmem_limit_bytes=16 << 20),
        name="project",
    )(after, *rows, w_query, in_hbm(q_gain.reshape(1, DH)))
    return out[:-2], out[-2], out[-1]


def attend_kernel(pieces, after_ref, *refs):
    *refs, token_ref = refs
    token_ref[...] = jnp.zeros_like(token_ref)
    query_refs, kv_refs, out_refs = refs[:pieces], refs[pieces:-pieces], refs[-pieces:]
    cores, group, half = query_refs[0].shape
    rows = cores * group
    sides = kv_refs[0].shape[0]
    lane = lax.broadcasted_iota(jnp.int32, (DH, DH), 1)
    for at in range(0, pieces, 4):
        stop = min(at + 4, pieces)
        queries = [ref[core] for ref in query_refs[at:stop] for core in range(cores)]
        queries = [x.astype(jnp.float32) for x in queries]
        queries = jnp.concatenate(queries, axis=0).astype(jnp.bfloat16)
        stats = [jnp.zeros((DH, DH), jnp.float32) for _ in range(at, stop)]
        for head in range(half // DH):
            cols = slice(head * DH, (head + 1) * DH)
            vals = slice(half + head * DH, half + (head + 1) * DH)
            keys = [ref[side, :, cols] for ref in kv_refs for side in range(sides)]
            values = [ref[side, :, vals] for ref in kv_refs for side in range(sides)]
            scores = lax.dot_general(
                queries[:, cols],
                jnp.concatenate(keys, axis=0),
                (((1,), (1,)), ((), ())),
                preferred_element_type=jnp.float32,
            )
            maxima = jnp.max(scores, axis=-1, keepdims=True)
            weights = jnp.exp(scores - maxima)
            sums = jnp.sum(weights, axis=-1, keepdims=True)
            weighted = jnp.dot(
                weights.astype(jnp.bfloat16),
                jnp.concatenate(values, axis=0),
                preferred_element_type=jnp.float32,
            )
            for j in range(at, stop):
                mine = slice((j - at) * rows, (j - at + 1) * rows)
                out_refs[j][:rows, cols] = weighted[mine]
                pad = jnp.zeros((DH - rows, 1), jnp.float32)
                top = jnp.concatenate([maxima[mine], pad], axis=0)
                total = jnp.concatenate([sums[mine], pad], axis=0)
                stat = jnp.where(lane == 2 * head, top, stats[j - at])
                stats[j - at] = jnp.where(lane == 2 * head + 1, total, stat)
        for j in range(at, stop):
            out_refs[j][rows:, DH:] = jnp.zeros((8, half - DH), jnp.float32)
            out_refs[j][rows:, :DH] = stats[j - at].T[:8]


def attend(after, queries, kv_parts):
    cores, group, half = queries[0].shape
    rows = cores * group
    return pl.pallas_call(
        functools.partial(attend_kernel, len(queries)),
        out_shape=[jax.ShapeDtypeStruct((rows + 8, half), jnp.float32)] * len(queries) + [TOKEN],
        compiler_params=pltpu.CompilerParams(vmem_limit_bytes=24 << 20),
        name="attend",
    )(after, *queries, *kv_parts)


def combine_kernel(pieces, after_ref, *refs):
    part_refs, out_refs = refs[:pieces], refs[pieces:]
    group, half = out_refs[0].shape
    rows = group * len(out_refs)
    stats = []
    for ref in part_refs:
        packed = ref[rows:, :DH]
        packed = jnp.concatenate([packed, jnp.zeros((DH - 8, DH), jnp.float32)], axis=0)
        stats.append(packed.T[:rows])
    for head in range(half // DH):
        cols = slice(head * DH, (head + 1) * DH)
        maxima = [stat[:, 2 * head : 2 * head + 1] for stat in stats]
        top = functools.reduce(jnp.maximum, maxima)
        total = jnp.zeros_like(top)
        attended = jnp.zeros((rows, DH), jnp.float32)
        for ref, stat, maximum in zip(part_refs, stats, maxima):
            factor = jnp.exp(maximum - top)
            total = total + stat[:, 2 * head + 1 : 2 * head + 2] * factor
            attended = attended + ref[:rows, cols] * factor
        attended = attended / total
        for side, out_ref in enumerate(out_refs):
            out_ref[:, cols] = attended[side * group : (side + 1) * group].astype(jnp.bfloat16)


def combine(after, parts, group, pair):
    half = parts[0].shape[1]
    return pl.pallas_call(
        functools.partial(combine_kernel, len(parts)),
        out_shape=[jax.ShapeDtypeStruct((group, half), jnp.bfloat16)] * pair,
        compiler_params=pltpu.CompilerParams(vmem_limit_bytes=16 << 20),
        name="combine",
    )(after, *parts)


def output_kernel(sides, share, spread_ref, rows_ref, mod_ref, *refs):
    side_refs, w_ref = refs[:sides], refs[sides]
    own_ref, *out_refs, token_ref, terms_ref = refs[sides + 1 :]
    token_ref[...] = jnp.zeros_like(token_ref)
    group, half = side_refs[0].shape
    slots, width = rows_ref.shape
    spread = spread_ref[...].astype(jnp.float32)
    parts = spread.shape[0] // slots
    main = [spread[k * slots : k * slots + 8] for k in range(parts)]
    shared = [spread[k * slots + 8 : k * slots + 16] for k in range(parts)]
    spread = jnp.concatenate(main + [sum(shared[1:], shared[0])], axis=0)
    spread = spread.astype(jnp.bfloat16)[:, :group]
    attended = [
        jnp.dot(spread, ref[...], preferred_element_type=jnp.float32).astype(jnp.bfloat16)
        for ref in side_refs
    ]
    core = my_core(sides)
    starts = [pl.multiple_of((core ^ side) * half, DH) for side in range(sides)]
    step = math.gcd(width, 1024)
    for col in range(0, width, step):
        terms = jnp.zeros((spread.shape[0], step), jnp.float32)
        for start, side in zip(starts, attended):
            terms = terms + jnp.dot(
                side, w_ref[pl.ds(start, half), col : col + step], preferred_element_type=jnp.float32
            )
        terms_ref[:, col : col + step] = terms
    uly = lax.axis_index("uly")
    shared = mod_ref[2:3, :] * terms_ref[8 * parts :, :] + rows_ref[8:, :]
    for k in range(parts):
        main = terms_ref[8 * k : 8 * k + 8, :]
        rows = pltpu.roll(shared, lax.rem(8 - share * (uly ^ k), 8), axis=0)
        if k == 0:
            own_ref[:8, :] = main
            own_ref[8:, :] = rows
        else:
            out_refs[k - 1][...] = pack(main, rows, share).astype(jnp.bfloat16)


def output(spread, rows_in, modulation, sides, w_out, parts, share):
    slots, width = rows_in.shape
    packed = jax.ShapeDtypeStruct((64 + 8 * share, width // 8), jnp.bfloat16)
    own = jax.ShapeDtypeStruct((slots, width), jnp.float32)
    return pl.pallas_call(
        functools.partial(output_kernel, len(sides), share),
        out_shape=[own] + [packed] * (parts - 1) + [TOKEN],
        scratch_shapes=[pltpu.VMEM((8 * parts + 8, width), jnp.float32)],
        compiler_params=pltpu.CompilerParams(vmem_limit_bytes=16 << 20),
        name="output",
    )(spread, rows_in, modulation, *sides, w_out)


def mlp_kernel(pieces, share, *refs):
    row_refs, (up_ref, down_ref) = refs[:pieces], refs[pieces : pieces + 2]
    *out_refs, act_ref, terms_ref = refs[pieces + 2 :]
    hidden, width = down_ref.shape
    rows = []
    for ref in row_refs:
        for j in range(ref.shape[0]):
            rows += unpack(ref[j].astype(jnp.float32), share)
    rows = jnp.concatenate(rows, axis=0).astype(jnp.bfloat16)
    step = math.gcd(hidden, 512)
    for col in range(0, hidden, step):
        lifted = jnp.dot(rows, up_ref[:, col : col + step], preferred_element_type=jnp.float32)
        act_ref[:, col : col + step] = jax.nn.gelu(lifted, approximate=True).astype(jnp.bfloat16)
    step = math.gcd(width, 512)
    for col in range(0, width, step):
        terms_ref[:, col : col + step] = jnp.dot(
            act_ref[...], down_ref[:, col : col + step], preferred_element_type=jnp.float32
        )
    for side, out_ref in enumerate(out_refs):
        count = out_ref.shape[0]
        for j in range(count):
            at = 16 * (side * count + j)
            packed = pack(terms_ref[at : at + 8, :], terms_ref[at + 8 : at + 16, :], share)
            out_ref[j] = packed.astype(out_ref.dtype)


def mlp(rows, w_up, w_down, share):
    hidden, width = w_down.shape
    count = 16 * sum(x.shape[0] for x in rows)
    return pl.pallas_call(
        functools.partial(mlp_kernel, len(rows), share),
        out_shape=[
            jax.ShapeDtypeStruct(x.shape, jnp.bfloat16 if side else jnp.float32)
            for side, x in enumerate(rows)
        ],
        scratch_shapes=[
            pltpu.VMEM((count, hidden), jnp.bfloat16),
            pltpu.VMEM((count, width), jnp.float32),
        ],
        compiler_params=pltpu.CompilerParams(vmem_limit_bytes=32 << 20),
        name="mlp",
    )(*rows, w_up, w_down)


def join_kernel(count, *refs):
    part_refs, out_ref = refs[:count], refs[-1]
    for at, ref in enumerate(part_refs):
        out_ref[at] = ref[...]


def join(parts, after=()):
    return pl.pallas_call(
        functools.partial(join_kernel, len(parts)),
        out_shape=jax.ShapeDtypeStruct((len(parts), *parts[0].shape), parts[0].dtype),
        compiler_params=pltpu.CompilerParams(vmem_limit_bytes=8 << 20),
        name="join",
    )(*parts, *after)


def total_of(refs):
    total = refs[0][...].astype(jnp.float32)
    for ref in refs[1:]:
        total = total + ref[...].astype(jnp.float32)
    return total


def renorm_kernel(share, hold_ref, rows_ref, mod_ref, own_ref, *refs):
    *term_refs, after_ref, normed_ref = refs
    main, shared = unpack(total_of(term_refs), share)
    main = rows_ref[:8, :] + mod_ref[2:3, :] * (own_ref[:8, :] + main)
    after = jnp.concatenate([main, own_ref[8:, :] + shared], axis=0)
    after_ref[...] = after
    normed = layer_norm(after, mod_ref[3:4, :], mod_ref[4:5, :])
    normed_ref[...] = pack(normed[:8], normed[8:], share).astype(jnp.bfloat16)


def renorm(after, rows_in, modulation, terms, share):
    return pl.pallas_call(
        functools.partial(renorm_kernel, share),
        out_shape=[
            jax.ShapeDtypeStruct(rows_in.shape, jnp.float32),
            jax.ShapeDtypeStruct(terms[1].shape, jnp.bfloat16),
        ],
        compiler_params=pltpu.CompilerParams(vmem_limit_bytes=8 << 20),
        name="renorm",
    )(after, rows_in, modulation, *terms)


def fold_kernel(sides, *refs):
    side_refs, out_refs = refs[:sides], refs[sides:]
    for j, out_ref in enumerate(out_refs):
        out_ref[...] = total_of([ref.at[j] for ref in side_refs]).astype(out_ref.dtype)


def fold(sides):
    chips, *shape = sides[0].shape
    return pl.pallas_call(
        functools.partial(fold_kernel, len(sides)),
        out_shape=[
            jax.ShapeDtypeStruct(shape, jnp.bfloat16 if j else jnp.float32) for j in range(chips)
        ],
        compiler_params=pltpu.CompilerParams(vmem_limit_bytes=8 << 20),
        name="fold",
    )(*sides)


def renew_kernel(share, after_ref, mod_ref, *refs):
    *term_refs, main_ref, shared_ref = refs
    main, shared = unpack(total_of(term_refs), share)
    gate = mod_ref[5:6, :]
    main_ref[...] = after_ref[:8, :] + gate * main
    shared = pack_shared(after_ref[8:, :] + gate * shared, share)
    shared_ref[...] = shared.astype(jnp.bfloat16)


def renew(after_attn, modulation, terms, share):
    width = after_attn.shape[1]
    return pl.pallas_call(
        functools.partial(renew_kernel, share),
        out_shape=[
            jax.ShapeDtypeStruct((8, width), jnp.float32),
            jax.ShapeDtypeStruct((8 * share, width // 8), jnp.bfloat16),
        ],
        compiler_params=pltpu.CompilerParams(vmem_limit_bytes=8 << 20),
        name="renew",
    )(after_attn, modulation, *terms)


def place_kernel(select_ref, cached_ref, main_ref, out_ref):
    select = select_ref[...]
    main = main_ref[...]
    rows = jnp.concatenate([main, jnp.zeros_like(main)], axis=0).astype(jnp.bfloat16)
    placed = jnp.dot(select, rows, preferred_element_type=jnp.float32)
    covered = jnp.sum(select.astype(jnp.float32), axis=1, keepdims=True)
    out_ref[...] = cached_ref[...].astype(jnp.float32) * (1.0 - covered) + placed


def place(select, cached, main):
    return pl.pallas_call(
        place_kernel,
        out_shape=jax.ShapeDtypeStruct(cached.shape, jnp.float32),
        compiler_params=pltpu.CompilerParams(vmem_limit_bytes=8 << 20),
        name="place",
    )(select, cached, main)


def finish_kernel(share, select_ref, placed_ref, *refs):
    *shared_refs, out_ref, stack_ref = refs
    parts, _, step = stack_ref.shape
    for k, ref in enumerate(shared_refs):
        stack_ref[k] = ref[...].astype(jnp.float32)
    uly = lax.axis_index("uly")
    per = 8 // share
    row = lax.broadcasted_iota(jnp.int32, (8, step), 0)
    blocks = [jnp.zeros((8, step), jnp.float32) for _ in range(8)]
    for part in range(parts):
        packed = stack_ref[uly ^ part]
        for c in range(8):
            block = packed[8 * (c // per) : 8 * (c // per) + 8]
            shift = share * (part - c % per) % 8
            if shift:
                block = pltpu.roll(block, shift, axis=0)
            wanted = (row >= share * part) & (row < share * (part + 1))
            blocks[c] = jnp.where(wanted, block, blocks[c])
    shared = jnp.concatenate(blocks, axis=1)
    rows = jnp.concatenate([jnp.zeros_like(shared), shared], axis=0).astype(jnp.bfloat16)
    placed = jnp.dot(select_ref[...], rows, preferred_element_type=jnp.float32)
    out_ref[...] = (placed_ref[...] + placed).astype(jnp.bfloat16)


def finish(select, placed, shared, share):
    return pl.pallas_call(
        functools.partial(finish_kernel, share),
        out_shape=jax.ShapeDtypeStruct(placed.shape, jnp.bfloat16),
        scratch_shapes=[pltpu.VMEM((len(shared), *shared[0].shape), jnp.float32)],
        compiler_params=pltpu.CompilerParams(vmem_limit_bytes=8 << 20),
        name="finish",
    )(select, placed, *shared)


def body(
    hidden_in,
    cached_out,
    cache_keys,
    cache_values,
    refresh_idx,
    modulation,
    q_gain,
    w_query,
    w_out,
    w_up,
    w_down,
):
    slots = refresh_idx.shape[0]
    uly_size = lax.axis_size("uly")
    blk_size = lax.axis_size("blk")
    local_heads = w_query.shape[1] // DH
    group = min(slots * uly_size, slots + (uly_size - 1) * OTHER)
    pair = 2 if blk_size % 2 == 0 and local_heads % 2 == 0 else 1
    chips = blk_size // pair
    share = (slots - OTHER) // uly_size

    rows_in, normed, select, modulation, sides = enter(
        refresh_idx, hidden_in, modulation, cache_keys, cache_values, uly_size, pair
    )
    sides = [trade(x, "blk", side) for side, x in enumerate(sides)]
    w_query, token = hold(normed, w_query)
    half_way = uly_size // 2
    group_rows = double(normed, "uly", 1, uly_size, {half_way: lambda x: relay(x, token)})
    cuts = [[half_way], [k for k in reversed(range(uly_size)) if k not in (1, half_way)]]
    first, token = merge_kv(sides, cuts[0], [group_rows[half_way]])
    second, token = merge_kv(sides, cuts[1], [token] + group_rows[1:])
    kv_parts = [trade(x, "uly", k) for k, x in zip(cuts[0] + cuts[1], first + second)]

    queries, spread, token = project(token, group_rows, w_query, q_gain, group, pair)
    last, _ = merge_kv(sides, [1], [token])
    kv_parts.append(trade(last[0], "uly", 1))
    w_out, token = hold(token, w_out)
    queries = join([trade(x, "blk", side) for side, x in enumerate(queries)])
    queries = double(queries, "blk", pair, chips)
    *parts, token = attend(token, queries, kv_parts)
    w_up, token = hold(token, w_up)
    parts = [trade(x, "blk", j * pair) for j, x in enumerate(parts)]
    attended = combine(token, parts, group, pair)
    attended = [trade(x, "blk", side) for side, x in enumerate(attended)]
    *terms, token = output(spread, rows_in, modulation, attended, w_out, uly_size, share)
    w_down, cached, token = hold(token, w_down, cached_out)
    terms = [trade(x, "uly", k) for k, x in enumerate(terms)]
    after_attn, norm_mlp = renorm(token, rows_in, modulation, terms, share)

    rows = [join([trade(norm_mlp, "blk", j * pair) for j in range(chips)])]
    if pair == 2:
        rows.append(trade(rows[0], "blk", 1))
    down = mlp(rows, w_up, w_down, share)
    down = [trade(x, "blk", side) for side, x in enumerate(down)]
    terms = [trade(x, "blk", j * pair) for j, x in enumerate(fold(down))]
    main, shared = renew(after_attn, modulation, terms, share)
    shared = [trade(shared, "uly", k) for k in range(uly_size)]
    return finish(select, place(select, cached, main), shared, share)


def solution(mesh):
    return jax.shard_map(
        body,
        mesh=mesh,
        in_specs=(
            P(("blk", "uly"), None),
            P(("blk", "uly"), None),
            P(("blk", "uly"), None),
            P(("blk", "uly"), None),
            P(("blk", "uly")),
            P(),
            P(),
            P(None, "uly"),
            P("uly", None),
            P(None, "blk"),
            P("blk", None),
        ),
        out_specs=P(("blk", "uly"), None),
        check_vma=False,
    )
```

```python
import functools
import math

import jax
import jax.numpy as jnp
from jax import lax
from jax.experimental import pallas as pl
from jax.experimental.pallas import tpu as pltpu
from jax.sharding import PartitionSpec as P

DH = 128
OTHER = 8
VMEM_SPEC = pl.BlockSpec(memory_space=pltpu.VMEM)
TOKEN = jax.ShapeDtypeStruct((8, DH), jnp.float32)
ANY_SPEC = pl.BlockSpec(memory_space=pl.ANY)


def double(x, axis, scale, count, on_arrival=()):
    have = {0: x}
    for k in sorted(range(1, count), key=lambda k: (bin(k).count("1"), -k)):
        low = k & -k
        have[k] = trade(have[k ^ low], axis, low * scale)
        if k in on_arrival:
            have[k] = on_arrival[k](have[k])
    return [have[k] for k in range(count)]


def layer_norm(row_block, shift_by, scale_by):
    average = jnp.mean(row_block, axis=-1, keepdims=True)
    centred = row_block - average
    spread = jnp.mean(centred * centred, axis=-1, keepdims=True)
    return centred * lax.rsqrt(spread + 1e-06) * (1.0 + scale_by) + shift_by


def trade(x, axis, flip):
    if flip == 0:
        return x
    return lax.ppermute(x, axis, [(i, i ^ flip) for i in range(lax.axis_size(axis))])


def in_hbm(x):
    return pltpu.with_memory_space_constraint(x, pltpu.HBM)


def hold_kernel(count, *refs):
    source_refs, sems = refs[1 : count + 1], refs[-1]
    *held_refs, token_ref = refs[count + 1 : -1]
    token_ref[...] = jnp.zeros_like(token_ref)
    copies = [
        pltpu.make_async_copy(source_ref, held_ref, sems.at[i])
        for i, (source_ref, held_ref) in enumerate(zip(source_refs, held_refs))
    ]
    for copy in copies:
        copy.start()
    for copy in copies:
        copy.wait()


def hold(after, *weights):
    count = len(weights)
    moved = sum(w.size * w.dtype.itemsize for w in weights)
    return pl.pallas_call(
        functools.partial(hold_kernel, count),
        in_specs=[VMEM_SPEC] + [ANY_SPEC] * count,
        out_specs=[VMEM_SPEC] * (count + 1),
        out_shape=[pltpu.VMEM(w.shape, w.dtype) for w in weights] + [TOKEN],
        scratch_shapes=[pltpu.SemaphoreType.DMA((count,))],
        cost_estimate=pl.CostEstimate(flops=0, bytes_accessed=moved, transcendentals=0),
        compiler_params=pltpu.CompilerParams(vmem_limit_bytes=2 << 20),
        name="hold",
    )(after, *[in_hbm(w) for w in weights])


def my_core(pair):
    return lax.rem(lax.axis_index("blk"), pair)


def enter_kernel(pair, idx_hbm, hidden_hbm, mod_hbm, key_hbm, value_hbm, *refs):
    rows_ref, normed_ref, select_ref, mod_ref, *side_refs = refs[: pair + 4]
    idx_ref, hidden_ref, sems, kv_sem = refs[pair + 4 :]
    copies = [
        pltpu.make_async_copy(source, target, sems.at[i])
        for i, (source, target) in enumerate(
            [(idx_hbm, idx_ref), (hidden_hbm, hidden_ref), (mod_hbm, mod_ref)]
        )
    ]
    for copy in copies:
        copy.start()
    parts, _, both = side_refs[0].shape
    half = both // 2
    uly, core = lax.axis_index("uly"), my_core(pair)
    kv_copies = []
    for side, side_ref in enumerate(side_refs):
        for flip in range(parts):
            start = pl.multiple_of(((uly ^ flip) * pair + (core ^ side)) * half, DH)
            for at, source in enumerate((key_hbm, value_hbm)):
                copy = pltpu.make_async_copy(
                    source.at[:, pl.ds(start, half)],
                    side_ref.at[flip, :, pl.ds(at * half, half)],
                    kv_sem.at[side, flip, at],
                )
                copy.start()
                kv_copies.append(copy)
    for copy in copies:
        copy.wait()
    tokens, width = hidden_ref.shape
    slots = idx_ref.shape[1]
    position = lax.broadcasted_iota(jnp.int32, (tokens, slots), 0)
    select = (position == idx_ref[...]).astype(jnp.float32).astype(jnp.bfloat16)
    select_ref[...] = select
    contract = (((0,), (0,)), ((), ()))
    rows = lax.dot_general(
        select, hidden_ref[...], contract, preferred_element_type=jnp.float32
    )
    live = lax.dot_general(
        select,
        jnp.ones((tokens, DH), jnp.bfloat16),
        contract,
        preferred_element_type=jnp.float32,
    )
    rows_ref[...] = rows
    normed = layer_norm(rows, mod_ref[0:1, :], mod_ref[1:2, :])
    normed_ref[:, :width] = normed.astype(jnp.bfloat16)
    normed_ref[:, width:] = live.astype(jnp.bfloat16)
    for copy in kv_copies:
        copy.wait()


def enter(refresh_idx, hidden_in, modulation, cache_keys, cache_values, parts, pair):
    slots = refresh_idx.shape[0]
    tokens, width = hidden_in.shape
    both = 2 * width // (parts * pair)
    out = pl.pallas_call(
        functools.partial(enter_kernel, pair),
        in_specs=[ANY_SPEC] * 5,
        out_specs=[VMEM_SPEC] * (pair + 4),
        out_shape=[
            pltpu.VMEM((slots, width), jnp.float32),
            pltpu.VMEM((slots, width + DH), jnp.bfloat16),
            pltpu.VMEM((tokens, slots), jnp.bfloat16),
            pltpu.VMEM(modulation.shape, modulation.dtype),
        ]
        + [pltpu.VMEM((parts, tokens, both), cache_keys.dtype)] * pair,
        scratch_shapes=[
            pltpu.VMEM((1, slots), jnp.int32),
            pltpu.VMEM(hidden_in.shape, hidden_in.dtype),
            pltpu.SemaphoreType.DMA((3,)),
            pltpu.SemaphoreType.DMA((pair, parts, 2)),
        ],
        compiler_params=pltpu.CompilerParams(vmem_limit_bytes=8 << 20),
        name="enter",
    )(
        *[
            in_hbm(x)
            for x in (refresh_idx.reshape(1, slots), hidden_in, modulation, cache_keys, cache_values)
        ]
    )
    return *out[:4], out[4:]


def merge_kv_kernel(sides, flips, *refs):
    *refs, token_ref = refs
    token_ref[...] = jnp.zeros_like(token_ref)
    for flip, out_ref in zip(flips, refs[-len(flips) :]):
        for side in range(sides):
            out_ref[side] = refs[side][flip]


def merge_kv(sides, flips, after):
    _, tokens, both = sides[0].shape
    *merged, token = pl.pallas_call(
        functools.partial(merge_kv_kernel, len(sides), flips),
        out_specs=[VMEM_SPEC] * (len(flips) + 1),
        out_shape=[pltpu.VMEM((len(sides), tokens, both), sides[0].dtype) for _ in flips]
        + [TOKEN],
        compiler_params=pltpu.CompilerParams(vmem_limit_bytes=8 << 20),
        name="merge_kv",
    )(*sides, *after)
    return merged, token


def relay_kernel(x_ref, after_ref, out_ref):
    out_ref[...] = x_ref[...]


def relay(x, after):
    return pl.pallas_call(
        relay_kernel,
        out_specs=VMEM_SPEC,
        out_shape=pltpu.VMEM(x.shape, x.dtype),
        compiler_params=pltpu.CompilerParams(vmem_limit_bytes=2 << 20),
        name="relay",
    )(x, after)


def project_kernel(pieces, after_ref, *refs):
    rows_refs, (w_ref, gain_hbm_ref) = refs[:pieces], refs[pieces : pieces + 2]
    *query_refs, spread_ref, token_ref, heads_ref, gain_ref, sem = refs[pieces + 2 :]
    token_ref[...] = jnp.zeros_like(token_ref)
    copy = pltpu.make_async_copy(gain_hbm_ref, gain_ref, sem)
    copy.start()
    core = my_core(len(query_refs))
    width = w_ref.shape[0]
    group, half = query_refs[0].shape
    rows = jnp.concatenate([ref[...] for ref in rows_refs], axis=0)
    everyone = rows.shape[0]
    flags = rows[:, width:]
    shape = (everyone, everyone)
    before = lax.broadcasted_iota(jnp.int32, shape, 1) < lax.broadcasted_iota(jnp.int32, shape, 0)
    before = before.astype(jnp.float32).astype(jnp.bfloat16)
    rank = jnp.dot(before, flags, preferred_element_type=jnp.float32)
    lane = lax.broadcasted_iota(jnp.int32, rank.shape, 1).astype(jnp.float32)
    spread = jnp.where((rank == lane) & (flags.astype(jnp.float32) > 0.0), 1.0, 0.0)
    spread = spread.astype(jnp.bfloat16)
    spread_ref[...] = spread
    live_rows = lax.dot_general(
        spread[:, :group],
        rows[:, :width],
        (((0,), (0,)), ((), ())),
        preferred_element_type=jnp.float32,
    ).astype(jnp.bfloat16)
    projected = jnp.dot(live_rows, w_ref[...], preferred_element_type=jnp.float32)
    copy.wait()
    for start in range(0, projected.shape[1], DH):
        head = projected[:, start : start + DH]
        squares = jnp.mean(head * head, axis=-1, keepdims=True)
        heads_ref[:, start : start + DH] = (
            head * lax.rsqrt(squares + 1e-06) * (gain_ref[...] / math.sqrt(DH))
        )
    for side, query_ref in enumerate(query_refs):
        start = pl.multiple_of((core ^ side) * half, DH)
        query_ref[...] = heads_ref[:, pl.ds(start, half)].astype(jnp.bfloat16)


def project(after, rows, w_query, q_gain, group, pair):
    half = w_query.shape[1] // pair
    everyone = len(rows) * rows[0].shape[0]
    query = jax.ShapeDtypeStruct((group, half), jnp.bfloat16)
    out = pl.pallas_call(
        functools.partial(project_kernel, len(rows)),
        in_specs=[VMEM_SPEC] * (len(rows) + 2) + [ANY_SPEC],
        out_shape=[query] * pair + [jax.ShapeDtypeStruct((everyone, DH), jnp.bfloat16), TOKEN],
        scratch_shapes=[
            pltpu.VMEM((group, w_query.shape[1]), jnp.float32),
            pltpu.VMEM((1, DH), jnp.float32),
            pltpu.SemaphoreType.DMA,
        ],
        compiler_params=pltpu.CompilerParams(vmem_limit_bytes=16 << 20),
        name="project",
    )(after, *rows, w_query, in_hbm(q_gain.reshape(1, DH)))
    return out[:-2], out[-2], out[-1]


def head_scores(queries, kv_refs, head):
    half = queries.shape[1]
    cols = slice(head * DH, (head + 1) * DH)
    vals = slice(half + head * DH, half + (head + 1) * DH)
    sides = kv_refs[0].shape[0]
    keys = [ref[side, :, cols] for ref in kv_refs for side in range(sides)]
    values = [ref[side, :, vals] for ref in kv_refs for side in range(sides)]
    scores = lax.dot_general(
        queries[:, cols],
        jnp.concatenate(keys, axis=0),
        (((1,), (1,)), ((), ())),
        preferred_element_type=jnp.float32,
    )
    return scores, jnp.concatenate(values, axis=0)


def stacked(refs):
    rows = [ref[core].astype(jnp.float32) for ref in refs for core in range(ref.shape[0])]
    return jnp.concatenate(rows, axis=0).astype(jnp.bfloat16)


def attend_first_kernel(pieces, *refs):
    query_refs, (*kv_refs, sum_ref, stat_ref) = refs[:pieces], refs[pieces:]
    cores, group, half = query_refs[0].shape
    rows = cores * group
    for at in range(0, pieces, 4):
        queries = stacked(query_refs[at : at + 4])
        mine = slice(at * rows, at * rows + queries.shape[0])
        lane = lax.broadcasted_iota(jnp.int32, (queries.shape[0], DH), 1)
        stats = jnp.zeros((queries.shape[0], DH), jnp.float32)
        for head in range(half // DH):
            scores, values = head_scores(queries, kv_refs, head)
            maxima = jnp.max(scores, axis=-1, keepdims=True)
            weights = jnp.exp(scores - maxima)
            total = jnp.sum(weights, axis=-1, keepdims=True)
            sum_ref[mine, head * DH : (head + 1) * DH] = jnp.dot(
                weights.astype(jnp.bfloat16), values, preferred_element_type=jnp.float32
            )
            stats = jnp.where(lane == 2 * head, maxima, stats)
            stats = jnp.where(lane == 2 * head + 1, total, stats)
        stat_ref[mine, :] = stats


def attend_first(queries, kv_parts):
    cores, group, half = queries[0].shape
    count = cores * group * len(queries)
    return pl.pallas_call(
        functools.partial(attend_first_kernel, len(queries)),
        out_shape=[
            jax.ShapeDtypeStruct((count, half), jnp.float32),
            jax.ShapeDtypeStruct((count, DH), jnp.float32),
        ],
        cost_estimate=pl.CostEstimate(flops=10**9, bytes_accessed=0, transcendentals=0),
        compiler_params=pltpu.CompilerParams(vmem_limit_bytes=24 << 20),
        name="attend_first",
    )(*queries, *kv_parts)


def attend_last_kernel(pieces, after_ref, sum_ref, stat_ref, *refs):
    *refs, token_ref = refs
    token_ref[...] = jnp.zeros_like(token_ref)
    query_refs, kv_refs, out_refs = refs[:pieces], refs[pieces:-pieces], refs[-pieces:]
    cores, group, half = query_refs[0].shape
    rows = cores * group
    lane = lax.broadcasted_iota(jnp.int32, (DH, DH), 1)
    for at in range(0, pieces, 4):
        stop = min(at + 4, pieces)
        queries = stacked(query_refs[at:stop])
        mine = slice(at * rows, stop * rows)
        before = stat_ref[mine, :]
        stats = [jnp.zeros((DH, DH), jnp.float32) for _ in range(at, stop)]
        for head in range(half // DH):
            cols = slice(head * DH, (head + 1) * DH)
            scores, values = head_scores(queries, kv_refs, head)
            earlier = before[:, 2 * head : 2 * head + 1]
            maxima = jnp.maximum(earlier, jnp.max(scores, axis=-1, keepdims=True))
            weights = jnp.exp(scores - maxima)
            factor = jnp.exp(earlier - maxima)
            total = before[:, 2 * head + 1 : 2 * head + 2] * factor
            total = total + jnp.sum(weights, axis=-1, keepdims=True)
            weighted = sum_ref[mine, cols] * factor + jnp.dot(
                weights.astype(jnp.bfloat16), values, preferred_element_type=jnp.float32
            )
            for j in range(at, stop):
                own = slice((j - at) * rows, (j - at + 1) * rows)
                out_refs[j][:rows, cols] = weighted[own]
                pad = jnp.zeros((DH - rows, 1), jnp.float32)
                top = jnp.concatenate([maxima[own], pad], axis=0)
                stat = jnp.where(lane == 2 * head, top, stats[j - at])
                full = jnp.concatenate([total[own], pad], axis=0)
                stats[j - at] = jnp.where(lane == 2 * head + 1, full, stat)
        for j in range(at, stop):
            out_refs[j][rows:, DH:] = jnp.zeros((8, half - DH), jnp.float32)
            out_refs[j][rows:, :DH] = stats[j - at].T[:8]


def attend_last(after, first, queries, kv_parts):
    cores, group, half = queries[0].shape
    rows = cores * group
    return pl.pallas_call(
        functools.partial(attend_last_kernel, len(queries)),
        out_shape=[jax.ShapeDtypeStruct((rows + 8, half), jnp.float32)] * len(queries) + [TOKEN],
        compiler_params=pltpu.CompilerParams(vmem_limit_bytes=24 << 20),
        name="attend_last",
    )(after, *first, *queries, *kv_parts)


def combine_kernel(pieces, after_ref, *refs):
    part_refs, out_refs = refs[:pieces], refs[pieces:]
    group, half = out_refs[0].shape
    rows = group * len(out_refs)
    stats = []
    for ref in part_refs:
        packed = ref[rows:, :DH]
        packed = jnp.concatenate([packed, jnp.zeros((DH - 8, DH), jnp.float32)], axis=0)
        stats.append(packed.T[:rows])
    for head in range(half // DH):
        cols = slice(head * DH, (head + 1) * DH)
        maxima = [stat[:, 2 * head : 2 * head + 1] for stat in stats]
        top = functools.reduce(jnp.maximum, maxima)
        total = jnp.zeros_like(top)
        attended = jnp.zeros((rows, DH), jnp.float32)
        for ref, stat, maximum in zip(part_refs, stats, maxima):
            factor = jnp.exp(maximum - top)
            total = total + stat[:, 2 * head + 1 : 2 * head + 2] * factor
            attended = attended + ref[:rows, cols] * factor
        attended = attended / total
        for side, out_ref in enumerate(out_refs):
            out_ref[:, cols] = attended[side * group : (side + 1) * group].astype(jnp.bfloat16)


def combine(after, parts, group, pair):
    half = parts[0].shape[1]
    return pl.pallas_call(
        functools.partial(combine_kernel, len(parts)),
        out_shape=[jax.ShapeDtypeStruct((group, half), jnp.bfloat16)] * pair,
        compiler_params=pltpu.CompilerParams(vmem_limit_bytes=16 << 20),
        name="combine",
    )(after, *parts)


def output_kernel(sides, spread_ref, *refs):
    side_refs, w_ref, (*out_refs, token_ref) = refs[:sides], refs[sides], refs[sides + 1 :]
    token_ref[...] = jnp.zeros_like(token_ref)
    group, half = side_refs[0].shape
    slots, width = out_refs[0].shape
    spread = spread_ref[:, :group]
    attended = [
        jnp.dot(spread, ref[...], preferred_element_type=jnp.float32).astype(jnp.bfloat16)
        for ref in side_refs
    ]
    core = my_core(sides)
    starts = [pl.multiple_of((core ^ side) * half, DH) for side in range(sides)]
    step = math.gcd(width, 1024)
    for col in range(0, width, step):
        terms = jnp.zeros((spread.shape[0], step), jnp.float32)
        for start, side in zip(starts, attended):
            terms = terms + jnp.dot(
                side, w_ref[pl.ds(start, half), col : col + step], preferred_element_type=jnp.float32
            )
        for k, out_ref in enumerate(out_refs):
            piece = terms[k * slots : (k + 1) * slots]
            out_ref[:, col : col + step] = piece.astype(out_ref.dtype)


def output(spread, sides, w_out, slots, parts):
    width = w_out.shape[1]
    return pl.pallas_call(
        functools.partial(output_kernel, len(sides)),
        out_shape=[
            jax.ShapeDtypeStruct((slots, width), jnp.bfloat16 if k else jnp.float32)
            for k in range(parts)
        ]
        + [TOKEN],
        compiler_params=pltpu.CompilerParams(vmem_limit_bytes=16 << 20),
        name="output",
    )(spread, *sides, w_out)


def mlp_kernel(rows_ref, *refs):
    up_ref, down_ref, out_ref, act_ref = refs
    rows = jnp.concatenate([rows_ref[j] for j in range(rows_ref.shape[0])], axis=0)
    hidden, width = down_ref.shape
    step = math.gcd(hidden, 512)
    for col in range(0, hidden, step):
        lifted = jnp.dot(rows, up_ref[:, col : col + step], preferred_element_type=jnp.float32)
        act_ref[:, col : col + step] = jax.nn.gelu(lifted, approximate=True).astype(jnp.bfloat16)
    step = math.gcd(width, 512)
    for col in range(0, width, step):
        down = jnp.dot(
            act_ref[...], down_ref[:, col : col + step], preferred_element_type=jnp.float32
        )
        out_ref[:, col : col + step] = down.astype(out_ref.dtype)


def mlp(rows, w_up, w_down, dtype):
    chips, slots, width = rows.shape
    hidden = w_down.shape[0]
    return pl.pallas_call(
        mlp_kernel,
        out_shape=jax.ShapeDtypeStruct((chips * slots, width), dtype),
        scratch_shapes=[pltpu.VMEM((chips * slots, hidden), jnp.bfloat16)],
        cost_estimate=pl.CostEstimate(
            flops=4 * chips * slots * width * hidden, bytes_accessed=0, transcendentals=0
        ),
        compiler_params=pltpu.CompilerParams(vmem_limit_bytes=16 << 20),
        name="mlp",
    )(rows, w_up, w_down)


def join_kernel(count, *refs):
    part_refs, out_ref = refs[:count], refs[-1]
    for at, ref in enumerate(part_refs):
        out_ref[at] = ref[...]


def join(parts, after=()):
    return pl.pallas_call(
        functools.partial(join_kernel, len(parts)),
        out_shape=jax.ShapeDtypeStruct((len(parts), *parts[0].shape), parts[0].dtype),
        compiler_params=pltpu.CompilerParams(vmem_limit_bytes=8 << 20),
        name="join",
    )(*parts, *after)


def renorm_kernel(hold_ref, rows_ref, mod_ref, *refs):
    *term_refs, after_ref, normed_ref = refs
    branch = term_refs[0][...]
    for ref in term_refs[1:]:
        branch = branch + ref[...].astype(jnp.float32)
    after = rows_ref[...] + mod_ref[2:3, :] * branch
    after_ref[...] = after
    normed_ref[...] = layer_norm(after, mod_ref[3:4, :], mod_ref[4:5, :]).astype(jnp.bfloat16)


def renorm(after, rows_in, modulation, terms):
    return pl.pallas_call(
        renorm_kernel,
        out_shape=[
            jax.ShapeDtypeStruct(rows_in.shape, jnp.float32),
            jax.ShapeDtypeStruct(rows_in.shape, jnp.bfloat16),
        ],
        compiler_params=pltpu.CompilerParams(vmem_limit_bytes=8 << 20),
        name="renorm",
    )(after, rows_in, modulation, *terms)


def fold_kernel(sides, *refs):
    side_refs, out_refs = refs[:sides], refs[sides:]
    slots = out_refs[0].shape[0]
    for j, out_ref in enumerate(out_refs):
        total = side_refs[0][j * slots : (j + 1) * slots]
        for ref in side_refs[1:]:
            total = total + ref[j * slots : (j + 1) * slots].astype(jnp.float32)
        out_ref[...] = total.astype(out_ref.dtype)


def fold(sides, slots):
    count, width = sides[0].shape
    return pl.pallas_call(
        functools.partial(fold_kernel, len(sides)),
        out_shape=[
            jax.ShapeDtypeStruct((slots, width), jnp.bfloat16 if j else jnp.float32)
            for j in range(count // slots)
        ],
        compiler_params=pltpu.CompilerParams(vmem_limit_bytes=8 << 20),
        name="fold",
    )(*sides)


def finish_kernel(select_ref, cached_ref, after_ref, mod_ref, *refs):
    *term_refs, out_ref = refs
    total = term_refs[0][...]
    for ref in term_refs[1:]:
        total = total + ref[...].astype(jnp.float32)
    renewed = (after_ref[...] + mod_ref[5:6, :] * total).astype(jnp.bfloat16)
    select = select_ref[...]
    placed = jnp.dot(select, renewed, preferred_element_type=jnp.float32)
    covered = jnp.sum(select.astype(jnp.float32), axis=1, keepdims=True)
    blended = cached_ref[...].astype(jnp.float32) * (1.0 - covered) + placed
    out_ref[...] = blended.astype(jnp.bfloat16)


def finish(select, cached, after_attn, modulation, terms):
    return pl.pallas_call(
        finish_kernel,
        out_shape=jax.ShapeDtypeStruct(cached.shape, jnp.bfloat16),
        compiler_params=pltpu.CompilerParams(vmem_limit_bytes=8 << 20),
        name="finish",
    )(select, cached, after_attn, modulation, *terms)


def body(
    hidden_in,
    cached_out,
    cache_keys,
    cache_values,
    refresh_idx,
    modulation,
    q_gain,
    w_query,
    w_out,
    w_up,
    w_down,
):
    slots = refresh_idx.shape[0]
    uly_size = lax.axis_size("uly")
    blk_size = lax.axis_size("blk")
    local_heads = w_query.shape[1] // DH
    group = min(slots * uly_size, slots + (uly_size - 1) * OTHER)
    pair = 2 if blk_size % 2 == 0 and local_heads % 2 == 0 else 1
    chips = blk_size // pair

    rows_in, normed, select, modulation, sides = enter(
        refresh_idx, hidden_in, modulation, cache_keys, cache_values, uly_size, pair
    )
    sides = [trade(x, "blk", side) for side, x in enumerate(sides)]
    w_query, token = hold(normed, w_query)
    half_way = uly_size // 2
    group_rows = double(normed, "uly", 1, uly_size, {half_way: lambda x: relay(x, token)})
    cuts = [[half_way, 0], [k for k in reversed(range(uly_size)) if k not in (0, 1, half_way)]]
    first, token = merge_kv(sides, cuts[0], [group_rows[half_way]])
    second, token = merge_kv(sides, cuts[1], [token] + group_rows[1:])
    kv_parts = [trade(x, "uly", k) for k, x in zip(cuts[0] + cuts[1], first + second)]

    queries, spread, token = project(token, group_rows, w_query, q_gain, group, pair)
    last, _ = merge_kv(sides, [1], [token])
    kv_parts.append(trade(last[0], "uly", 1))
    w_out, token = hold(token, w_out)
    queries = join([trade(x, "blk", side) for side, x in enumerate(queries)])
    queries = double(queries, "blk", pair, chips)
    first = attend_first(queries, kv_parts[:2])
    *parts, token = attend_last(token, first, queries, kv_parts[2:])
    w_up, token = hold(token, w_up)
    parts = [trade(x, "blk", j * pair) for j, x in enumerate(parts)]
    attended = combine(token, parts, group, pair)
    attended = [trade(x, "blk", side) for side, x in enumerate(attended)]
    *terms, token = output(spread, attended, w_out, slots, uly_size)
    w_down, cached, token = hold(token, w_down, cached_out)
    terms = [trade(x, "uly", k) for k, x in enumerate(terms)]
    after_attn, norm_mlp = renorm(token, rows_in, modulation, terms)

    rows = [join([trade(norm_mlp, "blk", j * pair) for j in range(chips)])]
    if pair == 2:
        rows.append(trade(rows[0], "blk", 1))
    kinds = [jnp.float32, jnp.bfloat16]
    down = [mlp(x, w_up, w_down, kind) for x, kind in zip(rows, kinds)]
    down = [trade(x, "blk", side) for side, x in enumerate(down)]
    terms = [trade(x, "blk", j * pair) for j, x in enumerate(fold(down, slots))]
    return finish(select, cached, after_attn, modulation, terms)


def solution(mesh):
    return jax.shard_map(
        body,
        mesh=mesh,
        in_specs=(
            P(("blk", "uly"), None),
            P(("blk", "uly"), None),
            P(("blk", "uly"), None),
            P(("blk", "uly"), None),
            P(("blk", "uly")),
            P(),
            P(),
            P(None, "uly"),
            P("uly", None),
            P(None, "blk"),
            P("blk", None),
        ),
        out_specs=P(("blk", "uly"), None),
        check_vma=False,
    )
```

```python
import functools
import math

import jax
import jax.numpy as jnp
from jax import lax
from jax.experimental import pallas as pl
from jax.experimental.pallas import tpu as pltpu
from jax.sharding import PartitionSpec as P

DH = 128
OTHER = 8
VMEM_SPEC = pl.BlockSpec(memory_space=pltpu.VMEM)
TOKEN = jax.ShapeDtypeStruct((8, DH), jnp.float32)
ANY_SPEC = pl.BlockSpec(memory_space=pl.ANY)


def double(x, axis, scale, count, on_arrival=()):
    have = {0: x}
    for k in sorted(range(1, count), key=lambda k: (bin(k).count("1"), -k)):
        low = k & -k
        have[k] = trade(have[k ^ low], axis, low * scale)
        if k in on_arrival:
            have[k] = on_arrival[k](have[k])
    return [have[k] for k in range(count)]


def layer_norm(row_block, shift_by, scale_by):
    average = jnp.mean(row_block, axis=-1, keepdims=True)
    centred = row_block - average
    spread = jnp.mean(centred * centred, axis=-1, keepdims=True)
    return centred * lax.rsqrt(spread + 1e-06) * (1.0 + scale_by) + shift_by


def trade(x, axis, flip):
    if flip == 0:
        return x
    return lax.ppermute(x, axis, [(i, i ^ flip) for i in range(lax.axis_size(axis))])


def in_hbm(x):
    return pltpu.with_memory_space_constraint(x, pltpu.HBM)


def hold_kernel(count, *refs):
    source_refs, sems = refs[1 : count + 1], refs[-1]
    *held_refs, token_ref = refs[count + 1 : -1]
    token_ref[...] = jnp.zeros_like(token_ref)
    copies = [
        pltpu.make_async_copy(source_ref, held_ref, sems.at[i])
        for i, (source_ref, held_ref) in enumerate(zip(source_refs, held_refs))
    ]
    for copy in copies:
        copy.start()
    for copy in copies:
        copy.wait()


def hold(after, *weights):
    count = len(weights)
    moved = sum(w.size * w.dtype.itemsize for w in weights)
    return pl.pallas_call(
        functools.partial(hold_kernel, count),
        in_specs=[VMEM_SPEC] + [ANY_SPEC] * count,
        out_specs=[VMEM_SPEC] * (count + 1),
        out_shape=[pltpu.VMEM(w.shape, w.dtype) for w in weights] + [TOKEN],
        scratch_shapes=[pltpu.SemaphoreType.DMA((count,))],
        cost_estimate=pl.CostEstimate(flops=0, bytes_accessed=moved, transcendentals=0),
        compiler_params=pltpu.CompilerParams(vmem_limit_bytes=2 << 20),
        name="hold",
    )(after, *[in_hbm(w) for w in weights])


def my_core(pair):
    return lax.rem(lax.axis_index("blk"), pair)


def enter_kernel(pair, idx_hbm, hidden_hbm, mod_hbm, key_hbm, value_hbm, *refs):
    rows_ref, normed_ref, select_ref, mod_ref, *side_refs = refs[: pair + 4]
    idx_ref, hidden_ref, sems, kv_sem = refs[pair + 4 :]
    copies = [
        pltpu.make_async_copy(source, target, sems.at[i])
        for i, (source, target) in enumerate(
            [(idx_hbm, idx_ref), (hidden_hbm, hidden_ref), (mod_hbm, mod_ref)]
        )
    ]
    for copy in copies:
        copy.start()
    parts, _, both = side_refs[0].shape
    half = both // 2
    uly, core = lax.axis_index("uly"), my_core(pair)
    kv_copies = []
    for side, side_ref in enumerate(side_refs):
        for flip in range(parts):
            start = pl.multiple_of(((uly ^ flip) * pair + (core ^ side)) * half, DH)
            for at, source in enumerate((key_hbm, value_hbm)):
                copy = pltpu.make_async_copy(
                    source.at[:, pl.ds(start, half)],
                    side_ref.at[flip, :, pl.ds(at * half, half)],
                    kv_sem.at[side, flip, at],
                )
                copy.start()
                kv_copies.append(copy)
    for copy in copies:
        copy.wait()
    tokens, width = hidden_ref.shape
    slots = idx_ref.shape[1]
    position = lax.broadcasted_iota(jnp.int32, (tokens, slots), 0)
    select = (position == idx_ref[...]).astype(jnp.float32).astype(jnp.bfloat16)
    select_ref[...] = select
    contract = (((0,), (0,)), ((), ()))
    rows = lax.dot_general(
        select, hidden_ref[...], contract, preferred_element_type=jnp.float32
    )
    live = lax.dot_general(
        select,
        jnp.ones((tokens, DH), jnp.bfloat16),
        contract,
        preferred_element_type=jnp.float32,
    )
    rows_ref[...] = rows
    normed = layer_norm(rows, mod_ref[0:1, :], mod_ref[1:2, :])
    normed_ref[:, :width] = normed.astype(jnp.bfloat16)
    normed_ref[:, width:] = live.astype(jnp.bfloat16)
    for copy in kv_copies:
        copy.wait()


def enter(refresh_idx, hidden_in, modulation, cache_keys, cache_values, parts, pair):
    slots = refresh_idx.shape[0]
    tokens, width = hidden_in.shape
    both = 2 * width // (parts * pair)
    out = pl.pallas_call(
        functools.partial(enter_kernel, pair),
        in_specs=[ANY_SPEC] * 5,
        out_specs=[VMEM_SPEC] * (pair + 4),
        out_shape=[
            pltpu.VMEM((slots, width), jnp.float32),
            pltpu.VMEM((slots, width + DH), jnp.bfloat16),
            pltpu.VMEM((tokens, slots), jnp.bfloat16),
            pltpu.VMEM(modulation.shape, modulation.dtype),
        ]
        + [pltpu.VMEM((parts, tokens, both), cache_keys.dtype)] * pair,
        scratch_shapes=[
            pltpu.VMEM((1, slots), jnp.int32),
            pltpu.VMEM(hidden_in.shape, hidden_in.dtype),
            pltpu.SemaphoreType.DMA((3,)),
            pltpu.SemaphoreType.DMA((pair, parts, 2)),
        ],
        compiler_params=pltpu.CompilerParams(vmem_limit_bytes=8 << 20),
        name="enter",
    )(
        *[
            in_hbm(x)
            for x in (refresh_idx.reshape(1, slots), hidden_in, modulation, cache_keys, cache_values)
        ]
    )
    return *out[:4], out[4:]


def merge_kv_kernel(sides, flips, *refs):
    *refs, token_ref = refs
    token_ref[...] = jnp.zeros_like(token_ref)
    for flip, out_ref in zip(flips, refs[-len(flips) :]):
        for side in range(sides):
            out_ref[side] = refs[side][flip]


def merge_kv(sides, flips, after):
    _, tokens, both = sides[0].shape
    *merged, token = pl.pallas_call(
        functools.partial(merge_kv_kernel, len(sides), flips),
        out_specs=[VMEM_SPEC] * (len(flips) + 1),
        out_shape=[pltpu.VMEM((len(sides), tokens, both), sides[0].dtype) for _ in flips]
        + [TOKEN],
        compiler_params=pltpu.CompilerParams(vmem_limit_bytes=8 << 20),
        name="merge_kv",
    )(*sides, *after)
    return merged, token


def relay_kernel(x_ref, after_ref, out_ref):
    out_ref[...] = x_ref[...]


def relay(x, after):
    return pl.pallas_call(
        relay_kernel,
        out_specs=VMEM_SPEC,
        out_shape=pltpu.VMEM(x.shape, x.dtype),
        compiler_params=pltpu.CompilerParams(vmem_limit_bytes=2 << 20),
        name="relay",
    )(x, after)


def project_kernel(pieces, after_ref, *refs):
    rows_refs, (w_ref, gain_hbm_ref) = refs[:pieces], refs[pieces : pieces + 2]
    *query_refs, spread_ref, token_ref, heads_ref, gain_ref, sem = refs[pieces + 2 :]
    token_ref[...] = jnp.zeros_like(token_ref)
    copy = pltpu.make_async_copy(gain_hbm_ref, gain_ref, sem)
    copy.start()
    core = my_core(len(query_refs))
    width = w_ref.shape[0]
    group, half = query_refs[0].shape
    rows = jnp.concatenate([ref[...] for ref in rows_refs], axis=0)
    everyone = rows.shape[0]
    flags = rows[:, width:]
    shape = (everyone, everyone)
    before = lax.broadcasted_iota(jnp.int32, shape, 1) < lax.broadcasted_iota(jnp.int32, shape, 0)
    before = before.astype(jnp.float32).astype(jnp.bfloat16)
    rank = jnp.dot(before, flags, preferred_element_type=jnp.float32)
    lane = lax.broadcasted_iota(jnp.int32, rank.shape, 1).astype(jnp.float32)
    spread = jnp.where((rank == lane) & (flags.astype(jnp.float32) > 0.0), 1.0, 0.0)
    spread = spread.astype(jnp.bfloat16)
    spread_ref[...] = spread
    live_rows = lax.dot_general(
        spread[:, :group],
        rows[:, :width],
        (((0,), (0,)), ((), ())),
        preferred_element_type=jnp.float32,
    ).astype(jnp.bfloat16)
    projected = jnp.dot(live_rows, w_ref[...], preferred_element_type=jnp.float32)
    copy.wait()
    for start in range(0, projected.shape[1], DH):
        head = projected[:, start : start + DH]
        squares = jnp.mean(head * head, axis=-1, keepdims=True)
        heads_ref[:, start : start + DH] = (
            head * lax.rsqrt(squares + 1e-06) * (gain_ref[...] / math.sqrt(DH))
        )
    for side, query_ref in enumerate(query_refs):
        start = pl.multiple_of((core ^ side) * half, DH)
        query_ref[...] = heads_ref[:, pl.ds(start, half)].astype(jnp.bfloat16)


def project(after, rows, w_query, q_gain, group, pair):
    half = w_query.shape[1] // pair
    everyone = len(rows) * rows[0].shape[0]
    query = jax.ShapeDtypeStruct((group, half), jnp.bfloat16)
    out = pl.pallas_call(
        functools.partial(project_kernel, len(rows)),
        in_specs=[VMEM_SPEC] * (len(rows) + 2) + [ANY_SPEC],
        out_shape=[query] * pair + [jax.ShapeDtypeStruct((everyone, DH), jnp.bfloat16), TOKEN],
        scratch_shapes=[
            pltpu.VMEM((group, w_query.shape[1]), jnp.float32),
            pltpu.VMEM((1, DH), jnp.float32),
            pltpu.SemaphoreType.DMA,
        ],
        compiler_params=pltpu.CompilerParams(vmem_limit_bytes=16 << 20),
        name="project",
    )(after, *rows, w_query, in_hbm(q_gain.reshape(1, DH)))
    return out[:-2], out[-2], out[-1]


def head_scores(queries, kv_refs, head):
    half = queries.shape[1]
    cols = slice(head * DH, (head + 1) * DH)
    vals = slice(half + head * DH, half + (head + 1) * DH)
    sides = kv_refs[0].shape[0]
    keys = [ref[side, :, cols] for ref in kv_refs for side in range(sides)]
    values = [ref[side, :, vals] for ref in kv_refs for side in range(sides)]
    scores = lax.dot_general(
        queries[:, cols],
        jnp.concatenate(keys, axis=0),
        (((1,), (1,)), ((), ())),
        preferred_element_type=jnp.float32,
    )
    return scores, jnp.concatenate(values, axis=0)


def stacked(refs):
    rows = [ref[core].astype(jnp.float32) for ref in refs for core in range(ref.shape[0])]
    return jnp.concatenate(rows, axis=0).astype(jnp.bfloat16)


def attend_first_kernel(pieces, *refs):
    query_refs, (*kv_refs, sum_ref, stat_ref) = refs[:pieces], refs[pieces:]
    cores, group, half = query_refs[0].shape
    rows = cores * group
    for at in range(0, pieces, 4):
        queries = stacked(query_refs[at : at + 4])
        mine = slice(at * rows, at * rows + queries.shape[0])
        lane = lax.broadcasted_iota(jnp.int32, (queries.shape[0], DH), 1)
        stats = jnp.zeros((queries.shape[0], DH), jnp.float32)
        for head in range(half // DH):
            scores, values = head_scores(queries, kv_refs, head)
            maxima = jnp.max(scores, axis=-1, keepdims=True)
            weights = jnp.exp(scores - maxima)
            total = jnp.sum(weights, axis=-1, keepdims=True)
            sum_ref[mine, head * DH : (head + 1) * DH] = jnp.dot(
                weights.astype(jnp.bfloat16), values, preferred_element_type=jnp.float32
            )
            stats = jnp.where(lane == 2 * head, maxima, stats)
            stats = jnp.where(lane == 2 * head + 1, total, stats)
        stat_ref[mine, :] = stats


def attend_first(queries, kv_parts):
    cores, group, half = queries[0].shape
    count = cores * group * len(queries)
    return pl.pallas_call(
        functools.partial(attend_first_kernel, len(queries)),
        out_shape=[
            jax.ShapeDtypeStruct((count, half), jnp.float32),
            jax.ShapeDtypeStruct((count, DH), jnp.float32),
        ],
        cost_estimate=pl.CostEstimate(flops=10**9, bytes_accessed=0, transcendentals=0),
        compiler_params=pltpu.CompilerParams(vmem_limit_bytes=24 << 20),
        name="attend_first",
    )(*queries, *kv_parts)


def attend_last_kernel(pieces, after_ref, sum_ref, stat_ref, *refs):
    *refs, token_ref = refs
    token_ref[...] = jnp.zeros_like(token_ref)
    query_refs, kv_refs, out_refs = refs[:pieces], refs[pieces:-pieces], refs[-pieces:]
    cores, group, half = query_refs[0].shape
    rows = cores * group
    pad = jnp.zeros((DH - rows, DH), jnp.float32)
    for at in range(0, pieces, 4):
        stop = min(at + 4, pieces)
        queries = stacked(query_refs[at:stop])
        mine = slice(at * rows, stop * rows)
        before = stat_ref[mine, :]
        lane = lax.broadcasted_iota(jnp.int32, before.shape, 1)
        stats = jnp.zeros_like(before)
        for head in range(half // DH):
            cols = slice(head * DH, (head + 1) * DH)
            scores, values = head_scores(queries, kv_refs, head)
            earlier = before[:, 2 * head : 2 * head + 1]
            maxima = jnp.maximum(earlier, jnp.max(scores, axis=-1, keepdims=True))
            weights = jnp.exp(scores - maxima)
            factor = jnp.exp(earlier - maxima)
            total = before[:, 2 * head + 1 : 2 * head + 2] * factor
            total = total + jnp.sum(weights, axis=-1, keepdims=True)
            weighted = sum_ref[mine, cols] * factor + jnp.dot(
                weights.astype(jnp.bfloat16), values, preferred_element_type=jnp.float32
            )
            stats = jnp.where(lane == 2 * head, maxima, stats)
            stats = jnp.where(lane == 2 * head + 1, total, stats)
            for j in range(at, stop):
                out_refs[j][:rows, cols] = weighted[(j - at) * rows : (j - at + 1) * rows]
        for j in range(at, stop):
            own = stats[(j - at) * rows : (j - at + 1) * rows]
            out_refs[j][rows:, DH:] = jnp.zeros((8, half - DH), jnp.float32)
            out_refs[j][rows:, :DH] = jnp.concatenate([own, pad], axis=0).T[:8]


def attend_last(after, first, queries, kv_parts):
    cores, group, half = queries[0].shape
    rows = cores * group
    return pl.pallas_call(
        functools.partial(attend_last_kernel, len(queries)),
        out_shape=[jax.ShapeDtypeStruct((rows + 8, half), jnp.float32)] * len(queries) + [TOKEN],
        compiler_params=pltpu.CompilerParams(vmem_limit_bytes=24 << 20),
        name="attend_last",
    )(after, *first, *queries, *kv_parts)


def combine_kernel(pieces, after_ref, *refs):
    part_refs, out_refs = refs[:pieces], refs[pieces:]
    group, half = out_refs[0].shape
    rows = group * len(out_refs)
    stats = []
    for ref in part_refs:
        packed = ref[rows:, :DH]
        packed = jnp.concatenate([packed, jnp.zeros((DH - 8, DH), jnp.float32)], axis=0)
        stats.append(packed.T[:rows])
    for head in range(half // DH):
        cols = slice(head * DH, (head + 1) * DH)
        maxima = [stat[:, 2 * head : 2 * head + 1] for stat in stats]
        top = functools.reduce(jnp.maximum, maxima)
        total = jnp.zeros_like(top)
        attended = jnp.zeros((rows, DH), jnp.float32)
        for ref, stat, maximum in zip(part_refs, stats, maxima):
            factor = jnp.exp(maximum - top)
            total = total + stat[:, 2 * head + 1 : 2 * head + 2] * factor
            attended = attended + ref[:rows, cols] * factor
        attended = attended / total
        for side, out_ref in enumerate(out_refs):
            out_ref[:, cols] = attended[side * group : (side + 1) * group].astype(jnp.bfloat16)


def combine(after, parts, group, pair):
    half = parts[0].shape[1]
    return pl.pallas_call(
        functools.partial(combine_kernel, len(parts)),
        out_shape=[jax.ShapeDtypeStruct((group, half), jnp.bfloat16)] * pair,
        compiler_params=pltpu.CompilerParams(vmem_limit_bytes=16 << 20),
        name="combine",
    )(after, *parts)


def output_kernel(sides, spread_ref, *refs):
    side_refs, w_ref, (*out_refs, token_ref) = refs[:sides], refs[sides], refs[sides + 1 :]
    token_ref[...] = jnp.zeros_like(token_ref)
    group, half = side_refs[0].shape
    slots, width = out_refs[0].shape
    spread = spread_ref[:, :group]
    attended = [
        jnp.dot(spread, ref[...], preferred_element_type=jnp.float32).astype(jnp.bfloat16)
        for ref in side_refs
    ]
    core = my_core(sides)
    starts = [pl.multiple_of((core ^ side) * half, DH) for side in range(sides)]
    step = math.gcd(width, 1024)
    for col in range(0, width, step):
        terms = jnp.zeros((spread.shape[0], step), jnp.float32)
        for start, side in zip(starts, attended):
            terms = terms + jnp.dot(
                side, w_ref[pl.ds(start, half), col : col + step], preferred_element_type=jnp.float32
            )
        for k, out_ref in enumerate(out_refs):
            piece = terms[k * slots : (k + 1) * slots]
            out_ref[:, col : col + step] = piece.astype(out_ref.dtype)


def output(spread, sides, w_out, slots, parts):
    width = w_out.shape[1]
    return pl.pallas_call(
        functools.partial(output_kernel, len(sides)),
        out_shape=[
            jax.ShapeDtypeStruct((slots, width), jnp.bfloat16 if k else jnp.float32)
            for k in range(parts)
        ]
        + [TOKEN],
        compiler_params=pltpu.CompilerParams(vmem_limit_bytes=16 << 20),
        name="output",
    )(spread, *sides, w_out)


def mlp_kernel(pieces, *refs):
    row_refs, (up_ref, down_ref) = refs[:pieces], refs[pieces : pieces + 2]
    *out_refs, act_ref = refs[pieces + 2 :]
    hidden, width = down_ref.shape
    rows = [ref[j] for ref in row_refs for j in range(ref.shape[0])]
    rows = jnp.concatenate(rows, axis=0)
    count = out_refs[0].shape[0]
    step = math.gcd(hidden, 512)
    for col in range(0, hidden, step):
        lifted = jnp.dot(rows, up_ref[:, col : col + step], preferred_element_type=jnp.float32)
        act_ref[:, col : col + step] = jax.nn.gelu(lifted, approximate=True).astype(jnp.bfloat16)
    step = math.gcd(width, 512)
    for col in range(0, width, step):
        down = jnp.dot(
            act_ref[...], down_ref[:, col : col + step], preferred_element_type=jnp.float32
        )
        for side, out_ref in enumerate(out_refs):
            piece = down[side * count : (side + 1) * count]
            out_ref[:, col : col + step] = piece.astype(out_ref.dtype)


def mlp(rows, w_up, w_down, pair):
    count = sum(x.shape[0] * x.shape[1] for x in rows)
    hidden, width = w_down.shape
    return pl.pallas_call(
        functools.partial(mlp_kernel, len(rows)),
        out_shape=[
            jax.ShapeDtypeStruct((count // pair, width), jnp.bfloat16 if side else jnp.float32)
            for side in range(pair)
        ],
        scratch_shapes=[pltpu.VMEM((count, hidden), jnp.bfloat16)],
        compiler_params=pltpu.CompilerParams(vmem_limit_bytes=32 << 20),
        name="mlp",
    )(*rows, w_up, w_down)


def join_kernel(count, *refs):
    part_refs, out_ref = refs[:count], refs[-1]
    for at, ref in enumerate(part_refs):
        out_ref[at] = ref[...]


def join(parts, after=()):
    return pl.pallas_call(
        functools.partial(join_kernel, len(parts)),
        out_shape=jax.ShapeDtypeStruct((len(parts), *parts[0].shape), parts[0].dtype),
        compiler_params=pltpu.CompilerParams(vmem_limit_bytes=8 << 20),
        name="join",
    )(*parts, *after)


def renorm_kernel(hold_ref, rows_ref, mod_ref, *refs):
    *term_refs, after_ref, normed_ref = refs
    branch = term_refs[0][...]
    for ref in term_refs[1:]:
        branch = branch + ref[...].astype(jnp.float32)
    after = rows_ref[...] + mod_ref[2:3, :] * branch
    after_ref[...] = after
    normed_ref[...] = layer_norm(after, mod_ref[3:4, :], mod_ref[4:5, :]).astype(jnp.bfloat16)


def renorm(after, rows_in, modulation, terms):
    return pl.pallas_call(
        renorm_kernel,
        out_shape=[
            jax.ShapeDtypeStruct(rows_in.shape, jnp.float32),
            jax.ShapeDtypeStruct(rows_in.shape, jnp.bfloat16),
        ],
        compiler_params=pltpu.CompilerParams(vmem_limit_bytes=8 << 20),
        name="renorm",
    )(after, rows_in, modulation, *terms)


def fold_kernel(sides, *refs):
    side_refs, out_refs = refs[:sides], refs[sides:]
    slots = out_refs[0].shape[0]
    for j, out_ref in enumerate(out_refs):
        total = side_refs[0][j * slots : (j + 1) * slots]
        for ref in side_refs[1:]:
            total = total + ref[j * slots : (j + 1) * slots].astype(jnp.float32)
        out_ref[...] = total.astype(out_ref.dtype)


def fold(sides, slots):
    count, width = sides[0].shape
    return pl.pallas_call(
        functools.partial(fold_kernel, len(sides)),
        out_shape=[
            jax.ShapeDtypeStruct((slots, width), jnp.bfloat16 if j else jnp.float32)
            for j in range(count // slots)
        ],
        compiler_params=pltpu.CompilerParams(vmem_limit_bytes=8 << 20),
        name="fold",
    )(*sides)


def finish_kernel(select_ref, cached_ref, after_ref, mod_ref, *refs):
    *term_refs, out_ref = refs
    total = term_refs[0][...]
    for ref in term_refs[1:]:
        total = total + ref[...].astype(jnp.float32)
    renewed = (after_ref[...] + mod_ref[5:6, :] * total).astype(jnp.bfloat16)
    select = select_ref[...]
    placed = jnp.dot(select, renewed, preferred_element_type=jnp.float32)
    covered = jnp.sum(select.astype(jnp.float32), axis=1, keepdims=True)
    blended = cached_ref[...].astype(jnp.float32) * (1.0 - covered) + placed
    out_ref[...] = blended.astype(jnp.bfloat16)


def finish(select, cached, after_attn, modulation, terms):
    return pl.pallas_call(
        finish_kernel,
        out_shape=jax.ShapeDtypeStruct(cached.shape, jnp.bfloat16),
        compiler_params=pltpu.CompilerParams(vmem_limit_bytes=8 << 20),
        name="finish",
    )(select, cached, after_attn, modulation, *terms)


def body(
    hidden_in,
    cached_out,
    cache_keys,
    cache_values,
    refresh_idx,
    modulation,
    q_gain,
    w_query,
    w_out,
    w_up,
    w_down,
):
    slots = refresh_idx.shape[0]
    uly_size = lax.axis_size("uly")
    blk_size = lax.axis_size("blk")
    local_heads = w_query.shape[1] // DH
    group = min(slots * uly_size, slots + (uly_size - 1) * OTHER)
    pair = 2 if blk_size % 2 == 0 and local_heads % 2 == 0 else 1
    chips = blk_size // pair

    rows_in, normed, select, modulation, sides = enter(
        refresh_idx, hidden_in, modulation, cache_keys, cache_values, uly_size, pair
    )
    sides = [trade(x, "blk", side) for side, x in enumerate(sides)]
    w_query, token = hold(normed, w_query)
    half_way = uly_size // 2
    cuts = [[half_way, 0], [k for k in reversed(range(uly_size)) if k not in (0, 1, half_way)]]
    first, token = merge_kv(sides, cuts[0], [token])
    group_rows = double(normed, "uly", 1, uly_size, {half_way: lambda x: relay(x, token)})
    second, token = merge_kv(sides, cuts[1], group_rows[1:])
    kv_parts = [trade(x, "uly", k) for k, x in zip(cuts[0] + cuts[1], first + second)]

    queries, spread, token = project(token, group_rows, w_query, q_gain, group, pair)
    last, _ = merge_kv(sides, [1], [token])
    kv_parts.append(trade(last[0], "uly", 1))
    w_out, token = hold(token, w_out)
    queries = join([trade(x, "blk", side) for side, x in enumerate(queries)])
    queries = double(queries, "blk", pair, chips)
    first = attend_first(queries, kv_parts[:2])
    *parts, token = attend_last(token, first, queries, kv_parts[2:])
    w_up, token = hold(token, w_up)
    parts = [trade(x, "blk", j * pair) for j, x in enumerate(parts)]
    attended = combine(token, parts, group, pair)
    attended = [trade(x, "blk", side) for side, x in enumerate(attended)]
    *terms, token = output(spread, attended, w_out, slots, uly_size)
    w_down, cached, token = hold(token, w_down, cached_out)
    terms = [trade(x, "uly", k) for k, x in enumerate(terms)]
    after_attn, norm_mlp = renorm(token, rows_in, modulation, terms)

    rows = [join([trade(norm_mlp, "blk", j * pair) for j in range(chips)])]
    if pair == 2:
        rows.append(trade(rows[0], "blk", 1))
    down = mlp(rows, w_up, w_down, pair)
    down = [trade(x, "blk", side) for side, x in enumerate(down)]
    terms = [trade(x, "blk", j * pair) for j, x in enumerate(fold(down, slots))]
    return finish(select, cached, after_attn, modulation, terms)


def solution(mesh):
    return jax.shard_map(
        body,
        mesh=mesh,
        in_specs=(
            P(("blk", "uly"), None),
            P(("blk", "uly"), None),
            P(("blk", "uly"), None),
            P(("blk", "uly"), None),
            P(("blk", "uly")),
            P(),
            P(),
            P(None, "uly"),
            P("uly", None),
            P(None, "blk"),
            P("blk", None),
        ),
        out_specs=P(("blk", "uly"), None),
        check_vma=False,
    )
```

```python
import functools
import math

import jax
import jax.numpy as jnp
from jax import lax
from jax.experimental import pallas as pl
from jax.experimental.pallas import tpu as pltpu
from jax.sharding import PartitionSpec as P

DH = 128
OTHER = 8
VMEM_SPEC = pl.BlockSpec(memory_space=pltpu.VMEM)
TOKEN = pltpu.VMEM((8, DH), jnp.float32)
ANY_SPEC = pl.BlockSpec(memory_space=pl.ANY)


def double(x, axis, scale, count, on_arrival=()):
    have = {0: x}
    for k in sorted(range(1, count), key=lambda k: (bin(k).count("1"), -k)):
        low = k & -k
        have[k] = trade(have[k ^ low], axis, low * scale)
        if k in on_arrival:
            have[k] = on_arrival[k](have[k])
    return [have[k] for k in range(count)]


def layer_norm(row_block, shift_by, scale_by):
    average = jnp.mean(row_block, axis=-1, keepdims=True)
    centred = row_block - average
    spread = jnp.mean(centred * centred, axis=-1, keepdims=True)
    return centred * lax.rsqrt(spread + 1e-06) * (1.0 + scale_by) + shift_by


def trade(x, axis, flip):
    if flip == 0:
        return x
    return lax.ppermute(x, axis, [(i, i ^ flip) for i in range(lax.axis_size(axis))])


def in_hbm(x):
    return pltpu.with_memory_space_constraint(x, pltpu.HBM)


def hold_kernel(count, *refs):
    source_refs, sems = refs[1 : count + 1], refs[-1]
    *held_refs, token_ref = refs[count + 1 : -1]
    token_ref[...] = jnp.zeros_like(token_ref)
    copies = [
        pltpu.make_async_copy(source_ref, held_ref, sems.at[i])
        for i, (source_ref, held_ref) in enumerate(zip(source_refs, held_refs))
    ]
    for copy in copies:
        copy.start()
    for copy in copies:
        copy.wait()


def hold(after, *weights):
    count = len(weights)
    moved = sum(w.size * w.dtype.itemsize for w in weights)
    return pl.pallas_call(
        functools.partial(hold_kernel, count),
        in_specs=[VMEM_SPEC] + [ANY_SPEC] * count,
        out_specs=[VMEM_SPEC] * (count + 1),
        out_shape=[pltpu.VMEM(w.shape, w.dtype) for w in weights] + [TOKEN],
        scratch_shapes=[pltpu.SemaphoreType.DMA((count,))],
        cost_estimate=pl.CostEstimate(flops=0, bytes_accessed=moved, transcendentals=0),
        compiler_params=pltpu.CompilerParams(vmem_limit_bytes=2 << 20),
        name="hold",
    )(after, *[in_hbm(w) for w in weights])


def my_core(pair):
    return lax.rem(lax.axis_index("blk"), pair)


def enter_kernel(pair, idx_hbm, hidden_hbm, mod_hbm, key_hbm, value_hbm, *refs):
    rows_ref, normed_ref, select_ref, mod_ref, *side_refs = refs[: pair + 4]
    idx_ref, hidden_ref, sems, kv_sem = refs[pair + 4 :]
    copies = [
        pltpu.make_async_copy(source, target, sems.at[i])
        for i, (source, target) in enumerate(
            [(idx_hbm, idx_ref), (hidden_hbm, hidden_ref), (mod_hbm, mod_ref)]
        )
    ]
    for copy in copies:
        copy.start()
    parts, _, both = side_refs[0].shape
    half = both // 2
    uly, core = lax.axis_index("uly"), my_core(pair)
    kv_copies = []
    for side, side_ref in enumerate(side_refs):
        for flip in range(parts):
            start = pl.multiple_of(((uly ^ flip) * pair + (core ^ side)) * half, DH)
            for at, source in enumerate((key_hbm, value_hbm)):
                copy = pltpu.make_async_copy(
                    source.at[:, pl.ds(start, half)],
                    side_ref.at[flip, :, pl.ds(at * half, half)],
                    kv_sem.at[side, flip, at],
                )
                copy.start()
                kv_copies.append(copy)
    for copy in copies:
        copy.wait()
    tokens, width = hidden_ref.shape
    slots = idx_ref.shape[1]
    position = lax.broadcasted_iota(jnp.int32, (tokens, slots), 0)
    select = (position == idx_ref[...]).astype(jnp.float32).astype(jnp.bfloat16)
    select_ref[...] = select
    contract = (((0,), (0,)), ((), ()))
    rows = lax.dot_general(
        select, hidden_ref[...], contract, preferred_element_type=jnp.float32
    )
    live = lax.dot_general(
        select,
        jnp.ones((tokens, DH), jnp.bfloat16),
        contract,
        preferred_element_type=jnp.float32,
    )
    rows_ref[...] = rows
    normed = layer_norm(rows, mod_ref[0:1, :], mod_ref[1:2, :])
    normed_ref[:, :width] = normed.astype(jnp.bfloat16)
    normed_ref[:, width:] = live.astype(jnp.bfloat16)
    for copy in kv_copies:
        copy.wait()


def enter(refresh_idx, hidden_in, modulation, cache_keys, cache_values, parts, pair):
    slots = refresh_idx.shape[0]
    tokens, width = hidden_in.shape
    both = 2 * width // (parts * pair)
    out = pl.pallas_call(
        functools.partial(enter_kernel, pair),
        in_specs=[ANY_SPEC] * 5,
        out_specs=[VMEM_SPEC] * (pair + 4),
        out_shape=[
            pltpu.VMEM((slots, width), jnp.float32),
            pltpu.VMEM((slots, width + DH), jnp.bfloat16),
            pltpu.VMEM((tokens, slots), jnp.bfloat16),
            pltpu.VMEM(modulation.shape, modulation.dtype),
        ]
        + [pltpu.VMEM((parts, tokens, both), cache_keys.dtype)] * pair,
        scratch_shapes=[
            pltpu.VMEM((1, slots), jnp.int32),
            pltpu.VMEM(hidden_in.shape, hidden_in.dtype),
            pltpu.SemaphoreType.DMA((3,)),
            pltpu.SemaphoreType.DMA((pair, parts, 2)),
        ],
        compiler_params=pltpu.CompilerParams(vmem_limit_bytes=8 << 20),
        name="enter",
    )(
        *[
            in_hbm(x)
            for x in (refresh_idx.reshape(1, slots), hidden_in, modulation, cache_keys, cache_values)
        ]
    )
    return *out[:4], out[4:]


def merge_kv_kernel(sides, flips, *refs):
    *refs, token_ref = refs
    token_ref[...] = jnp.zeros_like(token_ref)
    for flip, out_ref in zip(flips, refs[-len(flips) :]):
        for side in range(sides):
            out_ref[side] = refs[side][flip]


def merge_kv(sides, flips, after):
    _, tokens, both = sides[0].shape
    *merged, token = pl.pallas_call(
        functools.partial(merge_kv_kernel, len(sides), flips),
        out_specs=[VMEM_SPEC] * (len(flips) + 1),
        out_shape=[pltpu.VMEM((len(sides), tokens, both), sides[0].dtype) for _ in flips]
        + [TOKEN],
        compiler_params=pltpu.CompilerParams(vmem_limit_bytes=8 << 20),
        name="merge_kv",
    )(*sides, *after)
    return merged, token


def relay_kernel(x_ref, after_ref, out_ref):
    out_ref[...] = x_ref[...]


def relay(x, after):
    return pl.pallas_call(
        relay_kernel,
        out_specs=VMEM_SPEC,
        out_shape=pltpu.VMEM(x.shape, x.dtype),
        compiler_params=pltpu.CompilerParams(vmem_limit_bytes=2 << 20),
        name="relay",
    )(x, after)


def project_kernel(pieces, after_ref, *refs):
    rows_refs, (w_ref, gain_hbm_ref) = refs[:pieces], refs[pieces : pieces + 2]
    *query_refs, spread_ref, token_ref, heads_ref, gain_ref, sem = refs[pieces + 2 :]
    token_ref[...] = jnp.zeros_like(token_ref)
    copy = pltpu.make_async_copy(gain_hbm_ref, gain_ref, sem)
    copy.start()
    core = my_core(len(query_refs))
    width = w_ref.shape[0]
    group, half = query_refs[0].shape
    rows = jnp.concatenate([ref[...] for ref in rows_refs], axis=0)
    everyone = rows.shape[0]
    flags = rows[:, width:]
    shape = (everyone, everyone)
    before = lax.broadcasted_iota(jnp.int32, shape, 1) < lax.broadcasted_iota(jnp.int32, shape, 0)
    before = before.astype(jnp.float32).astype(jnp.bfloat16)
    rank = jnp.dot(before, flags, preferred_element_type=jnp.float32)
    lane = lax.broadcasted_iota(jnp.int32, rank.shape, 1).astype(jnp.float32)
    spread = jnp.where((rank == lane) & (flags.astype(jnp.float32) > 0.0), 1.0, 0.0)
    spread = spread.astype(jnp.bfloat16)
    spread_ref[...] = spread
    live_rows = lax.dot_general(
        spread[:, :group],
        rows[:, :width],
        (((0,), (0,)), ((), ())),
        preferred_element_type=jnp.float32,
    ).astype(jnp.bfloat16)
    projected = jnp.dot(live_rows, w_ref[...], preferred_element_type=jnp.float32)
    copy.wait()
    for start in range(0, projected.shape[1], DH):
        head = projected[:, start : start + DH]
        squares = jnp.mean(head * head, axis=-1, keepdims=True)
        heads_ref[:, start : start + DH] = (
            head * lax.rsqrt(squares + 1e-06) * (gain_ref[...] / math.sqrt(DH))
        )
    for side, query_ref in enumerate(query_refs):
        start = pl.multiple_of((core ^ side) * half, DH)
        query_ref[...] = heads_ref[:, pl.ds(start, half)].astype(jnp.bfloat16)


def project(after, rows, w_query, q_gain, group, pair):
    half = w_query.shape[1] // pair
    everyone = len(rows) * rows[0].shape[0]
    query = jax.ShapeDtypeStruct((group, half), jnp.bfloat16)
    out = pl.pallas_call(
        functools.partial(project_kernel, len(rows)),
        in_specs=[VMEM_SPEC] * (len(rows) + 2) + [ANY_SPEC],
        out_shape=[query] * pair + [jax.ShapeDtypeStruct((everyone, DH), jnp.bfloat16), TOKEN],
        scratch_shapes=[
            pltpu.VMEM((group, w_query.shape[1]), jnp.float32),
            pltpu.VMEM((1, DH), jnp.float32),
            pltpu.SemaphoreType.DMA,
        ],
        compiler_params=pltpu.CompilerParams(vmem_limit_bytes=16 << 20),
        name="project",
    )(after, *rows, w_query, in_hbm(q_gain.reshape(1, DH)))
    return out[:-2], out[-2], out[-1]


def head_scores(queries, kv_refs, head):
    half = queries.shape[1]
    cols = slice(head * DH, (head + 1) * DH)
    vals = slice(half + head * DH, half + (head + 1) * DH)
    sides = kv_refs[0].shape[0]
    keys = [ref[side, :, cols] for ref in kv_refs for side in range(sides)]
    values = [ref[side, :, vals] for ref in kv_refs for side in range(sides)]
    scores = lax.dot_general(
        queries[:, cols],
        jnp.concatenate(keys, axis=0),
        (((1,), (1,)), ((), ())),
        preferred_element_type=jnp.float32,
    )
    return scores, jnp.concatenate(values, axis=0)


def lanes_of(stats):
    packed = stats[:8]
    for at in range(8, stats.shape[0], 8):
        packed = packed + pltpu.roll(stats[at : at + 8], at, axis=1)
    return packed


def rows_of(packed, rows):
    parts = [packed] + [pltpu.roll(packed, DH - at, axis=1) for at in range(8, rows, 8)]
    return jnp.concatenate(parts, axis=0)


def stacked(refs):
    rows = [ref[core].astype(jnp.float32) for ref in refs for core in range(ref.shape[0])]
    return jnp.concatenate(rows, axis=0).astype(jnp.bfloat16)


def attend_first_kernel(pieces, *refs):
    query_refs, (*kv_refs, sum_ref, stat_ref) = refs[:pieces], refs[pieces:]
    cores, group, half = query_refs[0].shape
    rows = cores * group
    for at in range(0, pieces, 4):
        queries = stacked(query_refs[at : at + 4])
        mine = slice(at * rows, at * rows + queries.shape[0])
        lane = lax.broadcasted_iota(jnp.int32, (queries.shape[0], DH), 1)
        stats = jnp.zeros((queries.shape[0], DH), jnp.float32)
        for head in range(half // DH):
            scores, values = head_scores(queries, kv_refs, head)
            maxima = jnp.max(scores, axis=-1, keepdims=True)
            weights = jnp.exp(scores - maxima)
            total = jnp.sum(weights, axis=-1, keepdims=True)
            sum_ref[mine, head * DH : (head + 1) * DH] = jnp.dot(
                weights.astype(jnp.bfloat16), values, preferred_element_type=jnp.float32
            )
            stats = jnp.where(lane == 2 * head, maxima, stats)
            stats = jnp.where(lane == 2 * head + 1, total, stats)
        stat_ref[mine, :] = stats


def attend_first(queries, kv_parts):
    cores, group, half = queries[0].shape
    count = cores * group * len(queries)
    return pl.pallas_call(
        functools.partial(attend_first_kernel, len(queries)),
        out_shape=[
            jax.ShapeDtypeStruct((count, half), jnp.float32),
            jax.ShapeDtypeStruct((count, DH), jnp.float32),
        ],
        cost_estimate=pl.CostEstimate(flops=0, bytes_accessed=0, transcendentals=0),
        compiler_params=pltpu.CompilerParams(vmem_limit_bytes=24 << 20),
        name="attend_first",
    )(*queries, *kv_parts)


def attend_last_kernel(pieces, after_ref, sum_ref, stat_ref, *refs):
    *refs, token_ref = refs
    token_ref[...] = jnp.zeros_like(token_ref)
    query_refs, kv_refs, out_refs = refs[:pieces], refs[pieces:-pieces], refs[-pieces:]
    cores, group, half = query_refs[0].shape
    rows = cores * group
    for at in range(0, pieces, 4):
        stop = min(at + 4, pieces)
        queries = stacked(query_refs[at:stop])
        mine = slice(at * rows, stop * rows)
        before = stat_ref[mine, :]
        lane = lax.broadcasted_iota(jnp.int32, before.shape, 1)
        stats = jnp.zeros_like(before)
        for head in range(half // DH):
            cols = slice(head * DH, (head + 1) * DH)
            scores, values = head_scores(queries, kv_refs, head)
            earlier = before[:, 2 * head : 2 * head + 1]
            maxima = jnp.maximum(earlier, jnp.max(scores, axis=-1, keepdims=True))
            weights = jnp.exp(scores - maxima)
            factor = jnp.exp(earlier - maxima)
            total = before[:, 2 * head + 1 : 2 * head + 2] * factor
            total = total + jnp.sum(weights, axis=-1, keepdims=True)
            weighted = sum_ref[mine, cols] * factor + jnp.dot(
                weights.astype(jnp.bfloat16), values, preferred_element_type=jnp.float32
            )
            stats = jnp.where(lane == 2 * head, maxima, stats)
            stats = jnp.where(lane == 2 * head + 1, total, stats)
            for j in range(at, stop):
                out_refs[j][:rows, cols] = weighted[(j - at) * rows : (j - at + 1) * rows]
        for j in range(at, stop):
            own = stats[(j - at) * rows : (j - at + 1) * rows]
            out_refs[j][rows:, DH:] = jnp.zeros((8, half - DH), jnp.float32)
            out_refs[j][rows:, :DH] = lanes_of(own)


def attend_last(after, first, queries, kv_parts):
    cores, group, half = queries[0].shape
    rows = cores * group
    return pl.pallas_call(
        functools.partial(attend_last_kernel, len(queries)),
        out_shape=[jax.ShapeDtypeStruct((rows + 8, half), jnp.float32)] * len(queries) + [TOKEN],
        compiler_params=pltpu.CompilerParams(vmem_limit_bytes=24 << 20),
        name="attend_last",
    )(after, *first, *queries, *kv_parts)


def combine_kernel(pieces, after_ref, *refs):
    part_refs, out_refs = refs[:pieces], refs[pieces:]
    group, half = out_refs[0].shape
    rows = group * len(out_refs)
    stats = []
    for ref in part_refs:
        stats.append(rows_of(ref[rows:, :DH], rows))
    for head in range(half // DH):
        cols = slice(head * DH, (head + 1) * DH)
        maxima = [stat[:, 2 * head : 2 * head + 1] for stat in stats]
        top = functools.reduce(jnp.maximum, maxima)
        total = jnp.zeros_like(top)
        attended = jnp.zeros((rows, DH), jnp.float32)
        for ref, stat, maximum in zip(part_refs, stats, maxima):
            factor = jnp.exp(maximum - top)
            total = total + stat[:, 2 * head + 1 : 2 * head + 2] * factor
            attended = attended + ref[:rows, cols] * factor
        attended = attended / total
        for side, out_ref in enumerate(out_refs):
            out_ref[:, cols] = attended[side * group : (side + 1) * group].astype(jnp.bfloat16)


def combine(after, parts, group, pair):
    half = parts[0].shape[1]
    return pl.pallas_call(
        functools.partial(combine_kernel, len(parts)),
        out_shape=[jax.ShapeDtypeStruct((group, half), jnp.bfloat16)] * pair,
        compiler_params=pltpu.CompilerParams(vmem_limit_bytes=16 << 20),
        name="combine",
    )(after, *parts)


def output_kernel(sides, spread_ref, *refs):
    side_refs, w_ref, (*out_refs, token_ref) = refs[:sides], refs[sides], refs[sides + 1 :]
    token_ref[...] = jnp.zeros_like(token_ref)
    group, half = side_refs[0].shape
    slots, width = out_refs[0].shape
    spread = spread_ref[:, :group]
    attended = [
        jnp.dot(spread, ref[...], preferred_element_type=jnp.float32).astype(jnp.bfloat16)
        for ref in side_refs
    ]
    core = my_core(sides)
    starts = [pl.multiple_of((core ^ side) * half, DH) for side in range(sides)]
    step = math.gcd(width, 1024)
    for col in range(0, width, step):
        terms = jnp.zeros((spread.shape[0], step), jnp.float32)
        for start, side in zip(starts, attended):
            terms = terms + jnp.dot(
                side, w_ref[pl.ds(start, half), col : col + step], preferred_element_type=jnp.float32
            )
        for k, out_ref in enumerate(out_refs):
            piece = terms[k * slots : (k + 1) * slots]
            out_ref[:, col : col + step] = piece.astype(out_ref.dtype)


def output(spread, sides, w_out, slots, parts):
    width = w_out.shape[1]
    return pl.pallas_call(
        functools.partial(output_kernel, len(sides)),
        out_shape=[
            jax.ShapeDtypeStruct((slots, width), jnp.bfloat16 if k else jnp.float32)
            for k in range(parts)
        ]
        + [TOKEN],
        compiler_params=pltpu.CompilerParams(vmem_limit_bytes=16 << 20),
        name="output",
    )(spread, *sides, w_out)


def mlp_kernel(pieces, *refs):
    row_refs, (up_ref, down_ref) = refs[:pieces], refs[pieces : pieces + 2]
    *out_refs, act_ref = refs[pieces + 2 :]
    hidden, width = down_ref.shape
    rows = [ref[j] for ref in row_refs for j in range(ref.shape[0])]
    rows = jnp.concatenate(rows, axis=0)
    count = out_refs[0].shape[0]
    step = math.gcd(hidden, 512)
    for col in range(0, hidden, step):
        lifted = jnp.dot(rows, up_ref[:, col : col + step], preferred_element_type=jnp.float32)
        act_ref[:, col : col + step] = jax.nn.gelu(lifted, approximate=True).astype(jnp.bfloat16)
    step = math.gcd(width, 512)
    for col in range(0, width, step):
        down = jnp.dot(
            act_ref[...], down_ref[:, col : col + step], preferred_element_type=jnp.float32
        )
        for side, out_ref in enumerate(out_refs):
            piece = down[side * count : (side + 1) * count]
            out_ref[:, col : col + step] = piece.astype(out_ref.dtype)


def mlp(rows, w_up, w_down, pair):
    count = sum(x.shape[0] * x.shape[1] for x in rows)
    hidden, width = w_down.shape
    return pl.pallas_call(
        functools.partial(mlp_kernel, len(rows)),
        out_shape=[
            jax.ShapeDtypeStruct((count // pair, width), jnp.bfloat16 if side else jnp.float32)
            for side in range(pair)
        ],
        scratch_shapes=[pltpu.VMEM((count, hidden), jnp.bfloat16)],
        compiler_params=pltpu.CompilerParams(vmem_limit_bytes=32 << 20),
        name="mlp",
    )(*rows, w_up, w_down)


def join_kernel(count, *refs):
    part_refs, out_ref = refs[:count], refs[-1]
    for at, ref in enumerate(part_refs):
        out_ref[at] = ref[...]


def join(parts, after=()):
    return pl.pallas_call(
        functools.partial(join_kernel, len(parts)),
        out_shape=jax.ShapeDtypeStruct((len(parts), *parts[0].shape), parts[0].dtype),
        compiler_params=pltpu.CompilerParams(vmem_limit_bytes=8 << 20),
        name="join",
    )(*parts, *after)


def renorm_kernel(hold_ref, rows_ref, mod_ref, *refs):
    *term_refs, after_ref, normed_ref = refs
    branch = term_refs[0][...]
    for ref in term_refs[1:]:
        branch = branch + ref[...].astype(jnp.float32)
    after = rows_ref[...] + mod_ref[2:3, :] * branch
    after_ref[...] = after
    normed_ref[...] = layer_norm(after, mod_ref[3:4, :], mod_ref[4:5, :]).astype(jnp.bfloat16)


def renorm(after, rows_in, modulation, terms):
    return pl.pallas_call(
        renorm_kernel,
        out_shape=[
            jax.ShapeDtypeStruct(rows_in.shape, jnp.float32),
            jax.ShapeDtypeStruct(rows_in.shape, jnp.bfloat16),
        ],
        compiler_params=pltpu.CompilerParams(vmem_limit_bytes=8 << 20),
        name="renorm",
    )(after, rows_in, modulation, *terms)


def fold_kernel(sides, *refs):
    side_refs, out_refs = refs[:sides], refs[sides:]
    slots = out_refs[0].shape[0]
    for j, out_ref in enumerate(out_refs):
        total = side_refs[0][j * slots : (j + 1) * slots]
        for ref in side_refs[1:]:
            total = total + ref[j * slots : (j + 1) * slots].astype(jnp.float32)
        out_ref[...] = total.astype(out_ref.dtype)


def fold(sides, slots):
    count, width = sides[0].shape
    return pl.pallas_call(
        functools.partial(fold_kernel, len(sides)),
        out_shape=[
            jax.ShapeDtypeStruct((slots, width), jnp.bfloat16 if j else jnp.float32)
            for j in range(count // slots)
        ],
        compiler_params=pltpu.CompilerParams(vmem_limit_bytes=8 << 20),
        name="fold",
    )(*sides)


def finish_kernel(select_ref, cached_ref, after_ref, mod_ref, *refs):
    *term_refs, out_ref = refs
    total = term_refs[0][...]
    for ref in term_refs[1:]:
        total = total + ref[...].astype(jnp.float32)
    renewed = (after_ref[...] + mod_ref[5:6, :] * total).astype(jnp.bfloat16)
    select = select_ref[...]
    placed = jnp.dot(select, renewed, preferred_element_type=jnp.float32)
    covered = jnp.sum(select.astype(jnp.float32), axis=1, keepdims=True)
    blended = cached_ref[...].astype(jnp.float32) * (1.0 - covered) + placed
    out_ref[...] = blended.astype(jnp.bfloat16)


def finish(select, cached, after_attn, modulation, terms):
    return pl.pallas_call(
        finish_kernel,
        out_shape=jax.ShapeDtypeStruct(cached.shape, jnp.bfloat16),
        compiler_params=pltpu.CompilerParams(vmem_limit_bytes=8 << 20),
        name="finish",
    )(select, cached, after_attn, modulation, *terms)


def body(
    hidden_in,
    cached_out,
    cache_keys,
    cache_values,
    refresh_idx,
    modulation,
    q_gain,
    w_query,
    w_out,
    w_up,
    w_down,
):
    slots = refresh_idx.shape[0]
    uly_size = lax.axis_size("uly")
    blk_size = lax.axis_size("blk")
    local_heads = w_query.shape[1] // DH
    group = min(slots * uly_size, slots + (uly_size - 1) * OTHER)
    pair = 2 if blk_size % 2 == 0 and local_heads % 2 == 0 else 1
    chips = blk_size // pair

    rows_in, normed, select, modulation, sides = enter(
        refresh_idx, hidden_in, modulation, cache_keys, cache_values, uly_size, pair
    )
    sides = [trade(x, "blk", side) for side, x in enumerate(sides)]
    w_query, token = hold(normed, w_query)
    half_way = uly_size // 2
    cuts = [[half_way, 0], [k for k in reversed(range(uly_size)) if k not in (0, half_way)]]
    first, token = merge_kv(sides, cuts[0], [token])
    group_rows = double(normed, "uly", 1, uly_size, {half_way: lambda x: relay(x, token)})
    second, token = merge_kv(sides, cuts[1], group_rows[1:])
    kv_parts = [trade(x, "uly", k) for k, x in zip(cuts[0] + cuts[1], first + second)]

    queries, spread, token = project(token, group_rows, w_query, q_gain, group, pair)
    w_out, token = hold(token, w_out)
    queries = join([trade(x, "blk", side) for side, x in enumerate(queries)])
    queries = double(queries, "blk", pair, chips)
    first = attend_first(queries, kv_parts[:2])
    *parts, token = attend_last(token, first, queries, kv_parts[2:])
    w_up, token = hold(token, w_up)
    parts = [trade(x, "blk", j * pair) for j, x in enumerate(parts)]
    attended = combine(token, parts, group, pair)
    attended = [trade(x, "blk", side) for side, x in enumerate(attended)]
    *terms, token = output(spread, attended, w_out, slots, uly_size)
    w_down, cached, token = hold(token, w_down, cached_out)
    terms = [trade(x, "uly", k) for k, x in enumerate(terms)]
    after_attn, norm_mlp = renorm(token, rows_in, modulation, terms)

    rows = [join([trade(norm_mlp, "blk", j * pair) for j in range(chips)])]
    if pair == 2:
        rows.append(trade(rows[0], "blk", 1))
    down = mlp(rows, w_up, w_down, pair)
    down = [trade(x, "blk", side) for side, x in enumerate(down)]
    terms = [trade(x, "blk", j * pair) for j, x in enumerate(fold(down, slots))]
    return finish(select, cached, after_attn, modulation, terms)


def solution(mesh):
    return jax.shard_map(
        body,
        mesh=mesh,
        in_specs=(
            P(("blk", "uly"), None),
            P(("blk", "uly"), None),
            P(("blk", "uly"), None),
            P(("blk", "uly"), None),
            P(("blk", "uly")),
            P(),
            P(),
            P(None, "uly"),
            P("uly", None),
            P(None, "blk"),
            P("blk", None),
        ),
        out_specs=P(("blk", "uly"), None),
        check_vma=False,
    )
```

```python
import functools
import math

import jax
import jax.numpy as jnp
from jax import lax
from jax.experimental import pallas as pl
from jax.experimental.pallas import tpu as pltpu
from jax.sharding import PartitionSpec as P

DH = 128
OTHER = 8
VMEM_SPEC = pl.BlockSpec(memory_space=pltpu.VMEM)
TOKEN = pltpu.VMEM((8, DH), jnp.float32)
ANY_SPEC = pl.BlockSpec(memory_space=pl.ANY)


def double(x, axis, scale, count, on_arrival=()):
    have = {0: x}
    for k in sorted(range(1, count), key=lambda k: (bin(k).count("1"), -k)):
        low = k & -k
        have[k] = trade(have[k ^ low], axis, low * scale)
        if k in on_arrival:
            have[k] = on_arrival[k](have[k])
    return [have[k] for k in range(count)]


def layer_norm(row_block, shift_by, scale_by):
    average = jnp.mean(row_block, axis=-1, keepdims=True)
    centred = row_block - average
    spread = jnp.mean(centred * centred, axis=-1, keepdims=True)
    return centred * lax.rsqrt(spread + 1e-06) * (1.0 + scale_by) + shift_by


def trade(x, axis, flip):
    if flip == 0:
        return x
    return lax.ppermute(x, axis, [(i, i ^ flip) for i in range(lax.axis_size(axis))])


def in_hbm(x):
    return pltpu.with_memory_space_constraint(x, pltpu.HBM)


def hold_kernel(count, *refs):
    source_refs, sems = refs[1 : count + 1], refs[-1]
    *held_refs, token_ref = refs[count + 1 : -1]
    token_ref[...] = jnp.zeros_like(token_ref)
    copies = [
        pltpu.make_async_copy(source_ref, held_ref, sems.at[i])
        for i, (source_ref, held_ref) in enumerate(zip(source_refs, held_refs))
    ]
    for copy in copies:
        copy.start()
    for copy in copies:
        copy.wait()


def hold(after, *weights):
    count = len(weights)
    moved = sum(w.size * w.dtype.itemsize for w in weights)
    return pl.pallas_call(
        functools.partial(hold_kernel, count),
        in_specs=[VMEM_SPEC] + [ANY_SPEC] * count,
        out_specs=[VMEM_SPEC] * (count + 1),
        out_shape=[pltpu.VMEM(w.shape, w.dtype) for w in weights] + [TOKEN],
        scratch_shapes=[pltpu.SemaphoreType.DMA((count,))],
        cost_estimate=pl.CostEstimate(flops=0, bytes_accessed=moved, transcendentals=0),
        compiler_params=pltpu.CompilerParams(vmem_limit_bytes=2 << 20),
        name="hold",
    )(after, *[in_hbm(w) for w in weights])


def my_core(pair):
    return lax.rem(lax.axis_index("blk"), pair)


def enter_kernel(pair, idx_hbm, hidden_hbm, mod_hbm, key_hbm, value_hbm, *refs):
    rows_ref, normed_ref, select_ref, mod_ref, *side_refs = refs[: pair + 4]
    idx_ref, hidden_ref, sems, kv_sem = refs[pair + 4 :]
    copies = [
        pltpu.make_async_copy(source, target, sems.at[i])
        for i, (source, target) in enumerate(
            [(idx_hbm, idx_ref), (hidden_hbm, hidden_ref), (mod_hbm, mod_ref)]
        )
    ]
    for copy in copies:
        copy.start()
    parts, _, both = side_refs[0].shape
    half = both // 2
    uly, core = lax.axis_index("uly"), my_core(pair)
    kv_copies = []
    for side, side_ref in enumerate(side_refs):
        for flip in range(parts):
            start = pl.multiple_of(((uly ^ flip) * pair + (core ^ side)) * half, DH)
            for at, source in enumerate((key_hbm, value_hbm)):
                copy = pltpu.make_async_copy(
                    source.at[:, pl.ds(start, half)],
                    side_ref.at[flip, :, pl.ds(at * half, half)],
                    kv_sem.at[side, flip, at],
                )
                copy.start()
                kv_copies.append(copy)
    for copy in copies:
        copy.wait()
    tokens, width = hidden_ref.shape
    slots = idx_ref.shape[1]
    position = lax.broadcasted_iota(jnp.int32, (tokens, slots), 0)
    select = (position == idx_ref[...]).astype(jnp.float32).astype(jnp.bfloat16)
    select_ref[...] = select
    contract = (((0,), (0,)), ((), ()))
    rows = lax.dot_general(
        select, hidden_ref[...], contract, preferred_element_type=jnp.float32
    )
    live = lax.dot_general(
        select,
        jnp.ones((tokens, DH), jnp.bfloat16),
        contract,
        preferred_element_type=jnp.float32,
    )
    rows_ref[...] = rows
    normed = layer_norm(rows, mod_ref[0:1, :], mod_ref[1:2, :])
    normed_ref[:, :width] = normed.astype(jnp.bfloat16)
    normed_ref[:, width:] = live.astype(jnp.bfloat16)
    for copy in kv_copies:
        copy.wait()


def enter(refresh_idx, hidden_in, modulation, cache_keys, cache_values, parts, pair):
    slots = refresh_idx.shape[0]
    tokens, width = hidden_in.shape
    both = 2 * width // (parts * pair)
    out = pl.pallas_call(
        functools.partial(enter_kernel, pair),
        in_specs=[ANY_SPEC] * 5,
        out_specs=[VMEM_SPEC] * (pair + 4),
        out_shape=[
            pltpu.VMEM((slots, width), jnp.float32),
            pltpu.VMEM((slots, width + DH), jnp.bfloat16),
            pltpu.VMEM((tokens, slots), jnp.bfloat16),
            pltpu.VMEM(modulation.shape, modulation.dtype),
        ]
        + [pltpu.VMEM((parts, tokens, both), cache_keys.dtype)] * pair,
        scratch_shapes=[
            pltpu.VMEM((1, slots), jnp.int32),
            pltpu.VMEM(hidden_in.shape, hidden_in.dtype),
            pltpu.SemaphoreType.DMA((3,)),
            pltpu.SemaphoreType.DMA((pair, parts, 2)),
        ],
        compiler_params=pltpu.CompilerParams(vmem_limit_bytes=8 << 20),
        name="enter",
    )(
        *[
            in_hbm(x)
            for x in (refresh_idx.reshape(1, slots), hidden_in, modulation, cache_keys, cache_values)
        ]
    )
    return *out[:4], out[4:]


def merge_kv_kernel(sides, flips, *refs):
    *refs, token_ref = refs
    token_ref[...] = jnp.zeros_like(token_ref)
    for flip, out_ref in zip(flips, refs[-len(flips) :]):
        for side in range(sides):
            out_ref[side] = refs[side][flip]


def merge_kv(sides, flips, after):
    _, tokens, both = sides[0].shape
    *merged, token = pl.pallas_call(
        functools.partial(merge_kv_kernel, len(sides), flips),
        out_specs=[VMEM_SPEC] * (len(flips) + 1),
        out_shape=[pltpu.VMEM((len(sides), tokens, both), sides[0].dtype) for _ in flips]
        + [TOKEN],
        compiler_params=pltpu.CompilerParams(vmem_limit_bytes=8 << 20),
        name="merge_kv",
    )(*sides, *after)
    return merged, token


def relay_kernel(x_ref, after_ref, out_ref):
    out_ref[...] = x_ref[...]


def relay(x, after):
    return pl.pallas_call(
        relay_kernel,
        out_specs=VMEM_SPEC,
        out_shape=pltpu.VMEM(x.shape, x.dtype),
        compiler_params=pltpu.CompilerParams(vmem_limit_bytes=2 << 20),
        name="relay",
    )(x, after)


def project_kernel(pieces, after_ref, *refs):
    rows_refs, (w_ref, gain_hbm_ref) = refs[:pieces], refs[pieces : pieces + 2]
    *query_refs, spread_ref, token_ref, heads_ref, gain_ref, sem = refs[pieces + 2 :]
    token_ref[...] = jnp.zeros_like(token_ref)
    copy = pltpu.make_async_copy(gain_hbm_ref, gain_ref, sem)
    copy.start()
    core = my_core(len(query_refs))
    width = w_ref.shape[0]
    group, half = query_refs[0].shape
    rows = jnp.concatenate([ref[...] for ref in rows_refs], axis=0)
    everyone = rows.shape[0]
    flags = rows[:, width:]
    shape = (everyone, everyone)
    before = lax.broadcasted_iota(jnp.int32, shape, 1) < lax.broadcasted_iota(jnp.int32, shape, 0)
    before = before.astype(jnp.float32).astype(jnp.bfloat16)
    rank = jnp.dot(before, flags, preferred_element_type=jnp.float32)
    lane = lax.broadcasted_iota(jnp.int32, rank.shape, 1).astype(jnp.float32)
    spread = jnp.where((rank == lane) & (flags.astype(jnp.float32) > 0.0), 1.0, 0.0)
    spread = spread.astype(jnp.bfloat16)
    spread_ref[...] = spread
    live_rows = lax.dot_general(
        spread[:, :group],
        rows[:, :width],
        (((0,), (0,)), ((), ())),
        preferred_element_type=jnp.float32,
    ).astype(jnp.bfloat16)
    projected = jnp.dot(live_rows, w_ref[...], preferred_element_type=jnp.float32)
    copy.wait()
    for start in range(0, projected.shape[1], DH):
        head = projected[:, start : start + DH]
        squares = jnp.mean(head * head, axis=-1, keepdims=True)
        heads_ref[:, start : start + DH] = (
            head * lax.rsqrt(squares + 1e-06) * (gain_ref[...] / math.sqrt(DH))
        )
    for side, query_ref in enumerate(query_refs):
        start = pl.multiple_of((core ^ side) * half, DH)
        query_ref[...] = heads_ref[:, pl.ds(start, half)].astype(jnp.bfloat16)


def project(after, rows, w_query, q_gain, group, pair):
    half = w_query.shape[1] // pair
    everyone = len(rows) * rows[0].shape[0]
    query = jax.ShapeDtypeStruct((group, half), jnp.bfloat16)
    out = pl.pallas_call(
        functools.partial(project_kernel, len(rows)),
        in_specs=[VMEM_SPEC] * (len(rows) + 2) + [ANY_SPEC],
        out_shape=[query] * pair + [jax.ShapeDtypeStruct((everyone, DH), jnp.bfloat16), TOKEN],
        scratch_shapes=[
            pltpu.VMEM((group, w_query.shape[1]), jnp.float32),
            pltpu.VMEM((1, DH), jnp.float32),
            pltpu.SemaphoreType.DMA,
        ],
        compiler_params=pltpu.CompilerParams(vmem_limit_bytes=16 << 20),
        name="project",
    )(after, *rows, w_query, in_hbm(q_gain.reshape(1, DH)))
    return out[:-2], out[-2], out[-1]


def head_scores(queries, kv_refs, head):
    half = queries.shape[1]
    cols = slice(head * DH, (head + 1) * DH)
    vals = slice(half + head * DH, half + (head + 1) * DH)
    sides = kv_refs[0].shape[0]
    keys = [ref[side, :, cols] for ref in kv_refs for side in range(sides)]
    values = [ref[side, :, vals] for ref in kv_refs for side in range(sides)]
    scores = lax.dot_general(
        queries[:, cols],
        jnp.concatenate(keys, axis=0),
        (((1,), (1,)), ((), ())),
        preferred_element_type=jnp.float32,
    )
    return scores, jnp.concatenate(values, axis=0)


def lanes_of(stats):
    packed = stats[:8]
    for at in range(8, stats.shape[0], 8):
        packed = packed + pltpu.roll(stats[at : at + 8], at, axis=1)
    return packed


def rows_of(packed, rows):
    parts = [packed] + [pltpu.roll(packed, DH - at, axis=1) for at in range(8, rows, 8)]
    return jnp.concatenate(parts, axis=0)


def stacked(refs):
    rows = [ref[core].astype(jnp.float32) for ref in refs for core in range(ref.shape[0])]
    return jnp.concatenate(rows, axis=0).astype(jnp.bfloat16)


def along_lanes(column):
    return jnp.broadcast_to(column, (column.shape[0], DH))


def weights_of(scores, maxima):
    width = scores.shape[1]
    return [jnp.exp(scores[:, at : at + DH] - maxima) for at in range(0, width, DH)]


def attend_first_kernel(pieces, *refs):
    query_refs, (*kv_refs, sum_ref, max_ref, total_ref) = refs[:pieces], refs[pieces:]
    cores, group, half = query_refs[0].shape
    rows = cores * group
    for at in range(0, pieces, 4):
        queries = stacked(query_refs[at : at + 4])
        mine = slice(at * rows, at * rows + queries.shape[0])
        for head in range(half // DH):
            cols = slice(head * DH, (head + 1) * DH)
            scores, values = head_scores(queries, kv_refs, head)
            maxima = along_lanes(jnp.max(scores, axis=-1, keepdims=True))
            weights = jnp.concatenate(weights_of(scores, maxima), axis=1)
            max_ref[mine, cols] = maxima
            total_ref[mine, cols] = along_lanes(jnp.sum(weights, axis=-1, keepdims=True))
            sum_ref[mine, cols] = jnp.dot(
                weights.astype(jnp.bfloat16), values, preferred_element_type=jnp.float32
            )


def attend_first(queries, kv_parts):
    cores, group, half = queries[0].shape
    count = cores * group * len(queries)
    return pl.pallas_call(
        functools.partial(attend_first_kernel, len(queries)),
        out_specs=[VMEM_SPEC] * 3,
        out_shape=[pltpu.VMEM((count, half), jnp.float32)] * 3,
        cost_estimate=pl.CostEstimate(flops=0, bytes_accessed=0, transcendentals=0),
        compiler_params=pltpu.CompilerParams(vmem_limit_bytes=24 << 20),
        name="attend_first",
    )(*queries, *kv_parts)


def attend_last_kernel(pieces, after_ref, sum_ref, max_ref, total_ref, *refs):
    *refs, token_ref = refs
    token_ref[...] = jnp.zeros_like(token_ref)
    query_refs, kv_refs, out_refs = refs[:pieces], refs[pieces:-pieces], refs[-pieces:]
    cores, group, half = query_refs[0].shape
    rows = cores * group
    for at in range(0, pieces, 4):
        stop = min(at + 4, pieces)
        queries = stacked(query_refs[at:stop])
        mine = slice(at * rows, stop * rows)
        lane = lax.broadcasted_iota(jnp.int32, (queries.shape[0], DH), 1)
        stats = jnp.zeros((queries.shape[0], DH), jnp.float32)
        for head in range(half // DH):
            cols = slice(head * DH, (head + 1) * DH)
            scores, values = head_scores(queries, kv_refs, head)
            earlier = max_ref[mine, cols]
            maxima = along_lanes(jnp.max(scores, axis=-1, keepdims=True))
            maxima = jnp.maximum(earlier, maxima)
            weights = jnp.concatenate(weights_of(scores, maxima), axis=1)
            factor = jnp.exp(earlier - maxima)
            total = along_lanes(jnp.sum(weights, axis=-1, keepdims=True))
            total = total_ref[mine, cols] * factor + total
            weighted = sum_ref[mine, cols] * factor + jnp.dot(
                weights.astype(jnp.bfloat16), values, preferred_element_type=jnp.float32
            )
            stats = jnp.where(lane == 2 * head, maxima, stats)
            stats = jnp.where(lane == 2 * head + 1, total, stats)
            for j in range(at, stop):
                out_refs[j][:rows, cols] = weighted[(j - at) * rows : (j - at + 1) * rows]
        for j in range(at, stop):
            own = stats[(j - at) * rows : (j - at + 1) * rows]
            out_refs[j][rows:, DH:] = jnp.zeros((8, half - DH), jnp.float32)
            out_refs[j][rows:, :DH] = lanes_of(own)


def attend_last(after, first, queries, kv_parts):
    cores, group, half = queries[0].shape
    rows = cores * group
    return pl.pallas_call(
        functools.partial(attend_last_kernel, len(queries)),
        out_specs=[VMEM_SPEC] * (len(queries) + 1),
        out_shape=[pltpu.VMEM((rows + 8, half), jnp.float32)] * len(queries) + [TOKEN],
        compiler_params=pltpu.CompilerParams(vmem_limit_bytes=24 << 20),
        name="attend_last",
    )(after, *first, *queries, *kv_parts)


def combine_kernel(pieces, after_ref, *refs):
    part_refs, out_refs = refs[:pieces], refs[pieces:]
    group, half = out_refs[0].shape
    rows = group * len(out_refs)
    stats = []
    for ref in part_refs:
        stats.append(rows_of(ref[rows:, :DH], rows))
    for head in range(half // DH):
        cols = slice(head * DH, (head + 1) * DH)
        maxima = [stat[:, 2 * head : 2 * head + 1] for stat in stats]
        top = functools.reduce(jnp.maximum, maxima)
        total = jnp.zeros_like(top)
        attended = jnp.zeros((rows, DH), jnp.float32)
        for ref, stat, maximum in zip(part_refs, stats, maxima):
            factor = jnp.exp(maximum - top)
            total = total + stat[:, 2 * head + 1 : 2 * head + 2] * factor
            attended = attended + ref[:rows, cols] * factor
        attended = attended / total
        for side, out_ref in enumerate(out_refs):
            out_ref[:, cols] = attended[side * group : (side + 1) * group].astype(jnp.bfloat16)


def combine(after, parts, group, pair):
    half = parts[0].shape[1]
    return pl.pallas_call(
        functools.partial(combine_kernel, len(parts)),
        out_shape=[jax.ShapeDtypeStruct((group, half), jnp.bfloat16)] * pair,
        compiler_params=pltpu.CompilerParams(vmem_limit_bytes=16 << 20),
        name="combine",
    )(after, *parts)


def output_kernel(sides, spread_ref, *refs):
    side_refs, w_ref, (*out_refs, token_ref) = refs[:sides], refs[sides], refs[sides + 1 :]
    token_ref[...] = jnp.zeros_like(token_ref)
    group, half = side_refs[0].shape
    slots, width = out_refs[0].shape
    spread = spread_ref[:, :group]
    attended = [
        jnp.dot(spread, ref[...], preferred_element_type=jnp.float32).astype(jnp.bfloat16)
        for ref in side_refs
    ]
    core = my_core(sides)
    starts = [pl.multiple_of((core ^ side) * half, DH) for side in range(sides)]
    step = math.gcd(width, 1024)
    for col in range(0, width, step):
        terms = jnp.zeros((spread.shape[0], step), jnp.float32)
        for start, side in zip(starts, attended):
            terms = terms + jnp.dot(
                side, w_ref[pl.ds(start, half), col : col + step], preferred_element_type=jnp.float32
            )
        for k, out_ref in enumerate(out_refs):
            piece = terms[k * slots : (k + 1) * slots]
            out_ref[:, col : col + step] = piece.astype(out_ref.dtype)


def output(spread, sides, w_out, slots, parts):
    width = w_out.shape[1]
    return pl.pallas_call(
        functools.partial(output_kernel, len(sides)),
        out_shape=[
            jax.ShapeDtypeStruct((slots, width), jnp.bfloat16 if k else jnp.float32)
            for k in range(parts)
        ]
        + [TOKEN],
        compiler_params=pltpu.CompilerParams(vmem_limit_bytes=16 << 20),
        name="output",
    )(spread, *sides, w_out)


def mlp_kernel(pieces, *refs):
    row_refs, (up_ref, down_ref) = refs[:pieces], refs[pieces : pieces + 2]
    *out_refs, act_ref = refs[pieces + 2 :]
    hidden, width = down_ref.shape
    rows = [ref[j] for ref in row_refs for j in range(ref.shape[0])]
    rows = jnp.concatenate(rows, axis=0)
    count = out_refs[0].shape[0]
    step = math.gcd(hidden, 512)
    for col in range(0, hidden, step):
        lifted = jnp.dot(rows, up_ref[:, col : col + step], preferred_element_type=jnp.float32)
        act_ref[:, col : col + step] = jax.nn.gelu(lifted, approximate=True).astype(jnp.bfloat16)
    step = math.gcd(width, 512)
    for col in range(0, width, step):
        down = jnp.dot(
            act_ref[...], down_ref[:, col : col + step], preferred_element_type=jnp.float32
        )
        for side, out_ref in enumerate(out_refs):
            piece = down[side * count : (side + 1) * count]
            out_ref[:, col : col + step] = piece.astype(out_ref.dtype)


def mlp(rows, w_up, w_down, pair):
    count = sum(x.shape[0] * x.shape[1] for x in rows)
    hidden, width = w_down.shape
    return pl.pallas_call(
        functools.partial(mlp_kernel, len(rows)),
        out_shape=[
            jax.ShapeDtypeStruct((count // pair, width), jnp.bfloat16 if side else jnp.float32)
            for side in range(pair)
        ],
        scratch_shapes=[pltpu.VMEM((count, hidden), jnp.bfloat16)],
        compiler_params=pltpu.CompilerParams(vmem_limit_bytes=32 << 20),
        name="mlp",
    )(*rows, w_up, w_down)


def join_kernel(count, *refs):
    part_refs, out_ref = refs[:count], refs[-1]
    for at, ref in enumerate(part_refs):
        out_ref[at] = ref[...]


def join(parts, after=()):
    return pl.pallas_call(
        functools.partial(join_kernel, len(parts)),
        out_shape=jax.ShapeDtypeStruct((len(parts), *parts[0].shape), parts[0].dtype),
        compiler_params=pltpu.CompilerParams(vmem_limit_bytes=8 << 20),
        name="join",
    )(*parts, *after)


def renorm_kernel(hold_ref, rows_ref, mod_ref, *refs):
    *term_refs, after_ref, normed_ref = refs
    branch = term_refs[0][...]
    for ref in term_refs[1:]:
        branch = branch + ref[...].astype(jnp.float32)
    after = rows_ref[...] + mod_ref[2:3, :] * branch
    after_ref[...] = after
    normed_ref[...] = layer_norm(after, mod_ref[3:4, :], mod_ref[4:5, :]).astype(jnp.bfloat16)


def renorm(after, rows_in, modulation, terms):
    return pl.pallas_call(
        renorm_kernel,
        out_shape=[
            jax.ShapeDtypeStruct(rows_in.shape, jnp.float32),
            jax.ShapeDtypeStruct(rows_in.shape, jnp.bfloat16),
        ],
        compiler_params=pltpu.CompilerParams(vmem_limit_bytes=8 << 20),
        name="renorm",
    )(after, rows_in, modulation, *terms)


def fold_kernel(sides, *refs):
    side_refs, out_refs = refs[:sides], refs[sides:]
    slots = out_refs[0].shape[0]
    for j, out_ref in enumerate(out_refs):
        total = side_refs[0][j * slots : (j + 1) * slots]
        for ref in side_refs[1:]:
            total = total + ref[j * slots : (j + 1) * slots].astype(jnp.float32)
        out_ref[...] = total.astype(out_ref.dtype)


def fold(sides, slots):
    count, width = sides[0].shape
    return pl.pallas_call(
        functools.partial(fold_kernel, len(sides)),
        out_shape=[
            jax.ShapeDtypeStruct((slots, width), jnp.bfloat16 if j else jnp.float32)
            for j in range(count // slots)
        ],
        compiler_params=pltpu.CompilerParams(vmem_limit_bytes=8 << 20),
        name="fold",
    )(*sides)


def finish_kernel(select_ref, cached_ref, after_ref, mod_ref, *refs):
    *term_refs, out_ref = refs
    total = term_refs[0][...]
    for ref in term_refs[1:]:
        total = total + ref[...].astype(jnp.float32)
    renewed = (after_ref[...] + mod_ref[5:6, :] * total).astype(jnp.bfloat16)
    select = select_ref[...]
    placed = jnp.dot(select, renewed, preferred_element_type=jnp.float32)
    covered = jnp.sum(select.astype(jnp.float32), axis=1, keepdims=True)
    blended = cached_ref[...].astype(jnp.float32) * (1.0 - covered) + placed
    out_ref[...] = blended.astype(jnp.bfloat16)


def finish(select, cached, after_attn, modulation, terms):
    return pl.pallas_call(
        finish_kernel,
        out_shape=jax.ShapeDtypeStruct(cached.shape, jnp.bfloat16),
        compiler_params=pltpu.CompilerParams(vmem_limit_bytes=8 << 20),
        name="finish",
    )(select, cached, after_attn, modulation, *terms)


def body(
    hidden_in,
    cached_out,
    cache_keys,
    cache_values,
    refresh_idx,
    modulation,
    q_gain,
    w_query,
    w_out,
    w_up,
    w_down,
):
    slots = refresh_idx.shape[0]
    uly_size = lax.axis_size("uly")
    blk_size = lax.axis_size("blk")
    local_heads = w_query.shape[1] // DH
    group = min(slots * uly_size, slots + (uly_size - 1) * OTHER)
    pair = 2 if blk_size % 2 == 0 and local_heads % 2 == 0 else 1
    chips = blk_size // pair

    rows_in, normed, select, modulation, sides = enter(
        refresh_idx, hidden_in, modulation, cache_keys, cache_values, uly_size, pair
    )
    sides = [trade(x, "blk", side) for side, x in enumerate(sides)]
    w_query, token = hold(normed, w_query)
    half_way = uly_size // 2
    cuts = [[half_way, 0], [k for k in reversed(range(uly_size)) if k not in (0, half_way)]]
    first, token = merge_kv(sides, cuts[0], [token])
    group_rows = double(normed, "uly", 1, uly_size, {half_way: lambda x: relay(x, token)})
    second, token = merge_kv(sides, cuts[1], group_rows[1:])
    kv_parts = [trade(x, "uly", k) for k, x in zip(cuts[0] + cuts[1], first + second)]

    queries, spread, token = project(token, group_rows, w_query, q_gain, group, pair)
    w_out, token = hold(token, w_out)
    queries = join([trade(x, "blk", side) for side, x in enumerate(queries)])
    queries = double(queries, "blk", pair, chips)
    first = attend_first(queries, kv_parts[:2])
    *parts, token = attend_last(token, first, queries, kv_parts[2:])
    w_up, token = hold(token, w_up)
    parts = [trade(x, "blk", j * pair) for j, x in enumerate(parts)]
    attended = combine(token, parts, group, pair)
    attended = [trade(x, "blk", side) for side, x in enumerate(attended)]
    *terms, token = output(spread, attended, w_out, slots, uly_size)
    w_down, cached, token = hold(token, w_down, cached_out)
    terms = [trade(x, "uly", k) for k, x in enumerate(terms)]
    after_attn, norm_mlp = renorm(token, rows_in, modulation, terms)

    rows = [join([trade(norm_mlp, "blk", j * pair) for j in range(chips)])]
    if pair == 2:
        rows.append(trade(rows[0], "blk", 1))
    down = mlp(rows, w_up, w_down, pair)
    down = [trade(x, "blk", side) for side, x in enumerate(down)]
    terms = [trade(x, "blk", j * pair) for j, x in enumerate(fold(down, slots))]
    return finish(select, cached, after_attn, modulation, terms)


def solution(mesh):
    return jax.shard_map(
        body,
        mesh=mesh,
        in_specs=(
            P(("blk", "uly"), None),
            P(("blk", "uly"), None),
            P(("blk", "uly"), None),
            P(("blk", "uly"), None),
            P(("blk", "uly")),
            P(),
            P(),
            P(None, "uly"),
            P("uly", None),
            P(None, "blk"),
            P("blk", None),
        ),
        out_specs=P(("blk", "uly"), None),
        check_vma=False,
    )
```

```python
import functools
import math

import jax
import jax.numpy as jnp
from jax import lax
from jax.experimental import pallas as pl
from jax.experimental.pallas import tpu as pltpu
from jax.sharding import PartitionSpec as P

DH = 128
OTHER = 8
VMEM_SPEC = pl.BlockSpec(memory_space=pltpu.VMEM)
TOKEN = pltpu.VMEM((8, DH), jnp.float32)
ANY_SPEC = pl.BlockSpec(memory_space=pl.ANY)


def far_first(parts):
    return parts[:1] + parts[:0:-1]


def double(x, axis, scale, count, on_arrival=()):
    have = {0: x}
    for k in sorted(range(1, count), key=lambda k: (bin(k).count("1"), -k)):
        low = k & -k
        have[k] = trade(have[k ^ low], axis, low * scale)
        if k in on_arrival:
            have[k] = on_arrival[k](have[k])
    return [have[k] for k in range(count)]


def layer_norm(row_block, shift_by, scale_by):
    average = jnp.mean(row_block, axis=-1, keepdims=True)
    centred = row_block - average
    spread = jnp.mean(centred * centred, axis=-1, keepdims=True)
    return centred * lax.rsqrt(spread + 1e-06) * (1.0 + scale_by) + shift_by


def trade(x, axis, flip):
    if flip == 0:
        return x
    return lax.ppermute(x, axis, [(i, i ^ flip) for i in range(lax.axis_size(axis))])


def in_hbm(x):
    return pltpu.with_memory_space_constraint(x, pltpu.HBM)


def hold_kernel(count, *refs):
    source_refs, sems = refs[1 : count + 1], refs[-1]
    *held_refs, token_ref = refs[count + 1 : -1]
    token_ref[...] = jnp.zeros_like(token_ref)
    copies = [
        pltpu.make_async_copy(source_ref, held_ref, sems.at[i])
        for i, (source_ref, held_ref) in enumerate(zip(source_refs, held_refs))
    ]
    for copy in copies:
        copy.start()
    for copy in copies:
        copy.wait()


def hold(after, *weights):
    count = len(weights)
    moved = sum(w.size * w.dtype.itemsize for w in weights)
    return pl.pallas_call(
        functools.partial(hold_kernel, count),
        in_specs=[VMEM_SPEC] + [ANY_SPEC] * count,
        out_specs=[VMEM_SPEC] * (count + 1),
        out_shape=[pltpu.VMEM(w.shape, w.dtype) for w in weights] + [TOKEN],
        scratch_shapes=[pltpu.SemaphoreType.DMA((count,))],
        cost_estimate=pl.CostEstimate(flops=0, bytes_accessed=moved, transcendentals=0),
        compiler_params=pltpu.CompilerParams(vmem_limit_bytes=2 << 20),
        name="hold",
    )(after, *[in_hbm(w) for w in weights])


def my_core(pair):
    return lax.rem(lax.axis_index("blk"), pair)


def enter_kernel(pair, idx_hbm, hidden_hbm, mod_hbm, key_hbm, value_hbm, *refs):
    rows_ref, normed_ref, select_ref, mod_ref, *side_refs = refs[: pair + 4]
    idx_ref, hidden_ref, sems, kv_sem = refs[pair + 4 :]
    copies = [
        pltpu.make_async_copy(source, target, sems.at[i])
        for i, (source, target) in enumerate(
            [(idx_hbm, idx_ref), (hidden_hbm, hidden_ref), (mod_hbm, mod_ref)]
        )
    ]
    for copy in copies:
        copy.start()
    parts, _, both = side_refs[0].shape
    half = both // 2
    uly, core = lax.axis_index("uly"), my_core(pair)
    kv_copies = []
    for side, side_ref in enumerate(side_refs):
        for flip in range(parts):
            start = pl.multiple_of(((uly ^ flip) * pair + (core ^ side)) * half, DH)
            for at, source in enumerate((key_hbm, value_hbm)):
                copy = pltpu.make_async_copy(
                    source.at[:, pl.ds(start, half)],
                    side_ref.at[flip, :, pl.ds(at * half, half)],
                    kv_sem.at[side, flip, at],
                )
                copy.start()
                kv_copies.append(copy)
    for copy in copies:
        copy.wait()
    tokens, width = hidden_ref.shape
    slots = idx_ref.shape[1]
    position = lax.broadcasted_iota(jnp.int32, (tokens, slots), 0)
    select = (position == idx_ref[...]).astype(jnp.float32).astype(jnp.bfloat16)
    select_ref[...] = select
    contract = (((0,), (0,)), ((), ()))
    rows = lax.dot_general(
        select, hidden_ref[...], contract, preferred_element_type=jnp.float32
    )
    live = lax.dot_general(
        select,
        jnp.ones((tokens, DH), jnp.bfloat16),
        contract,
        preferred_element_type=jnp.float32,
    )
    rows_ref[...] = rows
    normed = layer_norm(rows, mod_ref[0:1, :], mod_ref[1:2, :])
    normed_ref[:, :width] = normed.astype(jnp.bfloat16)
    normed_ref[:, width:] = live.astype(jnp.bfloat16)
    for copy in kv_copies:
        copy.wait()


def enter(refresh_idx, hidden_in, modulation, cache_keys, cache_values, parts, pair):
    slots = refresh_idx.shape[0]
    tokens, width = hidden_in.shape
    both = 2 * width // (parts * pair)
    out = pl.pallas_call(
        functools.partial(enter_kernel, pair),
        in_specs=[ANY_SPEC] * 5,
        out_specs=[VMEM_SPEC] * (pair + 4),
        out_shape=[
            pltpu.VMEM((slots, width), jnp.float32),
            pltpu.VMEM((slots, width + DH), jnp.bfloat16),
            pltpu.VMEM((tokens, slots), jnp.bfloat16),
            pltpu.VMEM(modulation.shape, modulation.dtype),
        ]
        + [pltpu.VMEM((parts, tokens, both), cache_keys.dtype)] * pair,
        scratch_shapes=[
            pltpu.VMEM((1, slots), jnp.int32),
            pltpu.VMEM(hidden_in.shape, hidden_in.dtype),
            pltpu.SemaphoreType.DMA((3,)),
            pltpu.SemaphoreType.DMA((pair, parts, 2)),
        ],
        compiler_params=pltpu.CompilerParams(vmem_limit_bytes=8 << 20),
        name="enter",
    )(
        *[
            in_hbm(x)
            for x in (refresh_idx.reshape(1, slots), hidden_in, modulation, cache_keys, cache_values)
        ]
    )
    return *out[:4], out[4:]


def merge_kv_kernel(sides, flips, *refs):
    *refs, token_ref = refs
    token_ref[...] = jnp.zeros_like(token_ref)
    for flip, out_ref in zip(flips, refs[-len(flips) :]):
        for side in range(sides):
            out_ref[side] = refs[side][flip]


def merge_kv(sides, flips, after):
    _, tokens, both = sides[0].shape
    *merged, token = pl.pallas_call(
        functools.partial(merge_kv_kernel, len(sides), flips),
        out_specs=[VMEM_SPEC] * (len(flips) + 1),
        out_shape=[pltpu.VMEM((len(sides), tokens, both), sides[0].dtype) for _ in flips]
        + [TOKEN],
        compiler_params=pltpu.CompilerParams(vmem_limit_bytes=8 << 20),
        name="merge_kv",
    )(*sides, *after)
    return merged, token


def relay_kernel(x_ref, after_ref, out_ref):
    out_ref[...] = x_ref[...]


def relay(x, after):
    return pl.pallas_call(
        relay_kernel,
        out_specs=VMEM_SPEC,
        out_shape=pltpu.VMEM(x.shape, x.dtype),
        compiler_params=pltpu.CompilerParams(vmem_limit_bytes=2 << 20),
        name="relay",
    )(x, after)


def project_kernel(pieces, after_ref, *refs):
    rows_refs, (w_ref, gain_hbm_ref) = refs[:pieces], refs[pieces : pieces + 2]
    *query_refs, spread_ref, token_ref, heads_ref, gain_ref, sem = refs[pieces + 2 :]
    token_ref[...] = jnp.zeros_like(token_ref)
    copy = pltpu.make_async_copy(gain_hbm_ref, gain_ref, sem)
    copy.start()
    core = my_core(len(query_refs))
    width = w_ref.shape[0]
    group, half = query_refs[0].shape
    rows = jnp.concatenate([ref[...] for ref in rows_refs], axis=0)
    everyone = rows.shape[0]
    flags = rows[:, width:]
    shape = (everyone, everyone)
    before = lax.broadcasted_iota(jnp.int32, shape, 1) < lax.broadcasted_iota(jnp.int32, shape, 0)
    before = before.astype(jnp.float32).astype(jnp.bfloat16)
    rank = jnp.dot(before, flags, preferred_element_type=jnp.float32)
    lane = lax.broadcasted_iota(jnp.int32, rank.shape, 1).astype(jnp.float32)
    spread = jnp.where((rank == lane) & (flags.astype(jnp.float32) > 0.0), 1.0, 0.0)
    spread = spread.astype(jnp.bfloat16)
    spread_ref[...] = spread
    live_rows = lax.dot_general(
        spread[:, :group],
        rows[:, :width],
        (((0,), (0,)), ((), ())),
        preferred_element_type=jnp.float32,
    ).astype(jnp.bfloat16)
    projected = jnp.dot(live_rows, w_ref[...], preferred_element_type=jnp.float32)
    copy.wait()
    for start in range(0, projected.shape[1], DH):
        head = projected[:, start : start + DH]
        squares = jnp.mean(head * head, axis=-1, keepdims=True)
        heads_ref[:, start : start + DH] = (
            head * lax.rsqrt(squares + 1e-06) * (gain_ref[...] / math.sqrt(DH))
        )
    for side, query_ref in enumerate(query_refs):
        start = pl.multiple_of((core ^ side) * half, DH)
        query_ref[...] = heads_ref[:, pl.ds(start, half)].astype(jnp.bfloat16)


def project(after, rows, w_query, q_gain, group, pair):
    half = w_query.shape[1] // pair
    everyone = len(rows) * rows[0].shape[0]
    query = jax.ShapeDtypeStruct((group, half), jnp.bfloat16)
    out = pl.pallas_call(
        functools.partial(project_kernel, len(rows)),
        in_specs=[VMEM_SPEC] * (len(rows) + 2) + [ANY_SPEC],
        out_shape=[query] * pair + [jax.ShapeDtypeStruct((everyone, DH), jnp.bfloat16), TOKEN],
        scratch_shapes=[
            pltpu.VMEM((group, w_query.shape[1]), jnp.float32),
            pltpu.VMEM((1, DH), jnp.float32),
            pltpu.SemaphoreType.DMA,
        ],
        compiler_params=pltpu.CompilerParams(vmem_limit_bytes=16 << 20),
        name="project",
    )(after, *rows, w_query, in_hbm(q_gain.reshape(1, DH)))
    return out[:-2], out[-2], out[-1]


def head_scores(queries, kv_refs, head):
    half = queries.shape[1]
    cols = slice(head * DH, (head + 1) * DH)
    vals = slice(half + head * DH, half + (head + 1) * DH)
    sides = kv_refs[0].shape[0]
    keys = [ref[side, :, cols] for ref in kv_refs for side in range(sides)]
    values = [ref[side, :, vals] for ref in kv_refs for side in range(sides)]
    scores = lax.dot_general(
        queries[:, cols],
        jnp.concatenate(keys, axis=0),
        (((1,), (1,)), ((), ())),
        preferred_element_type=jnp.float32,
    )
    return scores, jnp.concatenate(values, axis=0)


def lanes_of(stats):
    packed = stats[:8]
    for at in range(8, stats.shape[0], 8):
        packed = packed + pltpu.roll(stats[at : at + 8], at, axis=1)
    return packed


def rows_of(packed, rows):
    parts = [packed] + [pltpu.roll(packed, DH - at, axis=1) for at in range(8, rows, 8)]
    return jnp.concatenate(parts, axis=0)


def stacked(refs):
    rows = [ref[core].astype(jnp.float32) for ref in refs for core in range(ref.shape[0])]
    return jnp.concatenate(rows, axis=0).astype(jnp.bfloat16)


def along_lanes(column):
    return jnp.broadcast_to(column, (column.shape[0], DH))


def weights_of(scores, maxima):
    width = scores.shape[1]
    return [jnp.exp(scores[:, at : at + DH] - maxima) for at in range(0, width, DH)]


def attend_first_kernel(pieces, *refs):
    query_refs, (*kv_refs, sum_ref, max_ref, total_ref) = refs[:pieces], refs[pieces:]
    cores, group, half = query_refs[0].shape
    rows = cores * group
    for at in range(0, pieces, 4):
        queries = stacked(query_refs[at : at + 4])
        mine = slice(at * rows, at * rows + queries.shape[0])
        for head in range(half // DH):
            cols = slice(head * DH, (head + 1) * DH)
            scores, values = head_scores(queries, kv_refs, head)
            maxima = along_lanes(jnp.max(scores, axis=-1, keepdims=True))
            weights = jnp.concatenate(weights_of(scores, maxima), axis=1)
            max_ref[mine, cols] = maxima
            total_ref[mine, cols] = along_lanes(jnp.sum(weights, axis=-1, keepdims=True))
            sum_ref[mine, cols] = jnp.dot(
                weights.astype(jnp.bfloat16), values, preferred_element_type=jnp.float32
            )


def attend_first(queries, kv_parts):
    cores, group, half = queries[0].shape
    count = cores * group * len(queries)
    return pl.pallas_call(
        functools.partial(attend_first_kernel, len(queries)),
        out_specs=[VMEM_SPEC] * 3,
        out_shape=[pltpu.VMEM((count, half), jnp.float32)] * 3,
        cost_estimate=pl.CostEstimate(flops=0, bytes_accessed=0, transcendentals=0),
        compiler_params=pltpu.CompilerParams(vmem_limit_bytes=24 << 20),
        name="attend_first",
    )(*queries, *kv_parts)


def attend_last_kernel(pieces, after_ref, sum_ref, max_ref, total_ref, *refs):
    *refs, token_ref = refs
    token_ref[...] = jnp.zeros_like(token_ref)
    query_refs, kv_refs, out_refs = refs[:pieces], refs[pieces:-pieces], refs[-pieces:]
    cores, group, half = query_refs[0].shape
    rows = cores * group
    for at in range(0, pieces, 4):
        stop = min(at + 4, pieces)
        queries = stacked(query_refs[at:stop])
        mine = slice(at * rows, stop * rows)
        lane = lax.broadcasted_iota(jnp.int32, (queries.shape[0], DH), 1)
        stats = jnp.zeros((queries.shape[0], DH), jnp.float32)
        for head in range(half // DH):
            cols = slice(head * DH, (head + 1) * DH)
            scores, values = head_scores(queries, kv_refs, head)
            earlier = max_ref[mine, cols]
            maxima = along_lanes(jnp.max(scores, axis=-1, keepdims=True))
            maxima = jnp.maximum(earlier, maxima)
            weights = jnp.concatenate(weights_of(scores, maxima), axis=1)
            factor = jnp.exp(earlier - maxima)
            total = along_lanes(jnp.sum(weights, axis=-1, keepdims=True))
            total = total_ref[mine, cols] * factor + total
            weighted = sum_ref[mine, cols] * factor + jnp.dot(
                weights.astype(jnp.bfloat16), values, preferred_element_type=jnp.float32
            )
            stats = jnp.where(lane == 2 * head, maxima, stats)
            stats = jnp.where(lane == 2 * head + 1, total, stats)
            for j in range(at, stop):
                out_refs[j][:rows, cols] = weighted[(j - at) * rows : (j - at + 1) * rows]
        for j in range(at, stop):
            own = stats[(j - at) * rows : (j - at + 1) * rows]
            out_refs[j][rows:, DH:] = jnp.zeros((8, half - DH), jnp.float32)
            out_refs[j][rows:, :DH] = lanes_of(own)


def attend_last(after, first, queries, kv_parts):
    cores, group, half = queries[0].shape
    rows = cores * group
    return pl.pallas_call(
        functools.partial(attend_last_kernel, len(queries)),
        out_specs=[VMEM_SPEC] * (len(queries) + 1),
        out_shape=[pltpu.VMEM((rows + 8, half), jnp.float32)] * len(queries) + [TOKEN],
        compiler_params=pltpu.CompilerParams(vmem_limit_bytes=24 << 20),
        name="attend_last",
    )(after, *first, *queries, *kv_parts)


def column(stats, at):
    lane = lax.broadcasted_iota(jnp.int32, stats.shape, 1)
    return along_lanes(jnp.sum(jnp.where(lane == at, stats, 0.0), axis=-1, keepdims=True))


def combine_kernel(pieces, after_ref, *refs):
    part_refs, out_refs = refs[:pieces], refs[pieces:]
    group, half = out_refs[0].shape
    rows = group * len(out_refs)
    stats = [rows_of(ref[rows:, :DH], rows) for ref in part_refs]
    for head in range(half // DH):
        cols = slice(head * DH, (head + 1) * DH)
        maxima = [column(stat, 2 * head) for stat in stats]
        top = functools.reduce(jnp.maximum, maxima)
        total = jnp.zeros_like(top)
        attended = jnp.zeros((rows, DH), jnp.float32)
        for ref, stat, maximum in zip(part_refs, stats, maxima):
            factor = jnp.exp(maximum - top)
            total = total + column(stat, 2 * head + 1) * factor
            attended = attended + ref[:rows, cols] * factor
        attended = attended / total
        for side, out_ref in enumerate(out_refs):
            out_ref[:, cols] = attended[side * group : (side + 1) * group].astype(jnp.bfloat16)


def combine(after, parts, group, pair):
    half = parts[0].shape[1]
    return pl.pallas_call(
        functools.partial(combine_kernel, len(parts)),
        out_shape=[jax.ShapeDtypeStruct((group, half), jnp.bfloat16)] * pair,
        compiler_params=pltpu.CompilerParams(vmem_limit_bytes=16 << 20),
        name="combine",
    )(after, *parts)


def output_kernel(sides, spread_ref, *refs):
    side_refs, w_ref, (*out_refs, token_ref) = refs[:sides], refs[sides], refs[sides + 1 :]
    token_ref[...] = jnp.zeros_like(token_ref)
    group, half = side_refs[0].shape
    slots, width = out_refs[0].shape
    spread = spread_ref[:, :group]
    attended = [
        jnp.dot(spread, ref[...], preferred_element_type=jnp.float32).astype(jnp.bfloat16)
        for ref in side_refs
    ]
    core = my_core(sides)
    starts = [pl.multiple_of((core ^ side) * half, DH) for side in range(sides)]
    step = math.gcd(width, 1024)
    for col in range(0, width, step):
        terms = jnp.zeros((spread.shape[0], step), jnp.float32)
        for start, side in zip(starts, attended):
            terms = terms + jnp.dot(
                side, w_ref[pl.ds(start, half), col : col + step], preferred_element_type=jnp.float32
            )
        for k, out_ref in enumerate(out_refs):
            piece = terms[k * slots : (k + 1) * slots]
            out_ref[:, col : col + step] = piece.astype(out_ref.dtype)


def output(spread, sides, w_out, slots, parts):
    width = w_out.shape[1]
    return pl.pallas_call(
        functools.partial(output_kernel, len(sides)),
        out_shape=[
            jax.ShapeDtypeStruct((slots, width), jnp.bfloat16 if k else jnp.float32)
            for k in range(parts)
        ]
        + [TOKEN],
        compiler_params=pltpu.CompilerParams(vmem_limit_bytes=16 << 20),
        name="output",
    )(spread, *sides, w_out)


def mlp_kernel(pieces, *refs):
    row_refs, (up_ref, down_ref) = refs[:pieces], refs[pieces : pieces + 2]
    *out_refs, act_ref = refs[pieces + 2 :]
    hidden, width = down_ref.shape
    rows = [ref[j] for ref in row_refs for j in range(ref.shape[0])]
    rows = jnp.concatenate(rows, axis=0)
    count = out_refs[0].shape[0]
    step = math.gcd(hidden, 512)
    for col in range(0, hidden, step):
        lifted = jnp.dot(rows, up_ref[:, col : col + step], preferred_element_type=jnp.float32)
        act_ref[:, col : col + step] = jax.nn.gelu(lifted, approximate=True).astype(jnp.bfloat16)
    step = math.gcd(width, 512)
    for col in range(0, width, step):
        down = jnp.dot(
            act_ref[...], down_ref[:, col : col + step], preferred_element_type=jnp.float32
        )
        for side, out_ref in enumerate(out_refs):
            piece = down[side * count : (side + 1) * count]
            out_ref[:, col : col + step] = piece.astype(out_ref.dtype)


def mlp(rows, w_up, w_down, pair):
    count = sum(x.shape[0] * x.shape[1] for x in rows)
    hidden, width = w_down.shape
    return pl.pallas_call(
        functools.partial(mlp_kernel, len(rows)),
        out_shape=[
            jax.ShapeDtypeStruct((count // pair, width), jnp.bfloat16 if side else jnp.float32)
            for side in range(pair)
        ],
        scratch_shapes=[pltpu.VMEM((count, hidden), jnp.bfloat16)],
        compiler_params=pltpu.CompilerParams(vmem_limit_bytes=32 << 20),
        name="mlp",
    )(*rows, w_up, w_down)


def join_kernel(count, *refs):
    part_refs, out_ref = refs[:count], refs[-1]
    for at, ref in enumerate(part_refs):
        out_ref[at] = ref[...]


def join(parts, after=()):
    return pl.pallas_call(
        functools.partial(join_kernel, len(parts)),
        out_shape=jax.ShapeDtypeStruct((len(parts), *parts[0].shape), parts[0].dtype),
        compiler_params=pltpu.CompilerParams(vmem_limit_bytes=8 << 20),
        name="join",
    )(*parts, *after)


def renorm_kernel(hold_ref, rows_ref, mod_ref, *refs):
    *term_refs, after_ref, normed_ref = refs
    branch = term_refs[0][...]
    for ref in term_refs[1:]:
        branch = branch + ref[...].astype(jnp.float32)
    after = rows_ref[...] + mod_ref[2:3, :] * branch
    after_ref[...] = after
    normed_ref[...] = layer_norm(after, mod_ref[3:4, :], mod_ref[4:5, :]).astype(jnp.bfloat16)


def renorm(after, rows_in, modulation, terms):
    return pl.pallas_call(
        renorm_kernel,
        out_shape=[
            jax.ShapeDtypeStruct(rows_in.shape, jnp.float32),
            jax.ShapeDtypeStruct(rows_in.shape, jnp.bfloat16),
        ],
        compiler_params=pltpu.CompilerParams(vmem_limit_bytes=8 << 20),
        name="renorm",
    )(after, rows_in, modulation, *terms)


def fold_kernel(sides, *refs):
    side_refs, out_refs = refs[:sides], refs[sides:]
    slots = out_refs[0].shape[0]
    for j, out_ref in enumerate(out_refs):
        total = side_refs[0][j * slots : (j + 1) * slots]
        for ref in side_refs[1:]:
            total = total + ref[j * slots : (j + 1) * slots].astype(jnp.float32)
        out_ref[...] = total.astype(out_ref.dtype)


def fold(sides, slots):
    count, width = sides[0].shape
    return pl.pallas_call(
        functools.partial(fold_kernel, len(sides)),
        out_shape=[
            jax.ShapeDtypeStruct((slots, width), jnp.bfloat16 if j else jnp.float32)
            for j in range(count // slots)
        ],
        compiler_params=pltpu.CompilerParams(vmem_limit_bytes=8 << 20),
        name="fold",
    )(*sides)


def finish_kernel(select_ref, cached_ref, after_ref, mod_ref, *refs):
    *term_refs, out_ref = refs
    total = term_refs[0][...]
    for ref in term_refs[1:]:
        total = total + ref[...].astype(jnp.float32)
    renewed = (after_ref[...] + mod_ref[5:6, :] * total).astype(jnp.bfloat16)
    select = select_ref[...]
    placed = jnp.dot(select, renewed, preferred_element_type=jnp.float32)
    covered = jnp.sum(select.astype(jnp.float32), axis=1, keepdims=True)
    blended = cached_ref[...].astype(jnp.float32) * (1.0 - covered) + placed
    out_ref[...] = blended.astype(jnp.bfloat16)


def finish(select, cached, after_attn, modulation, terms):
    return pl.pallas_call(
        finish_kernel,
        out_shape=jax.ShapeDtypeStruct(cached.shape, jnp.bfloat16),
        compiler_params=pltpu.CompilerParams(vmem_limit_bytes=8 << 20),
        name="finish",
    )(select, cached, after_attn, modulation, *terms)


def body(
    hidden_in,
    cached_out,
    cache_keys,
    cache_values,
    refresh_idx,
    modulation,
    q_gain,
    w_query,
    w_out,
    w_up,
    w_down,
):
    slots = refresh_idx.shape[0]
    uly_size = lax.axis_size("uly")
    blk_size = lax.axis_size("blk")
    local_heads = w_query.shape[1] // DH
    group = min(slots * uly_size, slots + (uly_size - 1) * OTHER)
    pair = 2 if blk_size % 2 == 0 and local_heads % 2 == 0 else 1
    chips = blk_size // pair

    rows_in, normed, select, modulation, sides = enter(
        refresh_idx, hidden_in, modulation, cache_keys, cache_values, uly_size, pair
    )
    sides = [trade(x, "blk", side) for side, x in enumerate(sides)]
    w_query, token = hold(normed, w_query)
    half_way = uly_size // 2
    cuts = [[half_way, 0], [k for k in reversed(range(uly_size)) if k not in (0, half_way)]]
    first, token = merge_kv(sides, cuts[0], [token])
    group_rows = double(normed, "uly", 1, uly_size, {half_way: lambda x: relay(x, token)})
    second, token = merge_kv(sides, cuts[1], group_rows[1:])
    kv_parts = [trade(x, "uly", k) for k, x in zip(cuts[0] + cuts[1], first + second)]

    queries, spread, token = project(token, group_rows, w_query, q_gain, group, pair)
    w_out, token = hold(token, w_out)
    queries = join([trade(x, "blk", side) for side, x in enumerate(queries)])
    queries = double(queries, "blk", pair, chips)
    first = attend_first(queries, kv_parts[:2])
    *parts, token = attend_last(token, first, queries, kv_parts[2:])
    w_up, token = hold(token, w_up)
    parts = far_first([trade(x, "blk", j * pair) for j, x in enumerate(parts)])
    attended = combine(token, parts, group, pair)
    attended = [trade(x, "blk", side) for side, x in enumerate(attended)]
    *terms, token = output(spread, attended, w_out, slots, uly_size)
    w_down, cached, token = hold(token, w_down, cached_out)
    terms = far_first([trade(x, "uly", k) for k, x in enumerate(terms)])
    after_attn, norm_mlp = renorm(token, rows_in, modulation, terms)

    rows = [join([trade(norm_mlp, "blk", j * pair) for j in range(chips)])]
    if pair == 2:
        rows.append(trade(rows[0], "blk", 1))
    down = mlp(rows, w_up, w_down, pair)
    down = [trade(x, "blk", side) for side, x in enumerate(down)]
    terms = far_first([trade(x, "blk", j * pair) for j, x in enumerate(fold(down, slots))])
    return finish(select, cached, after_attn, modulation, terms)


def solution(mesh):
    return jax.shard_map(
        body,
        mesh=mesh,
        in_specs=(
            P(("blk", "uly"), None),
            P(("blk", "uly"), None),
            P(("blk", "uly"), None),
            P(("blk", "uly"), None),
            P(("blk", "uly")),
            P(),
            P(),
            P(None, "uly"),
            P("uly", None),
            P(None, "blk"),
            P("blk", None),
        ),
        out_specs=P(("blk", "uly"), None),
        check_vma=False,
    )
```

```python
import functools
import math

import jax
import jax.numpy as jnp
from jax import lax
from jax.experimental import pallas as pl
from jax.experimental.pallas import tpu as pltpu
from jax.sharding import PartitionSpec as P

DH = 128
OTHER = 8
VMEM_SPEC = pl.BlockSpec(memory_space=pltpu.VMEM)
TOKEN = pltpu.VMEM((8, DH), jnp.float32)
ANY_SPEC = pl.BlockSpec(memory_space=pl.ANY)


def far_first(parts):
    return parts[:1] + parts[:0:-1]


def double(x, axis, scale, count, on_arrival=()):
    have = {0: x}
    for k in sorted(range(1, count), key=lambda k: (bin(k).count("1"), -k)):
        low = k & -k
        have[k] = trade(have[k ^ low], axis, low * scale)
        if k in on_arrival:
            have[k] = on_arrival[k](have[k])
    return [have[k] for k in range(count)]


def layer_norm(row_block, shift_by, scale_by):
    average = jnp.mean(row_block, axis=-1, keepdims=True)
    centred = row_block - average
    spread = jnp.mean(centred * centred, axis=-1, keepdims=True)
    return centred * lax.rsqrt(spread + 1e-06) * (1.0 + scale_by) + shift_by


def trade(x, axis, flip):
    if flip == 0:
        return x
    return lax.ppermute(x, axis, [(i, i ^ flip) for i in range(lax.axis_size(axis))])


def in_hbm(x):
    return pltpu.with_memory_space_constraint(x, pltpu.HBM)


def hold_kernel(count, *refs):
    source_refs, sems = refs[1 : count + 1], refs[-1]
    *held_refs, token_ref = refs[count + 1 : -1]
    token_ref[...] = jnp.zeros_like(token_ref)
    copies = [
        pltpu.make_async_copy(source_ref, held_ref, sems.at[i])
        for i, (source_ref, held_ref) in enumerate(zip(source_refs, held_refs))
    ]
    for copy in copies:
        copy.start()
    for copy in copies:
        copy.wait()


def hold(after, *weights):
    count = len(weights)
    moved = sum(w.size * w.dtype.itemsize for w in weights)
    return pl.pallas_call(
        functools.partial(hold_kernel, count),
        in_specs=[VMEM_SPEC] + [ANY_SPEC] * count,
        out_specs=[VMEM_SPEC] * (count + 1),
        out_shape=[pltpu.VMEM(w.shape, w.dtype) for w in weights] + [TOKEN],
        scratch_shapes=[pltpu.SemaphoreType.DMA((count,))],
        cost_estimate=pl.CostEstimate(flops=0, bytes_accessed=moved, transcendentals=0),
        compiler_params=pltpu.CompilerParams(vmem_limit_bytes=2 << 20),
        name="hold",
    )(after, *[in_hbm(w) for w in weights])


def my_core(pair):
    return lax.rem(lax.axis_index("blk"), pair)


def enter_kernel(pair, idx_hbm, hidden_hbm, mod_hbm, key_hbm, value_hbm, *refs):
    rows_ref, normed_ref, select_ref, mod_ref, *side_refs = refs[: pair + 4]
    idx_ref, hidden_ref, sems, kv_sem = refs[pair + 4 :]
    copies = [
        pltpu.make_async_copy(source, target, sems.at[i])
        for i, (source, target) in enumerate(
            [(idx_hbm, idx_ref), (hidden_hbm, hidden_ref), (mod_hbm, mod_ref)]
        )
    ]
    for copy in copies:
        copy.start()
    parts, _, both = side_refs[0].shape
    half = both // 2
    uly, core = lax.axis_index("uly"), my_core(pair)
    kv_copies = []
    for side, side_ref in enumerate(side_refs):
        for flip in range(parts):
            start = pl.multiple_of(((uly ^ flip) * pair + (core ^ side)) * half, DH)
            for at, source in enumerate((key_hbm, value_hbm)):
                copy = pltpu.make_async_copy(
                    source.at[:, pl.ds(start, half)],
                    side_ref.at[flip, :, pl.ds(at * half, half)],
                    kv_sem.at[side, flip, at],
                )
                copy.start()
                kv_copies.append(copy)
    for copy in copies:
        copy.wait()
    tokens, width = hidden_ref.shape
    slots = idx_ref.shape[1]
    position = lax.broadcasted_iota(jnp.int32, (tokens, slots), 0)
    select = (position == idx_ref[...]).astype(jnp.float32).astype(jnp.bfloat16)
    select_ref[...] = select
    contract = (((0,), (0,)), ((), ()))
    rows = lax.dot_general(
        select, hidden_ref[...], contract, preferred_element_type=jnp.float32
    )
    live = lax.dot_general(
        select,
        jnp.ones((tokens, DH), jnp.bfloat16),
        contract,
        preferred_element_type=jnp.float32,
    )
    rows_ref[...] = rows
    normed = layer_norm(rows, mod_ref[0:1, :], mod_ref[1:2, :])
    normed_ref[:, :width] = normed.astype(jnp.bfloat16)
    normed_ref[:, width:] = live.astype(jnp.bfloat16)
    for copy in kv_copies:
        copy.wait()


def enter(refresh_idx, hidden_in, modulation, cache_keys, cache_values, parts, pair):
    slots = refresh_idx.shape[0]
    tokens, width = hidden_in.shape
    both = 2 * width // (parts * pair)
    out = pl.pallas_call(
        functools.partial(enter_kernel, pair),
        in_specs=[ANY_SPEC] * 5,
        out_specs=[VMEM_SPEC] * (pair + 4),
        out_shape=[
            pltpu.VMEM((slots, width), jnp.float32),
            pltpu.VMEM((slots, width + DH), jnp.bfloat16),
            pltpu.VMEM((tokens, slots), jnp.bfloat16),
            pltpu.VMEM(modulation.shape, modulation.dtype),
        ]
        + [pltpu.VMEM((parts, tokens, both), cache_keys.dtype)] * pair,
        scratch_shapes=[
            pltpu.VMEM((1, slots), jnp.int32),
            pltpu.VMEM(hidden_in.shape, hidden_in.dtype),
            pltpu.SemaphoreType.DMA((3,)),
            pltpu.SemaphoreType.DMA((pair, parts, 2)),
        ],
        compiler_params=pltpu.CompilerParams(vmem_limit_bytes=8 << 20),
        name="enter",
    )(
        *[
            in_hbm(x)
            for x in (refresh_idx.reshape(1, slots), hidden_in, modulation, cache_keys, cache_values)
        ]
    )
    return *out[:4], out[4:]


def merge_kv_kernel(sides, flips, *refs):
    *refs, token_ref = refs
    token_ref[...] = jnp.zeros_like(token_ref)
    for flip, out_ref in zip(flips, refs[-len(flips) :]):
        for side in range(sides):
            out_ref[side] = refs[side][flip]


def merge_kv(sides, flips, after):
    _, tokens, both = sides[0].shape
    *merged, token = pl.pallas_call(
        functools.partial(merge_kv_kernel, len(sides), flips),
        out_specs=[VMEM_SPEC] * (len(flips) + 1),
        out_shape=[pltpu.VMEM((len(sides), tokens, both), sides[0].dtype) for _ in flips]
        + [TOKEN],
        compiler_params=pltpu.CompilerParams(vmem_limit_bytes=8 << 20),
        name="merge_kv",
    )(*sides, *after)
    return merged, token


def relay_kernel(x_ref, after_ref, out_ref):
    out_ref[...] = x_ref[...]


def relay(x, after):
    return pl.pallas_call(
        relay_kernel,
        out_specs=VMEM_SPEC,
        out_shape=pltpu.VMEM(x.shape, x.dtype),
        compiler_params=pltpu.CompilerParams(vmem_limit_bytes=2 << 20),
        name="relay",
    )(x, after)


def project_kernel(pieces, after_ref, *refs):
    rows_refs, (w_ref, gain_hbm_ref) = refs[:pieces], refs[pieces : pieces + 2]
    *query_refs, spread_ref, token_ref, heads_ref, gain_ref, sem = refs[pieces + 2 :]
    token_ref[...] = jnp.zeros_like(token_ref)
    copy = pltpu.make_async_copy(gain_hbm_ref, gain_ref, sem)
    copy.start()
    core = my_core(len(query_refs))
    width = w_ref.shape[0]
    group, half = query_refs[0].shape
    rows = jnp.concatenate([ref[...] for ref in rows_refs], axis=0)
    everyone = rows.shape[0]
    flags = rows[:, width:]
    shape = (everyone, everyone)
    before = lax.broadcasted_iota(jnp.int32, shape, 1) < lax.broadcasted_iota(jnp.int32, shape, 0)
    before = before.astype(jnp.float32).astype(jnp.bfloat16)
    rank = jnp.dot(before, flags, preferred_element_type=jnp.float32)
    lane = lax.broadcasted_iota(jnp.int32, rank.shape, 1).astype(jnp.float32)
    spread = jnp.where((rank == lane) & (flags.astype(jnp.float32) > 0.0), 1.0, 0.0)
    spread = spread.astype(jnp.bfloat16)
    spread_ref[...] = spread
    projected = jnp.dot(rows[:, :width], w_ref[...], preferred_element_type=jnp.float32)
    copy.wait()
    for start in range(0, projected.shape[1], DH):
        head = projected[:, start : start + DH]
        squares = jnp.mean(head * head, axis=-1, keepdims=True)
        head = head * lax.rsqrt(squares + 1e-06) * (gain_ref[...] / math.sqrt(DH))
        heads_ref[:, start : start + DH] = head.astype(jnp.bfloat16)
    for side, query_ref in enumerate(query_refs):
        start = pl.multiple_of((core ^ side) * half, DH)
        query_ref[...] = lax.dot_general(
            spread[:, :group],
            heads_ref[:, pl.ds(start, half)],
            (((0,), (0,)), ((), ())),
            preferred_element_type=jnp.float32,
        ).astype(jnp.bfloat16)


def project(after, rows, w_query, q_gain, group, pair):
    half = w_query.shape[1] // pair
    everyone = len(rows) * rows[0].shape[0]
    query = jax.ShapeDtypeStruct((group, half), jnp.bfloat16)
    out = pl.pallas_call(
        functools.partial(project_kernel, len(rows)),
        in_specs=[VMEM_SPEC] * (len(rows) + 2) + [ANY_SPEC],
        out_shape=[query] * pair + [jax.ShapeDtypeStruct((everyone, DH), jnp.bfloat16), TOKEN],
        scratch_shapes=[
            pltpu.VMEM((everyone, w_query.shape[1]), jnp.bfloat16),
            pltpu.VMEM((1, DH), jnp.float32),
            pltpu.SemaphoreType.DMA,
        ],
        compiler_params=pltpu.CompilerParams(vmem_limit_bytes=16 << 20),
        name="project",
    )(after, *rows, w_query, in_hbm(q_gain.reshape(1, DH)))
    return out[:-2], out[-2], out[-1]


def head_scores(queries, kv_refs, head):
    half = queries.shape[1]
    cols = slice(head * DH, (head + 1) * DH)
    vals = slice(half + head * DH, half + (head + 1) * DH)
    sides = kv_refs[0].shape[0]
    keys = [ref[side, :, cols] for ref in kv_refs for side in range(sides)]
    values = [ref[side, :, vals] for ref in kv_refs for side in range(sides)]
    scores = lax.dot_general(
        queries[:, cols],
        jnp.concatenate(keys, axis=0),
        (((1,), (1,)), ((), ())),
        preferred_element_type=jnp.float32,
    )
    return scores, jnp.concatenate(values, axis=0)


def lanes_of(stats):
    packed = stats[:8]
    for at in range(8, stats.shape[0], 8):
        packed = packed + pltpu.roll(stats[at : at + 8], at, axis=1)
    return packed


def rows_of(packed, rows):
    parts = [packed] + [pltpu.roll(packed, DH - at, axis=1) for at in range(8, rows, 8)]
    return jnp.concatenate(parts, axis=0)


def stacked(refs):
    rows = [ref[core].astype(jnp.float32) for ref in refs for core in range(ref.shape[0])]
    return jnp.concatenate(rows, axis=0).astype(jnp.bfloat16)


def along_lanes(column):
    return jnp.broadcast_to(column, (column.shape[0], DH))


def weights_of(scores, maxima):
    width = scores.shape[1]
    return [jnp.exp(scores[:, at : at + DH] - maxima) for at in range(0, width, DH)]


def attend_first_kernel(pieces, *refs):
    query_refs, (*kv_refs, sum_ref, max_ref, total_ref) = refs[:pieces], refs[pieces:]
    cores, group, half = query_refs[0].shape
    rows = cores * group
    for at in range(0, pieces, 4):
        queries = stacked(query_refs[at : at + 4])
        mine = slice(at * rows, at * rows + queries.shape[0])
        for head in range(half // DH):
            cols = slice(head * DH, (head + 1) * DH)
            scores, values = head_scores(queries, kv_refs, head)
            maxima = along_lanes(jnp.max(scores, axis=-1, keepdims=True))
            weights = jnp.concatenate(weights_of(scores, maxima), axis=1)
            max_ref[mine, cols] = maxima
            total_ref[mine, cols] = along_lanes(jnp.sum(weights, axis=-1, keepdims=True))
            sum_ref[mine, cols] = jnp.dot(
                weights.astype(jnp.bfloat16), values, preferred_element_type=jnp.float32
            )


def attend_first(queries, kv_parts):
    cores, group, half = queries[0].shape
    count = cores * group * len(queries)
    return pl.pallas_call(
        functools.partial(attend_first_kernel, len(queries)),
        out_specs=[VMEM_SPEC] * 3,
        out_shape=[pltpu.VMEM((count, half), jnp.float32)] * 3,
        cost_estimate=pl.CostEstimate(flops=0, bytes_accessed=0, transcendentals=0),
        compiler_params=pltpu.CompilerParams(vmem_limit_bytes=24 << 20),
        name="attend_first",
    )(*queries, *kv_parts)


def attend_last_kernel(pieces, after_ref, sum_ref, max_ref, total_ref, *refs):
    *refs, token_ref = refs
    token_ref[...] = jnp.zeros_like(token_ref)
    query_refs, kv_refs, out_refs = refs[:pieces], refs[pieces:-pieces], refs[-pieces:]
    cores, group, half = query_refs[0].shape
    rows = cores * group
    for at in range(0, pieces, 4):
        stop = min(at + 4, pieces)
        queries = stacked(query_refs[at:stop])
        mine = slice(at * rows, stop * rows)
        lane = lax.broadcasted_iota(jnp.int32, (queries.shape[0], DH), 1)
        stats = jnp.zeros((queries.shape[0], DH), jnp.float32)
        for head in range(half // DH):
            cols = slice(head * DH, (head + 1) * DH)
            scores, values = head_scores(queries, kv_refs, head)
            earlier = max_ref[mine, cols]
            maxima = along_lanes(jnp.max(scores, axis=-1, keepdims=True))
            maxima = jnp.maximum(earlier, maxima)
            weights = jnp.concatenate(weights_of(scores, maxima), axis=1)
            factor = jnp.exp(earlier - maxima)
            total = along_lanes(jnp.sum(weights, axis=-1, keepdims=True))
            total = total_ref[mine, cols] * factor + total
            weighted = sum_ref[mine, cols] * factor + jnp.dot(
                weights.astype(jnp.bfloat16), values, preferred_element_type=jnp.float32
            )
            stats = jnp.where(lane == 2 * head, maxima, stats)
            stats = jnp.where(lane == 2 * head + 1, total, stats)
            for j in range(at, stop):
                out_refs[j][:rows, cols] = weighted[(j - at) * rows : (j - at + 1) * rows]
        for j in range(at, stop):
            own = stats[(j - at) * rows : (j - at + 1) * rows]
            out_refs[j][rows:, DH:] = jnp.zeros((8, half - DH), jnp.float32)
            out_refs[j][rows:, :DH] = lanes_of(own)


def attend_last(after, first, queries, kv_parts):
    cores, group, half = queries[0].shape
    rows = cores * group
    return pl.pallas_call(
        functools.partial(attend_last_kernel, len(queries)),
        out_specs=[VMEM_SPEC] * (len(queries) + 1),
        out_shape=[pltpu.VMEM((rows + 8, half), jnp.float32)] * len(queries) + [TOKEN],
        compiler_params=pltpu.CompilerParams(vmem_limit_bytes=24 << 20),
        name="attend_last",
    )(after, *first, *queries, *kv_parts)


def column(stats, at):
    lane = lax.broadcasted_iota(jnp.int32, stats.shape, 1)
    return along_lanes(jnp.sum(jnp.where(lane == at, stats, 0.0), axis=-1, keepdims=True))


def combine_kernel(pieces, after_ref, *refs):
    part_refs, out_refs = refs[:pieces], refs[pieces:]
    group, half = out_refs[0].shape
    rows = group * len(out_refs)
    stats = [rows_of(ref[rows:, :DH], rows) for ref in part_refs]
    for head in range(half // DH):
        cols = slice(head * DH, (head + 1) * DH)
        maxima = [column(stat, 2 * head) for stat in stats]
        top = functools.reduce(jnp.maximum, maxima)
        total = jnp.zeros_like(top)
        attended = jnp.zeros((rows, DH), jnp.float32)
        for ref, stat, maximum in zip(part_refs, stats, maxima):
            factor = jnp.exp(maximum - top)
            total = total + column(stat, 2 * head + 1) * factor
            attended = attended + ref[:rows, cols] * factor
        attended = attended / total
        for side, out_ref in enumerate(out_refs):
            out_ref[:, cols] = attended[side * group : (side + 1) * group].astype(jnp.bfloat16)


def combine(after, parts, group, pair):
    half = parts[0].shape[1]
    return pl.pallas_call(
        functools.partial(combine_kernel, len(parts)),
        out_shape=[jax.ShapeDtypeStruct((group, half), jnp.bfloat16)] * pair,
        compiler_params=pltpu.CompilerParams(vmem_limit_bytes=16 << 20),
        name="combine",
    )(after, *parts)


def output_terms(side, pair, spread_ref, attended_ref, w_ref):
    group, half = attended_ref.shape
    width = w_ref.shape[1]
    attended = jnp.dot(
        spread_ref[:, :group], attended_ref[...], preferred_element_type=jnp.float32
    ).astype(jnp.bfloat16)
    start = pl.multiple_of((my_core(pair) ^ side) * half, DH)
    step = math.gcd(width, 1024)
    for col in range(0, width, step):
        cols = slice(col, col + step)
        yield cols, jnp.dot(
            attended, w_ref[pl.ds(start, half), cols], preferred_element_type=jnp.float32
        )


def output_first_kernel(pair, spread_ref, attended_ref, w_ref, out_ref):
    for cols, terms in output_terms(0, pair, spread_ref, attended_ref, w_ref):
        out_ref[:, cols] = terms


def output_first(spread, attended, w_out, pair):
    return pl.pallas_call(
        functools.partial(output_first_kernel, pair),
        out_specs=VMEM_SPEC,
        out_shape=pltpu.VMEM((spread.shape[0], w_out.shape[1]), jnp.float32),
        cost_estimate=pl.CostEstimate(flops=10**8, bytes_accessed=0, transcendentals=0),
        compiler_params=pltpu.CompilerParams(vmem_limit_bytes=16 << 20),
        name="output_first",
    )(spread, attended, w_out)


def output_last_kernel(pair, spread_ref, first_ref, *refs):
    *attended_refs, w_ref = refs[:pair]
    *out_refs, token_ref = refs[pair:]
    token_ref[...] = jnp.zeros_like(token_ref)
    slots = out_refs[0].shape[0]

    def write(cols, terms):
        for k, out_ref in enumerate(out_refs):
            out_ref[:, cols] = terms[k * slots : (k + 1) * slots].astype(out_ref.dtype)

    if not attended_refs:
        write(slice(None), first_ref[...])
    for attended_ref in attended_refs:
        for cols, terms in output_terms(1, pair, spread_ref, attended_ref, w_ref):
            write(cols, first_ref[:, cols] + terms)


def output_last(spread, first, others, w_out, slots, parts):
    width = w_out.shape[1]
    return pl.pallas_call(
        functools.partial(output_last_kernel, len(others) + 1),
        out_shape=[
            jax.ShapeDtypeStruct((slots, width), jnp.bfloat16 if k else jnp.float32)
            for k in range(parts)
        ]
        + [TOKEN],
        compiler_params=pltpu.CompilerParams(vmem_limit_bytes=16 << 20),
        name="output_last",
    )(spread, first, *others, w_out)


def mlp_kernel(pieces, *refs):
    row_refs, (up_ref, down_ref) = refs[:pieces], refs[pieces : pieces + 2]
    *out_refs, act_ref = refs[pieces + 2 :]
    hidden, width = down_ref.shape
    rows = [ref[j] for ref in row_refs for j in range(ref.shape[0])]
    rows = jnp.concatenate(rows, axis=0)
    count = out_refs[0].shape[0]
    step = math.gcd(hidden, 768)
    for col in range(0, hidden, step):
        lifted = jnp.dot(rows, up_ref[:, col : col + step], preferred_element_type=jnp.float32)
        act_ref[:, col : col + step] = jax.nn.gelu(lifted, approximate=True).astype(jnp.bfloat16)
    step = math.gcd(width, 1024)
    for col in range(0, width, step):
        down = jnp.dot(
            act_ref[...], down_ref[:, col : col + step], preferred_element_type=jnp.float32
        )
        for side, out_ref in enumerate(out_refs):
            piece = down[side * count : (side + 1) * count]
            out_ref[:, col : col + step] = piece.astype(out_ref.dtype)


def mlp(rows, w_up, w_down, pair):
    count = sum(x.shape[0] * x.shape[1] for x in rows)
    hidden, width = w_down.shape
    return pl.pallas_call(
        functools.partial(mlp_kernel, len(rows)),
        out_shape=[
            jax.ShapeDtypeStruct((count // pair, width), jnp.bfloat16 if side else jnp.float32)
            for side in range(pair)
        ],
        scratch_shapes=[pltpu.VMEM((count, hidden), jnp.bfloat16)],
        compiler_params=pltpu.CompilerParams(vmem_limit_bytes=32 << 20),
        name="mlp",
    )(*rows, w_up, w_down)


def join_kernel(count, *refs):
    part_refs, out_ref = refs[:count], refs[-1]
    for at, ref in enumerate(part_refs):
        out_ref[at] = ref[...]


def join(parts, after=()):
    return pl.pallas_call(
        functools.partial(join_kernel, len(parts)),
        out_shape=jax.ShapeDtypeStruct((len(parts), *parts[0].shape), parts[0].dtype),
        compiler_params=pltpu.CompilerParams(vmem_limit_bytes=8 << 20),
        name="join",
    )(*parts, *after)


def renorm_kernel(hold_ref, rows_ref, mod_ref, *refs):
    *term_refs, after_ref, normed_ref = refs
    branch = term_refs[0][...]
    for ref in term_refs[1:]:
        branch = branch + ref[...].astype(jnp.float32)
    after = rows_ref[...] + mod_ref[2:3, :] * branch
    after_ref[...] = after
    normed_ref[...] = layer_norm(after, mod_ref[3:4, :], mod_ref[4:5, :]).astype(jnp.bfloat16)


def renorm(after, rows_in, modulation, terms):
    return pl.pallas_call(
        renorm_kernel,
        out_shape=[
            jax.ShapeDtypeStruct(rows_in.shape, jnp.float32),
            jax.ShapeDtypeStruct(rows_in.shape, jnp.bfloat16),
        ],
        compiler_params=pltpu.CompilerParams(vmem_limit_bytes=8 << 20),
        name="renorm",
    )(after, rows_in, modulation, *terms)


def fold_kernel(sides, *refs):
    side_refs, out_refs = refs[:sides], refs[sides:]
    slots = out_refs[0].shape[0]
    for j, out_ref in enumerate(out_refs):
        total = side_refs[0][j * slots : (j + 1) * slots]
        for ref in side_refs[1:]:
            total = total + ref[j * slots : (j + 1) * slots].astype(jnp.float32)
        out_ref[...] = total.astype(out_ref.dtype)


def fold(sides, slots):
    count, width = sides[0].shape
    return pl.pallas_call(
        functools.partial(fold_kernel, len(sides)),
        out_shape=[
            jax.ShapeDtypeStruct((slots, width), jnp.bfloat16 if j else jnp.float32)
            for j in range(count // slots)
        ],
        compiler_params=pltpu.CompilerParams(vmem_limit_bytes=8 << 20),
        name="fold",
    )(*sides)


def finish_kernel(select_ref, cached_ref, after_ref, mod_ref, *refs):
    *term_refs, out_ref = refs
    total = term_refs[0][...]
    for ref in term_refs[1:]:
        total = total + ref[...].astype(jnp.float32)
    renewed = (after_ref[...] + mod_ref[5:6, :] * total).astype(jnp.bfloat16)
    select = select_ref[...]
    placed = jnp.dot(select, renewed, preferred_element_type=jnp.float32)
    covered = jnp.sum(select.astype(jnp.float32), axis=1, keepdims=True)
    blended = cached_ref[...].astype(jnp.float32) * (1.0 - covered) + placed
    out_ref[...] = blended.astype(jnp.bfloat16)


def finish(select, cached, after_attn, modulation, terms):
    return pl.pallas_call(
        finish_kernel,
        out_shape=jax.ShapeDtypeStruct(cached.shape, jnp.bfloat16),
        compiler_params=pltpu.CompilerParams(vmem_limit_bytes=8 << 20),
        name="finish",
    )(select, cached, after_attn, modulation, *terms)


def body(
    hidden_in,
    cached_out,
    cache_keys,
    cache_values,
    refresh_idx,
    modulation,
    q_gain,
    w_query,
    w_out,
    w_up,
    w_down,
):
    slots = refresh_idx.shape[0]
    uly_size = lax.axis_size("uly")
    blk_size = lax.axis_size("blk")
    local_heads = w_query.shape[1] // DH
    group = min(slots * uly_size, slots + (uly_size - 1) * OTHER)
    pair = 2 if blk_size % 2 == 0 and local_heads % 2 == 0 else 1
    chips = blk_size // pair

    rows_in, normed, select, modulation, sides = enter(
        refresh_idx, hidden_in, modulation, cache_keys, cache_values, uly_size, pair
    )
    sides = [trade(x, "blk", side) for side, x in enumerate(sides)]
    w_query, token = hold(normed, w_query)
    half_way = uly_size // 2
    cuts = [[half_way, 0], [k for k in reversed(range(uly_size)) if k not in (0, half_way)]]
    first, token = merge_kv(sides, cuts[0], [token])
    group_rows = double(normed, "uly", 1, uly_size, {half_way: lambda x: relay(x, token)})
    second, token = merge_kv(sides, cuts[1], group_rows[1:])
    kv_parts = [trade(x, "uly", k) for k, x in zip(cuts[0] + cuts[1], first + second)]

    queries, spread, token = project(token, group_rows, w_query, q_gain, group, pair)
    w_out, token = hold(token, w_out)
    queries = join([trade(x, "blk", side) for side, x in enumerate(queries)])
    queries = double(queries, "blk", pair, chips)
    first = attend_first(queries, kv_parts[:2])
    *parts, token = attend_last(token, first, queries, kv_parts[2:])
    w_up, token = hold(token, w_up)
    parts = far_first([trade(x, "blk", j * pair) for j, x in enumerate(parts)])
    attended = combine(token, parts, group, pair)
    mine, *others = attended
    others = [trade(x, "blk", 1) for x in others]
    terms = output_first(spread, mine, w_out, pair)
    *terms, token = output_last(spread, terms, others, w_out, slots, uly_size)
    w_down, cached, token = hold(token, w_down, cached_out)
    terms = far_first([trade(x, "uly", k) for k, x in enumerate(terms)])
    after_attn, norm_mlp = renorm(token, rows_in, modulation, terms)

    rows = [join([trade(norm_mlp, "blk", j * pair) for j in range(chips)])]
    if pair == 2:
        rows.append(trade(rows[0], "blk", 1))
    down = mlp(rows, w_up, w_down, pair)
    down = [trade(x, "blk", side) for side, x in enumerate(down)]
    terms = far_first([trade(x, "blk", j * pair) for j, x in enumerate(fold(down, slots))])
    return finish(select, cached, after_attn, modulation, terms)


def solution(mesh):
    return jax.shard_map(
        body,
        mesh=mesh,
        in_specs=(
            P(("blk", "uly"), None),
            P(("blk", "uly"), None),
            P(("blk", "uly"), None),
            P(("blk", "uly"), None),
            P(("blk", "uly")),
            P(),
            P(),
            P(None, "uly"),
            P("uly", None),
            P(None, "blk"),
            P("blk", None),
        ),
        out_specs=P(("blk", "uly"), None),
        check_vma=False,
    )
```

```python
import functools
import math

import jax
import jax.numpy as jnp
from jax import lax
from jax.experimental import pallas as pl
from jax.experimental.pallas import tpu as pltpu
from jax.sharding import PartitionSpec as P

DH = 128
OTHER = 8
VMEM_SPEC = pl.BlockSpec(memory_space=pltpu.VMEM)
TOKEN = pltpu.VMEM((8, DH), jnp.float32)
ANY_SPEC = pl.BlockSpec(memory_space=pl.ANY)


def far_first(parts):
    return parts[:1] + parts[:0:-1]


def double(x, axis, scale, count, on_arrival=()):
    have = {0: x}
    for k in sorted(range(1, count), key=lambda k: (bin(k).count("1"), -k)):
        low = k & -k
        have[k] = trade(have[k ^ low], axis, low * scale)
        if k in on_arrival:
            have[k] = on_arrival[k](have[k])
    return [have[k] for k in range(count)]


def layer_norm(row_block, shift_by, scale_by):
    average = jnp.mean(row_block, axis=-1, keepdims=True)
    centred = row_block - average
    spread = jnp.mean(centred * centred, axis=-1, keepdims=True)
    return centred * lax.rsqrt(spread + 1e-06) * (1.0 + scale_by) + shift_by


def trade(x, axis, flip):
    if flip == 0:
        return x
    return lax.ppermute(x, axis, [(i, i ^ flip) for i in range(lax.axis_size(axis))])


def in_hbm(x):
    return pltpu.with_memory_space_constraint(x, pltpu.HBM)


def hold_kernel(count, *refs):
    source_refs, sems = refs[1 : count + 1], refs[-1]
    *held_refs, token_ref = refs[count + 1 : -1]
    token_ref[...] = jnp.zeros_like(token_ref)
    copies = [
        pltpu.make_async_copy(source_ref, held_ref, sems.at[i])
        for i, (source_ref, held_ref) in enumerate(zip(source_refs, held_refs))
    ]
    for copy in copies:
        copy.start()
    for copy in copies:
        copy.wait()


def hold(after, *weights):
    count = len(weights)
    moved = sum(w.size * w.dtype.itemsize for w in weights)
    return pl.pallas_call(
        functools.partial(hold_kernel, count),
        in_specs=[VMEM_SPEC] + [ANY_SPEC] * count,
        out_specs=[VMEM_SPEC] * (count + 1),
        out_shape=[pltpu.VMEM(w.shape, w.dtype) for w in weights] + [TOKEN],
        scratch_shapes=[pltpu.SemaphoreType.DMA((count,))],
        cost_estimate=pl.CostEstimate(flops=0, bytes_accessed=moved, transcendentals=0),
        compiler_params=pltpu.CompilerParams(vmem_limit_bytes=2 << 20),
        name="hold",
    )(after, *[in_hbm(w) for w in weights])


def my_core(pair):
    return lax.rem(lax.axis_index("blk"), pair)


def enter_kernel(pair, idx_hbm, hidden_hbm, mod_hbm, key_hbm, value_hbm, *refs):
    rows_ref, normed_ref, select_ref, mod_ref, *side_refs = refs[: pair + 4]
    idx_ref, hidden_ref, sems, kv_sem = refs[pair + 4 :]
    copies = [
        pltpu.make_async_copy(source, target, sems.at[i])
        for i, (source, target) in enumerate(
            [(idx_hbm, idx_ref), (hidden_hbm, hidden_ref), (mod_hbm, mod_ref)]
        )
    ]
    for copy in copies:
        copy.start()
    parts, _, both = side_refs[0].shape
    half = both // 2
    uly, core = lax.axis_index("uly"), my_core(pair)
    kv_copies = []
    for side, side_ref in enumerate(side_refs):
        for flip in range(parts):
            start = pl.multiple_of(((uly ^ flip) * pair + (core ^ side)) * half, DH)
            for at, source in enumerate((key_hbm, value_hbm)):
                copy = pltpu.make_async_copy(
                    source.at[:, pl.ds(start, half)],
                    side_ref.at[flip, :, pl.ds(at * half, half)],
                    kv_sem.at[side, flip, at],
                )
                copy.start()
                kv_copies.append(copy)
    for copy in copies:
        copy.wait()
    tokens, width = hidden_ref.shape
    slots = idx_ref.shape[1]
    position = lax.broadcasted_iota(jnp.int32, (tokens, slots), 0)
    select = (position == idx_ref[...]).astype(jnp.float32).astype(jnp.bfloat16)
    select_ref[...] = select
    contract = (((0,), (0,)), ((), ()))
    rows = lax.dot_general(
        select, hidden_ref[...], contract, preferred_element_type=jnp.float32
    )
    live = lax.dot_general(
        select,
        jnp.ones((tokens, DH), jnp.bfloat16),
        contract,
        preferred_element_type=jnp.float32,
    )
    rows_ref[...] = rows
    normed = layer_norm(rows, mod_ref[0:1, :], mod_ref[1:2, :])
    normed_ref[:, :width] = normed.astype(jnp.bfloat16)
    normed_ref[:, width:] = live.astype(jnp.bfloat16)
    for copy in kv_copies:
        copy.wait()


def enter(refresh_idx, hidden_in, modulation, cache_keys, cache_values, parts, pair):
    slots = refresh_idx.shape[0]
    tokens, width = hidden_in.shape
    both = 2 * width // (parts * pair)
    out = pl.pallas_call(
        functools.partial(enter_kernel, pair),
        in_specs=[ANY_SPEC] * 5,
        out_specs=[VMEM_SPEC] * (pair + 4),
        out_shape=[
            pltpu.VMEM((slots, width), jnp.float32),
            pltpu.VMEM((slots, width + DH), jnp.bfloat16),
            pltpu.VMEM((tokens, slots), jnp.bfloat16),
            pltpu.VMEM(modulation.shape, modulation.dtype),
        ]
        + [pltpu.VMEM((parts, tokens, both), cache_keys.dtype)] * pair,
        scratch_shapes=[
            pltpu.VMEM((1, slots), jnp.int32),
            pltpu.VMEM(hidden_in.shape, hidden_in.dtype),
            pltpu.SemaphoreType.DMA((3,)),
            pltpu.SemaphoreType.DMA((pair, parts, 2)),
        ],
        compiler_params=pltpu.CompilerParams(vmem_limit_bytes=8 << 20),
        name="enter",
    )(
        *[
            in_hbm(x)
            for x in (refresh_idx.reshape(1, slots), hidden_in, modulation, cache_keys, cache_values)
        ]
    )
    return *out[:4], out[4:]


def merge_kv_kernel(sides, flips, *refs):
    *refs, token_ref = refs
    token_ref[...] = jnp.zeros_like(token_ref)
    for flip, out_ref in zip(flips, refs[-len(flips) :]):
        for side in range(sides):
            out_ref[side] = refs[side][flip]


def merge_kv(sides, flips, after):
    _, tokens, both = sides[0].shape
    *merged, token = pl.pallas_call(
        functools.partial(merge_kv_kernel, len(sides), flips),
        out_specs=[VMEM_SPEC] * (len(flips) + 1),
        out_shape=[pltpu.VMEM((len(sides), tokens, both), sides[0].dtype) for _ in flips]
        + [TOKEN],
        compiler_params=pltpu.CompilerParams(vmem_limit_bytes=8 << 20),
        name="merge_kv",
    )(*sides, *after)
    return merged, token


def relay_kernel(x_ref, after_ref, out_ref):
    out_ref[...] = x_ref[...]


def relay(x, after):
    return pl.pallas_call(
        relay_kernel,
        out_specs=VMEM_SPEC,
        out_shape=pltpu.VMEM(x.shape, x.dtype),
        compiler_params=pltpu.CompilerParams(vmem_limit_bytes=2 << 20),
        name="relay",
    )(x, after)


def project_kernel(pieces, after_ref, *refs):
    rows_refs, (w_ref, gain_hbm_ref) = refs[:pieces], refs[pieces : pieces + 2]
    *query_refs, spread_ref, token_ref, heads_ref, gain_ref, sem = refs[pieces + 2 :]
    token_ref[...] = jnp.zeros_like(token_ref)
    copy = pltpu.make_async_copy(gain_hbm_ref, gain_ref, sem)
    copy.start()
    core = my_core(len(query_refs))
    width = w_ref.shape[0]
    group, half = query_refs[0].shape
    rows = jnp.concatenate([ref[...] for ref in rows_refs], axis=0)
    everyone = rows.shape[0]
    flags = rows[:, width:]
    shape = (everyone, everyone)
    before = lax.broadcasted_iota(jnp.int32, shape, 1) < lax.broadcasted_iota(jnp.int32, shape, 0)
    before = before.astype(jnp.float32).astype(jnp.bfloat16)
    rank = jnp.dot(before, flags, preferred_element_type=jnp.float32)
    lane = lax.broadcasted_iota(jnp.int32, rank.shape, 1).astype(jnp.float32)
    spread = jnp.where((rank == lane) & (flags.astype(jnp.float32) > 0.0), 1.0, 0.0)
    spread = spread.astype(jnp.bfloat16)
    spread_ref[...] = spread
    live_rows = lax.dot_general(
        spread[:, :group],
        rows[:, :width],
        (((0,), (0,)), ((), ())),
        preferred_element_type=jnp.float32,
    ).astype(jnp.bfloat16)
    projected = jnp.dot(live_rows, w_ref[...], preferred_element_type=jnp.float32)
    copy.wait()
    for start in range(0, projected.shape[1], DH):
        head = projected[:, start : start + DH]
        squares = jnp.mean(head * head, axis=-1, keepdims=True)
        heads_ref[:, start : start + DH] = (
            head * lax.rsqrt(squares + 1e-06) * (gain_ref[...] / math.sqrt(DH))
        )
    for side, query_ref in enumerate(query_refs):
        start = pl.multiple_of((core ^ side) * half, DH)
        query_ref[...] = heads_ref[:, pl.ds(start, half)].astype(jnp.bfloat16)


def project(after, rows, w_query, q_gain, group, pair):
    half = w_query.shape[1] // pair
    everyone = len(rows) * rows[0].shape[0]
    query = jax.ShapeDtypeStruct((group, half), jnp.bfloat16)
    out = pl.pallas_call(
        functools.partial(project_kernel, len(rows)),
        in_specs=[VMEM_SPEC] * (len(rows) + 2) + [ANY_SPEC],
        out_shape=[query] * pair + [jax.ShapeDtypeStruct((everyone, DH), jnp.bfloat16), TOKEN],
        scratch_shapes=[
            pltpu.VMEM((group, w_query.shape[1]), jnp.float32),
            pltpu.VMEM((1, DH), jnp.float32),
            pltpu.SemaphoreType.DMA,
        ],
        compiler_params=pltpu.CompilerParams(vmem_limit_bytes=16 << 20),
        name="project",
    )(after, *rows, w_query, in_hbm(q_gain.reshape(1, DH)))
    return out[:-2], out[-2], out[-1]


def head_scores(queries, kv_refs, head):
    half = queries.shape[1]
    cols = slice(head * DH, (head + 1) * DH)
    vals = slice(half + head * DH, half + (head + 1) * DH)
    sides = kv_refs[0].shape[0]
    keys = [ref[side, :, cols] for ref in kv_refs for side in range(sides)]
    values = [ref[side, :, vals] for ref in kv_refs for side in range(sides)]
    scores = lax.dot_general(
        queries[:, cols],
        jnp.concatenate(keys, axis=0),
        (((1,), (1,)), ((), ())),
        preferred_element_type=jnp.float32,
    )
    return scores, jnp.concatenate(values, axis=0)


def lanes_of(stats):
    packed = stats[:8]
    for at in range(8, stats.shape[0], 8):
        packed = packed + pltpu.roll(stats[at : at + 8], at, axis=1)
    return packed


def rows_of(packed, rows):
    parts = [packed] + [pltpu.roll(packed, DH - at, axis=1) for at in range(8, rows, 8)]
    return jnp.concatenate(parts, axis=0)


def stacked(refs):
    rows = [ref[core].astype(jnp.float32) for ref in refs for core in range(ref.shape[0])]
    return jnp.concatenate(rows, axis=0).astype(jnp.bfloat16)


def along_lanes(column):
    return jnp.broadcast_to(column, (column.shape[0], DH))


def weights_of(scores, maxima):
    width = scores.shape[1]
    return [jnp.exp(scores[:, at : at + DH] - maxima) for at in range(0, width, DH)]


def attend_first_kernel(pieces, *refs):
    query_refs, (*kv_refs, sum_ref, max_ref, total_ref) = refs[:pieces], refs[pieces:]
    cores, group, half = query_refs[0].shape
    rows = cores * group
    for at in range(0, pieces, 4):
        queries = stacked(query_refs[at : at + 4])
        mine = slice(at * rows, at * rows + queries.shape[0])
        for head in range(half // DH):
            cols = slice(head * DH, (head + 1) * DH)
            scores, values = head_scores(queries, kv_refs, head)
            maxima = along_lanes(jnp.max(scores, axis=-1, keepdims=True))
            weights = jnp.concatenate(weights_of(scores, maxima), axis=1)
            max_ref[mine, cols] = maxima
            total_ref[mine, cols] = along_lanes(jnp.sum(weights, axis=-1, keepdims=True))
            sum_ref[mine, cols] = jnp.dot(
                weights.astype(jnp.bfloat16), values, preferred_element_type=jnp.float32
            )


def attend_first(queries, kv_parts):
    cores, group, half = queries[0].shape
    count = cores * group * len(queries)
    return pl.pallas_call(
        functools.partial(attend_first_kernel, len(queries)),
        out_specs=[VMEM_SPEC] * 3,
        out_shape=[pltpu.VMEM((count, half), jnp.float32)] * 3,
        cost_estimate=pl.CostEstimate(flops=0, bytes_accessed=0, transcendentals=0),
        compiler_params=pltpu.CompilerParams(vmem_limit_bytes=24 << 20),
        name="attend_first",
    )(*queries, *kv_parts)


def attend_last_kernel(pieces, after_ref, sum_ref, max_ref, total_ref, *refs):
    *refs, token_ref = refs
    token_ref[...] = jnp.zeros_like(token_ref)
    query_refs, kv_refs, out_refs = refs[:pieces], refs[pieces:-pieces], refs[-pieces:]
    cores, group, half = query_refs[0].shape
    rows = cores * group
    for at in range(0, pieces, 4):
        stop = min(at + 4, pieces)
        queries = stacked(query_refs[at:stop])
        mine = slice(at * rows, stop * rows)
        lane = lax.broadcasted_iota(jnp.int32, (queries.shape[0], DH), 1)
        stats = jnp.zeros((queries.shape[0], DH), jnp.float32)
        for head in range(half // DH):
            cols = slice(head * DH, (head + 1) * DH)
            scores, values = head_scores(queries, kv_refs, head)
            earlier = max_ref[mine, cols]
            maxima = along_lanes(jnp.max(scores, axis=-1, keepdims=True))
            maxima = jnp.maximum(earlier, maxima)
            weights = jnp.concatenate(weights_of(scores, maxima), axis=1)
            factor = jnp.exp(earlier - maxima)
            total = along_lanes(jnp.sum(weights, axis=-1, keepdims=True))
            total = total_ref[mine, cols] * factor + total
            weighted = sum_ref[mine, cols] * factor + jnp.dot(
                weights.astype(jnp.bfloat16), values, preferred_element_type=jnp.float32
            )
            stats = jnp.where(lane == 2 * head, maxima, stats)
            stats = jnp.where(lane == 2 * head + 1, total, stats)
            for j in range(at, stop):
                out_refs[j][:rows, cols] = weighted[(j - at) * rows : (j - at + 1) * rows]
        for j in range(at, stop):
            own = stats[(j - at) * rows : (j - at + 1) * rows]
            out_refs[j][rows:, DH:] = jnp.zeros((8, half - DH), jnp.float32)
            out_refs[j][rows:, :DH] = lanes_of(own)


def attend_last(after, first, queries, kv_parts):
    cores, group, half = queries[0].shape
    rows = cores * group
    return pl.pallas_call(
        functools.partial(attend_last_kernel, len(queries)),
        out_specs=[VMEM_SPEC] * (len(queries) + 1),
        out_shape=[pltpu.VMEM((rows + 8, half), jnp.float32)] * len(queries) + [TOKEN],
        compiler_params=pltpu.CompilerParams(vmem_limit_bytes=24 << 20),
        name="attend_last",
    )(after, *first, *queries, *kv_parts)


def column(stats, at):
    lane = lax.broadcasted_iota(jnp.int32, stats.shape, 1)
    return along_lanes(jnp.sum(jnp.where(lane == at, stats, 0.0), axis=-1, keepdims=True))


def combine_kernel(pieces, after_ref, *refs):
    part_refs, out_refs = refs[:pieces], refs[pieces:]
    group, half = out_refs[0].shape
    rows = group * len(out_refs)
    stats = [rows_of(ref[rows:, :DH], rows) for ref in part_refs]
    for head in range(half // DH):
        cols = slice(head * DH, (head + 1) * DH)
        maxima = [column(stat, 2 * head) for stat in stats]
        top = functools.reduce(jnp.maximum, maxima)
        total = jnp.zeros_like(top)
        attended = jnp.zeros((rows, DH), jnp.float32)
        for ref, stat, maximum in zip(part_refs, stats, maxima):
            factor = jnp.exp(maximum - top)
            total = total + column(stat, 2 * head + 1) * factor
            attended = attended + ref[:rows, cols] * factor
        attended = attended / total
        for side, out_ref in enumerate(out_refs):
            out_ref[:, cols] = attended[side * group : (side + 1) * group].astype(jnp.bfloat16)


def combine(after, parts, group, pair):
    half = parts[0].shape[1]
    return pl.pallas_call(
        functools.partial(combine_kernel, len(parts)),
        out_shape=[jax.ShapeDtypeStruct((group, half), jnp.bfloat16)] * pair,
        compiler_params=pltpu.CompilerParams(vmem_limit_bytes=16 << 20),
        name="combine",
    )(after, *parts)


def output_terms(side, pair, spread_ref, attended_ref, w_ref):
    group, half = attended_ref.shape
    width = w_ref.shape[1]
    attended = jnp.dot(
        spread_ref[:, :group], attended_ref[...], preferred_element_type=jnp.float32
    ).astype(jnp.bfloat16)
    start = pl.multiple_of((my_core(pair) ^ side) * half, DH)
    step = math.gcd(width, 1024)
    for col in range(0, width, step):
        cols = slice(col, col + step)
        yield cols, jnp.dot(
            attended, w_ref[pl.ds(start, half), cols], preferred_element_type=jnp.float32
        )


def output_first_kernel(pair, spread_ref, attended_ref, w_ref, out_ref):
    for cols, terms in output_terms(0, pair, spread_ref, attended_ref, w_ref):
        out_ref[:, cols] = terms


def output_first(spread, attended, w_out, pair):
    return pl.pallas_call(
        functools.partial(output_first_kernel, pair),
        out_specs=VMEM_SPEC,
        out_shape=pltpu.VMEM((spread.shape[0], w_out.shape[1]), jnp.float32),
        cost_estimate=pl.CostEstimate(flops=10**8, bytes_accessed=0, transcendentals=0),
        compiler_params=pltpu.CompilerParams(vmem_limit_bytes=16 << 20),
        name="output_first",
    )(spread, attended, w_out)


def output_last_kernel(pair, spread_ref, first_ref, *refs):
    *attended_refs, w_ref = refs[:pair]
    *out_refs, token_ref = refs[pair:]
    token_ref[...] = jnp.zeros_like(token_ref)
    slots = out_refs[0].shape[0]

    def write(cols, terms):
        for k, out_ref in enumerate(out_refs):
            out_ref[:, cols] = terms[k * slots : (k + 1) * slots].astype(out_ref.dtype)

    if not attended_refs:
        write(slice(None), first_ref[...])
    for attended_ref in attended_refs:
        for cols, terms in output_terms(1, pair, spread_ref, attended_ref, w_ref):
            write(cols, first_ref[:, cols] + terms)


def output_last(spread, first, others, w_out, slots, parts):
    width = w_out.shape[1]
    return pl.pallas_call(
        functools.partial(output_last_kernel, len(others) + 1),
        out_shape=[
            jax.ShapeDtypeStruct((slots, width), jnp.bfloat16 if k else jnp.float32)
            for k in range(parts)
        ]
        + [TOKEN],
        compiler_params=pltpu.CompilerParams(vmem_limit_bytes=16 << 20),
        name="output_last",
    )(spread, first, *others, w_out)


def mlp_kernel(pieces, *refs):
    row_refs, (up_ref, down_ref) = refs[:pieces], refs[pieces : pieces + 2]
    *out_refs, act_ref = refs[pieces + 2 :]
    hidden, width = down_ref.shape
    rows = [ref[j] for ref in row_refs for j in range(ref.shape[0])]
    rows = jnp.concatenate(rows, axis=0)
    count = out_refs[0].shape[0]
    step = math.gcd(hidden, 768)
    for col in range(0, hidden, step):
        lifted = jnp.dot(rows, up_ref[:, col : col + step], preferred_element_type=jnp.float32)
        act_ref[:, col : col + step] = jax.nn.gelu(lifted, approximate=True).astype(jnp.bfloat16)
    step = math.gcd(width, 1024)
    for col in range(0, width, step):
        down = jnp.dot(
            act_ref[...], down_ref[:, col : col + step], preferred_element_type=jnp.float32
        )
        for side, out_ref in enumerate(out_refs):
            piece = down[side * count : (side + 1) * count]
            out_ref[:, col : col + step] = piece.astype(out_ref.dtype)


def mlp(rows, w_up, w_down, pair):
    count = sum(x.shape[0] * x.shape[1] for x in rows)
    hidden, width = w_down.shape
    return pl.pallas_call(
        functools.partial(mlp_kernel, len(rows)),
        out_shape=[
            jax.ShapeDtypeStruct((count // pair, width), jnp.bfloat16 if side else jnp.float32)
            for side in range(pair)
        ],
        scratch_shapes=[pltpu.VMEM((count, hidden), jnp.bfloat16)],
        compiler_params=pltpu.CompilerParams(vmem_limit_bytes=32 << 20),
        name="mlp",
    )(*rows, w_up, w_down)


def join_kernel(count, *refs):
    part_refs, out_ref = refs[:count], refs[-1]
    for at, ref in enumerate(part_refs):
        out_ref[at] = ref[...]


def join(parts, after=()):
    return pl.pallas_call(
        functools.partial(join_kernel, len(parts)),
        out_shape=jax.ShapeDtypeStruct((len(parts), *parts[0].shape), parts[0].dtype),
        compiler_params=pltpu.CompilerParams(vmem_limit_bytes=8 << 20),
        name="join",
    )(*parts, *after)


def renorm_kernel(hold_ref, rows_ref, mod_ref, *refs):
    *term_refs, after_ref, normed_ref = refs
    branch = term_refs[0][...]
    for ref in term_refs[1:]:
        branch = branch + ref[...].astype(jnp.float32)
    after = rows_ref[...] + mod_ref[2:3, :] * branch
    after_ref[...] = after
    normed_ref[...] = layer_norm(after, mod_ref[3:4, :], mod_ref[4:5, :]).astype(jnp.bfloat16)


def renorm(after, rows_in, modulation, terms):
    return pl.pallas_call(
        renorm_kernel,
        out_shape=[
            jax.ShapeDtypeStruct(rows_in.shape, jnp.float32),
            jax.ShapeDtypeStruct(rows_in.shape, jnp.bfloat16),
        ],
        compiler_params=pltpu.CompilerParams(vmem_limit_bytes=8 << 20),
        name="renorm",
    )(after, rows_in, modulation, *terms)


def fold_kernel(sides, *refs):
    side_refs, out_refs = refs[:sides], refs[sides:]
    slots = out_refs[0].shape[0]
    for j, out_ref in enumerate(out_refs):
        total = side_refs[0][j * slots : (j + 1) * slots]
        for ref in side_refs[1:]:
            total = total + ref[j * slots : (j + 1) * slots].astype(jnp.float32)
        out_ref[...] = total.astype(out_ref.dtype)


def fold(sides, slots):
    count, width = sides[0].shape
    return pl.pallas_call(
        functools.partial(fold_kernel, len(sides)),
        out_shape=[
            jax.ShapeDtypeStruct((slots, width), jnp.bfloat16 if j else jnp.float32)
            for j in range(count // slots)
        ],
        compiler_params=pltpu.CompilerParams(vmem_limit_bytes=8 << 20),
        name="fold",
    )(*sides)


def finish_kernel(select_ref, cached_ref, after_ref, mod_ref, *refs):
    *term_refs, out_ref = refs
    total = term_refs[0][...]
    for ref in term_refs[1:]:
        total = total + ref[...].astype(jnp.float32)
    renewed = (after_ref[...] + mod_ref[5:6, :] * total).astype(jnp.bfloat16)
    select = select_ref[...]
    placed = jnp.dot(select, renewed, preferred_element_type=jnp.float32)
    covered = jnp.sum(select.astype(jnp.float32), axis=1, keepdims=True)
    blended = cached_ref[...].astype(jnp.float32) * (1.0 - covered) + placed
    out_ref[...] = blended.astype(jnp.bfloat16)


def finish(select, cached, after_attn, modulation, terms):
    return pl.pallas_call(
        finish_kernel,
        out_shape=jax.ShapeDtypeStruct(cached.shape, jnp.bfloat16),
        compiler_params=pltpu.CompilerParams(vmem_limit_bytes=8 << 20),
        name="finish",
    )(select, cached, after_attn, modulation, *terms)


def body(
    hidden_in,
    cached_out,
    cache_keys,
    cache_values,
    refresh_idx,
    modulation,
    q_gain,
    w_query,
    w_out,
    w_up,
    w_down,
):
    slots = refresh_idx.shape[0]
    uly_size = lax.axis_size("uly")
    blk_size = lax.axis_size("blk")
    local_heads = w_query.shape[1] // DH
    group = min(slots * uly_size, slots + (uly_size - 1) * OTHER)
    pair = 2 if blk_size % 2 == 0 and local_heads % 2 == 0 else 1
    chips = blk_size // pair

    rows_in, normed, select, modulation, sides = enter(
        refresh_idx, hidden_in, modulation, cache_keys, cache_values, uly_size, pair
    )
    sides = [trade(x, "blk", side) for side, x in enumerate(sides)]
    w_query, token = hold(normed, w_query)
    half_way = uly_size // 2
    cuts = [[half_way, 0], [k for k in range(uly_size) if k not in (0, half_way)]]
    first, token = merge_kv(sides, cuts[0], [token])
    group_rows = double(normed, "uly", 1, uly_size, {half_way: lambda x: relay(x, token)})
    second, token = merge_kv(sides, cuts[1], group_rows[1:])
    kv_parts = [trade(x, "uly", k) for k, x in zip(cuts[0] + cuts[1], first + second)]

    queries, spread, token = project(token, group_rows, w_query, q_gain, group, pair)
    w_out, token = hold(token, w_out)
    queries = join([trade(x, "blk", side) for side, x in enumerate(queries)])
    queries = double(queries, "blk", pair, chips)
    first = attend_first(queries, kv_parts[:2])
    *parts, token = attend_last(token, first, queries, kv_parts[2:])
    w_up, token = hold(token, w_up)
    parts = far_first([trade(x, "blk", j * pair) for j, x in enumerate(parts)])
    attended = combine(token, parts, group, pair)
    mine, *others = attended
    others = [trade(x, "blk", 1) for x in others]
    terms = output_first(spread, mine, w_out, pair)
    *terms, token = output_last(spread, terms, others, w_out, slots, uly_size)
    w_down, cached, token = hold(token, w_down, cached_out)
    terms = far_first([trade(x, "uly", k) for k, x in enumerate(terms)])
    after_attn, norm_mlp = renorm(token, rows_in, modulation, terms)

    rows = [join([trade(norm_mlp, "blk", j * pair) for j in range(chips)])]
    if pair == 2:
        rows.append(trade(rows[0], "blk", 1))
    down = mlp(rows, w_up, w_down, pair)
    down = [trade(x, "blk", side) for side, x in enumerate(down)]
    terms = far_first([trade(x, "blk", j * pair) for j, x in enumerate(fold(down, slots))])
    return finish(select, cached, after_attn, modulation, terms)


def solution(mesh):
    return jax.shard_map(
        body,
        mesh=mesh,
        in_specs=(
            P(("blk", "uly"), None),
            P(("blk", "uly"), None),
            P(("blk", "uly"), None),
            P(("blk", "uly"), None),
            P(("blk", "uly")),
            P(),
            P(),
            P(None, "uly"),
            P("uly", None),
            P(None, "blk"),
            P("blk", None),
        ),
        out_specs=P(("blk", "uly"), None),
        check_vma=False,
    )
```

```python
import functools
import math

import jax
import jax.numpy as jnp
from jax import lax
from jax.experimental import pallas as pl
from jax.experimental.pallas import tpu as pltpu
from jax.sharding import PartitionSpec as P

DH = 128
OTHER = 8
VMEM_SPEC = pl.BlockSpec(memory_space=pltpu.VMEM)
TOKEN = pltpu.VMEM((8, DH), jnp.float32)
ANY_SPEC = pl.BlockSpec(memory_space=pl.ANY)


def far_first(parts):
    return parts[:1] + parts[:0:-1]


def double(x, axis, scale, count, on_arrival=()):
    have = {0: x}
    for k in sorted(range(1, count), key=lambda k: (bin(k).count("1"), -k)):
        low = k & -k
        have[k] = trade(have[k ^ low], axis, low * scale)
        if k in on_arrival:
            have[k] = on_arrival[k](have[k])
    return [have[k] for k in range(count)]


def layer_norm(row_block, shift_by, scale_by):
    average = jnp.mean(row_block, axis=-1, keepdims=True)
    centred = row_block - average
    spread = jnp.mean(centred * centred, axis=-1, keepdims=True)
    return centred * lax.rsqrt(spread + 1e-06) * (1.0 + scale_by) + shift_by


def trade(x, axis, flip):
    if flip == 0:
        return x
    return lax.ppermute(x, axis, [(i, i ^ flip) for i in range(lax.axis_size(axis))])


def in_hbm(x):
    return pltpu.with_memory_space_constraint(x, pltpu.HBM)


def hold_kernel(count, *refs):
    source_refs, sems = refs[1 : count + 1], refs[-1]
    *held_refs, token_ref = refs[count + 1 : -1]
    token_ref[...] = jnp.zeros_like(token_ref)
    copies = [
        pltpu.make_async_copy(source_ref, held_ref, sems.at[i])
        for i, (source_ref, held_ref) in enumerate(zip(source_refs, held_refs))
    ]
    for copy in copies:
        copy.start()
    for copy in copies:
        copy.wait()


def hold(after, *weights):
    count = len(weights)
    moved = sum(w.size * w.dtype.itemsize for w in weights)
    return pl.pallas_call(
        functools.partial(hold_kernel, count),
        in_specs=[VMEM_SPEC] + [ANY_SPEC] * count,
        out_specs=[VMEM_SPEC] * (count + 1),
        out_shape=[pltpu.VMEM(w.shape, w.dtype) for w in weights] + [TOKEN],
        scratch_shapes=[pltpu.SemaphoreType.DMA((count,))],
        cost_estimate=pl.CostEstimate(flops=0, bytes_accessed=moved, transcendentals=0),
        compiler_params=pltpu.CompilerParams(vmem_limit_bytes=2 << 20),
        name="hold",
    )(after, *[in_hbm(w) for w in weights])


def my_core(pair):
    return lax.rem(lax.axis_index("blk"), pair)


def enter_kernel(pair, idx_hbm, hidden_hbm, mod_hbm, key_hbm, value_hbm, *refs):
    rows_ref, normed_ref, select_ref, mod_ref, *side_refs = refs[: pair + 4]
    idx_ref, hidden_ref, sems, kv_sem = refs[pair + 4 :]
    copies = [
        pltpu.make_async_copy(source, target, sems.at[i])
        for i, (source, target) in enumerate(
            [(idx_hbm, idx_ref), (hidden_hbm, hidden_ref), (mod_hbm, mod_ref)]
        )
    ]
    for copy in copies:
        copy.start()
    parts, _, both = side_refs[0].shape
    half = both // 2
    uly, core = lax.axis_index("uly"), my_core(pair)
    kv_copies = []
    for side, side_ref in enumerate(side_refs):
        for flip in range(parts):
            start = pl.multiple_of(((uly ^ flip) * pair + (core ^ side)) * half, DH)
            for at, source in enumerate((key_hbm, value_hbm)):
                copy = pltpu.make_async_copy(
                    source.at[:, pl.ds(start, half)],
                    side_ref.at[flip, :, pl.ds(at * half, half)],
                    kv_sem.at[side, flip, at],
                )
                copy.start()
                kv_copies.append(copy)
    for copy in copies:
        copy.wait()
    tokens, width = hidden_ref.shape
    slots = idx_ref.shape[1]
    position = lax.broadcasted_iota(jnp.int32, (tokens, slots), 0)
    select = (position == idx_ref[...]).astype(jnp.float32).astype(jnp.bfloat16)
    select_ref[...] = select
    contract = (((0,), (0,)), ((), ()))
    rows = lax.dot_general(
        select, hidden_ref[...], contract, preferred_element_type=jnp.float32
    )
    live = lax.dot_general(
        select,
        jnp.ones((tokens, DH), jnp.bfloat16),
        contract,
        preferred_element_type=jnp.float32,
    )
    rows_ref[...] = rows
    normed = layer_norm(rows, mod_ref[0:1, :], mod_ref[1:2, :])
    normed_ref[:, :width] = normed.astype(jnp.bfloat16)
    normed_ref[:, width:] = live.astype(jnp.bfloat16)
    for copy in kv_copies:
        copy.wait()


def enter(refresh_idx, hidden_in, modulation, cache_keys, cache_values, parts, pair):
    slots = refresh_idx.shape[0]
    tokens, width = hidden_in.shape
    both = 2 * width // (parts * pair)
    out = pl.pallas_call(
        functools.partial(enter_kernel, pair),
        in_specs=[ANY_SPEC] * 5,
        out_specs=[VMEM_SPEC] * (pair + 4),
        out_shape=[
            pltpu.VMEM((slots, width), jnp.float32),
            pltpu.VMEM((slots, width + DH), jnp.bfloat16),
            pltpu.VMEM((tokens, slots), jnp.bfloat16),
            pltpu.VMEM(modulation.shape, modulation.dtype),
        ]
        + [pltpu.VMEM((parts, tokens, both), cache_keys.dtype)] * pair,
        scratch_shapes=[
            pltpu.VMEM((1, slots), jnp.int32),
            pltpu.VMEM(hidden_in.shape, hidden_in.dtype),
            pltpu.SemaphoreType.DMA((3,)),
            pltpu.SemaphoreType.DMA((pair, parts, 2)),
        ],
        compiler_params=pltpu.CompilerParams(vmem_limit_bytes=8 << 20),
        name="enter",
    )(
        *[
            in_hbm(x)
            for x in (refresh_idx.reshape(1, slots), hidden_in, modulation, cache_keys, cache_values)
        ]
    )
    return *out[:4], out[4:]


def merge_kv_kernel(sides, flips, *refs):
    *refs, token_ref = refs
    token_ref[...] = jnp.zeros_like(token_ref)
    for flip, out_ref in zip(flips, refs[-len(flips) :]):
        for side in range(sides):
            out_ref[side] = refs[side][flip]


def merge_kv(sides, flips, after):
    _, tokens, both = sides[0].shape
    *merged, token = pl.pallas_call(
        functools.partial(merge_kv_kernel, len(sides), flips),
        out_specs=[VMEM_SPEC] * (len(flips) + 1),
        out_shape=[pltpu.VMEM((len(sides), tokens, both), sides[0].dtype) for _ in flips]
        + [TOKEN],
        compiler_params=pltpu.CompilerParams(vmem_limit_bytes=8 << 20),
        name="merge_kv",
    )(*sides, *after)
    return merged, token


def relay_kernel(x_ref, after_ref, out_ref):
    out_ref[...] = x_ref[...]


def relay(x, after):
    return pl.pallas_call(
        relay_kernel,
        out_specs=VMEM_SPEC,
        out_shape=pltpu.VMEM(x.shape, x.dtype),
        compiler_params=pltpu.CompilerParams(vmem_limit_bytes=2 << 20),
        name="relay",
    )(x, after)


def project_kernel(pieces, after_ref, *refs):
    rows_refs, (w_ref, gain_hbm_ref) = refs[:pieces], refs[pieces : pieces + 2]
    *query_refs, spread_ref, token_ref, heads_ref, gain_ref, sem = refs[pieces + 2 :]
    token_ref[...] = jnp.zeros_like(token_ref)
    copy = pltpu.make_async_copy(gain_hbm_ref, gain_ref, sem)
    copy.start()
    core = my_core(len(query_refs))
    width = w_ref.shape[0]
    group, half = query_refs[0].shape
    rows = jnp.concatenate([ref[...] for ref in rows_refs], axis=0)
    everyone = rows.shape[0]
    flags = rows[:, width:]
    shape = (everyone, everyone)
    before = lax.broadcasted_iota(jnp.int32, shape, 1) < lax.broadcasted_iota(jnp.int32, shape, 0)
    before = before.astype(jnp.float32).astype(jnp.bfloat16)
    rank = jnp.dot(before, flags, preferred_element_type=jnp.float32)
    lane = lax.broadcasted_iota(jnp.int32, rank.shape, 1).astype(jnp.float32)
    spread = jnp.where((rank == lane) & (flags.astype(jnp.float32) > 0.0), 1.0, 0.0)
    spread = spread.astype(jnp.bfloat16)
    spread_ref[...] = spread
    live_rows = lax.dot_general(
        spread[:, :group],
        rows[:, :width],
        (((0,), (0,)), ((), ())),
        preferred_element_type=jnp.float32,
    ).astype(jnp.bfloat16)
    projected = jnp.dot(live_rows, w_ref[...], preferred_element_type=jnp.float32)
    copy.wait()
    for start in range(0, projected.shape[1], DH):
        head = projected[:, start : start + DH]
        squares = jnp.mean(head * head, axis=-1, keepdims=True)
        heads_ref[:, start : start + DH] = (
            head * lax.rsqrt(squares + 1e-06) * (gain_ref[...] / math.sqrt(DH))
        )
    for side, query_ref in enumerate(query_refs):
        start = pl.multiple_of((core ^ side) * half, DH)
        query_ref[...] = heads_ref[:, pl.ds(start, half)].astype(jnp.bfloat16)


def project(after, rows, w_query, q_gain, group, pair):
    half = w_query.shape[1] // pair
    everyone = len(rows) * rows[0].shape[0]
    query = jax.ShapeDtypeStruct((group, half), jnp.bfloat16)
    out = pl.pallas_call(
        functools.partial(project_kernel, len(rows)),
        in_specs=[VMEM_SPEC] * (len(rows) + 2) + [ANY_SPEC],
        out_shape=[query] * pair + [jax.ShapeDtypeStruct((everyone, DH), jnp.bfloat16), TOKEN],
        scratch_shapes=[
            pltpu.VMEM((group, w_query.shape[1]), jnp.float32),
            pltpu.VMEM((1, DH), jnp.float32),
            pltpu.SemaphoreType.DMA,
        ],
        compiler_params=pltpu.CompilerParams(vmem_limit_bytes=16 << 20),
        name="project",
    )(after, *rows, w_query, in_hbm(q_gain.reshape(1, DH)))
    return out[:-2], out[-2], out[-1]


def head_scores(queries, kv_refs, head):
    half = queries.shape[1]
    cols = slice(head * DH, (head + 1) * DH)
    vals = slice(half + head * DH, half + (head + 1) * DH)
    sides = kv_refs[0].shape[0]
    keys = [ref[side, :, cols] for ref in kv_refs for side in range(sides)]
    values = [ref[side, :, vals] for ref in kv_refs for side in range(sides)]
    scores = lax.dot_general(
        queries[:, cols],
        jnp.concatenate(keys, axis=0),
        (((1,), (1,)), ((), ())),
        preferred_element_type=jnp.float32,
    )
    return scores, jnp.concatenate(values, axis=0)


def lanes_of(stats):
    packed = stats[:8]
    for at in range(8, stats.shape[0], 8):
        packed = packed + pltpu.roll(stats[at : at + 8], at, axis=1)
    return packed


def rows_of(packed, rows):
    parts = [packed] + [pltpu.roll(packed, DH - at, axis=1) for at in range(8, rows, 8)]
    return jnp.concatenate(parts, axis=0)


def stacked(refs):
    rows = [ref[core].astype(jnp.float32) for ref in refs for core in range(ref.shape[0])]
    return jnp.concatenate(rows, axis=0).astype(jnp.bfloat16)


def along_lanes(column):
    return jnp.broadcast_to(column, (column.shape[0], DH))


def weights_of(scores, maxima):
    width = scores.shape[1]
    return [jnp.exp(scores[:, at : at + DH] - maxima) for at in range(0, width, DH)]


def attend_first_kernel(pieces, *refs):
    query_refs, (*kv_refs, sum_ref, max_ref, total_ref) = refs[:pieces], refs[pieces:]
    cores, group, half = query_refs[0].shape
    rows = cores * group
    for at in range(0, pieces, 4):
        queries = stacked(query_refs[at : at + 4])
        mine = slice(at * rows, at * rows + queries.shape[0])
        for head in range(half // DH):
            cols = slice(head * DH, (head + 1) * DH)
            scores, values = head_scores(queries, kv_refs, head)
            maxima = along_lanes(jnp.max(scores, axis=-1, keepdims=True))
            weights = jnp.concatenate(weights_of(scores, maxima), axis=1)
            max_ref[mine, cols] = maxima
            total_ref[mine, cols] = along_lanes(jnp.sum(weights, axis=-1, keepdims=True))
            sum_ref[mine, cols] = jnp.dot(
                weights.astype(jnp.bfloat16), values, preferred_element_type=jnp.float32
            )


def attend_first(queries, kv_parts):
    cores, group, half = queries[0].shape
    count = cores * group * len(queries)
    return pl.pallas_call(
        functools.partial(attend_first_kernel, len(queries)),
        out_specs=[VMEM_SPEC] * 3,
        out_shape=[pltpu.VMEM((count, half), jnp.float32)] * 3,
        cost_estimate=pl.CostEstimate(flops=0, bytes_accessed=0, transcendentals=0),
        compiler_params=pltpu.CompilerParams(vmem_limit_bytes=24 << 20),
        name="attend_first",
    )(*queries, *kv_parts)


def attend_last_kernel(pieces, after_ref, sum_ref, max_ref, total_ref, *refs):
    *refs, token_ref = refs
    token_ref[...] = jnp.zeros_like(token_ref)
    query_refs, kv_refs, out_refs = refs[:pieces], refs[pieces:-pieces], refs[-pieces:]
    cores, group, half = query_refs[0].shape
    rows = cores * group
    for at in range(0, pieces, 4):
        stop = min(at + 4, pieces)
        queries = stacked(query_refs[at:stop])
        mine = slice(at * rows, stop * rows)
        lane = lax.broadcasted_iota(jnp.int32, (queries.shape[0], DH), 1)
        stats = jnp.zeros((queries.shape[0], DH), jnp.float32)
        for head in range(half // DH):
            cols = slice(head * DH, (head + 1) * DH)
            scores, values = head_scores(queries, kv_refs, head)
            earlier = max_ref[mine, cols]
            maxima = along_lanes(jnp.max(scores, axis=-1, keepdims=True))
            maxima = jnp.maximum(earlier, maxima)
            weights = jnp.concatenate(weights_of(scores, maxima), axis=1)
            factor = jnp.exp(earlier - maxima)
            total = along_lanes(jnp.sum(weights, axis=-1, keepdims=True))
            total = total_ref[mine, cols] * factor + total
            weighted = sum_ref[mine, cols] * factor + jnp.dot(
                weights.astype(jnp.bfloat16), values, preferred_element_type=jnp.float32
            )
            stats = jnp.where(lane == 2 * head, maxima, stats)
            stats = jnp.where(lane == 2 * head + 1, total, stats)
            for j in range(at, stop):
                own = weighted[(j - at) * rows : (j - at + 1) * rows]
                out_refs[j][head * rows : (head + 1) * rows, :] = own
        for j in range(at, stop):
            own = stats[(j - at) * rows : (j - at + 1) * rows]
            out_refs[j][half // DH * rows :, :] = lanes_of(own)


def attend_last(after, first, queries, kv_parts):
    cores, group, half = queries[0].shape
    rows = cores * group
    return pl.pallas_call(
        functools.partial(attend_last_kernel, len(queries)),
        out_specs=[VMEM_SPEC] * (len(queries) + 1),
        out_shape=[pltpu.VMEM((half // DH * rows + 8, DH), jnp.float32)] * len(queries) + [TOKEN],
        compiler_params=pltpu.CompilerParams(vmem_limit_bytes=24 << 20),
        name="attend_last",
    )(after, *first, *queries, *kv_parts)


def column(stats, at):
    lane = lax.broadcasted_iota(jnp.int32, stats.shape, 1)
    return along_lanes(jnp.sum(jnp.where(lane == at, stats, 0.0), axis=-1, keepdims=True))


def combine_kernel(pieces, after_ref, *refs):
    part_refs, out_refs = refs[:pieces], refs[pieces:]
    group, half = out_refs[0].shape
    rows = group * len(out_refs)
    stats = [rows_of(ref[half // DH * rows :, :], rows) for ref in part_refs]
    for head in range(half // DH):
        cols = slice(head * DH, (head + 1) * DH)
        maxima = [column(stat, 2 * head) for stat in stats]
        top = functools.reduce(jnp.maximum, maxima)
        total = jnp.zeros_like(top)
        attended = jnp.zeros((rows, DH), jnp.float32)
        for ref, stat, maximum in zip(part_refs, stats, maxima):
            factor = jnp.exp(maximum - top)
            total = total + column(stat, 2 * head + 1) * factor
            attended = attended + ref[head * rows : (head + 1) * rows, :] * factor
        attended = attended / total
        for side, out_ref in enumerate(out_refs):
            out_ref[:, cols] = attended[side * group : (side + 1) * group].astype(jnp.bfloat16)


def combine(after, parts, group, pair):
    half = (parts[0].shape[0] - 8) // (group * pair) * DH
    return pl.pallas_call(
        functools.partial(combine_kernel, len(parts)),
        out_shape=[jax.ShapeDtypeStruct((group, half), jnp.bfloat16)] * pair,
        compiler_params=pltpu.CompilerParams(vmem_limit_bytes=16 << 20),
        name="combine",
    )(after, *parts)


def output_terms(side, pair, spread_ref, attended_ref, w_ref):
    group, half = attended_ref.shape
    width = w_ref.shape[1]
    attended = jnp.dot(
        spread_ref[:, :group], attended_ref[...], preferred_element_type=jnp.float32
    ).astype(jnp.bfloat16)
    start = pl.multiple_of((my_core(pair) ^ side) * half, DH)
    step = math.gcd(width, 1024)
    for col in range(0, width, step):
        cols = slice(col, col + step)
        yield cols, jnp.dot(
            attended, w_ref[pl.ds(start, half), cols], preferred_element_type=jnp.float32
        )


def output_first_kernel(pair, spread_ref, attended_ref, w_ref, out_ref):
    for cols, terms in output_terms(0, pair, spread_ref, attended_ref, w_ref):
        out_ref[:, cols] = terms


def output_first(spread, attended, w_out, pair):
    return pl.pallas_call(
        functools.partial(output_first_kernel, pair),
        out_specs=VMEM_SPEC,
        out_shape=pltpu.VMEM((spread.shape[0], w_out.shape[1]), jnp.float32),
        cost_estimate=pl.CostEstimate(flops=10**8, bytes_accessed=0, transcendentals=0),
        compiler_params=pltpu.CompilerParams(vmem_limit_bytes=16 << 20),
        name="output_first",
    )(spread, attended, w_out)


def output_last_kernel(pair, spread_ref, first_ref, *refs):
    *attended_refs, w_ref = refs[:pair]
    *out_refs, token_ref = refs[pair:]
    token_ref[...] = jnp.zeros_like(token_ref)
    slots = out_refs[0].shape[0]

    def write(cols, terms):
        for k, out_ref in enumerate(out_refs):
            out_ref[:, cols] = terms[k * slots : (k + 1) * slots].astype(out_ref.dtype)

    if not attended_refs:
        write(slice(None), first_ref[...])
    for attended_ref in attended_refs:
        for cols, terms in output_terms(1, pair, spread_ref, attended_ref, w_ref):
            write(cols, first_ref[:, cols] + terms)


def output_last(spread, first, others, w_out, slots, parts):
    width = w_out.shape[1]
    return pl.pallas_call(
        functools.partial(output_last_kernel, len(others) + 1),
        out_shape=[
            jax.ShapeDtypeStruct((slots, width), jnp.bfloat16 if k else jnp.float32)
            for k in range(parts)
        ]
        + [TOKEN],
        compiler_params=pltpu.CompilerParams(vmem_limit_bytes=16 << 20),
        name="output_last",
    )(spread, first, *others, w_out)


def mlp_kernel(pieces, *refs):
    row_refs, (up_ref, down_ref) = refs[:pieces], refs[pieces : pieces + 2]
    *out_refs, act_ref = refs[pieces + 2 :]
    hidden, width = down_ref.shape
    rows = [ref[j] for ref in row_refs for j in range(ref.shape[0])]
    rows = jnp.concatenate(rows, axis=0)
    count = out_refs[0].shape[0]
    step = math.gcd(hidden, 768)
    for col in range(0, hidden, step):
        lifted = jnp.dot(rows, up_ref[:, col : col + step], preferred_element_type=jnp.float32)
        act_ref[:, col : col + step] = jax.nn.gelu(lifted, approximate=True).astype(jnp.bfloat16)
    step = math.gcd(width, 1024)
    for col in range(0, width, step):
        down = jnp.dot(
            act_ref[...], down_ref[:, col : col + step], preferred_element_type=jnp.float32
        )
        for side, out_ref in enumerate(out_refs):
            piece = down[side * count : (side + 1) * count]
            out_ref[:, col : col + step] = piece.astype(out_ref.dtype)


def mlp(rows, w_up, w_down, pair):
    count = sum(x.shape[0] * x.shape[1] for x in rows)
    hidden, width = w_down.shape
    return pl.pallas_call(
        functools.partial(mlp_kernel, len(rows)),
        out_shape=[
            jax.ShapeDtypeStruct((count // pair, width), jnp.bfloat16 if side else jnp.float32)
            for side in range(pair)
        ],
        scratch_shapes=[pltpu.VMEM((count, hidden), jnp.bfloat16)],
        compiler_params=pltpu.CompilerParams(vmem_limit_bytes=32 << 20),
        name="mlp",
    )(*rows, w_up, w_down)


def join_kernel(count, *refs):
    part_refs, out_ref = refs[:count], refs[-1]
    for at, ref in enumerate(part_refs):
        out_ref[at] = ref[...]


def join(parts, after=()):
    return pl.pallas_call(
        functools.partial(join_kernel, len(parts)),
        out_shape=jax.ShapeDtypeStruct((len(parts), *parts[0].shape), parts[0].dtype),
        compiler_params=pltpu.CompilerParams(vmem_limit_bytes=8 << 20),
        name="join",
    )(*parts, *after)


def renorm_kernel(hold_ref, rows_ref, mod_ref, *refs):
    *term_refs, after_ref, normed_ref = refs
    branch = term_refs[0][...]
    for ref in term_refs[1:]:
        branch = branch + ref[...].astype(jnp.float32)
    after = rows_ref[...] + mod_ref[2:3, :] * branch
    after_ref[...] = after
    normed_ref[...] = layer_norm(after, mod_ref[3:4, :], mod_ref[4:5, :]).astype(jnp.bfloat16)


def renorm(after, rows_in, modulation, terms):
    return pl.pallas_call(
        renorm_kernel,
        out_shape=[
            jax.ShapeDtypeStruct(rows_in.shape, jnp.float32),
            jax.ShapeDtypeStruct(rows_in.shape, jnp.bfloat16),
        ],
        compiler_params=pltpu.CompilerParams(vmem_limit_bytes=8 << 20),
        name="renorm",
    )(after, rows_in, modulation, *terms)


def fold_kernel(sides, *refs):
    side_refs, out_refs = refs[:sides], refs[sides:]
    slots = out_refs[0].shape[0]
    for j, out_ref in enumerate(out_refs):
        total = side_refs[0][j * slots : (j + 1) * slots]
        for ref in side_refs[1:]:
            total = total + ref[j * slots : (j + 1) * slots].astype(jnp.float32)
        out_ref[...] = total.astype(out_ref.dtype)


def fold(sides, slots):
    count, width = sides[0].shape
    return pl.pallas_call(
        functools.partial(fold_kernel, len(sides)),
        out_shape=[
            jax.ShapeDtypeStruct((slots, width), jnp.bfloat16 if j else jnp.float32)
            for j in range(count // slots)
        ],
        compiler_params=pltpu.CompilerParams(vmem_limit_bytes=8 << 20),
        name="fold",
    )(*sides)


def finish_kernel(select_ref, cached_ref, after_ref, mod_ref, *refs):
    *term_refs, out_ref = refs
    total = term_refs[0][...]
    for ref in term_refs[1:]:
        total = total + ref[...].astype(jnp.float32)
    renewed = (after_ref[...] + mod_ref[5:6, :] * total).astype(jnp.bfloat16)
    select = select_ref[...]
    placed = jnp.dot(select, renewed, preferred_element_type=jnp.float32)
    covered = jnp.sum(select.astype(jnp.float32), axis=1, keepdims=True)
    blended = cached_ref[...].astype(jnp.float32) * (1.0 - covered) + placed
    out_ref[...] = blended.astype(jnp.bfloat16)


def finish(select, cached, after_attn, modulation, terms):
    return pl.pallas_call(
        finish_kernel,
        out_shape=jax.ShapeDtypeStruct(cached.shape, jnp.bfloat16),
        compiler_params=pltpu.CompilerParams(vmem_limit_bytes=8 << 20),
        name="finish",
    )(select, cached, after_attn, modulation, *terms)


def body(
    hidden_in,
    cached_out,
    cache_keys,
    cache_values,
    refresh_idx,
    modulation,
    q_gain,
    w_query,
    w_out,
    w_up,
    w_down,
):
    slots = refresh_idx.shape[0]
    uly_size = lax.axis_size("uly")
    blk_size = lax.axis_size("blk")
    local_heads = w_query.shape[1] // DH
    group = min(slots * uly_size, slots + (uly_size - 1) * OTHER)
    pair = 2 if blk_size % 2 == 0 and local_heads % 2 == 0 else 1
    chips = blk_size // pair

    rows_in, normed, select, modulation, sides = enter(
        refresh_idx, hidden_in, modulation, cache_keys, cache_values, uly_size, pair
    )
    sides = [trade(x, "blk", side) for side, x in enumerate(sides)]
    w_query, token = hold(normed, w_query)
    half_way = uly_size // 2
    cuts = [[half_way, 0], [k for k in range(uly_size) if k not in (0, half_way)]]
    first, token = merge_kv(sides, cuts[0], [token])
    group_rows = double(normed, "uly", 1, uly_size, {half_way: lambda x: relay(x, token)})
    second, token = merge_kv(sides, cuts[1], group_rows[1:])
    kv_parts = [trade(x, "uly", k) for k, x in zip(cuts[0] + cuts[1], first + second)]

    queries, spread, token = project(token, group_rows, w_query, q_gain, group, pair)
    w_out, token = hold(token, w_out)
    queries = [trade(x, "blk", side) for side, x in enumerate(queries)]
    queries = join(queries, kv_parts[2:3])
    queries = far_first([trade(queries, "blk", j * pair) for j in range(chips)])
    queries = far_first(queries)
    first = attend_first(queries, kv_parts[:2])
    *parts, token = attend_last(token, first, queries, kv_parts[2:])
    w_up, token = hold(token, w_up)
    parts = far_first([trade(x, "blk", j * pair) for j, x in enumerate(parts)])
    attended = combine(token, parts, group, pair)
    mine, *others = attended
    others = [trade(x, "blk", 1) for x in others]
    terms = output_first(spread, mine, w_out, pair)
    *terms, token = output_last(spread, terms, others, w_out, slots, uly_size)
    w_down, cached, token = hold(token, w_down, cached_out)
    terms = far_first([trade(x, "uly", k) for k, x in enumerate(terms)])
    after_attn, norm_mlp = renorm(token, rows_in, modulation, terms)

    rows = [join([trade(norm_mlp, "blk", j * pair) for j in range(chips)])]
    if pair == 2:
        rows.append(trade(rows[0], "blk", 1))
    down = mlp(rows, w_up, w_down, pair)
    down = [trade(x, "blk", side) for side, x in enumerate(down)]
    terms = far_first([trade(x, "blk", j * pair) for j, x in enumerate(fold(down, slots))])
    return finish(select, cached, after_attn, modulation, terms)


def solution(mesh):
    return jax.shard_map(
        body,
        mesh=mesh,
        in_specs=(
            P(("blk", "uly"), None),
            P(("blk", "uly"), None),
            P(("blk", "uly"), None),
            P(("blk", "uly"), None),
            P(("blk", "uly")),
            P(),
            P(),
            P(None, "uly"),
            P("uly", None),
            P(None, "blk"),
            P("blk", None),
        ),
        out_specs=P(("blk", "uly"), None),
        check_vma=False,
    )
```

```python
import functools
import math

import jax
import jax.numpy as jnp
from jax import lax
from jax.experimental import pallas as pl
from jax.experimental.pallas import tpu as pltpu
from jax.sharding import PartitionSpec as P

DH = 128
OTHER = 8
VMEM_SPEC = pl.BlockSpec(memory_space=pltpu.VMEM)
TOKEN = pltpu.VMEM((8, DH), jnp.float32)
ANY_SPEC = pl.BlockSpec(memory_space=pl.ANY)


def far_first(parts):
    return parts[:1] + parts[:0:-1]


def double(x, axis, scale, count, on_arrival=()):
    have = {0: x}
    for k in sorted(range(1, count), key=lambda k: (bin(k).count("1"), -k)):
        low = k & -k
        have[k] = trade(have[k ^ low], axis, low * scale)
        if k in on_arrival:
            have[k] = on_arrival[k](have[k])
    return [have[k] for k in range(count)]


def layer_norm(row_block, shift_by, scale_by):
    average = jnp.mean(row_block, axis=-1, keepdims=True)
    centred = row_block - average
    spread = jnp.mean(centred * centred, axis=-1, keepdims=True)
    return centred * lax.rsqrt(spread + 1e-06) * (1.0 + scale_by) + shift_by


def trade(x, axis, flip):
    if flip == 0:
        return x
    return lax.ppermute(x, axis, [(i, i ^ flip) for i in range(lax.axis_size(axis))])


def in_hbm(x):
    return pltpu.with_memory_space_constraint(x, pltpu.HBM)


def hold_kernel(count, *refs):
    source_refs, sems = refs[1 : count + 1], refs[-1]
    *held_refs, token_ref = refs[count + 1 : -1]
    token_ref[...] = jnp.zeros_like(token_ref)
    copies = [
        pltpu.make_async_copy(source_ref, held_ref, sems.at[i])
        for i, (source_ref, held_ref) in enumerate(zip(source_refs, held_refs))
    ]
    for copy in copies:
        copy.start()
    for copy in copies:
        copy.wait()


def hold(after, *weights):
    count = len(weights)
    moved = sum(w.size * w.dtype.itemsize for w in weights)
    return pl.pallas_call(
        functools.partial(hold_kernel, count),
        in_specs=[VMEM_SPEC] + [ANY_SPEC] * count,
        out_specs=[VMEM_SPEC] * (count + 1),
        out_shape=[pltpu.VMEM(w.shape, w.dtype) for w in weights] + [TOKEN],
        scratch_shapes=[pltpu.SemaphoreType.DMA((count,))],
        cost_estimate=pl.CostEstimate(flops=0, bytes_accessed=moved, transcendentals=0),
        compiler_params=pltpu.CompilerParams(vmem_limit_bytes=2 << 20),
        name="hold",
    )(after, *[in_hbm(w) for w in weights])


def my_core(pair):
    return lax.rem(lax.axis_index("blk"), pair)


def enter_kernel(pair, idx_hbm, hidden_hbm, mod_hbm, key_hbm, value_hbm, *refs):
    rows_ref, normed_ref, select_ref, mod_ref, *side_refs = refs[: pair + 4]
    idx_ref, hidden_ref, sems, kv_sem = refs[pair + 4 :]
    copies = [
        pltpu.make_async_copy(source, target, sems.at[i])
        for i, (source, target) in enumerate(
            [(idx_hbm, idx_ref), (hidden_hbm, hidden_ref), (mod_hbm, mod_ref)]
        )
    ]
    for copy in copies:
        copy.start()
    parts, _, both = side_refs[0].shape
    half = both // 2
    uly, core = lax.axis_index("uly"), my_core(pair)
    kv_copies = []
    for side, side_ref in enumerate(side_refs):
        for flip in range(parts):
            start = pl.multiple_of(((uly ^ flip) * pair + (core ^ side)) * half, DH)
            for at, source in enumerate((key_hbm, value_hbm)):
                copy = pltpu.make_async_copy(
                    source.at[:, pl.ds(start, half)],
                    side_ref.at[flip, :, pl.ds(at * half, half)],
                    kv_sem.at[side, flip, at],
                )
                copy.start()
                kv_copies.append(copy)
    for copy in copies:
        copy.wait()
    tokens, width = hidden_ref.shape
    slots = idx_ref.shape[1]
    position = lax.broadcasted_iota(jnp.int32, (tokens, slots), 0)
    select = (position == idx_ref[...]).astype(jnp.float32).astype(jnp.bfloat16)
    select_ref[...] = select
    contract = (((0,), (0,)), ((), ()))
    rows = lax.dot_general(
        select, hidden_ref[...], contract, preferred_element_type=jnp.float32
    )
    live = lax.dot_general(
        select,
        jnp.ones((tokens, DH), jnp.bfloat16),
        contract,
        preferred_element_type=jnp.float32,
    )
    rows_ref[...] = rows
    normed = layer_norm(rows, mod_ref[0:1, :], mod_ref[1:2, :])
    normed_ref[:, :width] = normed.astype(jnp.bfloat16)
    normed_ref[:, width:] = live.astype(jnp.bfloat16)
    for copy in kv_copies:
        copy.wait()


def enter(refresh_idx, hidden_in, modulation, cache_keys, cache_values, parts, pair):
    slots = refresh_idx.shape[0]
    tokens, width = hidden_in.shape
    both = 2 * width // (parts * pair)
    out = pl.pallas_call(
        functools.partial(enter_kernel, pair),
        in_specs=[ANY_SPEC] * 5,
        out_specs=[VMEM_SPEC] * (pair + 4),
        out_shape=[
            pltpu.VMEM((slots, width), jnp.float32),
            pltpu.VMEM((slots, width + DH), jnp.bfloat16),
            pltpu.VMEM((tokens, slots), jnp.bfloat16),
            pltpu.VMEM(modulation.shape, modulation.dtype),
        ]
        + [pltpu.VMEM((parts, tokens, both), cache_keys.dtype)] * pair,
        scratch_shapes=[
            pltpu.VMEM((1, slots), jnp.int32),
            pltpu.VMEM(hidden_in.shape, hidden_in.dtype),
            pltpu.SemaphoreType.DMA((3,)),
            pltpu.SemaphoreType.DMA((pair, parts, 2)),
        ],
        compiler_params=pltpu.CompilerParams(vmem_limit_bytes=8 << 20),
        name="enter",
    )(
        *[
            in_hbm(x)
            for x in (refresh_idx.reshape(1, slots), hidden_in, modulation, cache_keys, cache_values)
        ]
    )
    return *out[:4], out[4:]


def merge_kv_kernel(sides, flips, *refs):
    *refs, token_ref = refs
    token_ref[...] = jnp.zeros_like(token_ref)
    for flip, out_ref in zip(flips, refs[-len(flips) :]):
        for side in range(sides):
            out_ref[side] = refs[side][flip]


def merge_kv(sides, flips, after):
    _, tokens, both = sides[0].shape
    *merged, token = pl.pallas_call(
        functools.partial(merge_kv_kernel, len(sides), flips),
        out_specs=[VMEM_SPEC] * (len(flips) + 1),
        out_shape=[pltpu.VMEM((len(sides), tokens, both), sides[0].dtype) for _ in flips]
        + [TOKEN],
        compiler_params=pltpu.CompilerParams(vmem_limit_bytes=8 << 20),
        name="merge_kv",
    )(*sides, *after)
    return merged, token


def relay_kernel(x_ref, after_ref, out_ref):
    out_ref[...] = x_ref[...]


def relay(x, after):
    return pl.pallas_call(
        relay_kernel,
        out_specs=VMEM_SPEC,
        out_shape=pltpu.VMEM(x.shape, x.dtype),
        compiler_params=pltpu.CompilerParams(vmem_limit_bytes=2 << 20),
        name="relay",
    )(x, after)


def project_kernel(pieces, after_ref, *refs):
    rows_refs, (w_ref, gain_hbm_ref) = refs[:pieces], refs[pieces : pieces + 2]
    *query_refs, spread_ref, token_ref, heads_ref, gain_ref, sem = refs[pieces + 2 :]
    token_ref[...] = jnp.zeros_like(token_ref)
    copy = pltpu.make_async_copy(gain_hbm_ref, gain_ref, sem)
    copy.start()
    core = my_core(len(query_refs))
    width = w_ref.shape[0]
    group, half = query_refs[0].shape
    rows = jnp.concatenate([ref[...] for ref in rows_refs], axis=0)
    everyone = rows.shape[0]
    flags = rows[:, width:]
    shape = (everyone, everyone)
    before = lax.broadcasted_iota(jnp.int32, shape, 1) < lax.broadcasted_iota(jnp.int32, shape, 0)
    before = before.astype(jnp.float32).astype(jnp.bfloat16)
    rank = jnp.dot(before, flags, preferred_element_type=jnp.float32)
    lane = lax.broadcasted_iota(jnp.int32, rank.shape, 1).astype(jnp.float32)
    spread = jnp.where((rank == lane) & (flags.astype(jnp.float32) > 0.0), 1.0, 0.0)
    spread = spread.astype(jnp.bfloat16)
    spread_ref[...] = spread
    live_rows = lax.dot_general(
        spread[:, :group],
        rows[:, :width],
        (((0,), (0,)), ((), ())),
        preferred_element_type=jnp.float32,
    ).astype(jnp.bfloat16)
    projected = jnp.dot(live_rows, w_ref[...], preferred_element_type=jnp.float32)
    copy.wait()
    for start in range(0, projected.shape[1], DH):
        head = projected[:, start : start + DH]
        squares = jnp.mean(head * head, axis=-1, keepdims=True)
        heads_ref[:, start : start + DH] = (
            head * lax.rsqrt(squares + 1e-06) * (gain_ref[...] / math.sqrt(DH))
        )
    for side, query_ref in enumerate(query_refs):
        start = pl.multiple_of((core ^ side) * half, DH)
        query_ref[...] = heads_ref[:, pl.ds(start, half)].astype(jnp.bfloat16)


def project(after, rows, w_query, q_gain, group, pair):
    half = w_query.shape[1] // pair
    everyone = len(rows) * rows[0].shape[0]
    query = jax.ShapeDtypeStruct((group, half), jnp.bfloat16)
    out = pl.pallas_call(
        functools.partial(project_kernel, len(rows)),
        in_specs=[VMEM_SPEC] * (len(rows) + 2) + [ANY_SPEC],
        out_shape=[query] * pair + [jax.ShapeDtypeStruct((everyone, DH), jnp.bfloat16), TOKEN],
        scratch_shapes=[
            pltpu.VMEM((group, w_query.shape[1]), jnp.float32),
            pltpu.VMEM((1, DH), jnp.float32),
            pltpu.SemaphoreType.DMA,
        ],
        compiler_params=pltpu.CompilerParams(vmem_limit_bytes=16 << 20),
        name="project",
    )(after, *rows, w_query, in_hbm(q_gain.reshape(1, DH)))
    return out[:-2], out[-2], out[-1]


def head_scores(queries, kv_refs, head):
    half = queries.shape[1]
    cols = slice(head * DH, (head + 1) * DH)
    vals = slice(half + head * DH, half + (head + 1) * DH)
    sides = kv_refs[0].shape[0]
    keys = [ref[side, :, cols] for ref in kv_refs for side in range(sides)]
    values = [ref[side, :, vals] for ref in kv_refs for side in range(sides)]
    scores = lax.dot_general(
        queries[:, cols],
        jnp.concatenate(keys, axis=0),
        (((1,), (1,)), ((), ())),
        preferred_element_type=jnp.float32,
    )
    return scores, jnp.concatenate(values, axis=0)


def lanes_of(stats):
    packed = stats[:8]
    for at in range(8, stats.shape[0], 8):
        packed = packed + pltpu.roll(stats[at : at + 8], at, axis=1)
    return packed


def rows_of(packed, rows):
    parts = [packed] + [pltpu.roll(packed, DH - at, axis=1) for at in range(8, rows, 8)]
    return jnp.concatenate(parts, axis=0)


def stacked(refs):
    rows = [ref[core].astype(jnp.float32) for ref in refs for core in range(ref.shape[0])]
    return jnp.concatenate(rows, axis=0).astype(jnp.bfloat16)


def along_lanes(column):
    return jnp.broadcast_to(column, (column.shape[0], DH))


def weights_of(scores, maxima):
    width = scores.shape[1]
    return [jnp.exp(scores[:, at : at + DH] - maxima) for at in range(0, width, DH)]


def attend_first_kernel(pieces, *refs):
    query_refs, (*kv_refs, sum_ref, max_ref, total_ref) = refs[:pieces], refs[pieces:]
    cores, group, half = query_refs[0].shape
    rows = cores * group
    for at in range(0, pieces, 4):
        queries = stacked(query_refs[at : at + 4])
        mine = slice(at * rows, at * rows + queries.shape[0])
        for head in range(half // DH):
            cols = slice(head * DH, (head + 1) * DH)
            scores, values = head_scores(queries, kv_refs, head)
            maxima = along_lanes(jnp.max(scores, axis=-1, keepdims=True))
            weights = jnp.concatenate(weights_of(scores, maxima), axis=1)
            max_ref[mine, cols] = maxima
            total_ref[mine, cols] = along_lanes(jnp.sum(weights, axis=-1, keepdims=True))
            sum_ref[mine, cols] = jnp.dot(
                weights.astype(jnp.bfloat16), values, preferred_element_type=jnp.float32
            )


def attend_first(queries, kv_parts):
    cores, group, half = queries[0].shape
    count = cores * group * len(queries)
    return pl.pallas_call(
        functools.partial(attend_first_kernel, len(queries)),
        out_specs=[VMEM_SPEC] * 3,
        out_shape=[pltpu.VMEM((count, half), jnp.float32)] * 3,
        cost_estimate=pl.CostEstimate(flops=0, bytes_accessed=0, transcendentals=0),
        compiler_params=pltpu.CompilerParams(vmem_limit_bytes=24 << 20),
        name="attend_first",
    )(*queries, *kv_parts)


def attend_last_kernel(pieces, after_ref, sum_ref, max_ref, total_ref, *refs):
    *refs, token_ref = refs
    token_ref[...] = jnp.zeros_like(token_ref)
    query_refs, kv_refs, out_refs = refs[:pieces], refs[pieces:-pieces], refs[-pieces:]
    cores, group, half = query_refs[0].shape
    rows = cores * group
    for at in range(0, pieces, 4):
        stop = min(at + 4, pieces)
        queries = stacked(query_refs[at:stop])
        mine = slice(at * rows, stop * rows)
        lane = lax.broadcasted_iota(jnp.int32, (queries.shape[0], DH), 1)
        stats = jnp.zeros((queries.shape[0], DH), jnp.float32)
        for head in range(half // DH):
            cols = slice(head * DH, (head + 1) * DH)
            scores, values = head_scores(queries, kv_refs, head)
            earlier = max_ref[mine, cols]
            maxima = along_lanes(jnp.max(scores, axis=-1, keepdims=True))
            maxima = jnp.maximum(earlier, maxima)
            weights = jnp.concatenate(weights_of(scores, maxima), axis=1)
            factor = jnp.exp(earlier - maxima)
            total = along_lanes(jnp.sum(weights, axis=-1, keepdims=True))
            total = total_ref[mine, cols] * factor + total
            weighted = sum_ref[mine, cols] * factor + jnp.dot(
                weights.astype(jnp.bfloat16), values, preferred_element_type=jnp.float32
            )
            stats = jnp.where(lane == 2 * head, maxima, stats)
            stats = jnp.where(lane == 2 * head + 1, total, stats)
            for j in range(at, stop):
                own = weighted[(j - at) * rows : (j - at + 1) * rows]
                out_refs[j][head * rows : (head + 1) * rows, :] = own
        for j in range(at, stop):
            own = stats[(j - at) * rows : (j - at + 1) * rows]
            out_refs[j][half // DH * rows :, :] = lanes_of(own)


def attend_last(after, first, queries, kv_parts):
    cores, group, half = queries[0].shape
    rows = cores * group
    return pl.pallas_call(
        functools.partial(attend_last_kernel, len(queries)),
        out_specs=[VMEM_SPEC] * (len(queries) + 1),
        out_shape=[pltpu.VMEM((half // DH * rows + 8, DH), jnp.float32)] * len(queries) + [TOKEN],
        compiler_params=pltpu.CompilerParams(vmem_limit_bytes=24 << 20),
        name="attend_last",
    )(after, *first, *queries, *kv_parts)


def column(stats, at):
    lane = lax.broadcasted_iota(jnp.int32, stats.shape, 1)
    return along_lanes(jnp.sum(jnp.where(lane == at, stats, 0.0), axis=-1, keepdims=True))


def combine_kernel(pieces, after_ref, *refs):
    part_refs, out_refs = refs[:pieces], refs[pieces:]
    group, half = out_refs[0].shape
    rows = group * len(out_refs)
    stats = [rows_of(ref[half // DH * rows :, :], rows) for ref in part_refs]
    for head in range(half // DH):
        cols = slice(head * DH, (head + 1) * DH)
        maxima = [column(stat, 2 * head) for stat in stats]
        top = functools.reduce(jnp.maximum, maxima)
        total = jnp.zeros_like(top)
        attended = jnp.zeros((rows, DH), jnp.float32)
        for ref, stat, maximum in zip(part_refs, stats, maxima):
            factor = jnp.exp(maximum - top)
            total = total + column(stat, 2 * head + 1) * factor
            attended = attended + ref[head * rows : (head + 1) * rows, :] * factor
        attended = attended / total
        for side, out_ref in enumerate(out_refs):
            out_ref[:, cols] = attended[side * group : (side + 1) * group].astype(jnp.bfloat16)


def combine(after, parts, group, pair):
    half = (parts[0].shape[0] - 8) // (group * pair) * DH
    return pl.pallas_call(
        functools.partial(combine_kernel, len(parts)),
        out_shape=[jax.ShapeDtypeStruct((group, half), jnp.bfloat16)] * pair,
        compiler_params=pltpu.CompilerParams(vmem_limit_bytes=16 << 20),
        name="combine",
    )(after, *parts)


def output_terms(side, pair, spread_ref, attended_ref, w_ref):
    group, half = attended_ref.shape
    width = w_ref.shape[1]
    attended = jnp.dot(
        spread_ref[:, :group], attended_ref[...], preferred_element_type=jnp.float32
    ).astype(jnp.bfloat16)
    start = pl.multiple_of((my_core(pair) ^ side) * half, DH)
    step = math.gcd(width, 1024)
    for col in range(0, width, step):
        cols = slice(col, col + step)
        yield cols, jnp.dot(
            attended, w_ref[pl.ds(start, half), cols], preferred_element_type=jnp.float32
        )


def output_first_kernel(pair, spread_ref, attended_ref, w_ref, out_ref):
    for cols, terms in output_terms(0, pair, spread_ref, attended_ref, w_ref):
        out_ref[:, cols] = terms


def output_first(spread, attended, w_out, pair):
    return pl.pallas_call(
        functools.partial(output_first_kernel, pair),
        out_specs=VMEM_SPEC,
        out_shape=pltpu.VMEM((spread.shape[0], w_out.shape[1]), jnp.float32),
        cost_estimate=pl.CostEstimate(flops=10**8, bytes_accessed=0, transcendentals=0),
        compiler_params=pltpu.CompilerParams(vmem_limit_bytes=16 << 20),
        name="output_first",
    )(spread, attended, w_out)


def output_last_kernel(pair, spread_ref, first_ref, *refs):
    *attended_refs, w_ref = refs[:pair]
    *out_refs, token_ref = refs[pair:]
    token_ref[...] = jnp.zeros_like(token_ref)
    slots = out_refs[0].shape[0]

    def write(cols, terms):
        for k, out_ref in enumerate(out_refs):
            out_ref[:, cols] = terms[k * slots : (k + 1) * slots].astype(out_ref.dtype)

    if not attended_refs:
        write(slice(None), first_ref[...])
    for attended_ref in attended_refs:
        for cols, terms in output_terms(1, pair, spread_ref, attended_ref, w_ref):
            write(cols, first_ref[:, cols] + terms)


def output_last(spread, first, others, w_out, slots, parts):
    width = w_out.shape[1]
    return pl.pallas_call(
        functools.partial(output_last_kernel, len(others) + 1),
        out_shape=[
            jax.ShapeDtypeStruct((slots, width), jnp.bfloat16 if k else jnp.float32)
            for k in range(parts)
        ]
        + [TOKEN],
        compiler_params=pltpu.CompilerParams(vmem_limit_bytes=16 << 20),
        name="output_last",
    )(spread, first, *others, w_out)


def mlp_kernel(pieces, *refs):
    row_refs, (up_ref, down_ref) = refs[:pieces], refs[pieces : pieces + 2]
    *out_refs, act_ref = refs[pieces + 2 :]
    hidden, width = down_ref.shape
    rows = [ref[j] for ref in row_refs for j in range(ref.shape[0])]
    rows = jnp.concatenate(rows, axis=0)
    count = out_refs[0].shape[0]
    step = math.gcd(hidden, 768)
    for col in range(0, hidden, step):
        lifted = jnp.dot(rows, up_ref[:, col : col + step], preferred_element_type=jnp.float32)
        act_ref[:, col : col + step] = jax.nn.gelu(lifted, approximate=True).astype(jnp.bfloat16)
    step = math.gcd(width, 1024)
    for col in range(0, width, step):
        down = jnp.dot(
            act_ref[...], down_ref[:, col : col + step], preferred_element_type=jnp.float32
        )
        for side, out_ref in enumerate(out_refs):
            piece = down[side * count : (side + 1) * count]
            out_ref[:, col : col + step] = piece.astype(out_ref.dtype)


def mlp(rows, w_up, w_down, pair):
    count = sum(x.shape[0] * x.shape[1] for x in rows)
    hidden, width = w_down.shape
    return pl.pallas_call(
        functools.partial(mlp_kernel, len(rows)),
        out_shape=[
            jax.ShapeDtypeStruct((count // pair, width), jnp.bfloat16 if side else jnp.float32)
            for side in range(pair)
        ],
        scratch_shapes=[pltpu.VMEM((count, hidden), jnp.bfloat16)],
        compiler_params=pltpu.CompilerParams(vmem_limit_bytes=32 << 20),
        name="mlp",
    )(*rows, w_up, w_down)


def join_kernel(count, *refs):
    part_refs, out_ref = refs[:count], refs[-1]
    for at, ref in enumerate(part_refs):
        out_ref[at] = ref[...]


def join(parts, after=()):
    return pl.pallas_call(
        functools.partial(join_kernel, len(parts)),
        out_shape=jax.ShapeDtypeStruct((len(parts), *parts[0].shape), parts[0].dtype),
        compiler_params=pltpu.CompilerParams(vmem_limit_bytes=8 << 20),
        name="join",
    )(*parts, *after)


def renorm_kernel(hold_ref, rows_ref, mod_ref, *refs):
    *term_refs, after_ref, normed_ref = refs
    branch = term_refs[0][...]
    for ref in term_refs[1:]:
        branch = branch + ref[...].astype(jnp.float32)
    after = rows_ref[...] + mod_ref[2:3, :] * branch
    after_ref[...] = after
    normed_ref[...] = layer_norm(after, mod_ref[3:4, :], mod_ref[4:5, :]).astype(jnp.bfloat16)


def renorm(after, rows_in, modulation, terms):
    return pl.pallas_call(
        renorm_kernel,
        out_shape=[
            jax.ShapeDtypeStruct(rows_in.shape, jnp.float32),
            jax.ShapeDtypeStruct(rows_in.shape, jnp.bfloat16),
        ],
        compiler_params=pltpu.CompilerParams(vmem_limit_bytes=8 << 20),
        name="renorm",
    )(after, rows_in, modulation, *terms)


def fold_kernel(sides, *refs):
    side_refs, out_refs = refs[:sides], refs[sides:]
    slots = out_refs[0].shape[0]
    for j, out_ref in enumerate(out_refs):
        total = side_refs[0][j * slots : (j + 1) * slots]
        for ref in side_refs[1:]:
            total = total + ref[j * slots : (j + 1) * slots].astype(jnp.float32)
        out_ref[...] = total.astype(out_ref.dtype)


def fold(sides, slots):
    count, width = sides[0].shape
    return pl.pallas_call(
        functools.partial(fold_kernel, len(sides)),
        out_shape=[
            jax.ShapeDtypeStruct((slots, width), jnp.bfloat16 if j else jnp.float32)
            for j in range(count // slots)
        ],
        compiler_params=pltpu.CompilerParams(vmem_limit_bytes=8 << 20),
        name="fold",
    )(*sides)


def finish_kernel(select_ref, cached_ref, after_ref, mod_ref, *refs):
    *term_refs, out_ref = refs
    total = term_refs[0][...]
    for ref in term_refs[1:]:
        total = total + ref[...].astype(jnp.float32)
    renewed = (after_ref[...] + mod_ref[5:6, :] * total).astype(jnp.bfloat16)
    select = select_ref[...]
    placed = jnp.dot(select, renewed, preferred_element_type=jnp.float32)
    covered = jnp.sum(select.astype(jnp.float32), axis=1, keepdims=True)
    blended = cached_ref[...].astype(jnp.float32) * (1.0 - covered) + placed
    out_ref[...] = blended.astype(jnp.bfloat16)


def finish(select, cached, after_attn, modulation, terms):
    return pl.pallas_call(
        finish_kernel,
        out_shape=jax.ShapeDtypeStruct(cached.shape, jnp.bfloat16),
        compiler_params=pltpu.CompilerParams(vmem_limit_bytes=8 << 20),
        name="finish",
    )(select, cached, after_attn, modulation, *terms)


def body(
    hidden_in,
    cached_out,
    cache_keys,
    cache_values,
    refresh_idx,
    modulation,
    q_gain,
    w_query,
    w_out,
    w_up,
    w_down,
):
    slots = refresh_idx.shape[0]
    uly_size = lax.axis_size("uly")
    blk_size = lax.axis_size("blk")
    local_heads = w_query.shape[1] // DH
    group = min(slots * uly_size, slots + (uly_size - 1) * OTHER)
    pair = 2 if blk_size % 2 == 0 and local_heads % 2 == 0 else 1
    chips = blk_size // pair

    rows_in, normed, select, modulation, sides = enter(
        refresh_idx, hidden_in, modulation, cache_keys, cache_values, uly_size, pair
    )
    sides = [trade(x, "blk", side) for side, x in enumerate(sides)]
    w_query, token = hold(normed, w_query)
    half_way = uly_size // 2
    cuts = [[half_way, 0], [k for k in range(uly_size) if k not in (0, half_way)]]
    first, token = merge_kv(sides, cuts[0], [token])
    group_rows = double(normed, "uly", 1, uly_size, {half_way: lambda x: relay(x, token)})
    second, token = merge_kv(sides, cuts[1], group_rows[1:])
    kv_parts = [trade(x, "uly", k) for k, x in zip(cuts[0] + cuts[1], first + second)]

    queries, spread, token = project(token, group_rows, w_query, q_gain, group, pair)
    w_out, token = hold(token, w_out)
    queries = [trade(x, "blk", side) for side, x in enumerate(queries)]
    queries = join(queries)
    queries = double(queries, "blk", pair, chips)
    first = attend_first(queries, kv_parts[:2])
    *parts, token = attend_last(token, first, queries, kv_parts[2:])
    w_up, token = hold(token, w_up)
    parts = far_first([trade(x, "blk", j * pair) for j, x in enumerate(parts)])
    attended = combine(token, parts, group, pair)
    mine, *others = attended
    others = [trade(x, "blk", 1) for x in others]
    terms = output_first(spread, mine, w_out, pair)
    *terms, token = output_last(spread, terms, others, w_out, slots, uly_size)
    w_down, cached, token = hold(token, w_down, cached_out)
    terms = far_first([trade(x, "uly", k) for k, x in enumerate(terms)])
    after_attn, norm_mlp = renorm(token, rows_in, modulation, terms)

    rows = [join([trade(norm_mlp, "blk", j * pair) for j in range(chips)])]
    if pair == 2:
        rows.append(trade(rows[0], "blk", 1))
    down = mlp(rows, w_up, w_down, pair)
    down = [trade(x, "blk", side) for side, x in enumerate(down)]
    terms = far_first([trade(x, "blk", j * pair) for j, x in enumerate(fold(down, slots))])
    return finish(select, cached, after_attn, modulation, terms)


def solution(mesh):
    return jax.shard_map(
        body,
        mesh=mesh,
        in_specs=(
            P(("blk", "uly"), None),
            P(("blk", "uly"), None),
            P(("blk", "uly"), None),
            P(("blk", "uly"), None),
            P(("blk", "uly")),
            P(),
            P(),
            P(None, "uly"),
            P("uly", None),
            P(None, "blk"),
            P("blk", None),
        ),
        out_specs=P(("blk", "uly"), None),
        check_vma=False,
    )
```

```python
import functools
import math

import jax
import jax.numpy as jnp
from jax import lax
from jax.experimental import pallas as pl
from jax.experimental.pallas import tpu as pltpu
from jax.sharding import PartitionSpec as P

DH = 128
OTHER = 8
VMEM_SPEC = pl.BlockSpec(memory_space=pltpu.VMEM)
TOKEN = pltpu.VMEM((8, DH), jnp.float32)
ANY_SPEC = pl.BlockSpec(memory_space=pl.ANY)


def far_first(parts):
    return parts[:1] + parts[:0:-1]


def double(x, axis, scale, count, on_arrival=()):
    have = {0: x}
    for k in sorted(range(1, count), key=lambda k: (bin(k).count("1"), -k)):
        low = k & -k
        have[k] = trade(have[k ^ low], axis, low * scale)
        if k in on_arrival:
            have[k] = on_arrival[k](have[k])
    return [have[k] for k in range(count)]


def layer_norm(row_block, shift_by, scale_by):
    average = jnp.mean(row_block, axis=-1, keepdims=True)
    centred = row_block - average
    spread = jnp.mean(centred * centred, axis=-1, keepdims=True)
    return centred * lax.rsqrt(spread + 1e-06) * (1.0 + scale_by) + shift_by


def trade(x, axis, flip):
    if flip == 0:
        return x
    return lax.ppermute(x, axis, [(i, i ^ flip) for i in range(lax.axis_size(axis))])


def in_hbm(x):
    return pltpu.with_memory_space_constraint(x, pltpu.HBM)


def hold_kernel(count, *refs):
    source_refs, sems = refs[1 : count + 1], refs[-1]
    *held_refs, token_ref = refs[count + 1 : -1]
    token_ref[...] = jnp.zeros_like(token_ref)
    copies = [
        pltpu.make_async_copy(source_ref, held_ref, sems.at[i])
        for i, (source_ref, held_ref) in enumerate(zip(source_refs, held_refs))
    ]
    for copy in copies:
        copy.start()
    for copy in copies:
        copy.wait()


def hold(after, *weights):
    count = len(weights)
    moved = sum(w.size * w.dtype.itemsize for w in weights)
    return pl.pallas_call(
        functools.partial(hold_kernel, count),
        in_specs=[VMEM_SPEC] + [ANY_SPEC] * count,
        out_specs=[VMEM_SPEC] * (count + 1),
        out_shape=[pltpu.VMEM(w.shape, w.dtype) for w in weights] + [TOKEN],
        scratch_shapes=[pltpu.SemaphoreType.DMA((count,))],
        cost_estimate=pl.CostEstimate(flops=0, bytes_accessed=moved, transcendentals=0),
        compiler_params=pltpu.CompilerParams(vmem_limit_bytes=2 << 20),
        name="hold",
    )(after, *[in_hbm(w) for w in weights])


def my_core(pair):
    return lax.rem(lax.axis_index("blk"), pair)


def enter_kernel(pair, idx_hbm, hidden_hbm, mod_hbm, key_hbm, value_hbm, *refs):
    rows_ref, normed_ref, select_ref, mod_ref, *side_refs = refs[: pair + 4]
    idx_ref, hidden_ref, sems, kv_sem = refs[pair + 4 :]
    copies = [
        pltpu.make_async_copy(source, target, sems.at[i])
        for i, (source, target) in enumerate(
            [(idx_hbm, idx_ref), (hidden_hbm, hidden_ref), (mod_hbm, mod_ref)]
        )
    ]
    for copy in copies:
        copy.start()
    parts, _, both = side_refs[0].shape
    half = both // 2
    uly, core = lax.axis_index("uly"), my_core(pair)
    kv_copies = []
    for side, side_ref in enumerate(side_refs):
        for flip in range(parts):
            start = pl.multiple_of(((uly ^ flip) * pair + (core ^ side)) * half, DH)
            for at, source in enumerate((key_hbm, value_hbm)):
                copy = pltpu.make_async_copy(
                    source.at[:, pl.ds(start, half)],
                    side_ref.at[flip, :, pl.ds(at * half, half)],
                    kv_sem.at[side, flip, at],
                )
                copy.start()
                kv_copies.append(copy)
    for copy in copies:
        copy.wait()
    tokens, width = hidden_ref.shape
    slots = idx_ref.shape[1]
    position = lax.broadcasted_iota(jnp.int32, (tokens, slots), 0)
    select = (position == idx_ref[...]).astype(jnp.float32).astype(jnp.bfloat16)
    select_ref[...] = select
    contract = (((0,), (0,)), ((), ()))
    rows = lax.dot_general(
        select, hidden_ref[...], contract, preferred_element_type=jnp.float32
    )
    live = lax.dot_general(
        select,
        jnp.ones((tokens, DH), jnp.bfloat16),
        contract,
        preferred_element_type=jnp.float32,
    )
    rows_ref[...] = rows
    normed = layer_norm(rows, mod_ref[0:1, :], mod_ref[1:2, :])
    normed_ref[:, :width] = normed.astype(jnp.bfloat16)
    normed_ref[:, width:] = live.astype(jnp.bfloat16)
    for copy in kv_copies:
        copy.wait()


def enter(refresh_idx, hidden_in, modulation, cache_keys, cache_values, parts, pair):
    slots = refresh_idx.shape[0]
    tokens, width = hidden_in.shape
    both = 2 * width // (parts * pair)
    out = pl.pallas_call(
        functools.partial(enter_kernel, pair),
        in_specs=[ANY_SPEC] * 5,
        out_specs=[VMEM_SPEC] * (pair + 4),
        out_shape=[
            pltpu.VMEM((slots, width), jnp.float32),
            pltpu.VMEM((slots, width + DH), jnp.bfloat16),
            pltpu.VMEM((tokens, slots), jnp.bfloat16),
            pltpu.VMEM(modulation.shape, modulation.dtype),
        ]
        + [pltpu.VMEM((parts, tokens, both), cache_keys.dtype)] * pair,
        scratch_shapes=[
            pltpu.VMEM((1, slots), jnp.int32),
            pltpu.VMEM(hidden_in.shape, hidden_in.dtype),
            pltpu.SemaphoreType.DMA((3,)),
            pltpu.SemaphoreType.DMA((pair, parts, 2)),
        ],
        compiler_params=pltpu.CompilerParams(vmem_limit_bytes=8 << 20),
        name="enter",
    )(
        *[
            in_hbm(x)
            for x in (refresh_idx.reshape(1, slots), hidden_in, modulation, cache_keys, cache_values)
        ]
    )
    return *out[:4], out[4:]


def merge_kv_kernel(sides, flips, *refs):
    *refs, token_ref = refs
    token_ref[...] = jnp.zeros_like(token_ref)
    for flip, out_ref in zip(flips, refs[-len(flips) :]):
        for side in range(sides):
            out_ref[side] = refs[side][flip]


def merge_kv(sides, flips, after):
    _, tokens, both = sides[0].shape
    *merged, token = pl.pallas_call(
        functools.partial(merge_kv_kernel, len(sides), flips),
        out_specs=[VMEM_SPEC] * (len(flips) + 1),
        out_shape=[pltpu.VMEM((len(sides), tokens, both), sides[0].dtype) for _ in flips]
        + [TOKEN],
        compiler_params=pltpu.CompilerParams(vmem_limit_bytes=8 << 20),
        name="merge_kv",
    )(*sides, *after)
    return merged, token


def relay_kernel(x_ref, after_ref, out_ref):
    out_ref[...] = x_ref[...]


def relay(x, after):
    return pl.pallas_call(
        relay_kernel,
        out_specs=VMEM_SPEC,
        out_shape=pltpu.VMEM(x.shape, x.dtype),
        compiler_params=pltpu.CompilerParams(vmem_limit_bytes=2 << 20),
        name="relay",
    )(x, after)


def project_kernel(pieces, after_ref, *refs):
    rows_refs, (w_ref, gain_hbm_ref) = refs[:pieces], refs[pieces : pieces + 2]
    *query_refs, spread_ref, token_ref, heads_ref, gain_ref, sem = refs[pieces + 2 :]
    token_ref[...] = jnp.zeros_like(token_ref)
    copy = pltpu.make_async_copy(gain_hbm_ref, gain_ref, sem)
    copy.start()
    core = my_core(len(query_refs))
    width = w_ref.shape[0]
    group, half = query_refs[0].shape
    rows = jnp.concatenate([ref[...] for ref in rows_refs], axis=0)
    everyone = rows.shape[0]
    flags = rows[:, width:]
    shape = (everyone, everyone)
    before = lax.broadcasted_iota(jnp.int32, shape, 1) < lax.broadcasted_iota(jnp.int32, shape, 0)
    before = before.astype(jnp.float32).astype(jnp.bfloat16)
    rank = jnp.dot(before, flags, preferred_element_type=jnp.float32)
    lane = lax.broadcasted_iota(jnp.int32, rank.shape, 1).astype(jnp.float32)
    spread = jnp.where((rank == lane) & (flags.astype(jnp.float32) > 0.0), 1.0, 0.0)
    spread = spread.astype(jnp.bfloat16)
    spread_ref[...] = spread
    live_rows = lax.dot_general(
        spread[:, :group],
        rows[:, :width],
        (((0,), (0,)), ((), ())),
        preferred_element_type=jnp.float32,
    ).astype(jnp.bfloat16)
    projected = jnp.dot(live_rows, w_ref[...], preferred_element_type=jnp.float32)
    copy.wait()
    for start in range(0, projected.shape[1], DH):
        head = projected[:, start : start + DH]
        squares = jnp.mean(head * head, axis=-1, keepdims=True)
        heads_ref[:, start : start + DH] = (
            head * lax.rsqrt(squares + 1e-06) * (gain_ref[...] / math.sqrt(DH))
        )
    for side, query_ref in enumerate(query_refs):
        start = pl.multiple_of((core ^ side) * half, DH)
        query_ref[...] = heads_ref[:, pl.ds(start, half)].astype(jnp.bfloat16)


def project(after, rows, w_query, q_gain, group, pair):
    half = w_query.shape[1] // pair
    everyone = len(rows) * rows[0].shape[0]
    query = jax.ShapeDtypeStruct((group, half), jnp.bfloat16)
    out = pl.pallas_call(
        functools.partial(project_kernel, len(rows)),
        in_specs=[VMEM_SPEC] * (len(rows) + 2) + [ANY_SPEC],
        out_shape=[query] * pair + [jax.ShapeDtypeStruct((everyone, DH), jnp.bfloat16), TOKEN],
        scratch_shapes=[
            pltpu.VMEM((group, w_query.shape[1]), jnp.float32),
            pltpu.VMEM((1, DH), jnp.float32),
            pltpu.SemaphoreType.DMA,
        ],
        compiler_params=pltpu.CompilerParams(vmem_limit_bytes=16 << 20),
        name="project",
    )(after, *rows, w_query, in_hbm(q_gain.reshape(1, DH)))
    return out[:-2], out[-2], out[-1]


def head_scores(queries, kv_refs, head):
    half = queries.shape[1]
    cols = slice(head * DH, (head + 1) * DH)
    vals = slice(half + head * DH, half + (head + 1) * DH)
    sides = kv_refs[0].shape[0]
    keys = [ref[side, :, cols] for ref in kv_refs for side in range(sides)]
    values = [ref[side, :, vals] for ref in kv_refs for side in range(sides)]
    scores = lax.dot_general(
        queries[:, cols],
        jnp.concatenate(keys, axis=0),
        (((1,), (1,)), ((), ())),
        preferred_element_type=jnp.float32,
    )
    return scores, jnp.concatenate(values, axis=0)


def lanes_of(stats):
    packed = stats[:8]
    for at in range(8, stats.shape[0], 8):
        packed = packed + pltpu.roll(stats[at : at + 8], at, axis=1)
    return packed


def rows_of(packed, rows):
    parts = [packed] + [pltpu.roll(packed, DH - at, axis=1) for at in range(8, rows, 8)]
    return jnp.concatenate(parts, axis=0)


def stacked(refs):
    rows = [ref[core].astype(jnp.float32) for ref in refs for core in range(ref.shape[0])]
    return jnp.concatenate(rows, axis=0).astype(jnp.bfloat16)


def along_lanes(column):
    return jnp.broadcast_to(column, (column.shape[0], DH))


def weights_of(scores, maxima):
    blocks = [scores[:, at : at + DH] for at in range(0, scores.shape[1], DH)]
    return [jnp.exp(block - maxima[:, : block.shape[1]]) for block in blocks]


def attend_first_kernel(pieces, *refs):
    query_refs, (*kv_refs, sum_ref, max_ref, total_ref) = refs[:pieces], refs[pieces:]
    cores, group, half = query_refs[0].shape
    rows = cores * group
    for at in range(0, pieces, 4):
        queries = stacked(query_refs[at : at + 4])
        mine = slice(at * rows, at * rows + queries.shape[0])
        for head in range(half // DH):
            cols = slice(head * DH, (head + 1) * DH)
            scores, values = head_scores(queries, kv_refs, head)
            maxima = along_lanes(jnp.max(scores, axis=-1, keepdims=True))
            weights = jnp.concatenate(weights_of(scores, maxima), axis=1)
            max_ref[mine, cols] = maxima
            total_ref[mine, cols] = along_lanes(jnp.sum(weights, axis=-1, keepdims=True))
            sum_ref[mine, cols] = jnp.dot(
                weights.astype(jnp.bfloat16), values, preferred_element_type=jnp.float32
            )


def attend_first(queries, kv_parts):
    cores, group, half = queries[0].shape
    count = cores * group * len(queries)
    return pl.pallas_call(
        functools.partial(attend_first_kernel, len(queries)),
        out_specs=[VMEM_SPEC] * 3,
        out_shape=[pltpu.VMEM((count, half), jnp.float32)] * 3,
        cost_estimate=pl.CostEstimate(flops=0, bytes_accessed=0, transcendentals=0),
        compiler_params=pltpu.CompilerParams(vmem_limit_bytes=24 << 20),
        name="attend_first",
    )(*queries, *kv_parts)


def attend_last_kernel(pieces, after_ref, sum_ref, max_ref, total_ref, *refs):
    *refs, token_ref = refs
    token_ref[...] = jnp.zeros_like(token_ref)
    query_refs, kv_refs, out_refs = refs[:pieces], refs[pieces:-pieces], refs[-pieces:]
    cores, group, half = query_refs[0].shape
    rows = cores * group
    for at in range(0, pieces, 4):
        stop = min(at + 4, pieces)
        queries = stacked(query_refs[at:stop])
        mine = slice(at * rows, stop * rows)
        lane = lax.broadcasted_iota(jnp.int32, (queries.shape[0], DH), 1)
        stats = jnp.zeros((queries.shape[0], DH), jnp.float32)
        for head in range(half // DH):
            cols = slice(head * DH, (head + 1) * DH)
            scores, values = head_scores(queries, kv_refs, head)
            earlier = max_ref[mine, cols]
            maxima = along_lanes(jnp.max(scores, axis=-1, keepdims=True))
            maxima = jnp.maximum(earlier, maxima)
            weights = jnp.concatenate(weights_of(scores, maxima), axis=1)
            factor = jnp.exp(earlier - maxima)
            total = along_lanes(jnp.sum(weights, axis=-1, keepdims=True))
            total = total_ref[mine, cols] * factor + total
            weighted = sum_ref[mine, cols] * factor + jnp.dot(
                weights.astype(jnp.bfloat16), values, preferred_element_type=jnp.float32
            )
            stats = jnp.where(lane == 2 * head, maxima, stats)
            stats = jnp.where(lane == 2 * head + 1, total, stats)
            for j in range(at, stop):
                own = weighted[(j - at) * rows : (j - at + 1) * rows]
                out_refs[j][head * rows : (head + 1) * rows, :] = own
        for j in range(at, stop):
            own = stats[(j - at) * rows : (j - at + 1) * rows]
            out_refs[j][half // DH * rows :, :] = lanes_of(own)


def attend_last(after, first, queries, kv_parts):
    cores, group, half = queries[0].shape
    rows = cores * group
    return pl.pallas_call(
        functools.partial(attend_last_kernel, len(queries)),
        out_specs=[VMEM_SPEC] * (len(queries) + 1),
        out_shape=[pltpu.VMEM((half // DH * rows + 8, DH), jnp.float32)] * len(queries) + [TOKEN],
        compiler_params=pltpu.CompilerParams(vmem_limit_bytes=24 << 20),
        name="attend_last",
    )(after, *first, *queries, *kv_parts)


def column(stats, at):
    lane = lax.broadcasted_iota(jnp.int32, stats.shape, 1)
    return along_lanes(jnp.sum(jnp.where(lane == at, stats, 0.0), axis=-1, keepdims=True))


def combine_kernel(pieces, after_ref, *refs):
    part_refs, out_refs = refs[:pieces], refs[pieces:]
    group, half = out_refs[0].shape
    rows = group * len(out_refs)
    stats = [rows_of(ref[half // DH * rows :, :], rows) for ref in part_refs]
    for head in range(half // DH):
        cols = slice(head * DH, (head + 1) * DH)
        maxima = [column(stat, 2 * head) for stat in stats]
        top = functools.reduce(jnp.maximum, maxima)
        total = jnp.zeros_like(top)
        attended = jnp.zeros((rows, DH), jnp.float32)
        for ref, stat, maximum in zip(part_refs, stats, maxima):
            factor = jnp.exp(maximum - top)
            total = total + column(stat, 2 * head + 1) * factor
            attended = attended + ref[head * rows : (head + 1) * rows, :] * factor
        attended = attended / total
        for side, out_ref in enumerate(out_refs):
            out_ref[:, cols] = attended[side * group : (side + 1) * group].astype(jnp.bfloat16)


def combine(after, parts, group, pair):
    half = (parts[0].shape[0] - 8) // (group * pair) * DH
    return pl.pallas_call(
        functools.partial(combine_kernel, len(parts)),
        out_shape=[jax.ShapeDtypeStruct((group, half), jnp.bfloat16)] * pair,
        compiler_params=pltpu.CompilerParams(vmem_limit_bytes=16 << 20),
        name="combine",
    )(after, *parts)


def output_terms(side, pair, spread_ref, attended_ref, w_ref):
    group, half = attended_ref.shape
    width = w_ref.shape[1]
    attended = jnp.dot(
        spread_ref[:, :group], attended_ref[...], preferred_element_type=jnp.float32
    ).astype(jnp.bfloat16)
    start = pl.multiple_of((my_core(pair) ^ side) * half, DH)
    step = math.gcd(width, 1024)
    for col in range(0, width, step):
        cols = slice(col, col + step)
        yield cols, jnp.dot(
            attended, w_ref[pl.ds(start, half), cols], preferred_element_type=jnp.float32
        )


def output_first_kernel(pair, spread_ref, attended_ref, w_ref, out_ref):
    for cols, terms in output_terms(0, pair, spread_ref, attended_ref, w_ref):
        out_ref[:, cols] = terms


def output_first(spread, attended, w_out, pair):
    return pl.pallas_call(
        functools.partial(output_first_kernel, pair),
        out_specs=VMEM_SPEC,
        out_shape=pltpu.VMEM((spread.shape[0], w_out.shape[1]), jnp.float32),
        cost_estimate=pl.CostEstimate(flops=10**8, bytes_accessed=0, transcendentals=0),
        compiler_params=pltpu.CompilerParams(vmem_limit_bytes=16 << 20),
        name="output_first",
    )(spread, attended, w_out)


def output_last_kernel(pair, spread_ref, first_ref, *refs):
    *attended_refs, w_ref = refs[:pair]
    *out_refs, token_ref = refs[pair:]
    token_ref[...] = jnp.zeros_like(token_ref)
    slots = out_refs[0].shape[0]

    def write(cols, terms):
        for k, out_ref in enumerate(out_refs):
            out_ref[:, cols] = terms[k * slots : (k + 1) * slots].astype(out_ref.dtype)

    if not attended_refs:
        write(slice(None), first_ref[...])
    for attended_ref in attended_refs:
        for cols, terms in output_terms(1, pair, spread_ref, attended_ref, w_ref):
            write(cols, first_ref[:, cols] + terms)


def output_last(spread, first, others, w_out, slots, parts):
    width = w_out.shape[1]
    return pl.pallas_call(
        functools.partial(output_last_kernel, len(others) + 1),
        out_shape=[
            jax.ShapeDtypeStruct((slots, width), jnp.bfloat16 if k else jnp.float32)
            for k in range(parts)
        ]
        + [TOKEN],
        compiler_params=pltpu.CompilerParams(vmem_limit_bytes=16 << 20),
        name="output_last",
    )(spread, first, *others, w_out)


def mlp_kernel(pieces, *refs):
    row_refs, (up_ref, down_ref) = refs[:pieces], refs[pieces : pieces + 2]
    *out_refs, act_ref = refs[pieces + 2 :]
    hidden, width = down_ref.shape
    rows = [ref[j] for ref in row_refs for j in range(ref.shape[0])]
    rows = jnp.concatenate(rows, axis=0)
    count = out_refs[0].shape[0]
    step = math.gcd(hidden, 768)
    for col in range(0, hidden, step):
        lifted = jnp.dot(rows, up_ref[:, col : col + step], preferred_element_type=jnp.float32)
        act_ref[:, col : col + step] = jax.nn.gelu(lifted, approximate=True).astype(jnp.bfloat16)
    step = math.gcd(width, 1024)
    for col in range(0, width, step):
        down = jnp.dot(
            act_ref[...], down_ref[:, col : col + step], preferred_element_type=jnp.float32
        )
        for side, out_ref in enumerate(out_refs):
            piece = down[side * count : (side + 1) * count]
            out_ref[:, col : col + step] = piece.astype(out_ref.dtype)


def mlp(rows, w_up, w_down, pair):
    count = sum(x.shape[0] * x.shape[1] for x in rows)
    hidden, width = w_down.shape
    return pl.pallas_call(
        functools.partial(mlp_kernel, len(rows)),
        out_shape=[
            jax.ShapeDtypeStruct((count // pair, width), jnp.bfloat16 if side else jnp.float32)
            for side in range(pair)
        ],
        scratch_shapes=[pltpu.VMEM((count, hidden), jnp.bfloat16)],
        compiler_params=pltpu.CompilerParams(vmem_limit_bytes=32 << 20),
        name="mlp",
    )(*rows, w_up, w_down)


def join_kernel(count, *refs):
    part_refs, out_ref = refs[:count], refs[-1]
    for at, ref in enumerate(part_refs):
        out_ref[at] = ref[...]


def join(parts, after=()):
    return pl.pallas_call(
        functools.partial(join_kernel, len(parts)),
        out_shape=jax.ShapeDtypeStruct((len(parts), *parts[0].shape), parts[0].dtype),
        compiler_params=pltpu.CompilerParams(vmem_limit_bytes=8 << 20),
        name="join",
    )(*parts, *after)


def renorm_kernel(hold_ref, rows_ref, mod_ref, *refs):
    *term_refs, after_ref, normed_ref = refs
    branch = term_refs[0][...]
    for ref in term_refs[1:]:
        branch = branch + ref[...].astype(jnp.float32)
    after = rows_ref[...] + mod_ref[2:3, :] * branch
    after_ref[...] = after
    normed_ref[...] = layer_norm(after, mod_ref[3:4, :], mod_ref[4:5, :]).astype(jnp.bfloat16)


def renorm(after, rows_in, modulation, terms):
    return pl.pallas_call(
        renorm_kernel,
        out_shape=[
            jax.ShapeDtypeStruct(rows_in.shape, jnp.float32),
            jax.ShapeDtypeStruct(rows_in.shape, jnp.bfloat16),
        ],
        compiler_params=pltpu.CompilerParams(vmem_limit_bytes=8 << 20),
        name="renorm",
    )(after, rows_in, modulation, *terms)


def fold_kernel(sides, *refs):
    side_refs, out_refs = refs[:sides], refs[sides:]
    slots = out_refs[0].shape[0]
    for j, out_ref in enumerate(out_refs):
        total = side_refs[0][j * slots : (j + 1) * slots]
        for ref in side_refs[1:]:
            total = total + ref[j * slots : (j + 1) * slots].astype(jnp.float32)
        out_ref[...] = total.astype(out_ref.dtype)


def fold(sides, slots):
    count, width = sides[0].shape
    return pl.pallas_call(
        functools.partial(fold_kernel, len(sides)),
        out_shape=[
            jax.ShapeDtypeStruct((slots, width), jnp.bfloat16 if j else jnp.float32)
            for j in range(count // slots)
        ],
        compiler_params=pltpu.CompilerParams(vmem_limit_bytes=8 << 20),
        name="fold",
    )(*sides)


def finish_kernel(select_ref, cached_ref, after_ref, mod_ref, *refs):
    *term_refs, out_ref = refs
    total = term_refs[0][...]
    for ref in term_refs[1:]:
        total = total + ref[...].astype(jnp.float32)
    renewed = (after_ref[...] + mod_ref[5:6, :] * total).astype(jnp.bfloat16)
    select = select_ref[...]
    placed = jnp.dot(select, renewed, preferred_element_type=jnp.float32)
    covered = jnp.sum(select.astype(jnp.float32), axis=1, keepdims=True)
    blended = cached_ref[...].astype(jnp.float32) * (1.0 - covered) + placed
    out_ref[...] = blended.astype(jnp.bfloat16)


def finish(select, cached, after_attn, modulation, terms):
    return pl.pallas_call(
        finish_kernel,
        out_shape=jax.ShapeDtypeStruct(cached.shape, jnp.bfloat16),
        compiler_params=pltpu.CompilerParams(vmem_limit_bytes=8 << 20),
        name="finish",
    )(select, cached, after_attn, modulation, *terms)


def body(
    hidden_in,
    cached_out,
    cache_keys,
    cache_values,
    refresh_idx,
    modulation,
    q_gain,
    w_query,
    w_out,
    w_up,
    w_down,
):
    slots = refresh_idx.shape[0]
    uly_size = lax.axis_size("uly")
    blk_size = lax.axis_size("blk")
    local_heads = w_query.shape[1] // DH
    group = min(slots * uly_size, slots + (uly_size - 1) * OTHER)
    pair = 2 if blk_size % 2 == 0 and local_heads % 2 == 0 else 1
    chips = blk_size // pair

    rows_in, normed, select, modulation, sides = enter(
        refresh_idx, hidden_in, modulation, cache_keys, cache_values, uly_size, pair
    )
    sides = [trade(x, "blk", side) for side, x in enumerate(sides)]
    w_query, token = hold(normed, w_query)
    half_way = uly_size // 2
    cuts = [[half_way, 0], [k for k in range(uly_size) if k not in (0, half_way)]]
    first, token = merge_kv(sides, cuts[0], [token])
    group_rows = double(normed, "uly", 1, uly_size, {half_way: lambda x: relay(x, token)})
    second, token = merge_kv(sides, cuts[1], group_rows[1:])
    kv_parts = [trade(x, "uly", k) for k, x in zip(cuts[0] + cuts[1], first + second)]

    queries, spread, token = project(token, group_rows, w_query, q_gain, group, pair)
    w_out, token = hold(token, w_out)
    queries = [trade(x, "blk", side) for side, x in enumerate(queries)]
    queries = join(queries)
    queries = double(queries, "blk", pair, chips)
    first = attend_first(queries, kv_parts[:3])
    *parts, token = attend_last(token, first, queries, kv_parts[3:])
    w_up, token = hold(token, w_up)
    parts = far_first([trade(x, "blk", j * pair) for j, x in enumerate(parts)])
    attended = combine(token, parts, group, pair)
    mine, *others = attended
    others = [trade(x, "blk", 1) for x in others]
    terms = output_first(spread, mine, w_out, pair)
    *terms, token = output_last(spread, terms, others, w_out, slots, uly_size)
    w_down, cached, token = hold(token, w_down, cached_out)
    terms = far_first([trade(x, "uly", k) for k, x in enumerate(terms)])
    after_attn, norm_mlp = renorm(token, rows_in, modulation, terms)

    rows = [join([trade(norm_mlp, "blk", j * pair) for j in range(chips)])]
    if pair == 2:
        rows.append(trade(rows[0], "blk", 1))
    down = mlp(rows, w_up, w_down, pair)
    down = [trade(x, "blk", side) for side, x in enumerate(down)]
    terms = far_first([trade(x, "blk", j * pair) for j, x in enumerate(fold(down, slots))])
    return finish(select, cached, after_attn, modulation, terms)


def solution(mesh):
    return jax.shard_map(
        body,
        mesh=mesh,
        in_specs=(
            P(("blk", "uly"), None),
            P(("blk", "uly"), None),
            P(("blk", "uly"), None),
            P(("blk", "uly"), None),
            P(("blk", "uly")),
            P(),
            P(),
            P(None, "uly"),
            P("uly", None),
            P(None, "blk"),
            P("blk", None),
        ),
        out_specs=P(("blk", "uly"), None),
        check_vma=False,
    )
```

```python
import functools
import math

import jax
import jax.numpy as jnp
from jax import lax
from jax.experimental import pallas as pl
from jax.experimental.pallas import tpu as pltpu
from jax.sharding import PartitionSpec as P

DH = 128
OTHER = 8
VMEM_SPEC = pl.BlockSpec(memory_space=pltpu.VMEM)
TOKEN = pltpu.VMEM((8, DH), jnp.float32)
ANY_SPEC = pl.BlockSpec(memory_space=pl.ANY)


def far_first(parts):
    return parts[:1] + parts[:0:-1]


def double(x, axis, scale, count, on_arrival=()):
    have = {0: x}
    for k in sorted(range(1, count), key=lambda k: (bin(k).count("1"), -k)):
        low = k & -k
        have[k] = trade(have[k ^ low], axis, low * scale)
        if k in on_arrival:
            have[k] = on_arrival[k](have[k])
    return [have[k] for k in range(count)]


def layer_norm(row_block, shift_by, scale_by):
    average = jnp.mean(row_block, axis=-1, keepdims=True)
    centred = row_block - average
    spread = jnp.mean(centred * centred, axis=-1, keepdims=True)
    return centred * lax.rsqrt(spread + 1e-06) * (1.0 + scale_by) + shift_by


def trade(x, axis, flip):
    if flip == 0:
        return x
    return lax.ppermute(x, axis, [(i, i ^ flip) for i in range(lax.axis_size(axis))])


def in_hbm(x):
    return pltpu.with_memory_space_constraint(x, pltpu.HBM)


def hold_kernel(count, *refs):
    source_refs, sems = refs[1 : count + 1], refs[-1]
    *held_refs, token_ref = refs[count + 1 : -1]
    token_ref[...] = jnp.zeros_like(token_ref)
    copies = [
        pltpu.make_async_copy(source_ref, held_ref, sems.at[i])
        for i, (source_ref, held_ref) in enumerate(zip(source_refs, held_refs))
    ]
    for copy in copies:
        copy.start()
    for copy in copies:
        copy.wait()


def hold(after, *weights):
    count = len(weights)
    moved = sum(w.size * w.dtype.itemsize for w in weights)
    return pl.pallas_call(
        functools.partial(hold_kernel, count),
        in_specs=[VMEM_SPEC] + [ANY_SPEC] * count,
        out_specs=[VMEM_SPEC] * (count + 1),
        out_shape=[pltpu.VMEM(w.shape, w.dtype) for w in weights] + [TOKEN],
        scratch_shapes=[pltpu.SemaphoreType.DMA((count,))],
        cost_estimate=pl.CostEstimate(flops=0, bytes_accessed=moved, transcendentals=0),
        compiler_params=pltpu.CompilerParams(vmem_limit_bytes=2 << 20),
        name="hold",
    )(after, *[in_hbm(w) for w in weights])


def my_core(pair):
    return lax.rem(lax.axis_index("blk"), pair)


def enter_kernel(pair, idx_hbm, hidden_hbm, mod_hbm, key_hbm, value_hbm, *refs):
    rows_ref, normed_ref, select_ref, mod_ref, *side_refs = refs[: pair + 4]
    idx_ref, hidden_ref, sems, kv_sem = refs[pair + 4 :]
    copies = [
        pltpu.make_async_copy(source, target, sems.at[i])
        for i, (source, target) in enumerate(
            [(idx_hbm, idx_ref), (hidden_hbm, hidden_ref), (mod_hbm, mod_ref)]
        )
    ]
    for copy in copies:
        copy.start()
    parts, _, both = side_refs[0].shape
    half = both // 2
    uly, core = lax.axis_index("uly"), my_core(pair)
    kv_copies = []
    for side, side_ref in enumerate(side_refs):
        for flip in range(parts):
            start = pl.multiple_of(((uly ^ flip) * pair + (core ^ side)) * half, DH)
            for at, source in enumerate((key_hbm, value_hbm)):
                copy = pltpu.make_async_copy(
                    source.at[:, pl.ds(start, half)],
                    side_ref.at[flip, :, pl.ds(at * half, half)],
                    kv_sem.at[side, flip, at],
                )
                copy.start()
                kv_copies.append(copy)
    for copy in copies:
        copy.wait()
    tokens, width = hidden_ref.shape
    slots = idx_ref.shape[1]
    position = lax.broadcasted_iota(jnp.int32, (tokens, slots), 0)
    select = (position == idx_ref[...]).astype(jnp.float32).astype(jnp.bfloat16)
    select_ref[...] = select
    contract = (((0,), (0,)), ((), ()))
    rows = lax.dot_general(
        select, hidden_ref[...], contract, preferred_element_type=jnp.float32
    )
    live = lax.dot_general(
        select,
        jnp.ones((tokens, DH), jnp.bfloat16),
        contract,
        preferred_element_type=jnp.float32,
    )
    rows_ref[...] = rows
    normed = layer_norm(rows, mod_ref[0:1, :], mod_ref[1:2, :])
    normed_ref[:, :width] = normed.astype(jnp.bfloat16)
    normed_ref[:, width:] = live.astype(jnp.bfloat16)
    for copy in kv_copies:
        copy.wait()


def enter(refresh_idx, hidden_in, modulation, cache_keys, cache_values, parts, pair):
    slots = refresh_idx.shape[0]
    tokens, width = hidden_in.shape
    both = 2 * width // (parts * pair)
    out = pl.pallas_call(
        functools.partial(enter_kernel, pair),
        in_specs=[ANY_SPEC] * 5,
        out_specs=[VMEM_SPEC] * (pair + 4),
        out_shape=[
            pltpu.VMEM((slots, width), jnp.float32),
            pltpu.VMEM((slots, width + DH), jnp.bfloat16),
            pltpu.VMEM((tokens, slots), jnp.bfloat16),
            pltpu.VMEM(modulation.shape, modulation.dtype),
        ]
        + [pltpu.VMEM((parts, tokens, both), cache_keys.dtype)] * pair,
        scratch_shapes=[
            pltpu.VMEM((1, slots), jnp.int32),
            pltpu.VMEM(hidden_in.shape, hidden_in.dtype),
            pltpu.SemaphoreType.DMA((3,)),
            pltpu.SemaphoreType.DMA((pair, parts, 2)),
        ],
        compiler_params=pltpu.CompilerParams(vmem_limit_bytes=8 << 20),
        name="enter",
    )(
        *[
            in_hbm(x)
            for x in (refresh_idx.reshape(1, slots), hidden_in, modulation, cache_keys, cache_values)
        ]
    )
    return *out[:4], out[4:]


def merge_kv_kernel(sides, flips, *refs):
    *refs, token_ref = refs
    token_ref[...] = jnp.zeros_like(token_ref)
    for flip, out_ref in zip(flips, refs[-len(flips) :]):
        for side in range(sides):
            out_ref[side] = refs[side][flip]


def merge_kv(sides, flips, after):
    _, tokens, both = sides[0].shape
    *merged, token = pl.pallas_call(
        functools.partial(merge_kv_kernel, len(sides), flips),
        out_specs=[VMEM_SPEC] * (len(flips) + 1),
        out_shape=[pltpu.VMEM((len(sides), tokens, both), sides[0].dtype) for _ in flips]
        + [TOKEN],
        compiler_params=pltpu.CompilerParams(vmem_limit_bytes=8 << 20),
        name="merge_kv",
    )(*sides, *after)
    return merged, token


def relay_kernel(x_ref, after_ref, out_ref):
    out_ref[...] = x_ref[...]


def relay(x, after):
    return pl.pallas_call(
        relay_kernel,
        out_specs=VMEM_SPEC,
        out_shape=pltpu.VMEM(x.shape, x.dtype),
        compiler_params=pltpu.CompilerParams(vmem_limit_bytes=2 << 20),
        name="relay",
    )(x, after)


def project_kernel(pieces, after_ref, *refs):
    rows_refs, (w_ref, gain_hbm_ref) = refs[:pieces], refs[pieces : pieces + 2]
    *query_refs, spread_ref, token_ref, heads_ref, gain_ref, sem = refs[pieces + 2 :]
    token_ref[...] = jnp.zeros_like(token_ref)
    copy = pltpu.make_async_copy(gain_hbm_ref, gain_ref, sem)
    copy.start()
    core = my_core(len(query_refs))
    width = w_ref.shape[0]
    group, half = query_refs[0].shape
    rows = jnp.concatenate([ref[...] for ref in rows_refs], axis=0)
    everyone = rows.shape[0]
    flags = rows[:, width:]
    shape = (everyone, everyone)
    before = lax.broadcasted_iota(jnp.int32, shape, 1) < lax.broadcasted_iota(jnp.int32, shape, 0)
    before = before.astype(jnp.float32).astype(jnp.bfloat16)
    rank = jnp.dot(before, flags, preferred_element_type=jnp.float32)
    lane = lax.broadcasted_iota(jnp.int32, rank.shape, 1).astype(jnp.float32)
    spread = jnp.where((rank == lane) & (flags.astype(jnp.float32) > 0.0), 1.0, 0.0)
    spread = spread.astype(jnp.bfloat16)
    spread_ref[...] = spread
    live_rows = lax.dot_general(
        spread[:, :group],
        rows[:, :width],
        (((0,), (0,)), ((), ())),
        preferred_element_type=jnp.float32,
    ).astype(jnp.bfloat16)
    projected = jnp.dot(live_rows, w_ref[...], preferred_element_type=jnp.float32)
    copy.wait()
    for start in range(0, projected.shape[1], DH):
        head = projected[:, start : start + DH]
        squares = jnp.mean(head * head, axis=-1, keepdims=True)
        heads_ref[:, start : start + DH] = (
            head * lax.rsqrt(squares + 1e-06) * (gain_ref[...] / math.sqrt(DH))
        )
    for side, query_ref in enumerate(query_refs):
        start = pl.multiple_of((core ^ side) * half, DH)
        query_ref[...] = heads_ref[:, pl.ds(start, half)].astype(jnp.bfloat16)


def project(after, rows, w_query, q_gain, group, pair):
    half = w_query.shape[1] // pair
    everyone = len(rows) * rows[0].shape[0]
    query = jax.ShapeDtypeStruct((group, half), jnp.bfloat16)
    out = pl.pallas_call(
        functools.partial(project_kernel, len(rows)),
        in_specs=[VMEM_SPEC] * (len(rows) + 2) + [ANY_SPEC],
        out_shape=[query] * pair + [jax.ShapeDtypeStruct((everyone, DH), jnp.bfloat16), TOKEN],
        scratch_shapes=[
            pltpu.VMEM((group, w_query.shape[1]), jnp.float32),
            pltpu.VMEM((1, DH), jnp.float32),
            pltpu.SemaphoreType.DMA,
        ],
        compiler_params=pltpu.CompilerParams(vmem_limit_bytes=16 << 20),
        name="project",
    )(after, *rows, w_query, in_hbm(q_gain.reshape(1, DH)))
    return out[:-2], out[-2], out[-1]


def head_scores(queries, kv_refs, head):
    half = queries.shape[1]
    cols = slice(head * DH, (head + 1) * DH)
    vals = slice(half + head * DH, half + (head + 1) * DH)
    sides = kv_refs[0].shape[0]
    keys = [ref[side, :, cols] for ref in kv_refs for side in range(sides)]
    values = [ref[side, :, vals] for ref in kv_refs for side in range(sides)]
    scores = lax.dot_general(
        queries[:, cols],
        jnp.concatenate(keys, axis=0),
        (((1,), (1,)), ((), ())),
        preferred_element_type=jnp.float32,
    )
    return scores, jnp.concatenate(values, axis=0)


def lanes_of(stats):
    packed = stats[:8]
    for at in range(8, stats.shape[0], 8):
        packed = packed + pltpu.roll(stats[at : at + 8], at, axis=1)
    return packed


def rows_of(packed, rows):
    parts = [packed] + [pltpu.roll(packed, DH - at, axis=1) for at in range(8, rows, 8)]
    return jnp.concatenate(parts, axis=0)


def stacked(refs):
    rows = [ref[core].astype(jnp.float32) for ref in refs for core in range(ref.shape[0])]
    return jnp.concatenate(rows, axis=0).astype(jnp.bfloat16)


def along_lanes(column):
    return jnp.broadcast_to(column, (column.shape[0], DH))


def weights_of(scores, maxima):
    width = scores.shape[1]
    return [jnp.exp(scores[:, at : at + DH] - maxima) for at in range(0, width, DH)]


def attend_first_kernel(pieces, *refs):
    query_refs, (*kv_refs, sum_ref, max_ref, total_ref) = refs[:pieces], refs[pieces:]
    cores, group, half = query_refs[0].shape
    rows = cores * group
    for at in range(0, pieces, 4):
        queries = stacked(query_refs[at : at + 4])
        mine = slice(at * rows, at * rows + queries.shape[0])
        for head in range(half // DH):
            cols = slice(head * DH, (head + 1) * DH)
            scores, values = head_scores(queries, kv_refs, head)
            maxima = along_lanes(jnp.max(scores, axis=-1, keepdims=True))
            weights = jnp.concatenate(weights_of(scores, maxima), axis=1)
            max_ref[mine, cols] = maxima
            total_ref[mine, cols] = along_lanes(jnp.sum(weights, axis=-1, keepdims=True))
            sum_ref[mine, cols] = jnp.dot(
                weights.astype(jnp.bfloat16), values, preferred_element_type=jnp.float32
            )


def attend_first(queries, kv_parts):
    cores, group, half = queries[0].shape
    count = cores * group * len(queries)
    return pl.pallas_call(
        functools.partial(attend_first_kernel, len(queries)),
        out_specs=[VMEM_SPEC] * 3,
        out_shape=[pltpu.VMEM((count, half), jnp.float32)] * 3,
        cost_estimate=pl.CostEstimate(flops=0, bytes_accessed=0, transcendentals=0),
        compiler_params=pltpu.CompilerParams(vmem_limit_bytes=24 << 20),
        name="attend_first",
    )(*queries, *kv_parts)


def attend_last_kernel(pieces, after_ref, sum_ref, max_ref, total_ref, *refs):
    *refs, token_ref = refs
    token_ref[...] = jnp.zeros_like(token_ref)
    query_refs, kv_refs, out_refs = refs[:pieces], refs[pieces:-pieces], refs[-pieces:]
    cores, group, half = query_refs[0].shape
    rows = cores * group
    for at in range(0, pieces, 4):
        stop = min(at + 4, pieces)
        queries = stacked(query_refs[at:stop])
        mine = slice(at * rows, stop * rows)
        lane = lax.broadcasted_iota(jnp.int32, (queries.shape[0], DH), 1)
        stats = jnp.zeros((queries.shape[0], DH), jnp.float32)
        for head in range(half // DH):
            cols = slice(head * DH, (head + 1) * DH)
            scores, values = head_scores(queries, kv_refs, head)
            earlier = max_ref[mine, cols]
            maxima = along_lanes(jnp.max(scores, axis=-1, keepdims=True))
            maxima = jnp.maximum(earlier, maxima)
            weights = jnp.concatenate(weights_of(scores, maxima), axis=1)
            factor = jnp.exp(earlier - maxima)
            total = along_lanes(jnp.sum(weights, axis=-1, keepdims=True))
            total = total_ref[mine, cols] * factor + total
            weighted = sum_ref[mine, cols] * factor + jnp.dot(
                weights.astype(jnp.bfloat16), values, preferred_element_type=jnp.float32
            )
            stats = jnp.where(lane == 2 * head, maxima, stats)
            stats = jnp.where(lane == 2 * head + 1, total, stats)
            for j in range(at, stop):
                own = weighted[(j - at) * rows : (j - at + 1) * rows]
                out_refs[j][head * rows : (head + 1) * rows, :] = own
        for j in range(at, stop):
            own = stats[(j - at) * rows : (j - at + 1) * rows]
            out_refs[j][half // DH * rows :, :] = lanes_of(own)


def attend_last(after, first, queries, kv_parts):
    cores, group, half = queries[0].shape
    rows = cores * group
    return pl.pallas_call(
        functools.partial(attend_last_kernel, len(queries)),
        out_specs=[VMEM_SPEC] * (len(queries) + 1),
        out_shape=[pltpu.VMEM((half // DH * rows + 8, DH), jnp.float32)] * len(queries) + [TOKEN],
        compiler_params=pltpu.CompilerParams(vmem_limit_bytes=24 << 20),
        name="attend_last",
    )(after, *first, *queries, *kv_parts)


def column(stats, at):
    lane = lax.broadcasted_iota(jnp.int32, stats.shape, 1)
    return along_lanes(jnp.sum(jnp.where(lane == at, stats, 0.0), axis=-1, keepdims=True))


def combine_kernel(pieces, after_ref, *refs):
    part_refs, out_refs = refs[:pieces], refs[pieces:]
    group, half = out_refs[0].shape
    rows = group * len(out_refs)
    stats = [rows_of(ref[half // DH * rows :, :], rows) for ref in part_refs]
    for head in range(half // DH):
        cols = slice(head * DH, (head + 1) * DH)
        maxima = [column(stat, 2 * head) for stat in stats]
        top = functools.reduce(jnp.maximum, maxima)
        total = jnp.zeros_like(top)
        attended = jnp.zeros((rows, DH), jnp.float32)
        for ref, stat, maximum in zip(part_refs, stats, maxima):
            factor = jnp.exp(maximum - top)
            total = total + column(stat, 2 * head + 1) * factor
            attended = attended + ref[head * rows : (head + 1) * rows, :] * factor
        attended = attended / total
        for side, out_ref in enumerate(out_refs):
            out_ref[:, cols] = attended[side * group : (side + 1) * group].astype(jnp.bfloat16)


def combine(after, parts, group, pair):
    half = (parts[0].shape[0] - 8) // (group * pair) * DH
    return pl.pallas_call(
        functools.partial(combine_kernel, len(parts)),
        out_shape=[jax.ShapeDtypeStruct((group, half), jnp.bfloat16)] * pair,
        compiler_params=pltpu.CompilerParams(vmem_limit_bytes=16 << 20),
        name="combine",
    )(after, *parts)


def output_terms(side, pair, spread_ref, attended_ref, w_ref):
    group, half = attended_ref.shape
    width = w_ref.shape[1]
    attended = jnp.dot(
        spread_ref[:, :group], attended_ref[...], preferred_element_type=jnp.float32
    ).astype(jnp.bfloat16)
    start = pl.multiple_of((my_core(pair) ^ side) * half, DH)
    step = math.gcd(width, 1024)
    for col in range(0, width, step):
        cols = slice(col, col + step)
        yield cols, jnp.dot(
            attended, w_ref[pl.ds(start, half), cols], preferred_element_type=jnp.float32
        )


def output_first_kernel(pair, spread_ref, attended_ref, w_ref, out_ref):
    for cols, terms in output_terms(0, pair, spread_ref, attended_ref, w_ref):
        out_ref[:, cols] = terms


def output_first(spread, attended, w_out, pair):
    return pl.pallas_call(
        functools.partial(output_first_kernel, pair),
        out_specs=VMEM_SPEC,
        out_shape=pltpu.VMEM((spread.shape[0], w_out.shape[1]), jnp.float32),
        cost_estimate=pl.CostEstimate(flops=10**8, bytes_accessed=0, transcendentals=0),
        compiler_params=pltpu.CompilerParams(vmem_limit_bytes=16 << 20),
        name="output_first",
    )(spread, attended, w_out)


def output_last_kernel(pair, spread_ref, first_ref, *refs):
    *attended_refs, w_ref = refs[:pair]
    *out_refs, token_ref = refs[pair:]
    token_ref[...] = jnp.zeros_like(token_ref)
    slots = out_refs[0].shape[0]

    def write(cols, terms):
        for k, out_ref in enumerate(out_refs):
            out_ref[:, cols] = terms[k * slots : (k + 1) * slots].astype(out_ref.dtype)

    if not attended_refs:
        write(slice(None), first_ref[...])
    for attended_ref in attended_refs:
        for cols, terms in output_terms(1, pair, spread_ref, attended_ref, w_ref):
            write(cols, first_ref[:, cols] + terms)


def output_last(spread, first, others, w_out, slots, parts):
    width = w_out.shape[1]
    return pl.pallas_call(
        functools.partial(output_last_kernel, len(others) + 1),
        out_shape=[
            jax.ShapeDtypeStruct((slots, width), jnp.bfloat16 if k else jnp.float32)
            for k in range(parts)
        ]
        + [TOKEN],
        compiler_params=pltpu.CompilerParams(vmem_limit_bytes=16 << 20),
        name="output_last",
    )(spread, first, *others, w_out)


def mlp_kernel(pieces, *refs):
    row_refs, (up_ref, down_ref) = refs[:pieces], refs[pieces : pieces + 2]
    *out_refs, act_ref = refs[pieces + 2 :]
    hidden, width = down_ref.shape
    rows = [ref[j] for ref in row_refs for j in range(ref.shape[0])]
    rows = jnp.concatenate(rows, axis=0)
    count = out_refs[0].shape[0]
    step = math.gcd(hidden, 768)
    for col in range(0, hidden, step):
        lifted = jnp.dot(rows, up_ref[:, col : col + step], preferred_element_type=jnp.float32)
        act_ref[:, col : col + step] = jax.nn.gelu(lifted, approximate=True).astype(jnp.bfloat16)
    step = math.gcd(width, 1024)
    for col in range(0, width, step):
        down = jnp.dot(
            act_ref[...], down_ref[:, col : col + step], preferred_element_type=jnp.float32
        )
        for side, out_ref in enumerate(out_refs):
            piece = down[side * count : (side + 1) * count]
            out_ref[:, col : col + step] = piece.astype(out_ref.dtype)


def mlp(rows, w_up, w_down, pair):
    count = sum(x.shape[0] * x.shape[1] for x in rows)
    hidden, width = w_down.shape
    return pl.pallas_call(
        functools.partial(mlp_kernel, len(rows)),
        out_shape=[
            jax.ShapeDtypeStruct((count // pair, width), jnp.bfloat16 if side else jnp.float32)
            for side in range(pair)
        ],
        scratch_shapes=[pltpu.VMEM((count, hidden), jnp.bfloat16)],
        compiler_params=pltpu.CompilerParams(vmem_limit_bytes=32 << 20),
        name="mlp",
    )(*rows, w_up, w_down)


def join_kernel(count, *refs):
    part_refs, out_ref = refs[:count], refs[-1]
    for at, ref in enumerate(part_refs):
        out_ref[at] = ref[...]


def join(parts, after=()):
    return pl.pallas_call(
        functools.partial(join_kernel, len(parts)),
        out_shape=jax.ShapeDtypeStruct((len(parts), *parts[0].shape), parts[0].dtype),
        compiler_params=pltpu.CompilerParams(vmem_limit_bytes=8 << 20),
        name="join",
    )(*parts, *after)


def renorm_kernel(hold_ref, rows_ref, mod_ref, *refs):
    *term_refs, after_ref, normed_ref = refs
    branch = term_refs[0][...]
    for ref in term_refs[1:]:
        branch = branch + ref[...].astype(jnp.float32)
    after = rows_ref[...] + mod_ref[2:3, :] * branch
    after_ref[...] = after
    normed_ref[...] = layer_norm(after, mod_ref[3:4, :], mod_ref[4:5, :]).astype(jnp.bfloat16)


def renorm(after, rows_in, modulation, terms):
    return pl.pallas_call(
        renorm_kernel,
        out_shape=[
            jax.ShapeDtypeStruct(rows_in.shape, jnp.float32),
            jax.ShapeDtypeStruct(rows_in.shape, jnp.bfloat16),
        ],
        compiler_params=pltpu.CompilerParams(vmem_limit_bytes=8 << 20),
        name="renorm",
    )(after, rows_in, modulation, *terms)


def fold_kernel(sides, *refs):
    side_refs, out_refs = refs[:sides], refs[sides:]
    slots = out_refs[0].shape[0]
    for j, out_ref in enumerate(out_refs):
        total = side_refs[0][j * slots : (j + 1) * slots]
        for ref in side_refs[1:]:
            total = total + ref[j * slots : (j + 1) * slots].astype(jnp.float32)
        out_ref[...] = total.astype(out_ref.dtype)


def fold(sides, slots):
    count, width = sides[0].shape
    return pl.pallas_call(
        functools.partial(fold_kernel, len(sides)),
        out_shape=[
            jax.ShapeDtypeStruct((slots, width), jnp.bfloat16 if j else jnp.float32)
            for j in range(count // slots)
        ],
        compiler_params=pltpu.CompilerParams(vmem_limit_bytes=8 << 20),
        name="fold",
    )(*sides)


def finish_kernel(select_ref, cached_ref, after_ref, mod_ref, *refs):
    *term_refs, out_hbm, out_ref, sems = refs
    select = select_ref[...]
    kept = 1.0 - jnp.sum(select.astype(jnp.float32), axis=1, keepdims=True)
    count = sems.shape[0]
    step = out_ref.shape[1] // count
    copies = []
    for block in range(count):
        cols = slice(block * step, (block + 1) * step)
        total = term_refs[0][:, cols]
        for ref in term_refs[1:]:
            total = total + ref[:, cols].astype(jnp.float32)
        renewed = (after_ref[:, cols] + mod_ref[5:6, cols] * total).astype(jnp.bfloat16)
        placed = jnp.dot(select, renewed, preferred_element_type=jnp.float32)
        blended = cached_ref[:, cols].astype(jnp.float32) * kept + placed
        out_ref[:, cols] = blended.astype(jnp.bfloat16)
        copy = pltpu.make_async_copy(out_ref.at[:, cols], out_hbm.at[:, cols], sems.at[block])
        copy.start()
        copies.append(copy)
    for copy in copies:
        copy.wait()


def finish(select, cached, after_attn, modulation, terms):
    return pl.pallas_call(
        finish_kernel,
        out_specs=ANY_SPEC,
        out_shape=jax.ShapeDtypeStruct(cached.shape, jnp.bfloat16),
        scratch_shapes=[pltpu.VMEM(cached.shape, jnp.bfloat16), pltpu.SemaphoreType.DMA((4,))],
        compiler_params=pltpu.CompilerParams(vmem_limit_bytes=8 << 20),
        name="finish",
    )(select, cached, after_attn, modulation, *terms)


def body(
    hidden_in,
    cached_out,
    cache_keys,
    cache_values,
    refresh_idx,
    modulation,
    q_gain,
    w_query,
    w_out,
    w_up,
    w_down,
):
    slots = refresh_idx.shape[0]
    uly_size = lax.axis_size("uly")
    blk_size = lax.axis_size("blk")
    local_heads = w_query.shape[1] // DH
    group = min(slots * uly_size, slots + (uly_size - 1) * OTHER)
    pair = 2 if blk_size % 2 == 0 and local_heads % 2 == 0 else 1
    chips = blk_size // pair

    rows_in, normed, select, modulation, sides = enter(
        refresh_idx, hidden_in, modulation, cache_keys, cache_values, uly_size, pair
    )
    sides = [trade(x, "blk", side) for side, x in enumerate(sides)]
    w_query, token = hold(normed, w_query)
    half_way = uly_size // 2
    cuts = [[half_way, 0], [k for k in range(uly_size) if k not in (0, half_way)]]
    first, token = merge_kv(sides, cuts[0], [token])
    group_rows = double(normed, "uly", 1, uly_size, {half_way: lambda x: relay(x, token)})
    second, token = merge_kv(sides, cuts[1], group_rows[1:])
    kv_parts = [trade(x, "uly", k) for k, x in zip(cuts[0] + cuts[1], first + second)]

    queries, spread, token = project(token, group_rows, w_query, q_gain, group, pair)
    w_out, token = hold(token, w_out)
    queries = [trade(x, "blk", side) for side, x in enumerate(queries)]
    queries = join(queries)
    queries = double(queries, "blk", pair, chips)
    first = attend_first(queries, kv_parts[:2])
    *parts, token = attend_last(token, first, queries, kv_parts[2:])
    w_up, token = hold(token, w_up)
    parts = far_first([trade(x, "blk", j * pair) for j, x in enumerate(parts)])
    attended = combine(token, parts, group, pair)
    mine, *others = attended
    others = [trade(x, "blk", 1) for x in others]
    terms = output_first(spread, mine, w_out, pair)
    *terms, token = output_last(spread, terms, others, w_out, slots, uly_size)
    w_down, cached, token = hold(token, w_down, cached_out)
    terms = far_first([trade(x, "uly", k) for k, x in enumerate(terms)])
    after_attn, norm_mlp = renorm(token, rows_in, modulation, terms)

    rows = [join([trade(norm_mlp, "blk", j * pair) for j in range(chips)])]
    if pair == 2:
        rows.append(trade(rows[0], "blk", 1))
    down = mlp(rows, w_up, w_down, pair)
    down = [trade(x, "blk", side) for side, x in enumerate(down)]
    terms = far_first([trade(x, "blk", j * pair) for j, x in enumerate(fold(down, slots))])
    return finish(select, cached, after_attn, modulation, terms)


def solution(mesh):
    return jax.shard_map(
        body,
        mesh=mesh,
        in_specs=(
            P(("blk", "uly"), None),
            P(("blk", "uly"), None),
            P(("blk", "uly"), None),
            P(("blk", "uly"), None),
            P(("blk", "uly")),
            P(),
            P(),
            P(None, "uly"),
            P("uly", None),
            P(None, "blk"),
            P("blk", None),
        ),
        out_specs=P(("blk", "uly"), None),
        check_vma=False,
    )
```
